32 devices in a mesh: ev: 8 (over y, x, core), neg: 4 (over z).
Axes of the slice: x: 2, y: 2, z: 4, core: 2. Of those that a mesh axis runs over, the one named last changes fastest.
Arguments:
- master: float32 [308224], P(('ev', 'neg'))
- first_moment: float32 [308224], P(('ev', 'neg'))
- second_moment: float32 [308224], P(('ev', 'neg')), as said below
- memory: float32 [2048, 100], P(('ev', 'neg')), may hold values from -3 to 3
- messages: bfloat16 [2048, 486], P(('ev', 'neg')), may hold values from -6 to 6
- static_ids: int32 [2048], P(('ev', 'neg')), may hold values from 0 to 1023
- node_features: bfloat16 [1024, 413], replicated, may hold values from -6 to 6
- neighbours: int32 [2048, 10], replicated, may hold values from 0 to 2047
- neighbour_times: float32 [2048, 10], replicated, may hold values from 0 to 100
- last_partner: int32 [2048], P(('ev', 'neg')), may hold values from 0 to 2047
- last_deltas: float32 [2048], P(('ev', 'neg')), may hold values from 0 to 50
- last_edges: bfloat16 [2048, 186], P(('ev', 'neg')), may hold values from -6 to 6
- sources: int32 [8192], P(('ev', 'neg')), may hold values from 0 to 2047
- targets: int32 [8192], P(('ev', 'neg')), may hold values from 0 to 2047
- times: float32 [8192], P('ev'), may hold values from 0 to 100
- negatives: int32 [8192, 4], P('ev', 'neg'), may hold values from 0 to 2047
- neg_counts: int32 [8192], P('ev'), may hold values from 1 to 4, as said below
Outputs:
- loss: float32 [], replicated
- neg_total: float32 [], replicated
- new_master: float32 [308224], P(('ev', 'neg'))
- new_first: float32 [308224], P(('ev', 'neg'))
- new_second: float32 [308224], P(('ev', 'neg'))
- new_memory: float32 [2048, 100], P(('ev', 'neg'))
- new_messages: float32 [2048, 486], P(('ev', 'neg'))
The draws below stay inside these ranges and needn't reach their ends.
Inputs may be any that keep to these rules, and one draw needn't show every extreme that they name: `neg_counts`: each event's count is at least 1 and at most 4; the first event has 1 and the last 4. `second_moment`: second moments are positive.
All inputs are finite; a program needn't handle non-finite values.
Results may differ from the reference program's by a relative error of at most 0.00085.
The reference program's roundings to bfloat16 on the way count: a program that leaves them out, or rounds other values in their place, can miss the bound.
Values may be sent and summed in bfloat16 or wider, within the bound.
No kernel may reach another device: no remote copies, remote signals or barrier semaphores. Data moves between devices by JAX's collectives and lax.ppermute only.
A program may use at most 256 MiB of HBM per device.

```python
import math
import jax
import jax.numpy as jnp
import numpy as np
from jax import lax

D = 100
TE = 100
EF = 186
NF = 413
PH = 100
HEADS = 2
NBR = 10
STEP = 10
FEATROWS = 1024
HS = 50
MSG = 486
NODES = 2048
EVENTS = 8192
NNEG = 4
PLIVE = 308101
PARAMS = 308224


def draw_master(key, part):
    key = jax.random.fold_in(key, 1)
    entries = [(MSG * 3 * D, MSG ** (-0.5)), (D * 3 * D, D ** (-0.5)), (6 * D, 0.3), (NF * D, NF ** (-0.5)), (TE, -1.0), (TE, -2.0), ((D + TE) * D, (D + TE) ** (-0.5)), ((D + TE) * 2 * D, (D + TE) ** (-0.5)), (D * D, 2.0 * D ** (-0.5)), (D * PH, D ** (-0.5)), (D * PH, D ** (-0.5)), (PH, 0.3), (PH, 2.0 * PH ** (-0.5)), (1, 0.5)]
    pieces = []
    for index, (amount, scale) in enumerate(entries):
        subkey = jax.random.fold_in(key, index)
        if scale == -1.0:
            pieces.append(jnp.exp(jax.random.uniform(subkey, (amount,), jnp.float32, math.log(0.02), 0.0)))
        elif scale == -2.0:
            pieces.append(jax.random.uniform(subkey, (amount,), jnp.float32, -math.pi, math.pi))
        else:
            pieces.append(scale * jax.random.normal(subkey, (amount,), jnp.float32))
    live = jnp.concatenate(pieces)
    return jnp.concatenate([live, jnp.zeros((PARAMS - PLIVE,), jnp.float32)])


def draw_first_moment(key, part):
    key = jax.random.fold_in(key, 2)
    scale = 0.111 * 0.5 / math.sqrt(EVENTS)
    return scale * jax.random.normal(key, (PARAMS,), jnp.float32)


def draw_second_moment(key, part):
    key = jax.random.fold_in(key, 3)
    scale = 0.001 * 0.25 / EVENTS
    return scale * jax.random.uniform(key, (PARAMS,), jnp.float32, 1.0, 4.0)


def draw_neg_counts(key, part):
    key = jax.random.fold_in(key, 4)
    rows = jnp.arange(EVENTS, dtype=jnp.int32)
    caps = 1 + (NNEG - 1) * (EVENTS + 2 * rows) // (3 * EVENTS)
    raw = jax.random.randint(key, (EVENTS,), 0, 1 << 20, dtype=jnp.int32)
    counts = 1 + raw % caps
    counts = counts.at[0].set(1).at[EVENTS - 1].set(NNEG)
    return counts.astype(jnp.int32)


def set_ends(drawn, rng, low, high):
    shape = drawn.shape
    spot = [jax.random.randint(jax.random.fold_in(rng, axis), (), 0, shape[axis]) for axis in range(len(shape))]
    drawn = drawn.at[tuple(spot)].set(low)
    longest = shape.index(max(shape))
    spot[longest] = (spot[longest] + 1) % shape[longest]
    return drawn.at[tuple(spot)].set(high)


def block_levels(key, dims, cuts, smallest, top_value):
    level = 1.0
    for axis_at, parts in cuts:
        draws = jax.random.uniform(jax.random.fold_in(jax.random.fold_in(key, 6), axis_at), (parts,), jnp.float32, smallest / len(cuts), top_value / len(cuts))
        level = level * jnp.repeat(jnp.exp(draws), dims[axis_at] // parts).reshape((-1,) + (1,) * (len(dims) - 1 - axis_at))
    return level


def rank_bounds(count, lean):
    loads = [(1 << 20) // math.isqrt(standing ** lean) + 1 for standing in range(1, count + 1)]
    deviation = 1 + sum(loads) // (1 << 30)
    return np.cumsum(np.array([max(1, weight // deviation) for weight in loads]))


def ranked(key, dims, number_of, skew):
    grid = rank_bounds(number_of, skew)
    lot = jax.random.randint(jax.random.fold_in(key, 1), dims, 0, int(grid[number_of - 1]))
    grade = jnp.searchsorted(jnp.asarray(grid, jnp.int32), lot, side="right")
    return jax.random.permutation(jax.random.fold_in(key, 2), number_of)[grade].astype(jnp.int32)


def noise(own_key, dims, spread, limit, cuts=(), kind=jnp.bfloat16):
    factor_of = block_levels(own_key, dims, cuts, -0.22, 0.18) if cuts else 1.0
    array = jax.random.normal(own_key, dims, jnp.float32) * spread * factor_of
    return jnp.minimum(jnp.maximum(array, -limit), limit).astype(kind)


def setup_inputs(seed: int = 0) -> dict:
    splits = jax.random.split(jax.random.key(seed), 18)
    return {
        "master": draw_master(jax.random.fold_in(splits[17], 71), 0),
        "first_moment": draw_first_moment(jax.random.fold_in(splits[17], 71), 0),
        "second_moment": draw_second_moment(jax.random.fold_in(splits[17], 71), 0),
        "memory": noise(splits[3], (NODES, D), 0.5, 3.0, ((0, 32),), jnp.float32),
        "messages": noise(splits[4], (NODES, MSG), 1.0, 6.0, ((0, 32),)),
        "static_ids": set_ends(jax.random.randint(splits[5], (NODES,), 0, FEATROWS), jax.random.fold_in(splits[5], 1), 0, FEATROWS - 1).astype(jnp.int32),
        "node_features": noise(splits[6], (FEATROWS, NF), 1.0, 6.0),
        "neighbours": set_ends(jax.random.randint(splits[7], (NODES, NBR), 0, NODES), jax.random.fold_in(splits[7], 1), 0, NODES - 1).astype(jnp.int32),
        "neighbour_times": jnp.clip(jax.random.uniform(splits[8], (NODES, NBR), jnp.float32, 0.0, 100.0), 0.0, 100.0),
        "last_partner": set_ends(jax.random.randint(splits[9], (NODES,), 0, NODES), jax.random.fold_in(splits[9], 1), 0, NODES - 1).astype(jnp.int32),
        "last_deltas": jnp.clip(50.0 * jax.random.uniform(splits[10], (NODES,), jnp.float32) ** block_levels(splits[10], (NODES,), ((0, 32),), -0.2, 0.2), 0.0, 50.0),
        "last_edges": noise(splits[11], (NODES, EF), 1.0, 6.0, ((0, 32),)),
        "sources": set_ends(ranked(splits[12], (EVENTS,), NODES, 2), jax.random.fold_in(splits[12], 3), 0, NODES - 1).astype(jnp.int32),
        "targets": set_ends(ranked(splits[13], (EVENTS,), NODES, 2), jax.random.fold_in(splits[13], 3), 0, NODES - 1).astype(jnp.int32),
        "times": jnp.clip(100.0 * jax.random.uniform(splits[14], (EVENTS,), jnp.float32) ** block_levels(splits[14], (EVENTS,), ((0, 8),), -0.2, 0.2), 0.0, 100.0),
        "negatives": set_ends(jax.random.randint(splits[15], (EVENTS, NNEG), 0, NODES), jax.random.fold_in(splits[15], 1), 0, NODES - 1).astype(jnp.int32),
        "neg_counts": draw_neg_counts(jax.random.fold_in(splits[17], 71), 0),
    }


@jax.custom_vjp
def low(v):
    return lax.optimization_barrier(v.astype(jnp.bfloat16)).astype(jnp.float32)

@jax.custom_vjp
def low_back(v):
    return v

def low_keep(v):
    return (low(v), None)

def low_pass(kept, grad):
    return (grad,)

def back_keep(v):
    return (v, None)

def back_low(kept, grad):
    return (low(grad),)
low.defvjp(low_keep, low_pass)
low_back.defvjp(back_keep, back_low)
beta_one = 0.9
beta_two = 0.999
rate_lr = 0.02
decay_wd = 0.01
eps_adam = 1e-08

def product(left, right):
    return jnp.dot(left, right, precision=lax.Precision.HIGHEST)

def unpack(flat):
    layout = [('w_gi', (MSG, 3 * D)), ('w_gh', (D, 3 * D)), ('b_g', (2, 3 * D)), ('w_feat', (NF, D)), ('w_time', (TE,)), ('b_time', (TE,)), ('w_query', (D + TE, D)), ('w_kv', (D + TE, 2 * D)), ('w_out', (D, D)), ('w_ps', (D, PH)), ('w_pd', (D, PH)), ('b_p1', (PH,)), ('w_p2', (PH,)), ('b_p2', (1,))]
    params = {}
    offset = 0
    for label, shape in layout:
        amount = math.prod(shape)
        params[label] = flat[offset:offset + amount].reshape(shape)
        offset += amount
    return params

def time_code(deltas, params):
    return jnp.cos(deltas[..., None] * params['w_time'] + params['b_time'])

def owner_pass(params, memory, messages, features):
    inputs = product(messages, params['w_gi']) + params['b_g'][0]
    hidden = product(low(memory), params['w_gh']) + params['b_g'][1]
    reset = jax.nn.sigmoid(inputs[:, :D] + hidden[:, :D])
    update = jax.nn.sigmoid(inputs[:, D:2 * D] + hidden[:, D:2 * D])
    candidate = jnp.tanh(inputs[:, 2 * D:] + reset * hidden[:, 2 * D:])
    renewed = (1.0 - update) * candidate + update * memory
    return (renewed + product(features, params['w_feat']), renewed)

def embed_rows(node_ids, at_times, table, neighbours, neighbour_times, params):
    own_rows = table[node_ids]
    width = own_rows.shape[0]
    zero_code = jnp.broadcast_to(jnp.cos(params['b_time']), (width, TE))
    queries = product(low(jnp.concatenate([own_rows, zero_code], 1)), params['w_query'])
    near_ids = neighbours[node_ids]
    deltas = at_times[:, None] - neighbour_times[node_ids]
    near_input = low(jnp.concatenate([table[near_ids], time_code(deltas, params)], 2))
    keys_vals = product(near_input.reshape(width * NBR, D + TE), params['w_kv']).reshape(width, NBR, 2 * D)
    keys = keys_vals[:, :, :D].reshape(width, NBR, HEADS, HS)
    values = keys_vals[:, :, D:].reshape(width, NBR, HEADS, HS)
    scores = jnp.einsum('bhe,bnhe->bhn', queries.reshape(width, HEADS, HS), keys, precision=lax.Precision.HIGHEST) / math.sqrt(HS)
    attention = jax.nn.softmax(scores, axis=-1)
    mixed = jnp.einsum('bhn,bnhe->bhe', attention, values, precision=lax.Precision.HIGHEST).reshape(width, D)
    return own_rows + product(low(mixed), params['w_out'])

def embed_items(node_ids, at_times, table, neighbours, neighbour_times, params):
    total = node_ids.shape[0]
    block = math.gcd(total, 512)

    def one_block(pieces):
        return embed_rows(pieces[0], pieces[1], table, neighbours, neighbour_times, params)
    result = lax.map(jax.checkpoint(one_block), (node_ids.reshape(-1, block), at_times.reshape(-1, block)))
    return result.reshape(total, D)

def predictor(left, right, params):
    hidden = jax.nn.gelu(product(left, params['w_ps']) + product(right, params['w_pd']) + params['b_p1'])
    return product(low(hidden), params['w_p2']) + params['b_p2'][0]

def adamw(master, first_state, second_state, grads):
    first_new = beta_one * first_state + (1.0 - beta_one) * grads
    second_new = beta_two * second_state + (1.0 - beta_two) * grads * grads
    corrected = first_new / (1.0 - beta_one ** STEP) / (jnp.sqrt(second_new / (1.0 - beta_two ** STEP)) + eps_adam)
    return (master - rate_lr * (corrected + decay_wd * master), first_new, second_new)

def reference(master, first_moment, second_moment, memory, messages, static_ids, node_features, neighbours, neighbour_times, last_partner, last_deltas, last_edges, sources, targets, times, negatives, neg_counts):
    feature_rows = node_features[static_ids].astype(jnp.float32)
    message_rows = messages.astype(jnp.float32)
    neg_total = jnp.sum(neg_counts).astype(jnp.float32)
    columns = jnp.arange(NNEG, dtype=jnp.int32)
    active = (columns[None, :] >= NNEG - neg_counts[:, None]).astype(jnp.float32)

    def forward(flat):
        params = unpack(low(flat))
        state, renewed = owner_pass(params, memory, message_rows, feature_rows)
        table = low(state)
        source_emb = low(embed_items(sources, times, table, neighbours, neighbour_times, params))
        target_emb = low(embed_items(targets, times, table, neighbours, neighbour_times, params))
        positive = predictor(source_emb, target_emb, params)
        negative_emb = low(embed_items(negatives.reshape(-1), jnp.repeat(times, NNEG), table, neighbours, neighbour_times, params))
        negative = predictor(jnp.repeat(source_emb, NNEG, axis=0), negative_emb, params).reshape(EVENTS, NNEG)
        loss = jnp.sum(jax.nn.softplus(-positive)) / EVENTS + jnp.sum(active * jax.nn.softplus(negative)) / neg_total
        return (loss, (renewed, table))
    loss, pullback, (renewed, table) = jax.vjp(forward, master, has_aux=True)
    grads = pullback(jnp.float32(1.0))[0]
    new_master, new_first, new_second = adamw(master, first_moment, second_moment, grads)
    params_low = unpack(low(master))
    carried = jnp.concatenate([table, table[last_partner], time_code(last_deltas, params_low), last_edges.astype(jnp.float32)], 1)
    return (loss, neg_total, new_master, new_first, new_second, renewed, carried)
```

```python
import math

import jax
import jax.numpy as jnp
from jax import lax
from jax.sharding import PartitionSpec as P

D = 100
TE = 100
NF = 413
PH = 100
HEADS = 2
NBR = 10
STEP = 10
HS = 50
MSG = 486


beta_one = 0.9
beta_two = 0.999
rate_lr = 0.02
decay_wd = 0.01
eps_adam = 1e-08


def round_value(value):
    return lax.optimization_barrier(value.astype(jnp.bfloat16)).astype(jnp.float32)


def round_keep(value):
    return (round_value(value), None)


def round_pass(kept, grad):
    return (grad,)


def build_rounding():
    rounder = jax.custom_vjp(round_value)
    rounder.defvjp(round_keep, round_pass)
    return rounder


def low(value):
    return build_rounding()(value)


def exact_product(left, right):
    return jnp.dot(left, right, precision=lax.Precision.HIGHEST)


def plain_product(left, right):
    return jnp.dot(
        left.astype(jnp.bfloat16), right.astype(jnp.bfloat16), preferred_element_type=jnp.float32
    )


def product_keep(left, right):
    return (plain_product(left, right), (left, right))


def product_back(kept, grad):
    unused, pullback = jax.vjp(exact_product, kept[0], kept[1])
    return pullback(grad)


def build_product():
    multiplier = jax.custom_vjp(plain_product)
    multiplier.defvjp(product_keep, product_back)
    return multiplier


def product(left, right):
    return build_product()(left, right)


def unpack(flat):
    layout = [
        ("w_gi", (MSG, 3 * D)),
        ("w_gh", (D, 3 * D)),
        ("b_g", (2, 3 * D)),
        ("w_feat", (NF, D)),
        ("w_time", (TE,)),
        ("b_time", (TE,)),
        ("w_query", (D + TE, D)),
        ("w_kv", (D + TE, 2 * D)),
        ("w_out", (D, D)),
        ("w_ps", (D, PH)),
        ("w_pd", (D, PH)),
        ("b_p1", (PH,)),
        ("w_p2", (PH,)),
        ("b_p2", (1,)),
    ]
    params = {}
    offset = 0
    for label, shape in layout:
        amount = math.prod(shape)
        params[label] = flat[offset : offset + amount].reshape(shape)
        offset += amount
    return params


def time_code(deltas, params):
    return jnp.cos(deltas[..., None] * params["w_time"] + params["b_time"])


def owner_pass(params, memory, messages, features):
    inputs = product(messages, params["w_gi"]) + params["b_g"][0]
    hidden = product(low(memory), params["w_gh"]) + params["b_g"][1]
    reset = jax.nn.sigmoid(inputs[:, :D] + hidden[:, :D])
    update = jax.nn.sigmoid(inputs[:, D : 2 * D] + hidden[:, D : 2 * D])
    candidate = jnp.tanh(inputs[:, 2 * D :] + reset * hidden[:, 2 * D :])
    renewed = (1.0 - update) * candidate + update * memory
    return (renewed + product(features, params["w_feat"]), renewed)


def embed_rows(node_ids, at_times, table, projected, neighbours, neighbour_times, params):
    own_rows = table[node_ids]
    width = own_rows.shape[0]
    zero_code = low(jnp.cos(params["b_time"]))[None, :]
    query_shift = product(zero_code, params["w_query"][D:])
    queries = projected[node_ids][:, :D] + query_shift
    near_ids = neighbours[node_ids]
    deltas = at_times[:, None] - neighbour_times[node_ids]
    near_codes = low(time_code(deltas, params)).reshape(width * NBR, TE)
    code_part = product(near_codes, params["w_kv"][D:]).reshape(width, NBR, 2 * D)
    keys_vals = projected[near_ids][:, :, D:] + code_part
    keys = keys_vals[:, :, :D].reshape(width, NBR, HEADS, HS)
    values = keys_vals[:, :, D:].reshape(width, NBR, HEADS, HS)
    scores = jnp.einsum(
        "bhe,bnhe->bhn", queries.reshape(width, HEADS, HS), keys, precision=lax.Precision.HIGHEST
    ) / math.sqrt(HS)
    attention = jax.nn.softmax(scores, axis=-1)
    mixed = jnp.einsum("bhn,bnhe->bhe", attention, values, precision=lax.Precision.HIGHEST).reshape(
        width, D
    )
    return own_rows + product(low(mixed), params["w_out"])


def embed_items(node_ids, at_times, table, neighbours, neighbour_times, params):
    total = node_ids.shape[0]
    block = math.gcd(total, 512)
    stacked = jnp.concatenate([params["w_query"][:D], params["w_kv"][:D]], 1)
    projected = product(table, stacked)

    def one_block(pieces):
        return embed_rows(
            pieces[0], pieces[1], table, projected, neighbours, neighbour_times, params
        )

    result = lax.map(
        jax.checkpoint(one_block), (node_ids.reshape(-1, block), at_times.reshape(-1, block))
    )
    return result.reshape(total, D)


def predictor(left, right, params):
    hidden = jax.nn.gelu(
        product(left, params["w_ps"]) + product(right, params["w_pd"]) + params["b_p1"]
    )
    return product(low(hidden), params["w_p2"]) + params["b_p2"][0]


def adamw(master, first_state, second_state, grads):
    first_new = beta_one * first_state + (1.0 - beta_one) * grads
    second_new = beta_two * second_state + (1.0 - beta_two) * grads * grads
    corrected = (
        first_new
        / (1.0 - beta_one**STEP)
        / (jnp.sqrt(second_new / (1.0 - beta_two**STEP)) + eps_adam)
    )
    return (master - rate_lr * (corrected + decay_wd * master), first_new, second_new)


def exchange_order(names):
    order = []
    for name in reversed(names):
        bits = (lax.axis_size(name) - 1).bit_length()
        rising = range(bits) if name == names[-1] else reversed(range(bits))
        order.extend((name, bit) for bit in rising)
    return order


def partner(array, name, bit):
    size = lax.axis_size(name)
    return lax.ppermute(array, name, [(i, i ^ (1 << bit)) for i in range(size)])


def my_bit(name, bit):
    return (lax.axis_index(name) >> bit) & 1


def gather_all(shard, names=("ev", "neg")):
    dims = {}
    position = 0
    for name in names:
        bits = (lax.axis_size(name) - 1).bit_length()
        for bit in reversed(range(bits)):
            dims[(name, bit)] = position
            position += 1
    held = shard
    done = []
    for name, bit in exchange_order(names):
        other = partner(held, name, bit)
        place = sum(1 for item in done if dims[item] < dims[(name, bit)])
        mine_first = my_bit(name, bit) == 0
        low_part = jnp.where(mine_first, held, other)
        high_part = jnp.where(mine_first, other, held)
        held = jnp.stack([low_part, high_part], axis=place)
        done.append((name, bit))
    return held.reshape((-1,) + shard.shape)


def scatter_sum(blocks, names=("ev", "neg")):
    dims = []
    for name in names:
        bits = (lax.axis_size(name) - 1).bit_length()
        dims.extend((name, bit) for bit in reversed(range(bits)))
    held = blocks.reshape((2,) * len(dims) + blocks.shape[1:])
    left = list(dims)
    for name, bit in reversed(exchange_order(names)):
        place = left.index((name, bit))
        mine = my_bit(name, bit)
        keep = lax.dynamic_index_in_dim(held, mine, place, keepdims=False)
        give = lax.dynamic_index_in_dim(held, 1 - mine, place, keepdims=False)
        held = keep + partner(give, name, bit)
        left.remove((name, bit))
    return held


def sum_all(value, names=("ev", "neg")):
    for name in names:
        for bit in range((lax.axis_size(name) - 1).bit_length()):
            value = value + partner(value, name, bit)
    return value


def lanes(flat):
    amount = flat.shape[-1]
    rows = -(-amount // 128)
    wide = jnp.pad(flat, [(0, 0)] * (flat.ndim - 1) + [(0, rows * 128 - amount)])
    return wide.reshape(flat.shape[:-1] + (rows, 128))


def on_device(
    master,
    first_moment,
    second_moment,
    memory,
    messages,
    static_ids,
    node_features,
    neighbours,
    neighbour_times,
    last_partner,
    last_deltas,
    last_edges,
    sources,
    targets,
    times,
    negatives,
    neg_counts,
):
    shard = master.shape[0]
    devices = lax.axis_size("ev") * lax.axis_size("neg")
    copies = gather_all(lanes(master.astype(jnp.bfloat16)))
    flat = copies.reshape(devices, -1)[:, :shard].reshape(-1).astype(jnp.float32)
    groups = lax.axis_size("neg")
    rank = lax.axis_index("neg")
    own_events = sources.shape[0]
    events_all = own_events * devices
    own_negatives = lax.all_to_all(negatives, "neg", split_axis=0, concat_axis=1, tiled=True)
    total_neg = own_negatives.shape[1]
    own_counts = lax.dynamic_slice_in_dim(neg_counts, rank * own_events, own_events)
    columns = jnp.arange(total_neg, dtype=jnp.int32)
    active = (columns[None, :] >= total_neg - own_counts[:, None]).astype(jnp.float32)
    neg_total = sum_all(jnp.sum(active))
    own_times = lax.dynamic_slice_in_dim(times, rank * own_events, own_events)
    feature_rows = node_features[static_ids].astype(jnp.float32)
    message_rows = messages.astype(jnp.float32)

    def owner_part(weights_flat):
        return owner_pass(unpack(weights_flat), memory, message_rows, feature_rows)

    state, owner_back, renewed = jax.vjp(owner_part, flat, has_aux=True)
    table = gather_all(state.astype(jnp.bfloat16)).reshape(-1, D).astype(jnp.float32)

    def own_part(weights_flat, table_in):
        params = unpack(weights_flat)
        items = jnp.concatenate([sources, targets, own_negatives.T.reshape(-1)])
        emb = low(
            embed_items(
                items,
                jnp.tile(own_times, 2 + total_neg),
                table_in,
                neighbours,
                neighbour_times,
                params,
            )
        ).reshape(2 + total_neg, own_events, D)
        source_emb = jnp.broadcast_to(emb[:1], (1 + total_neg, own_events, D)).reshape(-1, D)
        scores = predictor(source_emb, emb[1:].reshape(-1, D), params).reshape(-1, own_events)
        positive, negative = scores[0], scores[1:]
        return (
            jnp.sum(jax.nn.softplus(-positive)) / events_all
            + jnp.sum(active.T * jax.nn.softplus(negative)) / neg_total
        )

    local_loss, own_back = jax.vjp(own_part, flat, table)
    grad_flat_own, grad_table = own_back(jnp.float32(1.0))
    grad_state = scatter_sum(grad_table.reshape(devices, -1, D))
    grad_flat_node = owner_back(grad_state)[0]
    grads = grad_flat_own + grad_flat_node
    grad_shard = scatter_sum(lanes(grads.reshape(devices, shard))).reshape(-1)[:shard]
    loss = sum_all(local_loss)
    new_master, new_first, new_second = adamw(master, first_moment, second_moment, grad_shard)
    params_low = unpack(flat)
    own_table = low(state)
    carried = jnp.concatenate(
        [
            own_table,
            table[last_partner],
            time_code(last_deltas, params_low),
            last_edges.astype(jnp.float32),
        ],
        1,
    )
    return (loss, neg_total, new_master, new_first, new_second, renewed, carried)


def solution(mesh):
    return jax.shard_map(
        on_device,
        mesh=mesh,
        in_specs=(
            P(("ev", "neg")),
            P(("ev", "neg")),
            P(("ev", "neg")),
            P(("ev", "neg"), None),
            P(("ev", "neg"), None),
            P(("ev", "neg")),
            P(),
            P(),
            P(),
            P(("ev", "neg")),
            P(("ev", "neg")),
            P(("ev", "neg"), None),
            P(("ev", "neg")),
            P(("ev", "neg")),
            P("ev"),
            P("ev", "neg"),
            P("ev"),
        ),
        out_specs=(
            P(),
            P(),
            P(("ev", "neg")),
            P(("ev", "neg")),
            P(("ev", "neg")),
            P(("ev", "neg"), None),
            P(("ev", "neg"), None),
        ),
        check_vma=False,
    )
```

```python
import functools
import math

import jax
import jax.numpy as jnp
from jax import lax
from jax.experimental import pallas as pl
from jax.experimental.pallas import tpu as pltpu
from jax.sharding import PartitionSpec as P

D = 100
TE = 100
NF = 413
PH = 100
HEADS = 2
NBR = 10
STEP = 10
HS = 50
MSG = 486
PLIVE = 308101
NODE_LIVE = MSG * 3 * D + D * 3 * D + 2 * 3 * D + NF * D


beta_one = 0.9
beta_two = 0.999
rate_lr = 0.02
decay_wd = 0.01
eps_adam = 1e-08


def round_value(value):
    return lax.optimization_barrier(value.astype(jnp.bfloat16)).astype(jnp.float32)


def round_keep(value):
    return (round_value(value), None)


def round_pass(kept, grad):
    return (grad,)


def build_rounding():
    rounder = jax.custom_vjp(round_value)
    rounder.defvjp(round_keep, round_pass)
    return rounder


def low(value):
    return build_rounding()(value)


def exact_product(left, right):
    return jnp.dot(left, right, precision=lax.Precision.HIGHEST)


def plain_product(left, right):
    return jnp.dot(
        left.astype(jnp.bfloat16), right.astype(jnp.bfloat16), preferred_element_type=jnp.float32
    )


def product_keep(left, right):
    return (plain_product(left, right), (left, right))


def product_back(kept, grad):
    unused, pullback = jax.vjp(exact_product, kept[0], kept[1])
    return pullback(grad)


def build_product():
    multiplier = jax.custom_vjp(plain_product)
    multiplier.defvjp(product_keep, product_back)
    return multiplier


def product(left, right):
    return build_product()(left, right)


def unpack(flat):
    layout = [
        ("w_gi", (MSG, 3 * D)),
        ("w_gh", (D, 3 * D)),
        ("b_g", (2, 3 * D)),
        ("w_feat", (NF, D)),
        ("w_time", (TE,)),
        ("b_time", (TE,)),
        ("w_query", (D + TE, D)),
        ("w_kv", (D + TE, 2 * D)),
        ("w_out", (D, D)),
        ("w_ps", (D, PH)),
        ("w_pd", (D, PH)),
        ("b_p1", (PH,)),
        ("w_p2", (PH,)),
        ("b_p2", (1,)),
    ]
    params = {}
    offset = 0
    for label, shape in layout:
        amount = math.prod(shape)
        params[label] = flat[offset : offset + amount].reshape(shape)
        offset += amount
    return params


def time_code(deltas, params):
    return jnp.cos(deltas[..., None] * params["w_time"] + params["b_time"])


def owner_pass(params, memory, messages, features):
    inputs = product(messages, params["w_gi"]) + params["b_g"][0]
    hidden = product(low(memory), params["w_gh"]) + params["b_g"][1]
    reset = jax.nn.sigmoid(inputs[:, :D] + hidden[:, :D])
    update = jax.nn.sigmoid(inputs[:, D : 2 * D] + hidden[:, D : 2 * D])
    candidate = jnp.tanh(inputs[:, 2 * D :] + reset * hidden[:, 2 * D :])
    renewed = (1.0 - update) * candidate + update * memory
    return (renewed + product(features, params["w_feat"]), renewed)


def adamw(master, first_state, second_state, grads):
    first_new = beta_one * first_state + (1.0 - beta_one) * grads
    second_new = beta_two * second_state + (1.0 - beta_two) * grads * grads
    corrected = (
        first_new
        / (1.0 - beta_one**STEP)
        / (jnp.sqrt(second_new / (1.0 - beta_two**STEP)) + eps_adam)
    )
    return (master - rate_lr * (corrected + decay_wd * master), first_new, second_new)


F = 112
HP = 56
W = 128
CH = NBR // 2
LO = 256


def dot(left, right):
    return jnp.dot(left, right, preferred_element_type=jnp.float32)


def dot_nt(left, right):
    return lax.dot_general(
        left, right, (((1,), (1,)), ((), ())), preferred_element_type=jnp.float32
    )


def split_terms(value):
    first = value.astype(jnp.bfloat16)
    return first, (value - first.astype(jnp.float32)).astype(jnp.bfloat16)


def sine_cosine(angle):
    turns = jnp.round(angle * (2.0 / math.pi))
    rest = angle - turns * 1.5703125
    rest = rest - turns * 4.837512969970703e-4
    rest = rest - turns * 7.549789948768648e-8
    square = rest * rest
    sine = rest + rest * square * (
        -1.6666654611e-1 + square * (8.3321608736e-3 - square * 1.9515295891e-4)
    )
    cosine = (
        1.0
        - 0.5 * square
        + square
        * square
        * (4.166664568298827e-2 + square * (-1.388731625493765e-3 + square * 2.443315711809948e-5))
    )
    quadrant = turns.astype(jnp.int32)
    odd = (quadrant & 1) == 1
    cos_value = jnp.where(odd, sine, cosine)
    sin_value = jnp.where(odd, cosine, sine)
    cos_value = jnp.where(((quadrant + 1) & 2) == 2, -cos_value, cos_value)
    sin_value = jnp.where((quadrant & 2) == 2, -sin_value, sin_value)
    return cos_value, sin_value


def any_angle(angle):
    return jnp.cos(angle), jnp.sin(angle)


def pair(value):
    return jnp.concatenate([value, value], axis=1)


def fold(value):
    return value[:, :W] + value[:, W:]


def head_sums(value):
    return jnp.concatenate(
        [
            jnp.sum(value[:HP], axis=0, keepdims=True),
            jnp.sum(value[HP:], axis=0, keepdims=True),
        ],
        axis=0,
    )


def head_spread(value):
    lanes_of = value.shape[1]
    return jnp.concatenate(
        [
            jnp.broadcast_to(value[0:1], (HP, lanes_of)),
            jnp.broadcast_to(value[1:2], (HP, lanes_of)),
        ],
        axis=0,
    )


def one_hot(ids):
    place = ids & (LO - 1)
    rows = lax.broadcasted_iota(jnp.int32, (LO, ids.shape[1]), 0)
    return ids // LO, jnp.where(rows == place, 1.0, 0.0).astype(jnp.bfloat16)


def take_rows(table_ref, groups, ids):
    group, hot = one_hot(ids)
    found = dot(table_ref[...], hot)
    picked = jnp.zeros((F, ids.shape[1]), jnp.float32)
    for number in range(groups):
        picked = jnp.where(group == number, found[number * F : (number + 1) * F], picked)
    return picked


def step_kernel(
    halves,
    roles,
    groups,
    table_ref,
    near_ref,
    gaps_ref,
    items_ref,
    coef_ref,
    wide_ref,
    kvt_ref,
    kv_ref,
    qt_ref,
    q_ref,
    square_ref,
    loss_ref,
    gtab_ref,
    gkv_ref,
    gq_ref,
    gsquare_ref,
    gwide_ref,
    x_s,
    kv_s,
    sin_s,
    own_s,
    query_s,
    att_s,
    mix_s,
    z_s,
    dz_s,
    hot_s,
    right_s,
):
    nodes = groups * LO
    scale = 1.0 / math.sqrt(HS)
    w_time, b_time = wide_ref[0], wide_ref[1]
    b_p1, w_p2 = wide_ref[2], wide_ref[3]
    b_p2 = wide_ref[4][0:1]
    zero_cos, zero_sin = any_angle(b_time)
    furthest = jnp.max(jnp.abs(gaps_ref[...])) * jnp.max(jnp.abs(w_time)) + jnp.max(jnp.abs(b_time))
    moderate = furthest <= 8192.0
    zero_code = zero_cos.astype(jnp.bfloat16)
    for ref in (gtab_ref, gkv_ref, gq_ref, gsquare_ref, gwide_ref, loss_ref):
        ref[...] = jnp.zeros_like(ref)
    w_time2, b_time2 = pair(w_time), pair(b_time)

    def half_step(half, carry):
        def forward(trig, role, carry):
            block = half * roles + role
            own = take_rows(table_ref, groups, items_ref[block]).astype(jnp.bfloat16)
            own_s[role] = own
            query = dot(qt_ref[...], jnp.concatenate([own, zero_code], axis=0))
            query_s[role] = query
            query2 = pair(query)
            scores = []
            for c in range(CH):
                near = take_rows(table_ref, groups, near_ref[block, c : c + 1]).astype(jnp.bfloat16)
                angle = gaps_ref[block, c : c + 1] * w_time2 + b_time2
                cos_value, sin_value = trig(angle)
                sin_s[role, c] = sin_value
                x = jnp.concatenate([near, cos_value.astype(jnp.bfloat16)], axis=0)
                x_s[role, c] = x
                kv = dot(kvt_ref[...], x)
                kv_s[role, c] = kv
                scores.append(head_sums(kv[:F] * query2) * scale)
            top = scores[0]
            for c in range(1, CH):
                top = jnp.maximum(top, scores[c])
            top = pair(jnp.maximum(top[:, :W], top[:, W:]))
            powers = [jnp.exp(s - top) for s in scores]
            total = powers[0]
            for c in range(1, CH):
                total = total + powers[c]
            inverse = pair(1.0 / fold(total))
            mixed = jnp.zeros((F, 2 * W), jnp.float32)
            for c in range(CH):
                share = powers[c] * inverse
                att_s[role, c] = share
                mixed = mixed + head_spread(share) * kv_s[role, c, F:]
            mixed = fold(mixed).astype(jnp.bfloat16)
            mix_s[role] = mixed
            emb = own.astype(jnp.float32) + dot(square_ref[0], mixed)
            z_s[role] = emb.astype(jnp.bfloat16)
            return carry

        for usable, trig in ((moderate, sine_cosine), (jnp.logical_not(moderate), any_angle)):

            @pl.when(usable)
            def run_forward(trig=trig):
                lax.fori_loop(0, roles, functools.partial(forward, trig), 0)

        source = z_s[0]
        from_source = dot(square_ref[2], source) + b_p1
        d_source = jnp.zeros((F, W), jnp.float32)
        for role in range(1, roles):
            before = from_source + dot(square_ref[4], z_s[role])
            inner = 0.7978845608028654 * (before + 0.044715 * before * before * before)
            bend = jnp.tanh(inner)
            hidden = (0.5 * before * (1.0 + bend)).astype(jnp.bfloat16).astype(jnp.float32)
            slope = 0.5 * (1.0 + bend) + 0.5 * before * (1.0 - bend * bend) * (
                0.7978845608028654 * (1.0 + 3.0 * 0.044715 * before * before)
            )
            score = jnp.sum(hidden * w_p2, axis=0, keepdims=True) + b_p2
            sign = -1.0 if role == 1 else 1.0
            weight = coef_ref[half, role - 1 : role]
            signed = sign * score
            small = jnp.exp(-jnp.abs(signed))
            loss_ref[0:1] += weight * (jnp.maximum(signed, 0.0) + jnp.log1p(small))
            sigmoid = jnp.where(signed >= 0.0, 1.0, small) / (1.0 + small)
            d_score = (sign * weight) * sigmoid
            gwide_ref[3] += hidden * d_score
            gwide_ref[4, 0:1] += d_score
            d_before = w_p2 * d_score * slope
            gwide_ref[2] += d_before
            d_source = d_source + d_before
            terms = jnp.concatenate(split_terms(d_before), axis=1)
            gsquare_ref[2] += dot_nt(pair(z_s[role]), terms)
            dz_s[role] = fold(dot(square_ref[5], terms))
        terms = jnp.concatenate(split_terms(d_source), axis=1)
        gsquare_ref[1] += dot_nt(pair(source), terms)
        dz_s[0] = fold(dot(square_ref[3], terms))

        def backward(role, carry):
            block = half * roles + role
            d_emb = dz_s[role]
            terms = jnp.concatenate(split_terms(d_emb), axis=1)
            gsquare_ref[0] += dot_nt(pair(mix_s[role]), terms)
            d_mixed = pair(fold(dot(square_ref[1], terms)))
            query2 = pair(query_s[role])
            d_shares = [head_sums(d_mixed * kv_s[role, c, F:]) for c in range(CH)]
            total = jnp.zeros((2, 2 * W), jnp.float32)
            for c in range(CH):
                total = total + att_s[role, c] * d_shares[c]
            total = pair(fold(total))
            d_query = jnp.zeros((F, 2 * W), jnp.float32)
            for c in range(CH):
                share = att_s[role, c]
                d_score = head_spread(share * (d_shares[c] - total) * scale)
                d_query = d_query + d_score * kv_s[role, c, :F]
                d_kv = jnp.concatenate([d_score * query2, head_spread(share) * d_mixed], axis=0)
                upper, lower = split_terms(d_kv)
                x = x_s[role, c]
                gkv_ref[...] += dot_nt(x, upper) + dot_nt(x, lower)
                d_x = dot(kv_ref[...], upper) + dot(kv_ref[...], lower)
                turned = sin_s[role, c] * d_x[F:]
                gwide_ref[1] -= fold(turned)
                gwide_ref[0] -= fold(turned * gaps_ref[block, c : c + 1])
                upper, lower = split_terms(d_x[:F])
                lanes_at = slice(c * 2 * W, (c + 1) * 2 * W)
                right_s[:F, lanes_at] = upper
                right_s[F:, lanes_at] = lower
                group, hot = one_hot(near_ref[block, c : c + 1])
                for number in range(groups):
                    hot_s[number * LO : (number + 1) * LO, lanes_at] = jnp.where(
                        group == number, hot, jnp.zeros_like(hot)
                    )
            d_query = fold(d_query)
            terms = jnp.concatenate(split_terms(d_query), axis=1)
            own = own_s[role]
            code = jnp.concatenate([own, zero_code], axis=0)
            gq_ref[...] += dot_nt(pair(code), terms)
            d_code = fold(dot(q_ref[...], terms))
            gwide_ref[1] -= zero_sin * d_code[F:]
            upper, lower = split_terms(d_emb + d_code[:F])
            lanes_at = slice(CH * 2 * W, CH * 2 * W + W)
            right_s[:F, lanes_at] = upper
            right_s[F:, lanes_at] = lower
            group, hot = one_hot(items_ref[block])
            for number in range(groups):
                hot_s[number * LO : (number + 1) * LO, lanes_at] = jnp.where(
                    group == number, hot, jnp.zeros_like(hot)
                )
            for number in range(groups):
                rows = slice(number * LO, (number + 1) * LO)
                gtab_ref[rows] += dot_nt(hot_s[rows], right_s[...])
            return carry

        lax.fori_loop(0, roles, backward, 0)
        return carry

    lax.fori_loop(0, halves, half_step, 0)


def pad_heads(matrix, axis):
    shape = matrix.shape
    split = matrix.reshape(shape[:axis] + (HEADS, HS) + shape[axis + 1 :])
    widths = [(0, 0)] * split.ndim
    widths[axis + 1] = (0, HP - HS)
    return jnp.pad(split, widths).reshape(shape[:axis] + (F,) + shape[axis + 1 :])


def cut_heads(matrix, axis):
    shape = matrix.shape
    split = matrix.reshape(shape[:axis] + (HEADS, HP) + shape[axis + 1 :])
    return lax.slice_in_dim(split, 0, HS, axis=axis + 1).reshape(
        shape[:axis] + (D,) + shape[axis + 1 :]
    )


def pad_to(matrix, axis):
    widths = [(0, 0)] * matrix.ndim
    widths[axis] = (0, F - matrix.shape[axis])
    return jnp.pad(matrix, widths)


def event_step(params, table, items, item_times, coef, neighbours, neighbour_times):
    roles, events = items.shape
    halves = events // W
    nodes = table.shape[0]
    groups = nodes // LO
    blocks = halves * roles

    def by_block(array):
        split = array.reshape((roles, halves, W) + array.shape[2:])
        return jnp.swapaxes(split, 0, 1).reshape((blocks, W) + array.shape[2:])

    ids = by_block(items)
    near = jnp.swapaxes(neighbours[ids.reshape(-1)].reshape(blocks, W, NBR), 1, 2)
    near_times = jnp.swapaxes(neighbour_times[ids.reshape(-1)].reshape(blocks, W, NBR), 1, 2)
    at = by_block(jnp.broadcast_to(item_times[None], (roles, events)))
    near = near.reshape(blocks, CH, 2 * W)
    gaps = (at[:, None, :] - near_times).reshape(blocks, CH, 2 * W)
    coef = jnp.swapaxes(coef.reshape(roles - 1, halves, W), 0, 1)
    table_t = jnp.swapaxes(pad_to(table.reshape(groups, LO, D), 2), 1, 2).reshape(groups * F, LO)

    def stacked_rows(matrix):
        return jnp.concatenate([pad_to(matrix[:D], 0), pad_to(matrix[D:], 0)], 0)

    w_kv = params["w_kv"]
    w_kv = jnp.concatenate([pad_heads(w_kv[:, :D], 1), pad_heads(w_kv[:, D:], 1)], 1)
    w_kv = stacked_rows(w_kv)
    w_q = stacked_rows(pad_heads(params["w_query"], 1))
    w_out = pad_to(pad_heads(params["w_out"], 0), 1)
    w_ps = pad_to(pad_to(params["w_ps"], 0), 1)
    w_pd = pad_to(pad_to(params["w_pd"], 0), 1)
    square = jnp.stack([w_out.T, w_out, w_ps.T, w_ps, w_pd.T, w_pd])
    columns = jnp.stack(
        [
            pad_to(params["w_time"], 0),
            pad_to(params["b_time"], 0),
            pad_to(params["b_p1"], 0),
            pad_to(params["w_p2"], 0),
            jnp.broadcast_to(params["b_p2"], (F,)),
        ]
    ).astype(jnp.float32)
    wide = jnp.broadcast_to(columns[:, :, None], (5, F, W))
    full = 2 * CH * W + W
    outs = pl.pallas_call(
        functools.partial(step_kernel, halves, roles, groups),
        out_shape=(
            jax.ShapeDtypeStruct((1, W), jnp.float32),
            jax.ShapeDtypeStruct((nodes, 2 * F), jnp.float32),
            jax.ShapeDtypeStruct((2 * F, 2 * F), jnp.float32),
            jax.ShapeDtypeStruct((2 * F, F), jnp.float32),
            jax.ShapeDtypeStruct((3, F, F), jnp.float32),
            jax.ShapeDtypeStruct((5, F, W), jnp.float32),
        ),
        in_specs=[pl.BlockSpec(memory_space=pltpu.VMEM)] * 11,
        out_specs=(pl.BlockSpec(memory_space=pltpu.VMEM),) * 6,
        scratch_shapes=[
            pltpu.VMEM((roles, CH, 2 * F, 2 * W), jnp.bfloat16),
            pltpu.VMEM((roles, CH, 2 * F, 2 * W), jnp.float32),
            pltpu.VMEM((roles, CH, F, 2 * W), jnp.float32),
            pltpu.VMEM((roles, F, W), jnp.bfloat16),
            pltpu.VMEM((roles, F, W), jnp.float32),
            pltpu.VMEM((roles, CH, 2, 2 * W), jnp.float32),
            pltpu.VMEM((roles, F, W), jnp.bfloat16),
            pltpu.VMEM((roles, F, W), jnp.bfloat16),
            pltpu.VMEM((roles, F, W), jnp.float32),
            pltpu.VMEM((nodes, full), jnp.bfloat16),
            pltpu.VMEM((2 * F, full), jnp.bfloat16),
        ],
        compiler_params=pltpu.CompilerParams(vmem_limit_bytes=60 * 1024 * 1024),
    )(
        table_t,
        near,
        gaps,
        ids[:, None, :],
        coef,
        wide,
        w_kv.T,
        w_kv,
        w_q.T,
        w_q,
        square,
    )
    loss, g_table, g_kv, g_q, g_square, g_wide = outs

    def cut_rows(matrix):
        return jnp.concatenate([matrix[:D], matrix[F : F + D]], 0)

    g_kv = cut_rows(g_kv)
    g_wide = jnp.sum(g_wide, axis=2)
    grads = [
        g_wide[0, :TE],
        g_wide[1, :TE],
        cut_heads(cut_rows(g_q), 1).reshape(-1),
        jnp.concatenate([cut_heads(g_kv[:, :F], 1), cut_heads(g_kv[:, F:], 1)], 1).reshape(-1),
        cut_heads(g_square[0], 0)[:, :D].reshape(-1),
        g_square[1][:D, :PH].reshape(-1),
        g_square[2][:D, :PH].reshape(-1),
        g_wide[2, :PH],
        g_wide[3, :PH],
        g_wide[4, :1],
    ]
    return jnp.sum(loss), jnp.concatenate(grads), g_table[:, :D] + g_table[:, F : F + D]


def exchange_order(names):
    order = []
    for name in reversed(names):
        bits = (lax.axis_size(name) - 1).bit_length()
        rising = range(bits) if name == names[-1] else reversed(range(bits))
        order.extend((name, bit) for bit in rising)
    return order


def partner(array, name, bit):
    size = lax.axis_size(name)
    return lax.ppermute(array, name, [(i, i ^ (1 << bit)) for i in range(size)])


def my_bit(name, bit):
    return (lax.axis_index(name) >> bit) & 1


def gather_all(shard, names=("ev", "neg")):
    dims = {}
    position = 0
    for name in names:
        bits = (lax.axis_size(name) - 1).bit_length()
        for bit in reversed(range(bits)):
            dims[(name, bit)] = position
            position += 1
    held = shard
    done = []
    for name, bit in exchange_order(names):
        other = partner(held, name, bit)
        place = sum(1 for item in done if dims[item] < dims[(name, bit)])
        mine_first = my_bit(name, bit) == 0
        low_part = jnp.where(mine_first, held, other)
        high_part = jnp.where(mine_first, other, held)
        held = jnp.stack([low_part, high_part], axis=place)
        done.append((name, bit))
    return held.reshape((-1,) + shard.shape)


def scatter_sum(blocks, names=("ev", "neg")):
    dims = []
    for name in names:
        bits = (lax.axis_size(name) - 1).bit_length()
        dims.extend((name, bit) for bit in reversed(range(bits)))
    held = blocks.reshape((2,) * len(dims) + blocks.shape[1:])
    left = list(dims)
    for name, bit in reversed(exchange_order(names)):
        place = left.index((name, bit))
        mine = my_bit(name, bit)
        keep = lax.dynamic_index_in_dim(held, mine, place, keepdims=False)
        give = lax.dynamic_index_in_dim(held, 1 - mine, place, keepdims=False)
        held = keep + partner(give, name, bit)
        left.remove((name, bit))
    return held


def sum_all(value, names=("ev", "neg")):
    for name in names:
        for bit in range((lax.axis_size(name) - 1).bit_length()):
            value = value + partner(value, name, bit)
    return value


def lanes(flat):
    amount = flat.shape[-1]
    rows = -(-amount // 128)
    wide = jnp.pad(flat, [(0, 0)] * (flat.ndim - 1) + [(0, rows * 128 - amount)])
    return wide.reshape(flat.shape[:-1] + (rows, 128))


def on_device(
    master,
    first_moment,
    second_moment,
    memory,
    messages,
    static_ids,
    node_features,
    neighbours,
    neighbour_times,
    last_partner,
    last_deltas,
    last_edges,
    sources,
    targets,
    times,
    negatives,
    neg_counts,
):
    shard = master.shape[0]
    devices = lax.axis_size("ev") * lax.axis_size("neg")
    copies = gather_all(lanes(master.astype(jnp.bfloat16)))
    copies_flat = copies.reshape(devices, -1)[:, :shard].reshape(-1)
    flat = copies_flat.astype(jnp.float32)
    groups = lax.axis_size("neg")
    rank = lax.axis_index("neg")
    own_events = sources.shape[0]
    events_all = own_events * devices
    own_negatives = lax.all_to_all(negatives, "neg", split_axis=0, concat_axis=1, tiled=True)
    total_neg = own_negatives.shape[1]
    own_counts = lax.dynamic_slice_in_dim(neg_counts, rank * own_events, own_events)
    columns = jnp.arange(total_neg, dtype=jnp.int32)
    active = (columns[None, :] >= total_neg - own_counts[:, None]).astype(jnp.float32)
    neg_total = sum_all(jnp.sum(active))
    own_times = lax.dynamic_slice_in_dim(times, rank * own_events, own_events)
    feature_rows = node_features[static_ids].astype(jnp.float32)
    message_rows = messages.astype(jnp.float32)

    def owner_part(weights_flat):
        return owner_pass(unpack(weights_flat), memory, message_rows, feature_rows)

    state, owner_back, renewed = jax.vjp(owner_part, flat, has_aux=True)
    table_low = gather_all(state.astype(jnp.bfloat16)).reshape(-1, D)
    table = table_low.astype(jnp.float32)

    items = jnp.concatenate([sources[None], targets[None], own_negatives.T])
    coef = jnp.concatenate(
        [jnp.full((1, own_events), 1.0 / events_all, jnp.float32), active.T / neg_total]
    )
    local_loss, grad_event, grad_table = event_step(
        unpack(copies_flat), table_low, items, own_times, coef, neighbours, neighbour_times
    )
    grad_state = scatter_sum(grad_table.reshape(devices, -1, D))
    grad_flat_node = owner_back(grad_state)[0]
    rest = flat.shape[0] - PLIVE
    grads = jnp.concatenate([grad_flat_node[:NODE_LIVE], grad_event, jnp.zeros((rest,), jnp.float32)])
    grad_shard = scatter_sum(lanes(grads.reshape(devices, shard))).reshape(-1)[:shard]
    loss = sum_all(local_loss)
    new_master, new_first, new_second = adamw(master, first_moment, second_moment, grad_shard)
    params_low = unpack(flat)
    own_table = low(state)
    carried = jnp.concatenate(
        [
            own_table,
            table[last_partner],
            time_code(last_deltas, params_low),
            last_edges.astype(jnp.float32),
        ],
        1,
    )
    return (loss, neg_total, new_master, new_first, new_second, renewed, carried)


def solution(mesh):
    return jax.shard_map(
        on_device,
        mesh=mesh,
        in_specs=(
            P(("ev", "neg")),
            P(("ev", "neg")),
            P(("ev", "neg")),
            P(("ev", "neg"), None),
            P(("ev", "neg"), None),
            P(("ev", "neg")),
            P(),
            P(),
            P(),
            P(("ev", "neg")),
            P(("ev", "neg")),
            P(("ev", "neg"), None),
            P(("ev", "neg")),
            P(("ev", "neg")),
            P("ev"),
            P("ev", "neg"),
            P("ev"),
        ),
        out_specs=(
            P(),
            P(),
            P(("ev", "neg")),
            P(("ev", "neg")),
            P(("ev", "neg")),
            P(("ev", "neg"), None),
            P(("ev", "neg"), None),
        ),
        check_vma=False,
    )
```

```python
import functools
import math

import jax
import jax.numpy as jnp
from jax import lax
from jax.experimental import pallas as pl
from jax.experimental.pallas import tpu as pltpu
from jax.sharding import PartitionSpec as P

D = 100
TE = 100
NF = 413
PH = 100
HEADS = 2
NBR = 10
STEP = 10
HS = 50
MSG = 486
PLIVE = 308101
NODE_LIVE = MSG * 3 * D + D * 3 * D + 2 * 3 * D + NF * D


beta_one = 0.9
beta_two = 0.999
rate_lr = 0.02
decay_wd = 0.01
eps_adam = 1e-08


def round_value(value):
    return lax.optimization_barrier(value.astype(jnp.bfloat16)).astype(jnp.float32)


def round_keep(value):
    return (round_value(value), None)


def round_pass(kept, grad):
    return (grad,)


def build_rounding():
    rounder = jax.custom_vjp(round_value)
    rounder.defvjp(round_keep, round_pass)
    return rounder


def low(value):
    return build_rounding()(value)


def exact_product(left, right):
    return jnp.dot(left, right, precision=lax.Precision.HIGHEST)


def plain_product(left, right):
    return jnp.dot(
        left.astype(jnp.bfloat16), right.astype(jnp.bfloat16), preferred_element_type=jnp.float32
    )


def product_keep(left, right):
    return (plain_product(left, right), (left, right))


def product_back(kept, grad):
    unused, pullback = jax.vjp(exact_product, kept[0], kept[1])
    return pullback(grad)


def build_product():
    multiplier = jax.custom_vjp(plain_product)
    multiplier.defvjp(product_keep, product_back)
    return multiplier


def product(left, right):
    return build_product()(left, right)


def unpack(flat):
    layout = [
        ("w_gi", (MSG, 3 * D)),
        ("w_gh", (D, 3 * D)),
        ("b_g", (2, 3 * D)),
        ("w_feat", (NF, D)),
        ("w_time", (TE,)),
        ("b_time", (TE,)),
        ("w_query", (D + TE, D)),
        ("w_kv", (D + TE, 2 * D)),
        ("w_out", (D, D)),
        ("w_ps", (D, PH)),
        ("w_pd", (D, PH)),
        ("b_p1", (PH,)),
        ("w_p2", (PH,)),
        ("b_p2", (1,)),
    ]
    params = {}
    offset = 0
    for label, shape in layout:
        amount = math.prod(shape)
        params[label] = flat[offset : offset + amount].reshape(shape)
        offset += amount
    return params


def time_code(deltas, params):
    return jnp.cos(deltas[..., None] * params["w_time"] + params["b_time"])


def owner_pass(params, memory, messages, features):
    inputs = product(messages, params["w_gi"]) + params["b_g"][0]
    hidden = product(low(memory), params["w_gh"]) + params["b_g"][1]
    reset = jax.nn.sigmoid(inputs[:, :D] + hidden[:, :D])
    update = jax.nn.sigmoid(inputs[:, D : 2 * D] + hidden[:, D : 2 * D])
    candidate = jnp.tanh(inputs[:, 2 * D :] + reset * hidden[:, 2 * D :])
    renewed = (1.0 - update) * candidate + update * memory
    return (renewed + product(features, params["w_feat"]), renewed)


def adamw(master, first_state, second_state, grads):
    first_new = beta_one * first_state + (1.0 - beta_one) * grads
    second_new = beta_two * second_state + (1.0 - beta_two) * grads * grads
    corrected = (
        first_new
        / (1.0 - beta_one**STEP)
        / (jnp.sqrt(second_new / (1.0 - beta_two**STEP)) + eps_adam)
    )
    return (master - rate_lr * (corrected + decay_wd * master), first_new, second_new)


F = 112
HP = 56
W = 128
CH = NBR // 2
LO = 256


def dot(left, right):
    return jnp.dot(left, right, preferred_element_type=jnp.float32)


def dot_nt(left, right):
    return lax.dot_general(
        left, right, (((1,), (1,)), ((), ())), preferred_element_type=jnp.float32
    )


def split_terms(value):
    first = value.astype(jnp.bfloat16)
    return first, (value - first.astype(jnp.float32)).astype(jnp.bfloat16)


def sine_cosine(angle):
    turns = jnp.round(angle * (2.0 / math.pi))
    rest = angle - turns * 1.5703125
    rest = rest - turns * 4.837512969970703e-4
    rest = rest - turns * 7.549789948768648e-8
    square = rest * rest
    sine = rest + rest * square * (
        -1.6666654611e-1 + square * (8.3321608736e-3 - square * 1.9515295891e-4)
    )
    cosine = (
        1.0
        - 0.5 * square
        + square
        * square
        * (4.166664568298827e-2 + square * (-1.388731625493765e-3 + square * 2.443315711809948e-5))
    )
    quadrant = turns.astype(jnp.int32)
    odd = (quadrant & 1) == 1
    cos_value = jnp.where(odd, sine, cosine)
    sin_value = jnp.where(odd, cosine, sine)
    cos_value = jnp.where(((quadrant + 1) & 2) == 2, -cos_value, cos_value)
    sin_value = jnp.where((quadrant & 2) == 2, -sin_value, sin_value)
    return cos_value, sin_value


def any_angle(angle):
    return jnp.cos(angle), jnp.sin(angle)


def pair(value):
    return jnp.concatenate([value, value], axis=1)


def fold(value):
    return value[:, :W] + value[:, W:]


def head_sums(value):
    return jnp.concatenate(
        [
            jnp.sum(value[:HP], axis=0, keepdims=True),
            jnp.sum(value[HP:], axis=0, keepdims=True),
        ],
        axis=0,
    )


def head_spread(value):
    lanes_of = value.shape[1]
    return jnp.concatenate(
        [
            jnp.broadcast_to(value[0:1], (HP, lanes_of)),
            jnp.broadcast_to(value[1:2], (HP, lanes_of)),
        ],
        axis=0,
    )


def one_hot(ids):
    place = ids & (LO - 1)
    rows = lax.broadcasted_iota(jnp.int32, (LO, ids.shape[1]), 0)
    return ids // LO, jnp.where(rows == place, 1.0, 0.0).astype(jnp.bfloat16)


def take_rows(table_ref, groups, ids):
    group, hot = one_hot(ids)
    found = dot(table_ref[...], hot)
    picked = jnp.zeros((F, ids.shape[1]), jnp.float32)
    for number in range(groups):
        picked = jnp.where(group == number, found[number * F : (number + 1) * F], picked)
    return picked


def step_kernel(
    halves,
    roles,
    groups,
    table_ref,
    near_ref,
    gaps_ref,
    items_ref,
    coef_ref,
    wide_ref,
    kvt_ref,
    kv_ref,
    qt_ref,
    q_ref,
    square_ref,
    loss_ref,
    gtab_ref,
    gkv_ref,
    gq_ref,
    gsquare_ref,
    gwide_ref,
    x_s,
    kv_s,
    sin_s,
    own_s,
    query_s,
    att_s,
    mix_s,
    z_s,
    dz_s,
    hot_s,
    right_s,
):
    nodes = groups * LO
    scale = 1.0 / math.sqrt(HS)
    w_time, b_time = wide_ref[0], wide_ref[1]
    b_p1, w_p2 = wide_ref[2], wide_ref[3]
    b_p2 = wide_ref[4][0:1]
    zero_cos, zero_sin = any_angle(b_time)
    furthest = jnp.max(jnp.abs(gaps_ref[...])) * jnp.max(jnp.abs(w_time)) + jnp.max(jnp.abs(b_time))
    moderate = furthest <= 8192.0
    zero_code = zero_cos.astype(jnp.bfloat16)
    for ref in (gtab_ref, gkv_ref, gq_ref, gsquare_ref, gwide_ref, loss_ref):
        ref[...] = jnp.zeros_like(ref)
    w_time2, b_time2 = pair(w_time), pair(b_time)

    def half_step(half, carry):
        def forward(trig, role, carry):
            block = half * roles + role
            own = take_rows(table_ref, groups, items_ref[block]).astype(jnp.bfloat16)
            own_s[role] = own
            query = dot(qt_ref[...], jnp.concatenate([own, zero_code], axis=0))
            query_s[role] = query
            query2 = pair(query)
            scores = []
            for c in range(CH):
                near = take_rows(table_ref, groups, near_ref[block, c : c + 1]).astype(jnp.bfloat16)
                angle = gaps_ref[block, c : c + 1] * w_time2 + b_time2
                cos_value, sin_value = trig(angle)
                sin_s[role, c] = sin_value
                x = jnp.concatenate([near, cos_value.astype(jnp.bfloat16)], axis=0)
                x_s[role, c] = x
                kv = dot(kvt_ref[...], x)
                kv_s[role, c] = kv
                scores.append(head_sums(kv[:F] * query2) * scale)
            top = scores[0]
            for c in range(1, CH):
                top = jnp.maximum(top, scores[c])
            top = pair(jnp.maximum(top[:, :W], top[:, W:]))
            powers = [jnp.exp(s - top) for s in scores]
            total = powers[0]
            for c in range(1, CH):
                total = total + powers[c]
            inverse = pair(1.0 / fold(total))
            mixed = jnp.zeros((F, 2 * W), jnp.float32)
            for c in range(CH):
                share = powers[c] * inverse
                att_s[role, c] = share
                mixed = mixed + head_spread(share) * kv_s[role, c, F:]
            mixed = fold(mixed).astype(jnp.bfloat16)
            mix_s[role] = mixed
            emb = own.astype(jnp.float32) + dot(square_ref[0], mixed)
            z_s[role] = emb.astype(jnp.bfloat16)
            return carry

        for usable, trig in ((moderate, sine_cosine), (jnp.logical_not(moderate), any_angle)):

            @pl.when(usable)
            def run_forward(trig=trig):
                lax.fori_loop(0, roles, functools.partial(forward, trig), 0)

        source = z_s[0]
        from_source = dot(square_ref[2], source) + b_p1
        d_source = jnp.zeros((F, W), jnp.float32)
        for role in range(1, roles):
            before = from_source + dot(square_ref[4], z_s[role])
            inner = 0.7978845608028654 * (before + 0.044715 * before * before * before)
            bend = jnp.tanh(inner)
            hidden = (0.5 * before * (1.0 + bend)).astype(jnp.bfloat16).astype(jnp.float32)
            slope = 0.5 * (1.0 + bend) + 0.5 * before * (1.0 - bend * bend) * (
                0.7978845608028654 * (1.0 + 3.0 * 0.044715 * before * before)
            )
            score = jnp.sum(hidden * w_p2, axis=0, keepdims=True) + b_p2
            sign = -1.0 if role == 1 else 1.0
            weight = coef_ref[half, role - 1 : role]
            signed = sign * score
            small = jnp.exp(-jnp.abs(signed))
            loss_ref[0:1] += weight * (jnp.maximum(signed, 0.0) + jnp.log1p(small))
            sigmoid = jnp.where(signed >= 0.0, 1.0, small) / (1.0 + small)
            d_score = (sign * weight) * sigmoid
            gwide_ref[3] += hidden * d_score
            gwide_ref[4, 0:1] += d_score
            d_before = w_p2 * d_score * slope
            gwide_ref[2] += d_before
            d_source = d_source + d_before
            terms = jnp.concatenate(split_terms(d_before), axis=1)
            gsquare_ref[2] += dot_nt(pair(z_s[role]), terms)
            dz_s[role] = fold(dot(square_ref[5], terms))
        terms = jnp.concatenate(split_terms(d_source), axis=1)
        gsquare_ref[1] += dot_nt(pair(source), terms)
        dz_s[0] = fold(dot(square_ref[3], terms))

        def backward(role, carry):
            block = half * roles + role
            d_emb = dz_s[role]
            terms = jnp.concatenate(split_terms(d_emb), axis=1)
            gsquare_ref[0] += dot_nt(pair(mix_s[role]), terms)
            d_mixed = pair(fold(dot(square_ref[1], terms)))
            query2 = pair(query_s[role])
            d_shares = [head_sums(d_mixed * kv_s[role, c, F:]) for c in range(CH)]
            total = jnp.zeros((2, 2 * W), jnp.float32)
            for c in range(CH):
                total = total + att_s[role, c] * d_shares[c]
            total = pair(fold(total))
            d_query = jnp.zeros((F, 2 * W), jnp.float32)
            for c in range(CH):
                share = att_s[role, c]
                d_score = head_spread(share * (d_shares[c] - total) * scale)
                d_query = d_query + d_score * kv_s[role, c, :F]
                d_kv = jnp.concatenate([d_score * query2, head_spread(share) * d_mixed], axis=0)
                upper, lower = split_terms(d_kv)
                x = x_s[role, c]
                gkv_ref[...] += dot_nt(x, upper) + dot_nt(x, lower)
                d_x = dot(kv_ref[...], upper) + dot(kv_ref[...], lower)
                turned = sin_s[role, c] * d_x[F:]
                gwide_ref[1] -= fold(turned)
                gwide_ref[0] -= fold(turned * gaps_ref[block, c : c + 1])
                upper, lower = split_terms(d_x[:F])
                lanes_at = slice(c * 2 * W, (c + 1) * 2 * W)
                right_s[:F, lanes_at] = upper
                right_s[F:, lanes_at] = lower
                group, hot = one_hot(near_ref[block, c : c + 1])
                for number in range(groups):
                    hot_s[number * LO : (number + 1) * LO, lanes_at] = jnp.where(
                        group == number, hot, jnp.zeros_like(hot)
                    )
            d_query = fold(d_query)
            terms = jnp.concatenate(split_terms(d_query), axis=1)
            own = own_s[role]
            code = jnp.concatenate([own, zero_code], axis=0)
            gq_ref[...] += dot_nt(pair(code), terms)
            d_code = fold(dot(q_ref[...], terms))
            gwide_ref[1] -= zero_sin * d_code[F:]
            upper, lower = split_terms(d_emb + d_code[:F])
            lanes_at = slice(CH * 2 * W, CH * 2 * W + W)
            right_s[:F, lanes_at] = upper
            right_s[F:, lanes_at] = lower
            group, hot = one_hot(items_ref[block])
            for number in range(groups):
                hot_s[number * LO : (number + 1) * LO, lanes_at] = jnp.where(
                    group == number, hot, jnp.zeros_like(hot)
                )
            for number in range(groups):
                rows = slice(number * LO, (number + 1) * LO)
                gtab_ref[rows] += dot_nt(hot_s[rows], right_s[...])
            return carry

        lax.fori_loop(0, roles, backward, 0)
        return carry

    lax.fori_loop(0, halves, half_step, 0)


def pad_heads(matrix, axis):
    shape = matrix.shape
    split = matrix.reshape(shape[:axis] + (HEADS, HS) + shape[axis + 1 :])
    widths = [(0, 0)] * split.ndim
    widths[axis + 1] = (0, HP - HS)
    return jnp.pad(split, widths).reshape(shape[:axis] + (F,) + shape[axis + 1 :])


def cut_heads(matrix, axis):
    shape = matrix.shape
    split = matrix.reshape(shape[:axis] + (HEADS, HP) + shape[axis + 1 :])
    return lax.slice_in_dim(split, 0, HS, axis=axis + 1).reshape(
        shape[:axis] + (D,) + shape[axis + 1 :]
    )


def pad_to(matrix, axis):
    widths = [(0, 0)] * matrix.ndim
    widths[axis] = (0, F - matrix.shape[axis])
    return jnp.pad(matrix, widths)


def event_step(params, table, items, item_times, coef, neighbours, neighbour_times):
    roles, events = items.shape
    halves = events // W
    nodes = table.shape[0]
    groups = nodes // LO
    blocks = halves * roles

    def by_block(array):
        split = array.reshape((roles, halves, W) + array.shape[2:])
        return jnp.swapaxes(split, 0, 1).reshape((blocks, W) + array.shape[2:])

    ids = by_block(items)
    near = jnp.swapaxes(neighbours[ids.reshape(-1)].reshape(blocks, W, NBR), 1, 2)
    near_times = jnp.swapaxes(neighbour_times[ids.reshape(-1)].reshape(blocks, W, NBR), 1, 2)
    at = by_block(jnp.broadcast_to(item_times[None], (roles, events)))
    near = near.reshape(blocks, CH, 2 * W)
    gaps = (at[:, None, :] - near_times).reshape(blocks, CH, 2 * W)
    coef = jnp.swapaxes(coef.reshape(roles - 1, halves, W), 0, 1)
    table_t = jnp.swapaxes(pad_to(table.reshape(groups, LO, D), 2), 1, 2).reshape(groups * F, LO)

    def stacked_rows(matrix):
        return jnp.concatenate([pad_to(matrix[:D], 0), pad_to(matrix[D:], 0)], 0)

    w_kv = params["w_kv"]
    w_kv = jnp.concatenate([pad_heads(w_kv[:, :D], 1), pad_heads(w_kv[:, D:], 1)], 1)
    w_kv = stacked_rows(w_kv)
    w_q = stacked_rows(pad_heads(params["w_query"], 1))
    w_out = pad_to(pad_heads(params["w_out"], 0), 1)
    w_ps = pad_to(pad_to(params["w_ps"], 0), 1)
    w_pd = pad_to(pad_to(params["w_pd"], 0), 1)
    square = jnp.stack([w_out.T, w_out, w_ps.T, w_ps, w_pd.T, w_pd])
    columns = jnp.stack(
        [
            pad_to(params["w_time"], 0),
            pad_to(params["b_time"], 0),
            pad_to(params["b_p1"], 0),
            pad_to(params["w_p2"], 0),
            jnp.broadcast_to(params["b_p2"], (F,)),
        ]
    ).astype(jnp.float32)
    wide = jnp.broadcast_to(columns[:, :, None], (5, F, W))
    full = 2 * CH * W + W
    outs = pl.pallas_call(
        functools.partial(step_kernel, halves, roles, groups),
        out_shape=(
            jax.ShapeDtypeStruct((1, W), jnp.float32),
            jax.ShapeDtypeStruct((nodes, 2 * F), jnp.float32),
            jax.ShapeDtypeStruct((2 * F, 2 * F), jnp.float32),
            jax.ShapeDtypeStruct((2 * F, F), jnp.float32),
            jax.ShapeDtypeStruct((3, F, F), jnp.float32),
            jax.ShapeDtypeStruct((5, F, W), jnp.float32),
        ),
        in_specs=[pl.BlockSpec(memory_space=pltpu.VMEM)] * 11,
        out_specs=(pl.BlockSpec(memory_space=pltpu.VMEM),) * 6,
        scratch_shapes=[
            pltpu.VMEM((roles, CH, 2 * F, 2 * W), jnp.bfloat16),
            pltpu.VMEM((roles, CH, 2 * F, 2 * W), jnp.float32),
            pltpu.VMEM((roles, CH, F, 2 * W), jnp.float32),
            pltpu.VMEM((roles, F, W), jnp.bfloat16),
            pltpu.VMEM((roles, F, W), jnp.float32),
            pltpu.VMEM((roles, CH, 2, 2 * W), jnp.float32),
            pltpu.VMEM((roles, F, W), jnp.bfloat16),
            pltpu.VMEM((roles, F, W), jnp.bfloat16),
            pltpu.VMEM((roles, F, W), jnp.float32),
            pltpu.VMEM((nodes, full), jnp.bfloat16),
            pltpu.VMEM((2 * F, full), jnp.bfloat16),
        ],
        compiler_params=pltpu.CompilerParams(vmem_limit_bytes=60 * 1024 * 1024),
    )(
        table_t,
        near,
        gaps,
        ids[:, None, :],
        coef,
        wide,
        w_kv.T,
        w_kv,
        w_q.T,
        w_q,
        square,
    )
    loss, g_table, g_kv, g_q, g_square, g_wide = outs

    def cut_rows(matrix):
        return jnp.concatenate([matrix[:D], matrix[F : F + D]], 0)

    g_kv = cut_rows(g_kv)
    g_wide = jnp.sum(g_wide, axis=2)
    grads = [
        g_wide[0, :TE],
        g_wide[1, :TE],
        cut_heads(cut_rows(g_q), 1).reshape(-1),
        jnp.concatenate([cut_heads(g_kv[:, :F], 1), cut_heads(g_kv[:, F:], 1)], 1).reshape(-1),
        cut_heads(g_square[0], 0)[:, :D].reshape(-1),
        g_square[1][:D, :PH].reshape(-1),
        g_square[2][:D, :PH].reshape(-1),
        g_wide[2, :PH],
        g_wide[3, :PH],
        g_wide[4, :1],
    ]
    return jnp.sum(loss), jnp.concatenate(grads), g_table[:, :D] + g_table[:, F : F + D]


def exchange_order(names):
    order = []
    for name in reversed(names):
        bits = (lax.axis_size(name) - 1).bit_length()
        rising = range(bits) if name == names[-1] else reversed(range(bits))
        order.extend((name, bit) for bit in rising)
    return order


def partner(array, name, bit):
    size = lax.axis_size(name)
    return lax.ppermute(array, name, [(i, i ^ (1 << bit)) for i in range(size)])


def my_bit(name, bit):
    return (lax.axis_index(name) >> bit) & 1


def gather_all(shard):
    held = shard[None]
    for bit in range((lax.axis_size("neg") - 1).bit_length()):
        other = partner(held, "neg", bit)
        mine_first = my_bit("neg", bit) == 0
        held = jnp.concatenate(
            [jnp.where(mine_first, held, other), jnp.where(mine_first, other, held)]
        )
    return lax.all_gather(held, "ev", axis=0, tiled=True)


def scatter_sum(blocks, names=("ev", "neg")):
    dims = []
    for name in names:
        bits = (lax.axis_size(name) - 1).bit_length()
        dims.extend((name, bit) for bit in reversed(range(bits)))
    held = blocks.reshape((2,) * len(dims) + blocks.shape[1:])
    left = list(dims)
    for name, bit in reversed(exchange_order(names)):
        place = left.index((name, bit))
        mine = my_bit(name, bit)
        keep = lax.dynamic_index_in_dim(held, mine, place, keepdims=False)
        give = lax.dynamic_index_in_dim(held, 1 - mine, place, keepdims=False)
        held = keep + partner(give, name, bit)
        left.remove((name, bit))
    return held


def lanes(flat):
    amount = flat.shape[-1]
    rows = -(-amount // 128)
    wide = jnp.pad(flat, [(0, 0)] * (flat.ndim - 1) + [(0, rows * 128 - amount)])
    return wide.reshape(flat.shape[:-1] + (rows, 128))


def on_device(
    master,
    first_moment,
    second_moment,
    memory,
    messages,
    static_ids,
    node_features,
    neighbours,
    neighbour_times,
    last_partner,
    last_deltas,
    last_edges,
    sources,
    targets,
    times,
    negatives,
    neg_counts,
):
    shard = master.shape[0]
    devices = lax.axis_size("ev") * lax.axis_size("neg")
    groups = lax.axis_size("neg")
    rank = lax.axis_index("neg")
    own_events = sources.shape[0]
    events_all = own_events * devices
    own_counts = lax.dynamic_slice_in_dim(neg_counts, rank * own_events, own_events)
    amount = jnp.sum(own_counts)
    digits = jnp.stack([amount // 128, amount % 128]).astype(jnp.bfloat16)
    copies = gather_all(lanes(jnp.concatenate([master.astype(jnp.bfloat16), digits])))
    copies = copies.reshape(devices, -1)
    copies_flat = copies[:, :shard].reshape(-1)
    flat = copies_flat.astype(jnp.float32)
    counted = copies[:, shard : shard + 2].astype(jnp.float32)
    neg_total = jnp.sum(counted[:, 0]) * 128.0 + jnp.sum(counted[:, 1])
    own_negatives = lax.all_to_all(negatives, "neg", split_axis=0, concat_axis=1, tiled=True)
    total_neg = own_negatives.shape[1]
    columns = jnp.arange(total_neg, dtype=jnp.int32)
    active = (columns[None, :] >= total_neg - own_counts[:, None]).astype(jnp.float32)
    own_times = lax.dynamic_slice_in_dim(times, rank * own_events, own_events)
    feature_rows = node_features[static_ids].astype(jnp.float32)
    message_rows = messages.astype(jnp.float32)

    def owner_part(weights_flat):
        return owner_pass(unpack(weights_flat), memory, message_rows, feature_rows)

    state, owner_back, renewed = jax.vjp(owner_part, flat, has_aux=True)
    table_low = gather_all(state.astype(jnp.bfloat16)).reshape(-1, D)
    table = table_low.astype(jnp.float32)

    items = jnp.concatenate([sources[None], targets[None], own_negatives.T])
    coef = jnp.concatenate(
        [jnp.full((1, own_events), 1.0 / events_all, jnp.float32), active.T / neg_total]
    )
    local_loss, grad_event, grad_table = event_step(
        unpack(copies_flat), table_low, items, own_times, coef, neighbours, neighbour_times
    )
    grad_state = scatter_sum(grad_table.reshape(devices, -1, D))
    grad_flat_node = owner_back(grad_state)[0]
    rest = flat.shape[0] - PLIVE
    grads = jnp.concatenate([grad_flat_node[:NODE_LIVE], grad_event, jnp.zeros((rest,), jnp.float32)])
    losses = jnp.broadcast_to(local_loss, (devices, 1))
    totals = scatter_sum(lanes(jnp.concatenate([grads.reshape(devices, shard), losses], 1)))
    totals = totals.reshape(-1)
    grad_shard, loss = totals[:shard], totals[shard]
    new_master, new_first, new_second = adamw(master, first_moment, second_moment, grad_shard)
    params_low = unpack(flat)
    own_table = low(state)
    carried = jnp.concatenate(
        [
            own_table,
            table[last_partner],
            time_code(last_deltas, params_low),
            last_edges.astype(jnp.float32),
        ],
        1,
    )
    return (loss, neg_total, new_master, new_first, new_second, renewed, carried)


def solution(mesh):
    return jax.shard_map(
        on_device,
        mesh=mesh,
        in_specs=(
            P(("ev", "neg")),
            P(("ev", "neg")),
            P(("ev", "neg")),
            P(("ev", "neg"), None),
            P(("ev", "neg"), None),
            P(("ev", "neg")),
            P(),
            P(),
            P(),
            P(("ev", "neg")),
            P(("ev", "neg")),
            P(("ev", "neg"), None),
            P(("ev", "neg")),
            P(("ev", "neg")),
            P("ev"),
            P("ev", "neg"),
            P("ev"),
        ),
        out_specs=(
            P(),
            P(),
            P(("ev", "neg")),
            P(("ev", "neg")),
            P(("ev", "neg")),
            P(("ev", "neg"), None),
            P(("ev", "neg"), None),
        ),
        check_vma=False,
    )
```

```python
import functools
import math

import jax
import jax.numpy as jnp
from jax import lax
from jax.experimental import pallas as pl
from jax.experimental.pallas import tpu as pltpu
from jax.sharding import PartitionSpec as P

D = 100
TE = 100
NF = 413
PH = 100
HEADS = 2
NBR = 10
STEP = 10
HS = 50
MSG = 486
PARAMS = 308224


beta_one = 0.9
beta_two = 0.999
rate_lr = 0.02
decay_wd = 0.01
eps_adam = 1e-08

HP = 56
F = HEADS * HP
W = 128
LO = 256
L = 128
MSG_PAD = 512
HOT = 2048
NODE_STEP = 256
VMEM_BYTES = 60 * 1024 * 1024


def unpack(flat):
    layout = [
        ("w_gi", (MSG, 3 * D)),
        ("w_gh", (D, 3 * D)),
        ("b_g", (2, 3 * D)),
        ("w_feat", (NF, D)),
        ("w_time", (TE,)),
        ("b_time", (TE,)),
        ("w_query", (D + TE, D)),
        ("w_kv", (D + TE, 2 * D)),
        ("w_out", (D, D)),
        ("w_ps", (D, PH)),
        ("w_pd", (D, PH)),
        ("b_p1", (PH,)),
        ("w_p2", (PH,)),
        ("b_p2", (1,)),
    ]
    params = {}
    offset = 0
    for label, shape in layout:
        amount = math.prod(shape)
        params[label] = flat[offset : offset + amount].reshape(shape)
        offset += amount
    return params


def dot(left, right):
    return jnp.dot(left, right, preferred_element_type=jnp.float32)


def dot_nt(left, right):
    return lax.dot_general(
        left, right, (((1,), (1,)), ((), ())), preferred_element_type=jnp.float32
    )


def dot_tn(left, right):
    return lax.dot_general(
        left, right, (((0,), (0,)), ((), ())), preferred_element_type=jnp.float32
    )


def split_terms(value):
    first = value.astype(jnp.bfloat16)
    return first, (value - first.astype(jnp.float32)).astype(jnp.bfloat16)


def settled_terms(value):
    first = lax.optimization_barrier(value.astype(jnp.bfloat16))
    return first, (value - first.astype(jnp.float32)).astype(jnp.bfloat16)


def three_terms(value):
    first = value.astype(jnp.bfloat16)
    rest = value - first.astype(jnp.float32)
    second = rest.astype(jnp.bfloat16)
    return first, second, (rest - second.astype(jnp.float32)).astype(jnp.bfloat16)


def owner_pass(params, memory, messages, features):
    inputs = dot(messages, params["w_gi"]) + params["b_g"][0].astype(jnp.float32)
    hidden = dot(memory.astype(jnp.bfloat16), params["w_gh"]) + params["b_g"][1].astype(jnp.float32)
    reset = jax.nn.sigmoid(inputs[:, :D] + hidden[:, :D])
    update = jax.nn.sigmoid(inputs[:, D : 2 * D] + hidden[:, D : 2 * D])
    candidate = jnp.tanh(inputs[:, 2 * D :] + reset * hidden[:, 2 * D :])
    renewed = (1.0 - update) * candidate + update * memory
    return (renewed + dot(features, params["w_feat"]), renewed)


def adamw(master, first_state, second_state, grads):
    first_new = beta_one * first_state + (1.0 - beta_one) * grads
    second_new = beta_two * second_state + (1.0 - beta_two) * grads * grads
    corrected = (
        first_new
        / (1.0 - beta_one**STEP)
        / (jnp.sqrt(second_new / (1.0 - beta_two**STEP)) + eps_adam)
    )
    return (master - rate_lr * (corrected + decay_wd * master), first_new, second_new)


def sine_cosine(angle):
    turns = jnp.round(angle * (2.0 / math.pi))
    rest = angle - turns * 1.5703125
    rest = rest - turns * 4.837512969970703e-4
    rest = rest - turns * 7.549789948768648e-8
    square = rest * rest
    sine = rest + rest * square * (
        -1.6666654611e-1 + square * (8.3321608736e-3 - square * 1.9515295891e-4)
    )
    cosine = (
        1.0
        - 0.5 * square
        + square
        * square
        * (4.166664568298827e-2 + square * (-1.388731625493765e-3 + square * 2.443315711809948e-5))
    )
    quadrant = turns.astype(jnp.int32)
    odd = (quadrant & 1) == 1
    cos_value = jnp.where(odd, sine, cosine)
    sin_value = jnp.where(odd, cosine, sine)
    cos_value = jnp.where(((quadrant + 1) & 2) == 2, -cos_value, cos_value)
    sin_value = jnp.where((quadrant & 2) == 2, -sin_value, sin_value)
    return cos_value, sin_value


def any_angle(angle):
    return jnp.cos(angle), jnp.sin(angle)


def pair(value):
    return jnp.concatenate([value, value], axis=1)


def fold(value):
    return value[:, :W] + value[:, W:]


def tile(k):
    return slice(k * W, (k + 1) * W)


def hot_rows(hot_ref, ids, base=0):
    count = ids.shape[1]
    rows = lax.broadcasted_iota(jnp.int32, (LO, count), 0).astype(jnp.float32).astype(jnp.bfloat16)
    place = (ids & (LO - 1)).astype(jnp.float32)
    group = ids // LO - base // LO
    one, nought = jnp.ones_like(rows), jnp.zeros_like(rows)
    for number in range(hot_ref.shape[0] // LO):
        here = jnp.where(group == number, place, -1.0)
        here = jnp.broadcast_to(here, (LO, count)).astype(jnp.bfloat16)
        hot_ref[number * LO : (number + 1) * LO] = jnp.where(rows == here, one, nought)


def gather_columns(table_ref, hot_ref, ids):
    step = hot_ref.shape[0]
    found = None
    for base in range(0, table_ref.shape[1], step):
        hot_rows(hot_ref, ids, base)
        part = dot(table_ref[:, base : base + step], hot_ref[...])
        found = part if found is None else found + part
    return found


SRC, TGT, TIME, COUNT, NEG = 0, 1, 2, 3, 4
NEAR_ROWS = 16


def column_of(row, lanes_of):
    wide = jnp.transpose(jnp.broadcast_to(row, (L, row.shape[1])))
    return jnp.concatenate([wide] * (lanes_of // L), axis=1)


def prepare_kernel(
    columns,
    rank_ref,
    source_ref,
    target_ref,
    times_ref,
    numbers_ref,
    negatives_ref,
    static_ref,
    near_ref,
    then_ref,
    ids_ref,
    gaps_ref,
    counts_ref,
    tail_ref,
    live_ref,
    event_s,
    around_s,
    hot_s,
):
    halves = source_ref.shape[0]
    events = halves * W
    roles = 2 + columns
    mine = pl.ds(rank_ref[0] * halves, halves)
    event_s[...] = jnp.zeros_like(event_s)
    for row, held in enumerate(
        [source_ref[...], target_ref[...], times_ref[mine], numbers_ref[mine]]
        + [negatives_ref[j, mine] for j in range(columns)]
    ):
        held = held.astype(jnp.float32)
        for half in range(halves):
            event_s[row : row + 1, half * W : (half + 1) * W] = held[half : half + 1]
    counts = event_s[COUNT : COUNT + 1]
    here = lax.broadcasted_iota(jnp.int32, (events, events), 1)
    other = lax.broadcasted_iota(jnp.int32, (events, events), 0)
    count_of = column_of(counts, events)
    before = (count_of > counts) | ((count_of == counts) & (other < here))
    place = jnp.sum(jnp.where(before, 1.0, 0.0), axis=0, keepdims=True)
    order = jnp.where(other.astype(jnp.float32) == place, 1.0, 0.0).astype(jnp.bfloat16)
    ordered = sum(dot_nt(term, order) for term in three_terms(event_s[...]))
    total = jnp.sum(counts, axis=1, keepdims=True).astype(jnp.int32)
    static = column_of(static_ref[...].astype(jnp.float32), L).astype(jnp.int32)
    lane = lax.broadcasted_iota(jnp.int32, static.shape, 1)
    value = jnp.where(lane < 2, static, total)
    value = jnp.where((lane & 1) == 0, value >> 7, value & 127)
    tail_ref[...] = value.astype(jnp.float32).astype(jnp.bfloat16)
    counts = ordered[COUNT : COUNT + 1]
    for half in range(halves):
        counts_ref[half] = counts[:, half * W : (half + 1) * W]
        live_ref[half] = 2
    for number in range(columns):
        held = jnp.sum(jnp.where(counts >= number + 1.0, 1, 0))
        for half in range(halves):
            live_ref[half] += jnp.where(held > half * W, 1, 0).astype(jnp.int32)
    times = ordered[TIME : TIME + 1]
    around_s[...] = jnp.zeros_like(around_s)
    near = near_ref[...]
    parts = [(near >> 7).astype(jnp.float32), (near & 127).astype(jnp.float32)]
    parts = [part.astype(jnp.bfloat16) for part in parts] + list(three_terms(then_ref[...]))
    for number, part in enumerate(parts):
        around_s[number * NEAR_ROWS : number * NEAR_ROWS + NBR] = part
    for role in range(roles):
        row = (SRC, TGT)[role] if role < 2 else NEG + columns - 1 - (role - 2)
        nodes = ordered[row : row + 1].astype(jnp.int32)
        found = gather_columns(around_s, hot_s, nodes)
        near = found[:NBR] * 128.0 + found[NEAR_ROWS : NEAR_ROWS + NBR]
        near = near.astype(jnp.int32)
        then = (
            found[2 * NEAR_ROWS : 2 * NEAR_ROWS + NBR] + found[3 * NEAR_ROWS : 3 * NEAR_ROWS + NBR]
        ) + found[4 * NEAR_ROWS : 4 * NEAR_ROWS + NBR]
        gaps = times - then
        for half in range(halves):
            block, lanes_at = half * roles + role, slice(half * W, (half + 1) * W)
            for k in range(NBR):
                ids_ref[block, :, tile(k)] = near[k : k + 1, lanes_at]
                gaps_ref[block, :, tile(k)] = gaps[k : k + 1, lanes_at]
            ids_ref[block, :, NBR * W :] = nodes[:, lanes_at]


def step_kernel(
    halves,
    roles,
    own_nodes,
    events_all,
    live_ref,
    bit_ref,
    table_ref,
    ids_ref,
    gaps_ref,
    counts_ref,
    wide_ref,
    kvt_ref,
    kv_ref,
    qt_ref,
    q_ref,
    square_ref,
    loss_ref,
    count_ref,
    keep_ref,
    give_ref,
    gkv_ref,
    gq_ref,
    gsquare_ref,
    gsmall_ref,
    x_s,
    kv_s,
    sin_s,
    own_s,
    query_s,
    att_s,
    mix_s,
    z_s,
    dz_s,
    hot_s,
    right_s,
    upper_s,
    lower_s,
    rows_s,
    gkv_s,
    gq_s,
    gsquare_s,
    gwide_s,
):
    scale = 1.0 / math.sqrt(HS)
    near = NBR * W
    found = table_ref[F : F + 16].astype(jnp.float32)
    counted = jnp.sum(found, axis=1, keepdims=True)
    neg_total = (counted[2:3] * 128.0 + counted[3:4]) * (1.0 / own_nodes)
    count_ref[...] = jnp.broadcast_to(neg_total, (1, W))
    share = jnp.broadcast_to(1.0 / neg_total, (1, W))
    b_time = wide_ref[1]
    b_p1, w_p2 = wide_ref[2], wide_ref[3]
    b_p2 = wide_ref[4][0:1]
    zero_cos, zero_sin = any_angle(b_time)
    furthest = jnp.max(jnp.abs(gaps_ref[...])) * jnp.max(jnp.abs(wide_ref[0])) + jnp.max(
        jnp.abs(b_time)
    )
    moderate = furthest <= 8192.0
    zero_code = zero_cos.astype(jnp.bfloat16)
    for ref in (rows_s, right_s, gkv_s, gq_s, gsquare_s, gwide_s, loss_ref):
        ref[...] = jnp.zeros_like(ref)
    head_rows = (slice(0, HP), slice(HP, F))

    def half_step(half, carry):
        live = live_ref[half]

        def forward(trig, role, carry):
            block = half * roles + role
            for s in range(0, F, 16):
                rows = slice(s, s + 16)
                w_rows, b_rows = wide_ref[0, rows], wide_ref[1, rows]
                for k in range(NBR):
                    angle = gaps_ref[block, :, tile(k)] * w_rows + b_rows
                    cos_value, sin_value = trig(angle)
                    sin_s[role, rows, tile(k)] = sin_value
                    x_s[role, F + s : F + s + 16, tile(k)] = cos_value.astype(jnp.bfloat16)
            found = gather_columns(table_ref, hot_s, ids_ref[block])[:F].astype(jnp.bfloat16)
            x_s[role, :F] = found[:, :near]
            own = found[:, near:]
            own_s[role] = own
            query = dot(qt_ref[...], jnp.concatenate([own, zero_code], axis=0))
            query_s[role] = query
            kv_s[role] = dot(kvt_ref[...], x_s[role])
            mixed = []
            for h, rows in enumerate(head_rows):
                scores = jnp.concatenate(
                    [
                        jnp.sum(kv_s[role, rows, tile(k)] * query[rows], axis=0, keepdims=True)
                        for k in range(NBR)
                    ],
                    axis=0,
                )
                scores = scores * scale
                powers = jnp.exp(scores - jnp.max(scores, axis=0, keepdims=True))
                att_s[role, h] = powers / jnp.sum(powers, axis=0, keepdims=True)
                mixed_h = jnp.zeros((HP, W), jnp.float32)
                for k in range(NBR):
                    values = kv_s[role, F + h * HP : F + (h + 1) * HP, tile(k)]
                    mixed_h = mixed_h + att_s[role, h, k : k + 1] * values
                mixed.append(mixed_h)
            mixed = jnp.concatenate(mixed, axis=0).astype(jnp.bfloat16)
            mix_s[role] = mixed
            emb = own.astype(jnp.float32) + dot(square_ref[0], mixed)
            z_s[role] = emb.astype(jnp.bfloat16)
            return carry

        for usable, trig in ((moderate, sine_cosine), (jnp.logical_not(moderate), any_angle)):

            @pl.when(usable)
            def run_forward(trig=trig):
                lax.fori_loop(0, live, functools.partial(forward, trig), 0)

        source = z_s[0]
        from_source = dot(square_ref[2], source) + b_p1

        def predict(role, d_source):
            before = from_source + dot(square_ref[4], z_s[role])
            inner = 0.7978845608028654 * (before + 0.044715 * before * before * before)
            bend = jnp.tanh(inner)
            hidden = (0.5 * before * (1.0 + bend)).astype(jnp.bfloat16).astype(jnp.float32)
            slope = 0.5 * (1.0 + bend) + 0.5 * before * (1.0 - bend * bend) * (
                0.7978845608028654 * (1.0 + 3.0 * 0.044715 * before * before)
            )
            score = jnp.sum(hidden * w_p2, axis=0, keepdims=True) + b_p2
            positive = role == 1
            sign = jnp.where(positive, -1.0, 1.0)
            counted = counts_ref[half] >= (role - 1).astype(jnp.float32)
            weight = jnp.where(
                positive, 1.0 / events_all, jnp.where(counted, share, jnp.zeros((1, W)))
            )
            signed = sign * score
            small = jnp.exp(-jnp.abs(signed))
            loss_ref[0:1] += weight * (jnp.maximum(signed, 0.0) + jnp.log1p(small))
            sigmoid = jnp.where(signed >= 0.0, 1.0, small) / (1.0 + small)
            d_score = (sign * weight) * sigmoid
            gwide_s[3] += hidden * d_score
            gwide_s[4, 0:1] += d_score
            d_before = w_p2 * d_score * slope
            gwide_s[2] += d_before
            terms = jnp.concatenate(split_terms(d_before), axis=1)
            gsquare_s[2] += dot_nt(pair(z_s[role]), terms)
            dz_s[role] = fold(dot(square_ref[5], terms))
            return d_source + d_before

        d_source = lax.fori_loop(1, live, predict, jnp.zeros((F, W), jnp.float32))
        terms = jnp.concatenate(split_terms(d_source), axis=1)
        gsquare_s[1] += dot_nt(pair(source), terms)
        dz_s[0] = fold(dot(square_ref[3], terms))

        def backward(role, carry):
            block = half * roles + role
            d_emb = dz_s[role]
            terms = jnp.concatenate(split_terms(d_emb), axis=1)
            gsquare_s[0] += dot_nt(pair(mix_s[role]), terms)
            d_mixed = fold(dot(square_ref[1], terms))
            d_query = []
            for h, rows in enumerate(head_rows):
                d_mixed_h, query_h = d_mixed[rows], query_s[role, rows]
                value_rows = slice(F + h * HP, F + (h + 1) * HP)
                d_shares = jnp.concatenate(
                    [
                        jnp.sum(kv_s[role, value_rows, tile(k)] * d_mixed_h, axis=0, keepdims=True)
                        for k in range(NBR)
                    ],
                    axis=0,
                )
                share = att_s[role, h]
                total = jnp.sum(share * d_shares, axis=0, keepdims=True)
                d_scores = share * (d_shares - total) * scale
                d_query_h = jnp.zeros((HP, W), jnp.float32)
                for k in range(NBR):
                    d_score = d_scores[k : k + 1]
                    d_query_h = d_query_h + d_score * kv_s[role, rows, tile(k)]
                    for at, d_part in (
                        (rows, d_score * query_h),
                        (value_rows, att_s[role, h, k : k + 1] * d_mixed_h),
                    ):
                        upper_s[at, tile(k)], lower_s[at, tile(k)] = split_terms(d_part)
                d_query.append(d_query_h)
            x = x_s[role]
            upper, lower = upper_s[...], lower_s[...]
            gkv_s[...] += dot_nt(x, upper) + dot_nt(x, lower)
            d_x = dot(kv_ref[...], upper) + dot(kv_ref[...], lower)
            for s in range(0, F, 16):
                rows = slice(s, s + 16)
                to_b = jnp.zeros((16, W), jnp.float32)
                to_w = jnp.zeros((16, W), jnp.float32)
                for k in range(NBR):
                    first, second = split_terms(d_x[rows, tile(k)])
                    right_s[rows, tile(k)] = first
                    right_s[L + s : L + s + 16, tile(k)] = second
                    turned = sin_s[role, rows, tile(k)] * d_x[F + s : F + s + 16, tile(k)]
                    to_b = to_b + turned
                    to_w = to_w + turned * gaps_ref[block, :, tile(k)]
                gwide_s[1, rows] -= to_b
                gwide_s[0, rows] -= to_w
            d_query = jnp.concatenate(d_query, axis=0)
            terms = jnp.concatenate(split_terms(d_query), axis=1)
            code = jnp.concatenate([own_s[role], zero_code], axis=0)
            gq_s[...] += dot_nt(pair(code), terms)
            d_code = fold(dot(q_ref[...], terms))
            gwide_s[1] -= zero_sin * d_code[F:]
            right_s[:F, near:], right_s[L : L + F, near:] = split_terms(d_emb + d_code[:F])
            for base in range(0, rows_s.shape[0], hot_s.shape[0]):
                hot_rows(hot_s, ids_ref[block], base)
                rows_s[base : base + hot_s.shape[0]] += dot_nt(hot_s[...], right_s[...])
            return carry

        lax.fori_loop(0, live, backward, 0)
        return carry

    lax.fori_loop(0, halves, half_step, 0)
    region = keep_ref.shape[1]
    for number in range(keep_ref.shape[0]):
        for ref, bit in ((keep_ref, bit_ref[0]), (give_ref, 1 - bit_ref[0])):
            at = pl.ds(pl.multiple_of((2 * number + bit) * region, region), region)
            ref[number] = rows_s[at, :L] + rows_s[at, L:]

    def cut_rows(matrix):
        return jnp.concatenate([matrix[:D], matrix[F : F + D]], axis=0)

    def cut_heads(matrix, axis):
        return jnp.concatenate(
            [
                lax.slice_in_dim(matrix, h * HP, h * HP + HS, axis=axis)
                for h in range(matrix.shape[axis] // HP)
            ],
            axis=axis,
        )

    gkv_ref[...] = cut_heads(cut_rows(gkv_s[...]), 1)
    gq_ref[...] = cut_heads(cut_rows(gq_s[...]), 1)
    gsquare_ref[0] = cut_heads(gsquare_s[0], 0)[:, :D]
    gsquare_ref[1] = gsquare_s[1][:D, :PH]
    gsquare_ref[2] = gsquare_s[2][:D, :PH]
    ones = jnp.ones((8, W), jnp.bfloat16)
    for number in range(5):
        gsmall_ref[number] = sum(dot_nt(ones, term) for term in three_terms(gwide_s[number]))


def kernel_call(kernel, outs, ins, scratch, flops):
    def place(array):
        scalars = len(array.shape) == 1 and array.dtype == jnp.int32
        return pl.BlockSpec(memory_space=pltpu.SMEM if scalars else pltpu.VMEM)

    return pl.pallas_call(
        kernel,
        out_shape=tuple(outs),
        in_specs=[place(array) for array in ins],
        out_specs=tuple(place(array) for array in outs),
        scratch_shapes=[pltpu.VMEM(shape, dtype) for shape, dtype in scratch],
        compiler_params=pltpu.CompilerParams(vmem_limit_bytes=VMEM_BYTES),
        cost_estimate=pl.CostEstimate(flops=flops, bytes_accessed=10**6, transcendentals=0),
    )(*ins)


def array_of(shape, dtype=jnp.float32):
    return jax.ShapeDtypeStruct(shape, dtype)


def by_lanes(flat):
    return flat.reshape(flat.shape[:-1] + (-1, W))


def prepare(rank, sources, targets, times, counts, negatives, static_ids, neighbours, then):
    columns = negatives.shape[0]
    events = sources.shape[0]
    halves = events // W
    blocks = halves * (2 + columns)
    nodes = neighbours.shape[0]
    return kernel_call(
        functools.partial(prepare_kernel, columns),
        [
            array_of((blocks, 1, (NBR + 1) * W), jnp.int32),
            array_of((blocks, 1, NBR * W)),
            array_of((halves, 1, W)),
            array_of((static_ids.shape[0], L), jnp.bfloat16),
            array_of((halves,), jnp.int32),
        ],
        [
            rank[None],
            by_lanes(sources),
            by_lanes(targets),
            by_lanes(times),
            by_lanes(counts),
            by_lanes(negatives),
            static_ids[None],
            neighbours.T,
            then.T,
        ],
        [
            ((-(-(NEG + columns) // 16) * 16, events), jnp.float32),
            ((5 * NEAR_ROWS, nodes), jnp.bfloat16),
            ((min(nodes, HOT), events), jnp.bfloat16),
        ],
        flops=4 * 10**9,
    )


def weights_kernel(
    kv_in, q_in, out_in, source_in, other_in, small_in, kvt_ref, kv_ref, qt_ref, q_ref, square_ref, wide_ref, pad_s
):
    def padded(raw, row_parts, column_parts):
        pad_s[...] = jnp.zeros_like(pad_s)
        value = raw[...].astype(jnp.float32)
        for r_from, r_to, r_size in row_parts:
            for c_from, c_to, c_size in column_parts:
                pad_s[r_to : r_to + r_size, c_to : c_to + c_size] = value[
                    r_from : r_from + r_size, c_from : c_from + c_size
                ]
        return pad_s[...]

    plain = [(0, 0, D)]
    twice = [(0, 0, D), (D, F, TE)]
    heads = [(h * HS, h * HP, HS) for h in range(HEADS)]
    all_heads = [(h * HS, h * HP, HS) for h in range(2 * HEADS)]
    for raw, straight, turned, row_parts, column_parts in (
        (kv_in, kv_ref, kvt_ref, twice, all_heads),
        (q_in, q_ref, qt_ref, twice, heads),
        (out_in, square_ref.at[1], square_ref.at[0], heads, plain),
        (source_in, square_ref.at[3], square_ref.at[2], plain, plain),
        (other_in, square_ref.at[5], square_ref.at[4], plain, plain),
    ):
        full = padded(raw, row_parts, column_parts)
        n, m = straight.shape
        straight[...] = full[:n, :m].astype(jnp.bfloat16)
        turned[...] = jnp.transpose(full)[:m, :n].astype(jnp.bfloat16)
    for number in range(5):
        row = small_in[number : number + 1].astype(jnp.float32)
        wide_ref[number] = column_of(row, W)[:F]


def event_weights(params):
    small = jnp.stack(
        [
            jnp.pad(params["w_time"], (0, L - TE)),
            jnp.pad(params["b_time"], (0, L - TE)),
            jnp.pad(params["b_p1"], (0, L - PH)),
            jnp.pad(params["w_p2"], (0, L - PH)),
            jnp.broadcast_to(params["b_p2"], (L,)),
            *[jnp.zeros((L,), jnp.bfloat16)] * 3,
        ]
    )
    low_type = jnp.bfloat16
    return kernel_call(
        weights_kernel,
        [
            array_of((2 * F, 2 * F), low_type),
            array_of((2 * F, 2 * F), low_type),
            array_of((F, 2 * F), low_type),
            array_of((2 * F, F), low_type),
            array_of((6, F, F), low_type),
            array_of((5, F, W)),
        ],
        [params[name] for name in ("w_kv", "w_query", "w_out", "w_ps", "w_pd")] + [small],
        [((2 * L, 2 * L), jnp.float32)],
        flops=10**8,
    )


def event_step(weights, table, prepared, regions, own_nodes, events_all):
    ids, gaps, counts, live = prepared
    kvt, kv, qt, q, square, wide = weights
    nodes = table.shape[0]
    halves = counts.shape[0]
    roles = ids.shape[0] // halves
    table_t = table.T

    near = NBR * W
    full = near + W
    low_type, high_type = jnp.bfloat16, jnp.float32
    half_table = array_of((regions // 2, nodes // regions, L))
    loss, count, keep, give, g_kv, g_q, g_square, g_small = kernel_call(
        functools.partial(step_kernel, halves, roles, own_nodes, events_all),
        [
            array_of((1, W)),
            array_of((1, W)),
            half_table,
            half_table,
            array_of((D + TE, 2 * D)),
            array_of((D + TE, D)),
            array_of((3, D, PH)),
            array_of((5, 8, F)),
        ],
        [
            live,
            my_bit("ev", 0)[None],
            table_t,
            ids,
            gaps,
            counts,
            wide,
            kvt,
            kv,
            qt,
            q,
            square,
        ],
        [
            ((roles, 2 * F, near), low_type),
            ((roles, 2 * F, near), high_type),
            ((roles, F, near), high_type),
            ((roles, F, W), low_type),
            ((roles, F, W), high_type),
            ((roles, HEADS, NBR, W), high_type),
            ((roles, F, W), low_type),
            ((roles, F, W), low_type),
            ((roles, F, W), high_type),
            ((min(nodes, HOT), full), low_type),
            ((2 * L, full), low_type),
            ((2 * F, near), low_type),
            ((2 * F, near), low_type),
            ((nodes, 2 * L), high_type),
            ((2 * F, 2 * F), high_type),
            ((2 * F, F), high_type),
            ((3, F, F), high_type),
            ((5, F, W), high_type),
        ],
        flops=4 * 10**10,
    )
    grads = [
        g_small[0, 0, :TE],
        g_small[1, 0, :TE],
        g_q,
        g_kv,
        g_square[0],
        g_square[1],
        g_square[2],
        g_small[2, 0, :PH],
        g_small[3, 0, :PH],
        g_small[4, 0, :1],
    ]
    return jnp.sum(loss), count[0, 0], keep, give, grads


def node_kernel(
    start_ref,
    near_ref,
    far_ref,
    static_ref,
    keep_ref,
    came_ref,
    gi_ref,
    gh_ref,
    bias_ref,
    features_ref,
    ggi_ref,
    ggh_ref,
    gbias_ref,
    gfeat_ref,
    upper_s,
    lower_s,
    state_s,
    order_s,
    hot_s,
    gi_s,
    gh_s,
    bias_s,
):
    part_nodes = near_ref.shape[0]
    shards = start_ref.shape[0]
    shard = 2 * part_nodes // shards
    for ref, raw_ref in ((gi_s, gi_ref), (gh_s, gh_ref), (bias_s, bias_ref)):
        ref[...] = jnp.zeros_like(ref)
        for g in range(3):
            ref[: raw_ref.shape[0], g * L : g * L + D] = raw_ref[:, g * D : (g + 1) * D]

    def arrange(number, carry):
        source = pl.ds(pl.multiple_of(start_ref[number], shard), shard)
        order_s[pl.ds(pl.multiple_of(number * shard, shard), shard)] = (
            keep_ref[source] + came_ref[source]
        )
        return carry

    lax.fori_loop(0, shards, arrange, 0)

    def some(rows_ref, first, step, sums):
        at = pl.ds(pl.multiple_of(step * NODE_STEP, NODE_STEP), NODE_STEP)
        into = pl.ds(pl.multiple_of(first + step * NODE_STEP, NODE_STEP), NODE_STEP)
        stored = rows_ref[at, MSG_PAD : MSG_PAD + L]
        held = stored.astype(jnp.float32) + rows_ref[at, MSG_PAD + L :].astype(jnp.float32)
        inputs = dot(rows_ref[at, :MSG_PAD], gi_s[...]) + bias_s[0:1]
        hidden = dot(stored, gh_s[...]) + bias_s[1:2]
        reset = jax.nn.sigmoid(inputs[:, :L] + hidden[:, :L])
        update = jax.nn.sigmoid(inputs[:, L : 2 * L] + hidden[:, L : 2 * L])
        fresh = hidden[:, 2 * L :]
        candidate = jnp.tanh(inputs[:, 2 * L :] + reset * fresh)
        d_state = order_s[into]
        d_third = d_state * (1.0 - update) * (1.0 - candidate * candidate)
        d_fresh = d_third * reset
        d_first = d_third * fresh * reset * (1.0 - reset)
        d_second = d_state * (held - candidate) * update * (1.0 - update)
        news = []
        for number, part in enumerate((d_first, d_second, d_third, d_fresh)):
            lanes_at = slice(number * L, (number + 1) * L)
            news.append(jnp.sum(part, axis=0, keepdims=True))
            upper_s[into, lanes_at], lower_s[into, lanes_at] = split_terms(part)
        state_s[into, :L], state_s[into, L:] = split_terms(keep_ref[into] + came_ref[into])
        return sums + jnp.concatenate(news, axis=1)

    total = jnp.zeros((1, 4 * L), jnp.float32)
    wide_gi, wide_gh = 0.0, 0.0
    for part, rows_ref in enumerate((near_ref, far_ref)):
        first = part * part_nodes
        total = lax.fori_loop(
            0, part_nodes // NODE_STEP, functools.partial(some, rows_ref, first), total
        )
        messages = rows_ref[:, :MSG_PAD]
        stored = rows_ref[:, MSG_PAD : MSG_PAD + L]
        for ref in (upper_s, lower_s):
            terms = ref[first : first + part_nodes]
            wide_gi = wide_gi + dot_tn(messages, terms[:, : 3 * L])
            wide_gh = wide_gh + dot_tn(stored, terms)

    def gates(matrix, order):
        return jnp.concatenate([matrix[:, g * L : g * L + D] for g in order], axis=1)

    gbias_ref[...] = jnp.concatenate([gates(total, (0, 1, 2)), gates(total, (0, 1, 3))], axis=0)
    ggi_ref[...] = gates(wide_gi[:MSG], (0, 1, 2))
    ggh_ref[...] = gates(wide_gh[:D], (0, 1, 3))
    hot_rows(hot_s, static_ref[...])
    by_feature = dot(hot_s[...], state_s[...])
    terms = split_terms(by_feature[:, :L] + by_feature[:, L:])
    wide = dot_tn(features_ref[...], terms[0]) + dot_tn(features_ref[...], terms[1])
    gfeat_ref[...] = wide[:, :D]


def node_grads(params, start, near, far, static_ids, node_features, keep, came):
    nodes = keep.shape[0]
    return list(
        kernel_call(
            node_kernel,
            [
                array_of((MSG, 3 * D)),
                array_of((D, 3 * D)),
                array_of((2, 3 * D)),
                array_of((NF, D)),
            ],
            [
                start,
                near,
                far,
                static_ids,
                keep,
                came,
                params["w_gi"],
                params["w_gh"],
                params["b_g"].astype(jnp.float32),
                node_features,
            ],
            [
                ((nodes, 4 * L), jnp.bfloat16),
                ((nodes, 4 * L), jnp.bfloat16),
                ((nodes, 2 * L), jnp.bfloat16),
                ((nodes, L), jnp.float32),
                ((node_features.shape[0], nodes), jnp.bfloat16),
                ((MSG_PAD, 3 * L), jnp.bfloat16),
                ((L, 3 * L), jnp.bfloat16),
                ((8, 3 * L), jnp.float32),
            ],
            flops=8 * 10**9,
        )
    )


def partner(array, name, bit):
    size = lax.axis_size(name)
    return lax.ppermute(array, name, [(i, i ^ (1 << bit)) for i in range(size)])


def my_bit(name, bit):
    return (lax.axis_index(name) >> bit) & 1


def bits_of(name):
    return (lax.axis_size(name) - 1).bit_length()


def exchange(held, done, name, bit):
    other = partner(held, name, bit)
    mine_first = my_bit(name, bit) == 0
    done = sorted(done + [(name == "neg", -bit)])
    place = done.index((name == "neg", -bit))
    parts = [jnp.where(mine_first, held, other), jnp.where(mine_first, other, held)]
    return jnp.stack(parts, axis=place), done


def gather_neg(shard):
    held, done = shard, []
    for bit in range(bits_of("neg")):
        held, done = exchange(held, done, "neg", bit)
    return held, done


def gather_ev(held, done):
    for bit in list(range(1, bits_of("ev"))) + [0]:
        held, done = exchange(held, done, "ev", bit)
    return held


def reduce_bit(held, bits, bit):
    place = bits.index(bit)
    mine = my_bit("ev", bit)
    keep = lax.dynamic_index_in_dim(held, mine, place, keepdims=False)
    give = lax.dynamic_index_in_dim(held, 1 - mine, place, keepdims=False)
    return keep + partner(give, "ev", bit), [other for other in bits if other != bit]


def scatter_ev(blocks):
    count = bits_of("ev")
    bits = list(reversed(range(count)))
    held = blocks.reshape((2,) * count + blocks.shape[1:])
    for bit in range(count - 2):
        held, bits = reduce_bit(held, bits, bit)
    middle = held.shape[-2] // 16 * 8
    parts = [(held[..., :middle, :], bits), (held[..., middle:, :], bits)]
    for turn in range(2):
        parts = [
            reduce_bit(part, left, bits[(turn + number) % 2])
            for number, (part, left) in enumerate(parts)
        ]
    return jnp.concatenate([part for part, left in parts], axis=-2)


def scatter_neg(blocks):
    return jnp.sum(lax.all_to_all(blocks, "neg", split_axis=0, concat_axis=0, tiled=True), axis=0)


def lanes(flat):
    amount = flat.shape[-1]
    rows = -(-amount // 128)
    wide = jnp.pad(flat, [(0, 0)] * (flat.ndim - 1) + [(0, rows * 128 - amount)])
    return wide.reshape(flat.shape[:-1] + (rows, 128))


def from_digits(pairs, axis):
    pairs = pairs.astype(jnp.float32)
    high, low = (lax.index_in_dim(pairs, place, axis, keepdims=False) for place in (0, 1))
    return high * 128.0 + low


def on_device(
    master,
    first_moment,
    second_moment,
    memory,
    messages,
    static_ids,
    node_features,
    neighbours,
    neighbour_times,
    last_partner,
    last_deltas,
    last_edges,
    sources,
    targets,
    times,
    negatives,
    neg_counts,
):
    shard = master.shape[0]
    groups = lax.axis_size("neg")
    regions = lax.axis_size("ev")
    devices = regions * groups
    rank = lax.axis_index("neg")
    own_events = sources.shape[0]
    own_nodes = memory.shape[0]
    local_neg = negatives.shape[1]
    total_neg = local_neg * groups
    events_all = own_events * devices

    copies, copies_done = gather_neg(lanes(master.astype(jnp.bfloat16)))
    all_negatives = gather_neg(by_lanes(negatives.T))[0].reshape(total_neg, -1)

    terms = settled_terms(memory)
    rows = jnp.concatenate(
        [
            jnp.pad(messages, ((0, 0), (0, MSG_PAD - MSG))),
            jnp.pad(terms[0], ((0, 0), (0, L - D))),
            jnp.pad(terms[1], ((0, 0), (0, L - D))),
        ],
        1,
    )
    start = ((lax.axis_index("ev") // 2) * groups + rank)[None]
    last_ev = bits_of("ev") - 1
    stages = [
        [("ev", bit) for bit in range(1, last_ev)],
        [("neg", bit) for bit in reversed(range(1, bits_of("neg")))],
        [("ev", last_ev)],
        [("neg", 0)],
    ]
    for name, bit in sum(stages, []):
        flip = (1 << bit) if name == "neg" else (1 << (bit - 1)) * groups
        start = jnp.concatenate([start, start ^ flip])

    def further(rows, stage):
        for name, bit in stage:
            rows = jnp.concatenate([rows, partner(rows, name, bit)])
        return rows

    rows = further(rows, stages[0])
    copies, rows = lax.optimization_barrier((copies, rows))
    copies = gather_ev(copies, copies_done)
    rows = further(rows, stages[1])

    ids, gaps, counts, tail, live = prepare(
        rank,
        sources,
        targets,
        times,
        neg_counts,
        all_negatives,
        static_ids,
        neighbours,
        neighbour_times,
    )

    flat = copies.reshape(devices, -1)[:, :shard].reshape(-1)
    state, renewed = owner_pass(unpack(flat), memory, messages, node_features[static_ids])
    sending = jnp.concatenate(
        [jnp.pad(state.astype(jnp.bfloat16), ((0, 0), (0, F - D))), tail[:, : L - F]], 1
    )
    flat, sending, rows = lax.optimization_barrier((flat, sending, rows))
    params = unpack(flat)
    rows = further(rows, stages[2])
    table = gather_ev(*gather_neg(sending)).reshape(-1, L)
    table, rows = lax.optimization_barrier((table, rows))
    far_rows = partner(rows, *stages[3][0])
    local_loss, neg_total, keep, give, grad_event = event_step(
        event_weights(params), table, (ids, gaps, counts, live), regions, own_nodes, events_all
    )
    flat, give, far_rows, local_loss, grad_event = lax.optimization_barrier(
        (flat, give, far_rows, local_loss, grad_event)
    )
    params = unpack(flat)
    static_all = from_digits(table[:, F : F + 2], 1).astype(jnp.int32)
    static_mine = lax.dynamic_index_in_dim(
        static_all.reshape(regions // 2, 2, -1), my_bit("ev", 0), 1, keepdims=False
    ).reshape(1, -1)
    came = partner(give, "ev", 0).reshape(-1, L)
    pieces = node_grads(
        params,
        start * own_nodes,
        rows,
        far_rows,
        static_mine,
        node_features,
        keep.reshape(-1, L),
        came,
    )
    grads = jnp.zeros((shard * devices,), jnp.float32)
    offset = sum(piece.size for piece in pieces)
    for piece in grad_event:
        grads = lax.dynamic_update_slice(grads, piece.reshape(-1), (offset,))
        offset += piece.size
    offset = 0
    for piece in pieces:
        grads = lax.dynamic_update_slice(grads, piece.reshape(-1), (offset,))
        offset += piece.size
    blocks = lanes(grads.reshape(regions, -1))
    block_rows = blocks.shape[1]
    losses = jnp.broadcast_to(local_loss, (regions, 1, L))
    blocks = jnp.concatenate([blocks, losses, jnp.zeros((regions, 7 - block_rows % 8, L))], 1)
    summed = scatter_ev(blocks)
    shares = summed[:block_rows].reshape(-1)[: shard * groups].reshape(groups, shard)
    losses = jnp.broadcast_to(summed[block_rows, :1], (groups, 1))
    totals = scatter_neg(lanes(jnp.concatenate([shares, losses], 1))).reshape(-1)
    grad_shard, loss = totals[:shard], totals[shard]
    new_master, new_first, new_second = adamw(master, first_moment, second_moment, grad_shard)
    codes = jnp.cos(
        last_deltas[:, None] * params["w_time"].astype(jnp.float32)
        + params["b_time"].astype(jnp.float32)
    )
    carried = jnp.concatenate(
        [
            sending[:, :D].astype(jnp.float32),
            table[last_partner][:, :D].astype(jnp.float32),
            codes,
            last_edges.astype(jnp.float32),
        ],
        1,
    )
    return (loss, neg_total, new_master, new_first, new_second, renewed, carried)


def solution(mesh):
    return jax.shard_map(
        on_device,
        mesh=mesh,
        in_specs=(
            P(("ev", "neg")),
            P(("ev", "neg")),
            P(("ev", "neg")),
            P(("ev", "neg"), None),
            P(("ev", "neg"), None),
            P(("ev", "neg")),
            P(),
            P(),
            P(),
            P(("ev", "neg")),
            P(("ev", "neg")),
            P(("ev", "neg"), None),
            P(("ev", "neg")),
            P(("ev", "neg")),
            P("ev"),
            P("ev", "neg"),
            P("ev"),
        ),
        out_specs=(
            P(),
            P(),
            P(("ev", "neg")),
            P(("ev", "neg")),
            P(("ev", "neg")),
            P(("ev", "neg"), None),
            P(("ev", "neg"), None),
        ),
        check_vma=False,
    )
```

```python
import functools
import math

import jax
import jax.numpy as jnp
from jax import lax
from jax.experimental import pallas as pl
from jax.experimental.pallas import tpu as pltpu
from jax.sharding import PartitionSpec as P

D = 100
TE = 100
NF = 413
PH = 100
HEADS = 2
NBR = 10
STEP = 10
HS = 50
MSG = 486
PARAMS_LIVE = 308101


beta_one = 0.9
beta_two = 0.999
rate_lr = 0.02
decay_wd = 0.01
eps_adam = 1e-08

HP = 56
F = HEADS * HP
W = 128
LO = 256
L = 128
MSG_PAD = 512
CHUNK = 10
HOT = 2048
EVENT_ROW = 1696
NODE_STEP = 256
VMEM_BYTES = 60 * 1024 * 1024


def unpack(flat):
    layout = [
        ("w_gi", (MSG, 3 * D)),
        ("w_gh", (D, 3 * D)),
        ("b_g", (2, 3 * D)),
        ("w_feat", (NF, D)),
        ("w_time", (TE,)),
        ("b_time", (TE,)),
        ("w_query", (D + TE, D)),
        ("w_kv", (D + TE, 2 * D)),
        ("w_out", (D, D)),
        ("w_ps", (D, PH)),
        ("w_pd", (D, PH)),
        ("b_p1", (PH,)),
        ("w_p2", (PH,)),
        ("b_p2", (1,)),
    ]
    params = {}
    offset = 0
    for label, shape in layout:
        amount = math.prod(shape)
        params[label] = flat[offset : offset + amount].reshape(shape)
        offset += amount
    return params


def dot(left, right):
    return jnp.dot(left, right, preferred_element_type=jnp.float32)


def dot_nt(left, right):
    return lax.dot_general(
        left, right, (((1,), (1,)), ((), ())), preferred_element_type=jnp.float32
    )


def dot_tn(left, right):
    return lax.dot_general(
        left, right, (((0,), (0,)), ((), ())), preferred_element_type=jnp.float32
    )


def split_terms(value):
    first = value.astype(jnp.bfloat16)
    return first, (value - first.astype(jnp.float32)).astype(jnp.bfloat16)


def settled_terms(value):
    first = lax.optimization_barrier(value.astype(jnp.bfloat16))
    return first, (value - first.astype(jnp.float32)).astype(jnp.bfloat16)


def three_terms(value):
    first = value.astype(jnp.bfloat16)
    rest = value - first.astype(jnp.float32)
    second = rest.astype(jnp.bfloat16)
    return first, second, (rest - second.astype(jnp.float32)).astype(jnp.bfloat16)


def owner_pass(params, memory, messages, features):
    inputs = dot(messages, params["w_gi"]) + params["b_g"][0].astype(jnp.float32)
    hidden = dot(memory.astype(jnp.bfloat16), params["w_gh"]) + params["b_g"][1].astype(jnp.float32)
    reset = jax.nn.sigmoid(inputs[:, :D] + hidden[:, :D])
    update = jax.nn.sigmoid(inputs[:, D : 2 * D] + hidden[:, D : 2 * D])
    candidate = jnp.tanh(inputs[:, 2 * D :] + reset * hidden[:, 2 * D :])
    renewed = (1.0 - update) * candidate + update * memory
    return (renewed + dot(features, params["w_feat"]), renewed)


def adamw(master, first_state, second_state, grads):
    first_new = beta_one * first_state + (1.0 - beta_one) * grads
    second_new = beta_two * second_state + (1.0 - beta_two) * grads * grads
    corrected = (
        first_new
        / (1.0 - beta_one**STEP)
        / (jnp.sqrt(second_new / (1.0 - beta_two**STEP)) + eps_adam)
    )
    return (master - rate_lr * (corrected + decay_wd * master), first_new, second_new)


def sine_cosine(angle):
    turns = jnp.round(angle * (2.0 / math.pi))
    rest = angle - turns * 1.5703125
    rest = rest - turns * 4.837512969970703e-4
    rest = rest - turns * 7.549789948768648e-8
    square = rest * rest
    sine = rest + rest * square * (
        -1.6666654611e-1 + square * (8.3321608736e-3 - square * 1.9515295891e-4)
    )
    cosine = (
        1.0
        - 0.5 * square
        + square
        * square
        * (4.166664568298827e-2 + square * (-1.388731625493765e-3 + square * 2.443315711809948e-5))
    )
    quadrant = turns.astype(jnp.int32)
    odd = (quadrant & 1) == 1
    cos_value = jnp.where(odd, sine, cosine)
    sin_value = jnp.where(odd, cosine, sine)
    cos_value = jnp.where(((quadrant + 1) & 2) == 2, -cos_value, cos_value)
    sin_value = jnp.where((quadrant & 2) == 2, -sin_value, sin_value)
    return cos_value, sin_value


def any_angle(angle):
    return jnp.cos(angle), jnp.sin(angle)


def pair(value):
    return jnp.concatenate([value, value], axis=1)


def fold(value):
    return value[:, :W] + value[:, W:]


def tile(k):
    return slice(k * W, (k + 1) * W)


def hot_rows(hot_ref, ids, base=0):
    count = ids.shape[1]
    rows = lax.broadcasted_iota(jnp.int32, (LO, count), 0).astype(jnp.float32).astype(jnp.bfloat16)
    place = (ids & (LO - 1)).astype(jnp.float32)
    group = ids // LO - base // LO
    one, nought = jnp.ones_like(rows), jnp.zeros_like(rows)
    for number in range(hot_ref.shape[0] // LO):
        here = jnp.where(group == number, place, -1.0)
        here = jnp.broadcast_to(here, (LO, count)).astype(jnp.bfloat16)
        hot_ref[number * LO : (number + 1) * LO] = jnp.where(rows == here, one, nought)


def gather_columns(table_ref, hot_ref, ids):
    step = hot_ref.shape[0]
    found = None
    for base in range(0, table_ref.shape[1], step):
        hot_rows(hot_ref, ids, base)
        part = dot(table_ref[:, base : base + step], hot_ref[...])
        found = part if found is None else found + part
    return found


SRC, TGT, TIME, COUNT, NEG = 0, 1, 2, 3, 4
ID, AT, EVENT = 0, 1, 2
NEAR_ROWS = 16


def column_of(row, lanes_of):
    wide = jnp.transpose(jnp.broadcast_to(row, (L, row.shape[1])))
    return jnp.concatenate([wide] * (lanes_of // L), axis=1)


def prepare_kernel(
    columns,
    rank_ref,
    source_ref,
    target_ref,
    times_ref,
    numbers_ref,
    negatives_ref,
    static_ref,
    near_ref,
    then_ref,
    ids_ref,
    gaps_ref,
    slots_ref,
    valid_ref,
    tail_ref,
    live_ref,
    event_s,
    pair_s,
    around_s,
    hot_s,
):
    halves = source_ref.shape[0]
    events = halves * W
    mine = pl.ds(rank_ref[0] * halves, halves)
    event_s[...] = jnp.zeros_like(event_s)
    for row, held in enumerate(
        [source_ref[...], target_ref[...], times_ref[mine], numbers_ref[mine]]
        + [negatives_ref[j, mine] for j in range(columns)]
    ):
        held = held.astype(jnp.float32)
        for half in range(halves):
            event_s[row : row + 1, half * W : (half + 1) * W] = held[half : half + 1]
    counts = event_s[COUNT : COUNT + 1]
    shape = (events, events)
    earlier = lax.broadcasted_iota(jnp.int32, shape, 0) < lax.broadcasted_iota(jnp.int32, shape, 1)
    earlier = jnp.where(earlier, 1.0, 0.0).astype(jnp.bfloat16)
    event = lax.broadcasted_iota(jnp.int32, (1, events), 1).astype(jnp.float32)
    wanted = lax.broadcasted_iota(jnp.int32, (columns * events, events), 0).astype(jnp.float32)
    taken = jnp.zeros((1, 1), jnp.float32)
    packed = jnp.zeros((16, columns * events), jnp.float32)
    for number in range(columns):
        active = counts >= number + 1.0
        ones = jnp.broadcast_to(jnp.where(active, 1.0, 0.0), (16, events))
        place = taken + dot(ones.astype(jnp.bfloat16), earlier)[0:1]
        taken = taken + jnp.sum(ones[0:1], axis=1, keepdims=True)
        place = jnp.where(active, place, -1.0)
        order = jnp.where(wanted == place, 1.0, 0.0).astype(jnp.bfloat16)
        row = NEG + columns - 1 - number
        pair_s[...] = jnp.zeros_like(pair_s)
        pair_s[ID : ID + 1] = event_s[row : row + 1]
        pair_s[AT : AT + 1] = event_s[TIME : TIME + 1]
        pair_s[EVENT : EVENT + 1] = event
        packed = packed + sum(dot_nt(term, order) for term in three_terms(pair_s[...]))
    slot = lax.broadcasted_iota(jnp.int32, (1, columns * events), 1).astype(jnp.float32)
    valid = jnp.where(slot < taken, 1.0, 0.0)
    live_ref[0] = halves + (jnp.sum(counts).astype(jnp.int32) + W - 1) // W
    total = jnp.sum(counts, axis=1, keepdims=True).astype(jnp.int32)
    static = column_of(static_ref[...].astype(jnp.float32), L).astype(jnp.int32)
    lane = lax.broadcasted_iota(jnp.int32, static.shape, 1)
    value = jnp.where(lane < 2, static, total)
    value = jnp.where((lane & 1) == 0, value >> 7, value & 127)
    tail_ref[...] = value.astype(jnp.float32).astype(jnp.bfloat16)
    around_s[...] = jnp.zeros_like(around_s)
    near = near_ref[...]
    parts = [(near >> 7).astype(jnp.float32), (near & 127).astype(jnp.float32)]
    parts = [part.astype(jnp.bfloat16) for part in parts] + list(three_terms(then_ref[...]))
    for number, part in enumerate(parts):
        around_s[number * NEAR_ROWS : number * NEAR_ROWS + NBR] = part
    sets = [
        (event_s[SRC : SRC + 1], event_s[TIME : TIME + 1], event, jnp.ones((1, events))),
        (event_s[TGT : TGT + 1], event_s[TIME : TIME + 1], event, jnp.ones((1, events))),
    ]
    for number in range(columns):
        part = slice(number * events, (number + 1) * events)
        sets.append((packed[ID : ID + 1, part], packed[AT : AT + 1, part], packed[EVENT : EVENT + 1, part], valid[:, part]))
    for number, (nodes, times, of_event, counted) in enumerate(sets):
        nodes = nodes.astype(jnp.int32)
        found = gather_columns(around_s, hot_s, nodes)
        near = found[:NBR] * 128.0 + found[NEAR_ROWS : NEAR_ROWS + NBR]
        near = near.astype(jnp.int32)
        then = (
            found[2 * NEAR_ROWS : 2 * NEAR_ROWS + NBR] + found[3 * NEAR_ROWS : 3 * NEAR_ROWS + NBR]
        ) + found[4 * NEAR_ROWS : 4 * NEAR_ROWS + NBR]
        gaps = times - then
        for half in range(halves):
            block, lanes_at = number * halves + half, slice(half * W, (half + 1) * W)
            for k in range(NBR):
                ids_ref[block, :, tile(k)] = near[k : k + 1, lanes_at]
                gaps_ref[block, :, tile(k)] = gaps[k : k + 1, lanes_at]
            ids_ref[block, :, NBR * W :] = nodes[:, lanes_at]
            slots_ref[block] = of_event[:, lanes_at].astype(jnp.int32)
            valid_ref[block] = counted[:, lanes_at]


def step_kernel(
    halves,
    own_nodes,
    events_all,
    live_ref,
    bit_ref,
    table_ref,
    ids_ref,
    gaps_ref,
    slots_ref,
    valid_ref,
    wide_ref,
    kvt_ref,
    kv_ref,
    qt_ref,
    q_ref,
    square_ref,
    loss_ref,
    count_ref,
    keep_ref,
    give_ref,
    gkv_ref,
    gq_ref,
    gout_ref,
    gsource_ref,
    gother_ref,
    gtime_ref,
    gbase_ref,
    gp1_ref,
    gp2_ref,
    gend_ref,
    x_s,
    kv_s,
    sin_s,
    own_s,
    query_s,
    att_s,
    mix_s,
    z_s,
    dz_s,
    sources_s,
    dsources_s,
    hot_s,
    right_s,
    upper_s,
    lower_s,
    rows_s,
    gkv_s,
    gq_s,
    gsquare_s,
    gwide_s,
):
    scale = 1.0 / math.sqrt(HS)
    near = NBR * W
    found = table_ref[F : F + 16].astype(jnp.float32)
    counted = jnp.sum(found, axis=1, keepdims=True)
    neg_total = (counted[2:3] * 128.0 + counted[3:4]) * (1.0 / own_nodes)
    count_ref[...] = jnp.broadcast_to(neg_total, (1, W))
    share = jnp.broadcast_to(1.0 / neg_total, (1, W))
    b_time = wide_ref[1]
    b_p1, w_p2 = wide_ref[2], wide_ref[3]
    b_p2 = wide_ref[4][0:1]
    zero_cos, zero_sin = any_angle(b_time)
    furthest = jnp.max(jnp.abs(gaps_ref[...])) * jnp.max(jnp.abs(wide_ref[0])) + jnp.max(
        jnp.abs(b_time)
    )
    moderate = furthest <= 8192.0
    zero_code = zero_cos.astype(jnp.bfloat16)
    for ref in (rows_s, right_s, gkv_s, gq_s, gsquare_s, gwide_s, dsources_s, loss_ref):
        ref[...] = jnp.zeros_like(ref)
    head_rows = (slice(0, HP), slice(HP, F))
    live = live_ref[0]

    def forward(trig, slot, block):
        for s in range(0, F, 16):
            rows = slice(s, s + 16)
            w_rows, b_rows = wide_ref[0, rows], wide_ref[1, rows]
            for k in range(NBR):
                angle = gaps_ref[block, :, tile(k)] * w_rows + b_rows
                cos_value, sin_value = trig(angle)
                sin_s[slot, rows, tile(k)] = sin_value
                x_s[slot, F + s : F + s + 16, tile(k)] = cos_value.astype(jnp.bfloat16)
        found = gather_columns(table_ref, hot_s, ids_ref[block])[:F].astype(jnp.bfloat16)
        x_s[slot, :F] = found[:, :near]
        own = found[:, near:]
        own_s[slot] = own
        query = dot(qt_ref[...], jnp.concatenate([own, zero_code], axis=0))
        query_s[slot] = query
        kv_s[slot] = dot(kvt_ref[...], x_s[slot])
        mixed = []
        for h, rows in enumerate(head_rows):
            scores = jnp.concatenate(
                [
                    jnp.sum(kv_s[slot, rows, tile(k)] * query[rows], axis=0, keepdims=True)
                    for k in range(NBR)
                ],
                axis=0,
            )
            scores = scores * scale
            powers = jnp.exp(scores - jnp.max(scores, axis=0, keepdims=True))
            att_s[slot, h] = powers / jnp.sum(powers, axis=0, keepdims=True)
            mixed_h = jnp.zeros((HP, W), jnp.float32)
            for k in range(NBR):
                values = kv_s[slot, F + h * HP : F + (h + 1) * HP, tile(k)]
                mixed_h = mixed_h + att_s[slot, h, k : k + 1] * values
            mixed.append(mixed_h)
        mixed = jnp.concatenate(mixed, axis=0).astype(jnp.bfloat16)
        mix_s[slot] = mixed
        emb = own.astype(jnp.float32) + dot(square_ref[0], mixed)
        z_s[slot] = emb.astype(jnp.bfloat16)

    def predict(slot, block):
        events = lax.broadcasted_iota(jnp.int32, (halves * W, W), 0)
        of_event = jnp.where(events == slots_ref[block], 1.0, 0.0).astype(jnp.bfloat16)
        source = dot(sources_s[...], of_event).astype(jnp.bfloat16)
        z = z_s[slot]
        before = dot(square_ref[2], source) + dot(square_ref[4], z) + b_p1
        inner = 0.7978845608028654 * (before + 0.044715 * before * before * before)
        bend = jnp.tanh(inner)
        hidden = (0.5 * before * (1.0 + bend)).astype(jnp.bfloat16).astype(jnp.float32)
        slope = 0.5 * (1.0 + bend) + 0.5 * before * (1.0 - bend * bend) * (
            0.7978845608028654 * (1.0 + 3.0 * 0.044715 * before * before)
        )
        score = jnp.sum(hidden * w_p2, axis=0, keepdims=True) + b_p2
        positive = block < 2 * halves
        sign = jnp.where(positive, -1.0, 1.0)
        weight = valid_ref[block] * jnp.where(positive, 1.0 / events_all, share)
        signed = sign * score
        small = jnp.exp(-jnp.abs(signed))
        loss_ref[...] += weight * (jnp.maximum(signed, 0.0) + jnp.log1p(small))
        sigmoid = jnp.where(signed >= 0.0, 1.0, small) / (1.0 + small)
        d_score = (sign * weight) * sigmoid
        gwide_s[3] += hidden * d_score
        gwide_s[4, 0:1] += d_score
        d_before = w_p2 * d_score * slope
        gwide_s[2] += d_before
        terms = jnp.concatenate(split_terms(d_before), axis=1)
        gsquare_s[2] += dot_nt(pair(z), terms)
        dz_s[slot] = fold(dot(square_ref[5], terms))
        dsources_s[...] += dot_nt(terms, pair(of_event))

    def backward(slot, block):
        d_emb = dz_s[slot]
        terms = jnp.concatenate(split_terms(d_emb), axis=1)
        gsquare_s[0] += dot_nt(pair(mix_s[slot]), terms)
        d_mixed = fold(dot(square_ref[1], terms))
        d_query = []
        for h, rows in enumerate(head_rows):
            d_mixed_h, query_h = d_mixed[rows], query_s[slot, rows]
            value_rows = slice(F + h * HP, F + (h + 1) * HP)
            d_shares = jnp.concatenate(
                [
                    jnp.sum(kv_s[slot, value_rows, tile(k)] * d_mixed_h, axis=0, keepdims=True)
                    for k in range(NBR)
                ],
                axis=0,
            )
            part = att_s[slot, h]
            total = jnp.sum(part * d_shares, axis=0, keepdims=True)
            d_scores = part * (d_shares - total) * scale
            d_query_h = jnp.zeros((HP, W), jnp.float32)
            for k in range(NBR):
                d_score = d_scores[k : k + 1]
                d_query_h = d_query_h + d_score * kv_s[slot, rows, tile(k)]
                for at, d_part in (
                    (rows, d_score * query_h),
                    (value_rows, att_s[slot, h, k : k + 1] * d_mixed_h),
                ):
                    upper_s[at, tile(k)], lower_s[at, tile(k)] = split_terms(d_part)
            d_query.append(d_query_h)
        x = x_s[slot]
        upper, lower = upper_s[...], lower_s[...]
        gkv_s[...] += dot_nt(x, upper) + dot_nt(x, lower)
        d_x = dot(kv_ref[...], upper) + dot(kv_ref[...], lower)
        for s in range(0, F, 16):
            rows = slice(s, s + 16)
            to_b = jnp.zeros((16, W), jnp.float32)
            to_w = jnp.zeros((16, W), jnp.float32)
            for k in range(NBR):
                first, second = split_terms(d_x[rows, tile(k)])
                right_s[rows, tile(k)] = first
                right_s[L + s : L + s + 16, tile(k)] = second
                turned = sin_s[slot, rows, tile(k)] * d_x[F + s : F + s + 16, tile(k)]
                to_b = to_b + turned
                to_w = to_w + turned * gaps_ref[block, :, tile(k)]
            gwide_s[1, rows] -= to_b
            gwide_s[0, rows] -= to_w
        d_query = jnp.concatenate(d_query, axis=0)
        terms = jnp.concatenate(split_terms(d_query), axis=1)
        code = jnp.concatenate([own_s[slot], zero_code], axis=0)
        gq_s[...] += dot_nt(pair(code), terms)
        d_code = fold(dot(q_ref[...], terms))
        gwide_s[1] -= zero_sin * d_code[F:]
        right_s[:F, near:], right_s[L : L + F, near:] = split_terms(d_emb + d_code[:F])
        for base in range(0, rows_s.shape[0], hot_s.shape[0]):
            hot_rows(hot_s, ids_ref[block], base)
            rows_s[base : base + hot_s.shape[0]] += dot_nt(hot_s[...], right_s[...])

    most = ids_ref.shape[0] - halves
    chunks = -(-most // CHUNK)
    for chunk in range(chunks):
        base = chunk * CHUNK
        count = jnp.clip(live - base, 0, CHUNK)
        first = halves + base if chunk else 0

        def run_forward(trig, base=base, count=count, first=first):
            def one(block, carry):
                forward(trig, block - base, block)
                return carry

            lax.fori_loop(first, halves + base + count, one, 0)

        for usable, trig in ((moderate, sine_cosine), (jnp.logical_not(moderate), any_angle)):
            pl.when(usable)(functools.partial(run_forward, trig))
        if not chunk:
            for half in range(halves):
                sources_s[:, half * W : (half + 1) * W] = z_s[half]

        def score(number, carry, base=base):
            predict(halves + number, halves + base + number)
            return carry

        lax.fori_loop(0, count, score, 0)
        if chunk == chunks - 1:
            for half in range(halves):
                d_source = dsources_s[:, half * W : (half + 1) * W]
                terms = jnp.concatenate(split_terms(d_source), axis=1)
                gsquare_s[1] += dot_nt(pair(z_s[half]), terms)
                dz_s[half] = fold(dot(square_ref[3], terms))

        def back(slot, carry, base=base):
            backward(slot, jnp.where(slot < halves, slot, slot + base))
            return carry

        lax.fori_loop(0 if chunk == chunks - 1 else halves, halves + count, back, 0)
    region = keep_ref.shape[1]
    for number in range(keep_ref.shape[0]):
        for ref, bit in ((keep_ref, bit_ref[0]), (give_ref, 1 - bit_ref[0])):
            at = pl.ds(pl.multiple_of((2 * number + bit) * region, region), region)
            ref[number] = rows_s[at, :L] + rows_s[at, L:]

    def cut_rows(matrix):
        return jnp.concatenate([matrix[:D], matrix[F : F + D]], axis=0)

    def cut_heads(matrix, axis):
        return jnp.concatenate(
            [
                lax.slice_in_dim(matrix, h * HP, h * HP + HS, axis=axis)
                for h in range(matrix.shape[axis] // HP)
            ],
            axis=axis,
        )

    gkv_ref[...] = cut_heads(cut_rows(gkv_s[...]), 1)
    gq_ref[...] = cut_heads(cut_rows(gq_s[...]), 1)
    gout_ref[...] = cut_heads(gsquare_s[0], 0)[:, :D]
    gsource_ref[...] = gsquare_s[1][:D, :PH]
    gother_ref[...] = gsquare_s[2][:D, :PH]
    ones = jnp.ones((8, W), jnp.bfloat16)
    for number, ref in enumerate((gtime_ref, gbase_ref, gp1_ref, gp2_ref, gend_ref)):
        total = sum(dot_nt(ones, term) for term in three_terms(gwide_s[number]))
        ref[...] = total[0:1, : ref.shape[1]]


def kernel_call(kernel, outs, ins, scratch, flops):
    def place(array):
        scalars = len(array.shape) == 1 and array.dtype == jnp.int32
        return pl.BlockSpec(memory_space=pltpu.SMEM if scalars else pltpu.VMEM)

    return pl.pallas_call(
        kernel,
        out_shape=tuple(outs),
        in_specs=[place(array) for array in ins],
        out_specs=tuple(place(array) for array in outs),
        scratch_shapes=[pltpu.VMEM(shape, dtype) for shape, dtype in scratch],
        compiler_params=pltpu.CompilerParams(vmem_limit_bytes=VMEM_BYTES),
        cost_estimate=pl.CostEstimate(flops=flops, bytes_accessed=10**6, transcendentals=0),
    )(*ins)


def array_of(shape, dtype=jnp.float32):
    return jax.ShapeDtypeStruct(shape, dtype)


def by_lanes(flat):
    return flat.reshape(flat.shape[:-1] + (-1, W))


def prepare(rank, sources, targets, times, counts, negatives, static_ids, neighbours, then):
    columns = negatives.shape[0]
    events = sources.shape[0]
    halves = events // W
    blocks = halves * (2 + columns)
    nodes = neighbours.shape[0]
    return kernel_call(
        functools.partial(prepare_kernel, columns),
        [
            array_of((blocks, 1, (NBR + 1) * W), jnp.int32),
            array_of((blocks, 1, NBR * W)),
            array_of((blocks, 1, W), jnp.int32),
            array_of((blocks, 1, W)),
            array_of((static_ids.shape[0], L), jnp.bfloat16),
            array_of((1,), jnp.int32),
        ],
        [
            rank[None],
            by_lanes(sources),
            by_lanes(targets),
            by_lanes(times),
            by_lanes(counts),
            by_lanes(negatives),
            static_ids[None],
            neighbours.T,
            then.T,
        ],
        [
            ((-(-(NEG + columns) // 16) * 16, events), jnp.float32),
            ((16, events), jnp.float32),
            ((5 * NEAR_ROWS, nodes), jnp.bfloat16),
            ((min(nodes, HOT), events), jnp.bfloat16),
        ],
        flops=4 * 10**9,
    )


def weights_kernel(
    kv_in, q_in, out_in, source_in, other_in, small_in, kvt_ref, kv_ref, qt_ref, q_ref, square_ref, wide_ref, pad_s
):
    def padded(raw, row_parts, column_parts):
        pad_s[...] = jnp.zeros_like(pad_s)
        value = raw[...].astype(jnp.float32)
        for r_from, r_to, r_size in row_parts:
            for c_from, c_to, c_size in column_parts:
                pad_s[r_to : r_to + r_size, c_to : c_to + c_size] = value[
                    r_from : r_from + r_size, c_from : c_from + c_size
                ]
        return pad_s[...]

    plain = [(0, 0, D)]
    twice = [(0, 0, D), (D, F, TE)]
    heads = [(h * HS, h * HP, HS) for h in range(HEADS)]
    all_heads = [(h * HS, h * HP, HS) for h in range(2 * HEADS)]
    for raw, straight, turned, row_parts, column_parts in (
        (kv_in, kv_ref, kvt_ref, twice, all_heads),
        (q_in, q_ref, qt_ref, twice, heads),
        (out_in, square_ref.at[1], square_ref.at[0], heads, plain),
        (source_in, square_ref.at[3], square_ref.at[2], plain, plain),
        (other_in, square_ref.at[5], square_ref.at[4], plain, plain),
    ):
        full = padded(raw, row_parts, column_parts)
        n, m = straight.shape
        straight[...] = full[:n, :m].astype(jnp.bfloat16)
        turned[...] = jnp.transpose(full)[:m, :n].astype(jnp.bfloat16)
    for number in range(5):
        row = small_in[number : number + 1].astype(jnp.float32)
        wide_ref[number] = column_of(row, W)[:F]


def event_weights(params):
    small = jnp.stack(
        [
            jnp.pad(params["w_time"], (0, L - TE)),
            jnp.pad(params["b_time"], (0, L - TE)),
            jnp.pad(params["b_p1"], (0, L - PH)),
            jnp.pad(params["w_p2"], (0, L - PH)),
            jnp.broadcast_to(params["b_p2"], (L,)),
            *[jnp.zeros((L,), jnp.bfloat16)] * 3,
        ]
    )
    low_type = jnp.bfloat16
    return kernel_call(
        weights_kernel,
        [
            array_of((2 * F, 2 * F), low_type),
            array_of((2 * F, 2 * F), low_type),
            array_of((F, 2 * F), low_type),
            array_of((2 * F, F), low_type),
            array_of((6, F, F), low_type),
            array_of((5, F, W)),
        ],
        [params[name] for name in ("w_kv", "w_query", "w_out", "w_ps", "w_pd")] + [small],
        [((2 * L, 2 * L), jnp.float32)],
        flops=10**8,
    )


def event_step(weights, table_t, prepared, regions, own_nodes, events_all, halves):
    ids, gaps, slots, valid, live = prepared
    kvt, kv, qt, q, square, wide = weights
    nodes = table_t.shape[1]
    near = NBR * W
    full = near + W
    low_type, high_type = jnp.bfloat16, jnp.float32
    half_table = array_of((regions // 2, nodes // regions, L))
    places = halves + min(CHUNK, ids.shape[0] - halves)
    loss, count, keep, give, g_kv, g_q, g_out, g_source, g_other, *g_rows = kernel_call(
        functools.partial(step_kernel, halves, own_nodes, events_all),
        [
            array_of((1, W)),
            array_of((1, W)),
            half_table,
            half_table,
            array_of((D + TE, 2 * D)),
            array_of((D + TE, D)),
            array_of((D, D)),
            array_of((D, PH)),
            array_of((D, PH)),
            *[array_of((1, width)) for width in (TE, TE, PH, PH, 1)],
        ],
        [
            live,
            my_bit("ev", 0)[None],
            table_t,
            ids,
            gaps,
            slots,
            valid,
            wide,
            kvt,
            kv,
            qt,
            q,
            square,
        ],
        [
            ((places, 2 * F, near), low_type),
            ((places, 2 * F, near), high_type),
            ((places, F, near), high_type),
            ((places, F, W), low_type),
            ((places, F, W), high_type),
            ((places, HEADS, NBR, W), high_type),
            ((places, F, W), low_type),
            ((places, F, W), low_type),
            ((places, F, W), high_type),
            ((F, halves * W), low_type),
            ((F, halves * W), high_type),
            ((min(nodes, HOT), full), low_type),
            ((2 * L, full), low_type),
            ((2 * F, near), low_type),
            ((2 * F, near), low_type),
            ((nodes, 2 * L), high_type),
            ((2 * F, 2 * F), high_type),
            ((2 * F, F), high_type),
            ((3, F, F), high_type),
            ((5, F, W), high_type),
        ],
        flops=4 * 10**10,
    )
    grads = [*g_rows[:2], g_q, g_kv, g_out, g_source, g_other, *g_rows[2:]]
    return loss, count[0, 0], keep, give, grads


def flatten_into(flat_ref, tile_ref, matrix, offset):
    count, width = matrix.shape
    tiles = -(-width // L)
    for number in range(tiles):
        part = matrix[:, number * L : (number + 1) * L]
        if part.shape[1] < L:
            part = jnp.concatenate([part, jnp.zeros((count, L - part.shape[1]), jnp.float32)], axis=1)
        tile_ref[number, :count] = part
    cycle = L // math.gcd(width, L)
    stride = width * cycle // L
    for first in range(min(cycle, count)):
        amount = -(-(count - first) // cycle)
        row, shift = divmod(offset + width * first, L)
        pieces = -(-(shift + width) // L)
        rows = pl.ds(first, amount, stride=cycle) if amount > 1 else slice(first, first + 1)
        parts = [tile_ref[number, rows] for number in range(tiles)]
        if shift:
            parts.insert(0, jnp.zeros((amount, shift), jnp.float32))
        held = jnp.concatenate(parts, axis=1) if len(parts) > 1 else parts[0]
        for piece in range(pieces):
            at = row + piece
            rows = pl.ds(at, amount, stride=stride) if amount > 1 else slice(at, at + 1)
            news = held[:, piece * L : min((piece + 1) * L, held.shape[1])]
            if news.shape[1] < L:
                news = jnp.concatenate([news, jnp.zeros((amount, L - news.shape[1]), jnp.float32)], axis=1)
            flat_ref[rows] += news


def flatten_kernel(offsets, *refs):
    *ins, flat_ref, tile_ref = refs
    flat_ref[...] = jnp.zeros_like(flat_ref)
    for offset, ref in zip(offsets, ins):
        flatten_into(flat_ref, tile_ref, ref[...], offset)


def flat_events(pieces, offset, rows):
    offsets = []
    for piece in pieces:
        offsets.append(offset - EVENT_ROW * L)
        offset += piece.size
    return kernel_call(
        functools.partial(flatten_kernel, offsets),
        [array_of((rows - EVENT_ROW, L))],
        pieces,
        [((2, D + TE, L), jnp.float32)],
        flops=2 * 10**9,
    )[0]


def node_kernel(
    regions,
    start_ref,
    bit_ref,
    rows_a_ref,
    rows_b_ref,
    rows_c_ref,
    rows_d_ref,
    table_ref,
    events_ref,
    keep_ref,
    came_ref,
    gi_ref,
    gh_ref,
    bias_ref,
    features_ref,
    flat_ref,
    tile_s,
    upper_s,
    lower_s,
    state_s,
    order_s,
    hot_s,
    gi_s,
    gh_s,
    bias_s,
    static_s,
):
    part_refs = (rows_a_ref, rows_b_ref, rows_c_ref, rows_d_ref)
    part_nodes = rows_a_ref.shape[0]
    shards = start_ref.shape[0]
    shard = len(part_refs) * part_nodes // shards
    flat_ref[:EVENT_ROW] = jnp.zeros((EVENT_ROW, L), jnp.float32)
    flat_ref[EVENT_ROW:] = events_ref[...]
    for ref, raw_ref in ((gi_s, gi_ref), (gh_s, gh_ref), (bias_s, bias_ref)):
        ref[...] = jnp.zeros_like(ref)
        for g in range(3):
            ref[: raw_ref.shape[0], g * L : g * L + D] = raw_ref[:, g * D : (g + 1) * D].astype(ref.dtype)

    def arrange(number, carry):
        source = pl.ds(pl.multiple_of(start_ref[number], shard), shard)
        order_s[pl.ds(pl.multiple_of(number * shard, shard), shard)] = (
            keep_ref[source] + came_ref[source]
        )
        return carry

    lax.fori_loop(0, shards, arrange, 0)

    def some(rows_ref, first, step, sums):
        at = pl.ds(pl.multiple_of(step * NODE_STEP, NODE_STEP), NODE_STEP)
        into = pl.ds(pl.multiple_of(first + step * NODE_STEP, NODE_STEP), NODE_STEP)
        stored = rows_ref[at, MSG_PAD : MSG_PAD + L]
        held = stored.astype(jnp.float32) + rows_ref[at, MSG_PAD + L :].astype(jnp.float32)
        inputs = dot(rows_ref[at, :MSG_PAD], gi_s[...]) + bias_s[0:1]
        hidden = dot(stored, gh_s[...]) + bias_s[1:2]
        reset = jax.nn.sigmoid(inputs[:, :L] + hidden[:, :L])
        update = jax.nn.sigmoid(inputs[:, L : 2 * L] + hidden[:, L : 2 * L])
        fresh = hidden[:, 2 * L :]
        candidate = jnp.tanh(inputs[:, 2 * L :] + reset * fresh)
        d_state = order_s[into]
        d_third = d_state * (1.0 - update) * (1.0 - candidate * candidate)
        d_fresh = d_third * reset
        d_first = d_third * fresh * reset * (1.0 - reset)
        d_second = d_state * (held - candidate) * update * (1.0 - update)
        news = []
        for number, part in enumerate((d_first, d_second, d_third, d_fresh)):
            lanes_at = slice(number * L, (number + 1) * L)
            news.append(jnp.sum(part, axis=0, keepdims=True))
            upper_s[into, lanes_at], lower_s[into, lanes_at] = split_terms(part)
        state_s[into, :L], state_s[into, L:] = split_terms(keep_ref[into] + came_ref[into])
        return sums + jnp.concatenate(news, axis=1)

    total = jnp.zeros((1, 4 * L), jnp.float32)
    wide_gi, wide_gh = 0.0, 0.0
    for part, rows_ref in enumerate(part_refs):
        first = part * part_nodes
        total = lax.fori_loop(
            0, part_nodes // NODE_STEP, functools.partial(some, rows_ref, first), total
        )
        messages = rows_ref[:, :MSG_PAD]
        stored = rows_ref[:, MSG_PAD : MSG_PAD + L]
        for ref in (upper_s, lower_s):
            terms = ref[first : first + part_nodes]
            wide_gi = wide_gi + dot_tn(messages, terms[:, : 3 * L])
            wide_gh = wide_gh + dot_tn(stored, terms)

    def gates(matrix, order):
        return jnp.concatenate([matrix[:, g * L : g * L + D] for g in order], axis=1)

    pieces = [
        gates(wide_gi[:MSG], (0, 1, 2)),
        gates(wide_gh[:D], (0, 1, 3)),
        gates(total, (0, 1, 2)),
        gates(total, (0, 1, 3)),
    ]
    mine = len(part_refs) * part_nodes // regions
    for number in range(regions):
        at = pl.ds(pl.multiple_of((2 * number + bit_ref[0]) * mine, mine), mine)
        pairs = table_ref[F : F + 16, at].astype(jnp.float32)
        static_s[:, number * mine : (number + 1) * mine] = pairs[0:1] * 128.0 + pairs[1:2]
    hot_rows(hot_s, static_s[...].astype(jnp.int32))
    by_feature = dot(hot_s[...], state_s[...])
    terms = split_terms(by_feature[:, :L] + by_feature[:, L:])
    wide = dot_tn(features_ref[...], terms[0]) + dot_tn(features_ref[...], terms[1])
    pieces.append(wide[:, :D])
    offset = 0
    for piece in pieces:
        flatten_into(flat_ref, tile_s, piece, offset)
        offset += piece.size


def node_grads(params, start, rows, table_t, node_features, events, keep, came, regions):
    nodes = keep.shape[0]
    return kernel_call(
        functools.partial(node_kernel, regions // 2),
        [array_of((EVENT_ROW + events.shape[0], L))],
        [
            start,
            my_bit("ev", 0)[None],
            *rows,
            table_t,
            events,
            keep,
            came,
            params["w_gi"],
            params["w_gh"],
            params["b_g"],
            node_features,
        ],
        [
            ((3, MSG, L), jnp.float32),
            ((nodes, 4 * L), jnp.bfloat16),
            ((nodes, 4 * L), jnp.bfloat16),
            ((nodes, 2 * L), jnp.bfloat16),
            ((nodes, L), jnp.float32),
            ((node_features.shape[0], nodes), jnp.bfloat16),
            ((MSG_PAD, 3 * L), jnp.bfloat16),
            ((L, 3 * L), jnp.bfloat16),
            ((8, 3 * L), jnp.float32),
            ((1, nodes), jnp.float32),
        ],
        flops=8 * 10**9,
    )[0]


def partner(array, name, bit):
    size = lax.axis_size(name)
    return lax.ppermute(array, name, [(i, i ^ (1 << bit)) for i in range(size)])


def my_bit(name, bit):
    return (lax.axis_index(name) >> bit) & 1


def bits_of(name):
    return (lax.axis_size(name) - 1).bit_length()


def exchange(held, done, name, bit):
    other = partner(held, name, bit)
    mine_first = my_bit(name, bit) == 0
    done = sorted(done + [(name == "neg", -bit)])
    place = done.index((name == "neg", -bit))
    parts = [jnp.where(mine_first, held, other), jnp.where(mine_first, other, held)]
    return jnp.stack(parts, axis=place), done


def gather_neg(shard):
    held, done = shard, []
    for bit in range(bits_of("neg")):
        held, done = exchange(held, done, "neg", bit)
    return held, done


def gather_ev(held, done):
    for bit in list(range(1, bits_of("ev"))) + [0]:
        held, done = exchange(held, done, "ev", bit)
    return held


def reduce_bit(held, bits, bit):
    place = bits.index(bit)
    mine = my_bit("ev", bit)
    keep = lax.dynamic_index_in_dim(held, mine, place, keepdims=False)
    give = lax.dynamic_index_in_dim(held, 1 - mine, place, keepdims=False)
    return keep + partner(give, "ev", bit), [other for other in bits if other != bit]


def scatter_ev(blocks):
    count = bits_of("ev")
    bits = list(reversed(range(count)))
    held = blocks.reshape((2,) * count + blocks.shape[1:])
    for bit in range(count - 2):
        held, bits = reduce_bit(held, bits, bit)
    middle = held.shape[-2] // 16 * 8
    parts = [(held[..., :middle, :], bits), (held[..., middle:, :], bits)]
    for turn in range(2):
        parts = [
            reduce_bit(part, left, bits[(turn + number) % 2])
            for number, (part, left) in enumerate(parts)
        ]
    return jnp.concatenate([part for part, left in parts], axis=-2)


def scatter_neg(blocks):
    return jnp.sum(lax.all_to_all(blocks, "neg", split_axis=0, concat_axis=0, tiled=True), axis=0)


def lanes(flat):
    amount = flat.shape[-1]
    rows = -(-amount // 128)
    wide = jnp.pad(flat, [(0, 0)] * (flat.ndim - 1) + [(0, rows * 128 - amount)])
    return wide.reshape(flat.shape[:-1] + (rows, 128))


def from_digits(pairs, axis):
    pairs = pairs.astype(jnp.float32)
    high, low = (lax.index_in_dim(pairs, place, axis, keepdims=False) for place in (0, 1))
    return high * 128.0 + low


def on_device(
    master,
    first_moment,
    second_moment,
    memory,
    messages,
    static_ids,
    node_features,
    neighbours,
    neighbour_times,
    last_partner,
    last_deltas,
    last_edges,
    sources,
    targets,
    times,
    negatives,
    neg_counts,
):
    shard = master.shape[0]
    groups = lax.axis_size("neg")
    regions = lax.axis_size("ev")
    devices = regions * groups
    rank = lax.axis_index("neg")
    own_events = sources.shape[0]
    own_nodes = memory.shape[0]
    local_neg = negatives.shape[1]
    total_neg = local_neg * groups
    events_all = own_events * devices

    copies, copies_done = gather_neg(lanes(master.astype(jnp.bfloat16)))
    all_negatives = gather_neg(by_lanes(negatives.T))[0].reshape(total_neg, -1)

    terms = settled_terms(memory)
    rows = jnp.concatenate(
        [
            jnp.pad(messages, ((0, 0), (0, MSG_PAD - MSG))),
            jnp.pad(terms[0], ((0, 0), (0, L - D))),
            jnp.pad(terms[1], ((0, 0), (0, L - D))),
        ],
        1,
    )
    start = ((lax.axis_index("ev") // 2) * groups + rank)[None]
    last_ev = bits_of("ev") - 1
    stages = [
        [("ev", bit) for bit in range(1, last_ev)],
        [("neg", bit) for bit in reversed(range(1, bits_of("neg")))],
    ]

    def flip_of(name, bit):
        return (1 << bit) if name == "neg" else (1 << (bit - 1)) * groups

    for name, bit in sum(stages, []):
        start = jnp.concatenate([start, start ^ flip_of(name, bit)])
    flips = (flip_of("ev", last_ev), flip_of("neg", 0))
    start = jnp.concatenate([start, start ^ flips[0], start ^ flips[1], start ^ flips[0] ^ flips[1]])

    def further(rows, stage):
        for name, bit in stage:
            rows = jnp.concatenate([rows, partner(rows, name, bit)])
        return rows

    rows = further(rows, stages[0])
    copies, rows = lax.optimization_barrier((copies, rows))
    copies = gather_ev(copies, copies_done)
    rows = further(rows, stages[1])

    ids, gaps, slots, valid, tail, live = prepare(
        rank,
        sources,
        targets,
        times,
        neg_counts,
        all_negatives,
        static_ids,
        neighbours,
        neighbour_times,
    )

    flat = copies.reshape(devices, -1)[:, :shard].reshape(-1)
    early = unpack(flat)
    state, renewed = owner_pass(early, memory, messages, node_features[static_ids])
    sending = jnp.concatenate(
        [jnp.pad(state.astype(jnp.bfloat16), ((0, 0), (0, F - D))), tail[:, : L - F]], 1
    )
    flat, sending, rows = lax.optimization_barrier((flat, sending, rows))
    params = unpack(flat)
    weights = event_weights(params)
    table, table_done = gather_neg(sending)
    table, weights = lax.optimization_barrier((table, weights))
    table = gather_ev(table, table_done).reshape(-1, L)
    table, rows = lax.optimization_barrier((table, rows))
    across = [(i, i ^ (regions // 2 * groups) ^ 1) for i in range(devices)]
    far_rows = [
        partner(rows, "ev", last_ev),
        partner(rows, "neg", 0),
        lax.ppermute(rows, ("ev", "neg"), across),
    ]
    table_t = table.T
    local_loss, neg_total, keep, give, grad_event = event_step(
        weights,
        table_t,
        (ids, gaps, slots, valid, live),
        regions,
        own_nodes,
        events_all,
        own_events // W,
    )
    give, far_rows, local_loss, grad_event = lax.optimization_barrier(
        (give, far_rows, local_loss, grad_event)
    )
    came = partner(give, "ev", 0).reshape(-1, L)
    flat_rows = shard * devices // L
    event_size = sum(piece.size for piece in grad_event)
    event_flat = flat_events(grad_event, PARAMS_LIVE - event_size, flat_rows)
    grads = node_grads(
        early,
        start * own_nodes,
        [rows, *far_rows],
        table_t,
        node_features,
        event_flat,
        keep.reshape(-1, L),
        came,
        regions,
    )
    blocks = lanes(grads.reshape(regions, -1))
    block_rows = blocks.shape[1]
    losses = jnp.broadcast_to(local_loss, (regions, 1, L))
    blocks = jnp.concatenate([blocks, losses, jnp.zeros((regions, 7 - block_rows % 8, L))], 1)
    summed = scatter_ev(blocks)
    shares = summed[:block_rows].reshape(-1)[: shard * groups].reshape(groups, shard)
    losses = jnp.broadcast_to(jnp.sum(summed[block_rows]), (groups, 1))
    totals = scatter_neg(lanes(jnp.concatenate([shares, losses], 1))).reshape(-1)
    grad_shard, loss = totals[:shard], totals[shard]
    new_master, new_first, new_second = adamw(master, first_moment, second_moment, grad_shard)
    codes = jnp.cos(
        last_deltas[:, None] * params["w_time"].astype(jnp.float32)
        + params["b_time"].astype(jnp.float32)
    )
    carried = jnp.concatenate(
        [
            sending[:, :D].astype(jnp.float32),
            table[last_partner][:, :D].astype(jnp.float32),
            codes,
            last_edges.astype(jnp.float32),
        ],
        1,
    )
    return (loss, neg_total, new_master, new_first, new_second, renewed, carried)


def solution(mesh):
    return jax.shard_map(
        on_device,
        mesh=mesh,
        in_specs=(
            P(("ev", "neg")),
            P(("ev", "neg")),
            P(("ev", "neg")),
            P(("ev", "neg"), None),
            P(("ev", "neg"), None),
            P(("ev", "neg")),
            P(),
            P(),
            P(),
            P(("ev", "neg")),
            P(("ev", "neg")),
            P(("ev", "neg"), None),
            P(("ev", "neg")),
            P(("ev", "neg")),
            P("ev"),
            P("ev", "neg"),
            P("ev"),
        ),
        out_specs=(
            P(),
            P(),
            P(("ev", "neg")),
            P(("ev", "neg")),
            P(("ev", "neg")),
            P(("ev", "neg"), None),
            P(("ev", "neg"), None),
        ),
        check_vma=False,
    )
```

```python
import functools
import math

import jax
import jax.numpy as jnp
from jax import lax
from jax.experimental import pallas as pl
from jax.experimental.pallas import tpu as pltpu
from jax.sharding import PartitionSpec as P

D = 100
TE = 100
NF = 413
PH = 100
HEADS = 2
NBR = 10
STEP = 10
HS = 50
MSG = 486
NODE_PARAMS = 3 * D * (MSG + D + 2) + NF * D


beta_one = 0.9
beta_two = 0.999
rate_lr = 0.02
decay_wd = 0.01
eps_adam = 1e-08

HP = 56
F = HEADS * HP
W = 128
LO = 256
L = 128
MSG_PAD = 512
CHUNK = 10
HOT = 2048
EVENT_ROW = 1696
NODE_STEP = 256
VMEM_BYTES = 60 * 1024 * 1024


def unpack(flat):
    layout = [
        ("w_gi", (MSG, 3 * D)),
        ("w_gh", (D, 3 * D)),
        ("b_g", (2, 3 * D)),
        ("w_feat", (NF, D)),
        ("w_time", (TE,)),
        ("b_time", (TE,)),
        ("w_query", (D + TE, D)),
        ("w_kv", (D + TE, 2 * D)),
        ("w_out", (D, D)),
        ("w_ps", (D, PH)),
        ("w_pd", (D, PH)),
        ("b_p1", (PH,)),
        ("w_p2", (PH,)),
        ("b_p2", (1,)),
    ]
    params = {}
    offset = 0
    for label, shape in layout:
        amount = math.prod(shape)
        params[label] = flat[offset : offset + amount].reshape(shape)
        offset += amount
    return params


def dot(left, right):
    return jnp.dot(left, right, preferred_element_type=jnp.float32)


def dot_nt(left, right):
    return lax.dot_general(
        left, right, (((1,), (1,)), ((), ())), preferred_element_type=jnp.float32
    )


def dot_tn(left, right):
    return lax.dot_general(
        left, right, (((0,), (0,)), ((), ())), preferred_element_type=jnp.float32
    )


def split_terms(value):
    first = value.astype(jnp.bfloat16)
    return first, (value - first.astype(jnp.float32)).astype(jnp.bfloat16)


def settled_terms(value):
    first = lax.optimization_barrier(value.astype(jnp.bfloat16))
    return first, (value - first.astype(jnp.float32)).astype(jnp.bfloat16)


def three_terms(value):
    first = value.astype(jnp.bfloat16)
    rest = value - first.astype(jnp.float32)
    second = rest.astype(jnp.bfloat16)
    return first, second, (rest - second.astype(jnp.float32)).astype(jnp.bfloat16)


def owner_pass(params, memory, messages, features):
    inputs = dot(messages, params["w_gi"]) + params["b_g"][0].astype(jnp.float32)
    hidden = dot(memory.astype(jnp.bfloat16), params["w_gh"]) + params["b_g"][1].astype(jnp.float32)
    reset = jax.nn.sigmoid(inputs[:, :D] + hidden[:, :D])
    update = jax.nn.sigmoid(inputs[:, D : 2 * D] + hidden[:, D : 2 * D])
    candidate = jnp.tanh(inputs[:, 2 * D :] + reset * hidden[:, 2 * D :])
    renewed = (1.0 - update) * candidate + update * memory
    return (renewed + dot(features, params["w_feat"]), renewed)


def adamw(master, first_state, second_state, grads):
    first_new = beta_one * first_state + (1.0 - beta_one) * grads
    second_new = beta_two * second_state + (1.0 - beta_two) * grads * grads
    corrected = (
        first_new
        / (1.0 - beta_one**STEP)
        / (jnp.sqrt(second_new / (1.0 - beta_two**STEP)) + eps_adam)
    )
    return (master - rate_lr * (corrected + decay_wd * master), first_new, second_new)


def sine_cosine(angle):
    turns = jnp.round(angle * (2.0 / math.pi))
    rest = angle - turns * 1.5703125
    rest = rest - turns * 4.837512969970703e-4
    rest = rest - turns * 7.549789948768648e-8
    square = rest * rest
    sine = rest + rest * square * (
        -1.6666654611e-1 + square * (8.3321608736e-3 - square * 1.9515295891e-4)
    )
    cosine = (
        1.0
        - 0.5 * square
        + square
        * square
        * (4.166664568298827e-2 + square * (-1.388731625493765e-3 + square * 2.443315711809948e-5))
    )
    quadrant = turns.astype(jnp.int32)
    odd = (quadrant & 1) == 1
    cos_value = jnp.where(odd, sine, cosine)
    sin_value = jnp.where(odd, cosine, sine)
    cos_value = jnp.where(((quadrant + 1) & 2) == 2, -cos_value, cos_value)
    sin_value = jnp.where((quadrant & 2) == 2, -sin_value, sin_value)
    return cos_value, sin_value


def any_angle(angle):
    return jnp.cos(angle), jnp.sin(angle)


def pair(value):
    return jnp.concatenate([value, value], axis=1)


def fold(value):
    return value[:, :W] + value[:, W:]


def tile(k):
    return slice(k * W, (k + 1) * W)


def hot_rows(hot_ref, ids, base=0):
    count = ids.shape[1]
    rows = lax.broadcasted_iota(jnp.int32, (LO, count), 0).astype(jnp.float32).astype(jnp.bfloat16)
    place = (ids & (LO - 1)).astype(jnp.float32)
    group = ids // LO - base // LO
    one, nought = jnp.ones_like(rows), jnp.zeros_like(rows)
    for number in range(hot_ref.shape[0] // LO):
        here = jnp.where(group == number, place, -1.0)
        here = jnp.broadcast_to(here, (LO, count)).astype(jnp.bfloat16)
        hot_ref[number * LO : (number + 1) * LO] = jnp.where(rows == here, one, nought)


def gather_columns(table_ref, hot_ref, ids):
    step = hot_ref.shape[0]
    found = None
    for base in range(0, table_ref.shape[1], step):
        hot_rows(hot_ref, ids, base)
        part = dot(table_ref[:, base : base + step], hot_ref[...])
        found = part if found is None else found + part
    return found


SRC, TGT, TIME, COUNT, NEG = 0, 1, 2, 3, 4
ID, AT, EVENT = 0, 1, 2
NEAR_ROWS = 16


def column_of(row, lanes_of):
    wide = jnp.transpose(jnp.broadcast_to(row, (L, row.shape[1])))
    return jnp.concatenate([wide] * (lanes_of // L), axis=1)


def pack_kernel(halves, rank_ref, numbers_ref, static_ref, messages_ref, memory_ref, rows_ref, tail_ref):
    rows_ref[...] = jnp.zeros_like(rows_ref)
    rows_ref[:, :MSG] = messages_ref[...]
    terms = split_terms(memory_ref[...])
    rows_ref[:, MSG_PAD : MSG_PAD + D] = terms[0]
    rows_ref[:, MSG_PAD + L : MSG_PAD + L + D] = terms[1]
    counts = numbers_ref[pl.ds(rank_ref[0] * halves, halves)].astype(jnp.float32)
    total = jnp.sum(jnp.sum(counts, axis=1, keepdims=True), axis=0, keepdims=True)
    static = column_of(static_ref[...].astype(jnp.float32), L).astype(jnp.int32)
    lane = lax.broadcasted_iota(jnp.int32, static.shape, 1)
    value = jnp.where(lane < 2, static, total.astype(jnp.int32))
    value = jnp.where((lane & 1) == 0, value >> 7, value & 127)
    tail_ref[...] = value.astype(jnp.float32).astype(jnp.bfloat16)


def pack(rank, counts, static_ids, messages, memory, halves):
    nodes = static_ids.shape[0]
    return kernel_call(
        functools.partial(pack_kernel, halves),
        [array_of((nodes, MSG_PAD + 2 * L), jnp.bfloat16), array_of((nodes, L), jnp.bfloat16)],
        [rank[None], by_lanes(counts), static_ids[None], messages, memory],
        [],
        flops=10**8,
    )


def prepare_kernel(
    rank_ref,
    source_ref,
    target_ref,
    times_ref,
    numbers_ref,
    digits_ref,
    near_ref,
    then_ref,
    ids_ref,
    gaps_ref,
    slots_ref,
    valid_ref,
    live_ref,
    event_s,
    pair_s,
    negatives_s,
    around_s,
    hot_s,
):
    groups, digit_rows, _ = digits_ref.shape
    rows = times_ref.shape[0]
    local = digit_rows // (2 * rows)
    columns = groups * local
    found = digits_ref[...].astype(jnp.float32)
    negatives_s[...] = found[:, : digit_rows // 2] * 128.0 + found[:, digit_rows // 2 :]
    halves = source_ref.shape[0]
    events = halves * W
    mine = pl.ds(rank_ref[0] * halves, halves)
    event_s[...] = jnp.zeros_like(event_s)
    for row, held in enumerate(
        [source_ref[...], target_ref[...], times_ref[mine], numbers_ref[mine]]
        + [
            negatives_s[group, pl.ds(j * rows + rank_ref[0] * halves, halves)]
            for group in range(groups)
            for j in range(local)
        ]
    ):
        held = held.astype(jnp.float32)
        for half in range(halves):
            event_s[row : row + 1, half * W : (half + 1) * W] = held[half : half + 1]
    counts = event_s[COUNT : COUNT + 1]
    shape = (events, events)
    earlier = lax.broadcasted_iota(jnp.int32, shape, 0) < lax.broadcasted_iota(jnp.int32, shape, 1)
    earlier = jnp.where(earlier, 1.0, 0.0).astype(jnp.bfloat16)
    event = lax.broadcasted_iota(jnp.int32, (1, events), 1).astype(jnp.float32)
    wanted = lax.broadcasted_iota(jnp.int32, (columns * events, events), 0).astype(jnp.float32)
    taken = jnp.zeros((1, 1), jnp.float32)
    packed = jnp.zeros((16, columns * events), jnp.float32)
    for number in range(columns):
        active = counts >= float(columns - number)
        ones = jnp.broadcast_to(jnp.where(active, 1.0, 0.0), (16, events))
        place = taken + dot(ones.astype(jnp.bfloat16), earlier)[0:1]
        taken = taken + jnp.sum(ones[0:1], axis=1, keepdims=True)
        place = jnp.where(active, place, -1.0)
        order = jnp.where(wanted == place, 1.0, 0.0).astype(jnp.bfloat16)
        row = NEG + number
        pair_s[...] = jnp.zeros_like(pair_s)
        pair_s[ID : ID + 1] = event_s[row : row + 1]
        pair_s[AT : AT + 1] = event_s[TIME : TIME + 1]
        pair_s[EVENT : EVENT + 1] = event
        packed = packed + sum(dot_nt(term, order) for term in three_terms(pair_s[...]))
    slot = lax.broadcasted_iota(jnp.int32, (1, columns * events), 1).astype(jnp.float32)
    valid = jnp.where(slot < taken, 1.0, 0.0)
    live_ref[0] = halves + (jnp.sum(counts).astype(jnp.int32) + W - 1) // W
    around_s[...] = jnp.zeros_like(around_s)
    near = near_ref[...]
    parts = [(near >> 7).astype(jnp.float32), (near & 127).astype(jnp.float32)]
    parts = [part.astype(jnp.bfloat16) for part in parts] + list(three_terms(then_ref[...]))
    for number, part in enumerate(parts):
        around_s[number * NEAR_ROWS : number * NEAR_ROWS + NBR] = part
    sets = [
        (event_s[SRC : SRC + 1], event_s[TIME : TIME + 1], event, jnp.ones((1, events))),
        (event_s[TGT : TGT + 1], event_s[TIME : TIME + 1], event, jnp.ones((1, events))),
    ]
    for number in range(columns):
        part = slice(number * events, (number + 1) * events)
        sets.append((packed[ID : ID + 1, part], packed[AT : AT + 1, part], packed[EVENT : EVENT + 1, part], valid[:, part]))
    for number, (nodes, times, of_event, counted) in enumerate(sets):
        nodes = nodes.astype(jnp.int32)
        found = gather_columns(around_s, hot_s, nodes)
        near = found[:NBR] * 128.0 + found[NEAR_ROWS : NEAR_ROWS + NBR]
        near = near.astype(jnp.int32)
        then = (
            found[2 * NEAR_ROWS : 2 * NEAR_ROWS + NBR] + found[3 * NEAR_ROWS : 3 * NEAR_ROWS + NBR]
        ) + found[4 * NEAR_ROWS : 4 * NEAR_ROWS + NBR]
        gaps = times - then
        for half in range(halves):
            block, lanes_at = number * halves + half, slice(half * W, (half + 1) * W)
            for k in range(NBR):
                ids_ref[block, :, tile(k)] = near[k : k + 1, lanes_at]
                gaps_ref[block, :, tile(k)] = gaps[k : k + 1, lanes_at]
            ids_ref[block, :, NBR * W :] = nodes[:, lanes_at]
            slots_ref[block] = of_event[:, lanes_at].astype(jnp.int32)
            valid_ref[block] = counted[:, lanes_at]


def step_kernel(
    halves,
    own_nodes,
    events_all,
    live_ref,
    bit_ref,
    table_ref,
    ids_ref,
    gaps_ref,
    slots_ref,
    valid_ref,
    wide_ref,
    kvt_ref,
    kv_ref,
    qt_ref,
    q_ref,
    square_ref,
    loss_ref,
    count_ref,
    keep_ref,
    give_ref,
    gkv_ref,
    gq_ref,
    gout_ref,
    gsource_ref,
    gother_ref,
    gtime_ref,
    gbase_ref,
    gp1_ref,
    gp2_ref,
    gend_ref,
    x_s,
    kv_s,
    sin_s,
    own_s,
    query_s,
    att_s,
    mix_s,
    z_s,
    dz_s,
    sources_s,
    dsources_s,
    hot_s,
    right_s,
    upper_s,
    lower_s,
    rows_s,
    gkv_s,
    gq_s,
    gsquare_s,
    gwide_s,
):
    scale = 1.0 / math.sqrt(HS)
    near = NBR * W
    found = table_ref[F : F + 16].astype(jnp.float32)
    counted = jnp.sum(found, axis=1, keepdims=True)
    neg_total = (counted[2:3] * 128.0 + counted[3:4]) * (1.0 / own_nodes)
    count_ref[...] = jnp.broadcast_to(neg_total, (1, W))
    share = jnp.broadcast_to(1.0 / neg_total, (1, W))
    b_time = wide_ref[1]
    b_p1, w_p2 = wide_ref[2], wide_ref[3]
    b_p2 = wide_ref[4][0:1]
    zero_cos, zero_sin = any_angle(b_time)
    furthest = jnp.max(jnp.abs(gaps_ref[...])) * jnp.max(jnp.abs(wide_ref[0])) + jnp.max(
        jnp.abs(b_time)
    )
    moderate = furthest <= 8192.0
    zero_code = zero_cos.astype(jnp.bfloat16)
    for ref in (rows_s, right_s, gkv_s, gq_s, gsquare_s, gwide_s, dsources_s, loss_ref):
        ref[...] = jnp.zeros_like(ref)
    head_rows = (slice(0, HP), slice(HP, F))
    live = live_ref[0]

    def forward(trig, slot, block):
        for s in range(0, F, 16):
            rows = slice(s, s + 16)
            w_rows, b_rows = wide_ref[0, rows], wide_ref[1, rows]
            for k in range(NBR):
                angle = gaps_ref[block, :, tile(k)] * w_rows + b_rows
                cos_value, sin_value = trig(angle)
                sin_s[slot, rows, tile(k)] = sin_value
                x_s[slot, F + s : F + s + 16, tile(k)] = cos_value.astype(jnp.bfloat16)
        found = gather_columns(table_ref, hot_s, ids_ref[block])[:F].astype(jnp.bfloat16)
        x_s[slot, :F] = found[:, :near]
        own = found[:, near:]
        own_s[slot] = own
        query = dot(qt_ref[...], jnp.concatenate([own, zero_code], axis=0))
        query_s[slot] = query
        kv_s[slot] = dot(kvt_ref[...], x_s[slot])
        mixed = []
        for h, rows in enumerate(head_rows):
            scores = jnp.concatenate(
                [
                    jnp.sum(kv_s[slot, rows, tile(k)] * query[rows], axis=0, keepdims=True)
                    for k in range(NBR)
                ],
                axis=0,
            )
            scores = scores * scale
            powers = jnp.exp(scores - jnp.max(scores, axis=0, keepdims=True))
            att_s[slot, h] = powers / jnp.sum(powers, axis=0, keepdims=True)
            mixed_h = jnp.zeros((HP, W), jnp.float32)
            for k in range(NBR):
                values = kv_s[slot, F + h * HP : F + (h + 1) * HP, tile(k)]
                mixed_h = mixed_h + att_s[slot, h, k : k + 1] * values
            mixed.append(mixed_h)
        mixed = jnp.concatenate(mixed, axis=0).astype(jnp.bfloat16)
        mix_s[slot] = mixed
        emb = own.astype(jnp.float32) + dot(square_ref[0], mixed)
        z_s[slot] = emb.astype(jnp.bfloat16)

    def predict(slot, block):
        events = lax.broadcasted_iota(jnp.int32, (halves * W, W), 0)
        of_event = jnp.where(events == slots_ref[block], 1.0, 0.0).astype(jnp.bfloat16)
        source = dot(sources_s[...], of_event).astype(jnp.bfloat16)
        z = z_s[slot]
        before = dot(square_ref[2], source) + dot(square_ref[4], z) + b_p1
        inner = 0.7978845608028654 * (before + 0.044715 * before * before * before)
        bend = jnp.tanh(inner)
        hidden = (0.5 * before * (1.0 + bend)).astype(jnp.bfloat16).astype(jnp.float32)
        slope = 0.5 * (1.0 + bend) + 0.5 * before * (1.0 - bend * bend) * (
            0.7978845608028654 * (1.0 + 3.0 * 0.044715 * before * before)
        )
        score = jnp.sum(hidden * w_p2, axis=0, keepdims=True) + b_p2
        positive = block < 2 * halves
        sign = jnp.where(positive, -1.0, 1.0)
        weight = valid_ref[block] * jnp.where(positive, 1.0 / events_all, share)
        signed = sign * score
        small = jnp.exp(-jnp.abs(signed))
        loss_ref[...] += weight * (jnp.maximum(signed, 0.0) + jnp.log1p(small))
        sigmoid = jnp.where(signed >= 0.0, 1.0, small) / (1.0 + small)
        d_score = (sign * weight) * sigmoid
        gwide_s[3] += hidden * d_score
        gwide_s[4, 0:1] += d_score
        d_before = w_p2 * d_score * slope
        gwide_s[2] += d_before
        terms = jnp.concatenate(split_terms(d_before), axis=1)
        gsquare_s[2] += dot_nt(pair(z), terms)
        dz_s[slot] = fold(dot(square_ref[5], terms))
        dsources_s[...] += dot_nt(terms, pair(of_event))

    def backward(slot, block):
        d_emb = dz_s[slot]
        terms = jnp.concatenate(split_terms(d_emb), axis=1)
        gsquare_s[0] += dot_nt(pair(mix_s[slot]), terms)
        d_mixed = fold(dot(square_ref[1], terms))
        d_query = []
        for h, rows in enumerate(head_rows):
            d_mixed_h, query_h = d_mixed[rows], query_s[slot, rows]
            value_rows = slice(F + h * HP, F + (h + 1) * HP)
            d_shares = jnp.concatenate(
                [
                    jnp.sum(kv_s[slot, value_rows, tile(k)] * d_mixed_h, axis=0, keepdims=True)
                    for k in range(NBR)
                ],
                axis=0,
            )
            part = att_s[slot, h]
            total = jnp.sum(part * d_shares, axis=0, keepdims=True)
            d_scores = part * (d_shares - total) * scale
            d_query_h = jnp.zeros((HP, W), jnp.float32)
            for k in range(NBR):
                d_score = d_scores[k : k + 1]
                d_query_h = d_query_h + d_score * kv_s[slot, rows, tile(k)]
                for at, d_part in (
                    (rows, d_score * query_h),
                    (value_rows, att_s[slot, h, k : k + 1] * d_mixed_h),
                ):
                    upper_s[at, tile(k)], lower_s[at, tile(k)] = split_terms(d_part)
            d_query.append(d_query_h)
        x = x_s[slot]
        upper, lower = upper_s[...], lower_s[...]
        gkv_s[...] += dot_nt(x, upper) + dot_nt(x, lower)
        d_x = dot(kv_ref[...], upper) + dot(kv_ref[...], lower)
        for s in range(0, F, 16):
            rows = slice(s, s + 16)
            to_b = jnp.zeros((16, W), jnp.float32)
            to_w = jnp.zeros((16, W), jnp.float32)
            for k in range(NBR):
                first, second = split_terms(d_x[rows, tile(k)])
                right_s[rows, tile(k)] = first
                right_s[L + s : L + s + 16, tile(k)] = second
                turned = sin_s[slot, rows, tile(k)] * d_x[F + s : F + s + 16, tile(k)]
                to_b = to_b + turned
                to_w = to_w + turned * gaps_ref[block, :, tile(k)]
            gwide_s[1, rows] -= to_b
            gwide_s[0, rows] -= to_w
        d_query = jnp.concatenate(d_query, axis=0)
        terms = jnp.concatenate(split_terms(d_query), axis=1)
        code = jnp.concatenate([own_s[slot], zero_code], axis=0)
        gq_s[...] += dot_nt(pair(code), terms)
        d_code = fold(dot(q_ref[...], terms))
        gwide_s[1] -= zero_sin * d_code[F:]
        right_s[:F, near:], right_s[L : L + F, near:] = split_terms(d_emb + d_code[:F])
        for base in range(0, rows_s.shape[0], hot_s.shape[0]):
            hot_rows(hot_s, ids_ref[block], base)
            rows_s[base : base + hot_s.shape[0]] += dot_nt(hot_s[...], right_s[...])

    most = ids_ref.shape[0] - halves
    chunks = -(-most // CHUNK)
    for chunk in range(chunks):
        base = chunk * CHUNK
        count = jnp.clip(live - base, 0, CHUNK)
        first = halves + base if chunk else 0

        def run_forward(trig, base=base, count=count, first=first):
            def one(block, carry):
                forward(trig, block - base, block)
                return carry

            lax.fori_loop(first, halves + base + count, one, 0)

        for usable, trig in ((moderate, sine_cosine), (jnp.logical_not(moderate), any_angle)):
            pl.when(usable)(functools.partial(run_forward, trig))
        if not chunk:
            for half in range(halves):
                sources_s[:, half * W : (half + 1) * W] = z_s[half]

        def score(number, carry, base=base):
            predict(halves + number, halves + base + number)
            return carry

        lax.fori_loop(0, count, score, 0)
        if chunk == chunks - 1:
            for half in range(halves):
                d_source = dsources_s[:, half * W : (half + 1) * W]
                terms = jnp.concatenate(split_terms(d_source), axis=1)
                gsquare_s[1] += dot_nt(pair(z_s[half]), terms)
                dz_s[half] = fold(dot(square_ref[3], terms))

        def back(slot, carry, base=base):
            backward(slot, jnp.where(slot < halves, slot, slot + base))
            return carry

        lax.fori_loop(0 if chunk == chunks - 1 else halves, halves + count, back, 0)
    region = keep_ref.shape[1]
    for number in range(keep_ref.shape[0]):
        for ref, bit in ((keep_ref, bit_ref[0]), (give_ref, 1 - bit_ref[0])):
            at = pl.ds(pl.multiple_of((2 * number + bit) * region, region), region)
            ref[number] = rows_s[at, :L] + rows_s[at, L:]

    def cut_rows(matrix):
        return jnp.concatenate([matrix[:D], matrix[F : F + D]], axis=0)

    def cut_heads(matrix, axis):
        return jnp.concatenate(
            [
                lax.slice_in_dim(matrix, h * HP, h * HP + HS, axis=axis)
                for h in range(matrix.shape[axis] // HP)
            ],
            axis=axis,
        )

    gkv_ref[...] = cut_heads(cut_rows(gkv_s[...]), 1)
    gq_ref[...] = cut_heads(cut_rows(gq_s[...]), 1)
    gout_ref[...] = cut_heads(gsquare_s[0], 0)[:, :D]
    gsource_ref[...] = gsquare_s[1][:D, :PH]
    gother_ref[...] = gsquare_s[2][:D, :PH]
    ones = jnp.ones((8, W), jnp.bfloat16)
    for number, ref in enumerate((gtime_ref, gbase_ref, gp1_ref, gp2_ref, gend_ref)):
        total = sum(dot_nt(ones, term) for term in three_terms(gwide_s[number]))
        ref[...] = total[0:1, : ref.shape[1]]


def kernel_call(kernel, outs, ins, scratch, flops):
    def place(array):
        scalars = len(array.shape) == 1 and array.dtype == jnp.int32
        return pl.BlockSpec(memory_space=pltpu.SMEM if scalars else pltpu.VMEM)

    return pl.pallas_call(
        kernel,
        out_shape=tuple(outs),
        in_specs=[place(array) for array in ins],
        out_specs=tuple(place(array) for array in outs),
        scratch_shapes=[pltpu.VMEM(shape, dtype) for shape, dtype in scratch],
        compiler_params=pltpu.CompilerParams(vmem_limit_bytes=VMEM_BYTES),
        cost_estimate=pl.CostEstimate(flops=flops, bytes_accessed=10**6, transcendentals=0),
    )(*ins)


def array_of(shape, dtype=jnp.float32):
    return jax.ShapeDtypeStruct(shape, dtype)


def by_lanes(flat):
    return flat.reshape(flat.shape[:-1] + (-1, W))


def prepare(rank, sources, targets, times, counts, negatives, neighbours, then):
    groups, digit_rows, _ = negatives.shape
    columns = groups * (digit_rows * W // (2 * times.shape[0]))
    events = sources.shape[0]
    halves = events // W
    blocks = halves * (2 + columns)
    nodes = neighbours.shape[0]
    return kernel_call(
        prepare_kernel,
        [
            array_of((blocks, 1, (NBR + 1) * W), jnp.int32),
            array_of((blocks, 1, NBR * W)),
            array_of((blocks, 1, W), jnp.int32),
            array_of((blocks, 1, W)),
            array_of((1,), jnp.int32),
        ],
        [
            rank[None],
            by_lanes(sources),
            by_lanes(targets),
            by_lanes(times),
            by_lanes(counts),
            negatives,
            neighbours.T,
            then.T,
        ],
        [
            ((-(-(NEG + columns) // 16) * 16, events), jnp.float32),
            ((16, events), jnp.float32),
            ((groups, digit_rows // 2, L), jnp.float32),
            ((5 * NEAR_ROWS, nodes), jnp.bfloat16),
            ((min(nodes, HOT), events), jnp.bfloat16),
        ],
        flops=4 * 10**9,
    )


def unflatten_from(flat_ref, tile_ref, shape, offset):
    count, width = shape
    tiles = -(-width // L)
    cycle = L // math.gcd(width, L)
    stride = width * cycle // L
    for first in range(min(cycle, count)):
        amount = -(-(count - first) // cycle)
        row, shift = divmod(offset + width * first, L)
        pieces = -(-(shift + width) // L)
        held = [
            flat_ref[pl.ds(row + piece, amount, stride=stride) if amount > 1 else slice(row + piece, row + piece + 1)]
            for piece in range(pieces)
        ]
        held = jnp.concatenate(held, axis=1) if pieces > 1 else held[0]
        held = held[:, shift : shift + width]
        rows = pl.ds(first, amount, stride=cycle) if amount > 1 else slice(first, first + 1)
        for number in range(tiles):
            part = held[:, number * L : (number + 1) * L]
            if part.shape[1] < L:
                part = jnp.concatenate([part, jnp.zeros((amount, L - part.shape[1]), jnp.float32)], axis=1)
            tile_ref[number, rows] = part
    tiled = [tile_ref[number, :count] for number in range(tiles)]
    return jnp.concatenate(tiled, axis=1)[:, :width] if tiles > 1 else tiled[0][:, :width]


def weights_kernel(
    offset, flat_in, kvt_ref, kv_ref, qt_ref, q_ref, square_ref, wide_ref, flat_s, tile_s, pad_s
):
    flat_s[...] = flat_in[...].astype(jnp.float32)

    def padded(value, row_parts, column_parts):
        pad_s[...] = jnp.zeros_like(pad_s)
        for r_from, r_to, r_size in row_parts:
            for c_from, c_to, c_size in column_parts:
                pad_s[r_to : r_to + r_size, c_to : c_to + c_size] = value[
                    r_from : r_from + r_size, c_from : c_from + c_size
                ]
        return pad_s[...]

    plain = [(0, 0, D)]
    twice = [(0, 0, D), (D, F, TE)]
    heads = [(h * HS, h * HP, HS) for h in range(HEADS)]
    all_heads = [(h * HS, h * HP, HS) for h in range(2 * HEADS)]

    def vector(width):
        nonlocal offset
        value = unflatten_from(flat_s, tile_s, (1, width), offset)
        offset += width
        return jnp.concatenate([value, jnp.zeros((1, L - width), jnp.float32)], axis=1)

    wide_ref[0] = column_of(vector(TE), W)[:F]
    wide_ref[1] = column_of(vector(TE), W)[:F]
    for shape, straight, turned, row_parts, column_parts in (
        ((D + TE, D), q_ref, qt_ref, twice, heads),
        ((D + TE, 2 * D), kv_ref, kvt_ref, twice, all_heads),
        ((D, D), square_ref.at[1], square_ref.at[0], heads, plain),
        ((D, PH), square_ref.at[3], square_ref.at[2], plain, plain),
        ((D, PH), square_ref.at[5], square_ref.at[4], plain, plain),
    ):
        full = padded(unflatten_from(flat_s, tile_s, shape, offset), row_parts, column_parts)
        offset += shape[0] * shape[1]
        n, m = straight.shape
        straight[...] = full[:n, :m].astype(jnp.bfloat16)
        turned[...] = jnp.transpose(full)[:m, :n].astype(jnp.bfloat16)
    wide_ref[2] = column_of(vector(PH), W)[:F]
    wide_ref[3] = column_of(vector(PH), W)[:F]
    wide_ref[4] = jnp.broadcast_to(vector(1)[:, :1], (F, W))


def event_weights(flat, offset):
    rows = flat.reshape(-1, L)[EVENT_ROW:]
    low_type = jnp.bfloat16
    return kernel_call(
        functools.partial(weights_kernel, offset - EVENT_ROW * L),
        [
            array_of((2 * F, 2 * F), low_type),
            array_of((2 * F, 2 * F), low_type),
            array_of((F, 2 * F), low_type),
            array_of((2 * F, F), low_type),
            array_of((6, F, F), low_type),
            array_of((5, F, W)),
        ],
        [rows],
        [
            (rows.shape, jnp.float32),
            ((2, -(-(D + TE) // 8) * 8, L), jnp.float32),
            ((2 * L, 2 * L), jnp.float32),
        ],
        flops=4 * 10**9,
    )


def event_step(weights, table_t, prepared, regions, own_nodes, events_all, halves):
    ids, gaps, slots, valid, live = prepared
    kvt, kv, qt, q, square, wide = weights
    nodes = table_t.shape[1]
    near = NBR * W
    full = near + W
    low_type, high_type = jnp.bfloat16, jnp.float32
    half_table = array_of((regions // 2, nodes // regions, L))
    places = halves + min(CHUNK, ids.shape[0] - halves)
    loss, count, keep, give, g_kv, g_q, g_out, g_source, g_other, *g_rows = kernel_call(
        functools.partial(step_kernel, halves, own_nodes, events_all),
        [
            array_of((1, W)),
            array_of((1, W)),
            half_table,
            half_table,
            array_of((D + TE, 2 * D)),
            array_of((D + TE, D)),
            array_of((D, D)),
            array_of((D, PH)),
            array_of((D, PH)),
            *[array_of((1, width)) for width in (TE, TE, PH, PH, 1)],
        ],
        [
            live,
            my_bit("ev", 0)[None],
            table_t,
            ids,
            gaps,
            slots,
            valid,
            wide,
            kvt,
            kv,
            qt,
            q,
            square,
        ],
        [
            ((places, 2 * F, near), low_type),
            ((places, 2 * F, near), high_type),
            ((places, F, near), high_type),
            ((places, F, W), low_type),
            ((places, F, W), high_type),
            ((places, HEADS, NBR, W), high_type),
            ((places, F, W), low_type),
            ((places, F, W), low_type),
            ((places, F, W), high_type),
            ((F, halves * W), low_type),
            ((F, halves * W), high_type),
            ((min(nodes, HOT), full), low_type),
            ((2 * L, full), low_type),
            ((2 * F, near), low_type),
            ((2 * F, near), low_type),
            ((nodes, 2 * L), high_type),
            ((2 * F, 2 * F), high_type),
            ((2 * F, F), high_type),
            ((3, F, F), high_type),
            ((5, F, W), high_type),
        ],
        flops=4 * 10**10,
    )
    grads = [*g_rows[:2], g_q, g_kv, g_out, g_source, g_other, *g_rows[2:]]
    return loss, count[0, 0], keep, give, grads


def flatten_into(flat_ref, tile_ref, matrix, offset):
    count, width = matrix.shape
    tiles = -(-width // L)
    for number in range(tiles):
        part = matrix[:, number * L : (number + 1) * L]
        if part.shape[1] < L:
            part = jnp.concatenate([part, jnp.zeros((count, L - part.shape[1]), jnp.float32)], axis=1)
        tile_ref[number, :count] = part
    cycle = L // math.gcd(width, L)
    stride = width * cycle // L
    for first in range(min(cycle, count)):
        amount = -(-(count - first) // cycle)
        row, shift = divmod(offset + width * first, L)
        pieces = -(-(shift + width) // L)
        rows = pl.ds(first, amount, stride=cycle) if amount > 1 else slice(first, first + 1)
        parts = [tile_ref[number, rows] for number in range(tiles)]
        if shift:
            parts.insert(0, jnp.zeros((amount, shift), jnp.float32))
        held = jnp.concatenate(parts, axis=1) if len(parts) > 1 else parts[0]
        for piece in range(pieces):
            at = row + piece
            rows = pl.ds(at, amount, stride=stride) if amount > 1 else slice(at, at + 1)
            news = held[:, piece * L : min((piece + 1) * L, held.shape[1])]
            if news.shape[1] < L:
                news = jnp.concatenate([news, jnp.zeros((amount, L - news.shape[1]), jnp.float32)], axis=1)
            flat_ref[rows] += news


def flatten_kernel(offsets, *refs):
    *ins, flat_ref, tile_ref = refs
    flat_ref[...] = jnp.zeros_like(flat_ref)
    for offset, ref in zip(offsets, ins):
        flatten_into(flat_ref, tile_ref, ref[...], offset)


def flat_events(pieces, offset, rows):
    offsets = []
    for piece in pieces:
        offsets.append(offset - EVENT_ROW * L)
        offset += piece.size
    return kernel_call(
        functools.partial(flatten_kernel, offsets),
        [array_of((rows - EVENT_ROW, L))],
        pieces,
        [((2, D + TE, L), jnp.float32)],
        flops=2 * 10**9,
    )[0]


def node_kernel(
    start_ref,
    bit_ref,
    rows_a_ref,
    rows_b_ref,
    rows_c_ref,
    rows_d_ref,
    table_ref,
    events_ref,
    near_ref,
    came_ref,
    loss_ref,
    gi_ref,
    gh_ref,
    bias_ref,
    features_ref,
    keep_ref,
    give_ref,
    flat_ref,
    grad_s,
    tile_s,
    upper_s,
    lower_s,
    state_s,
    order_s,
    hot_s,
    gi_s,
    gh_s,
    bias_s,
    static_s,
):
    part_refs = (rows_a_ref, rows_b_ref, rows_c_ref, rows_d_ref)
    regions = near_ref.shape[0]
    part_nodes = rows_a_ref.shape[0]
    shards = start_ref.shape[0]
    shard = len(part_refs) * part_nodes // shards
    flat_ref[:EVENT_ROW] = jnp.zeros((EVENT_ROW, L), jnp.float32)
    flat_ref[EVENT_ROW:] = events_ref[...]
    for ref, raw_ref in ((gi_s, gi_ref), (gh_s, gh_ref), (bias_s, bias_ref)):
        ref[...] = jnp.zeros_like(ref)
        for g in range(3):
            ref[: raw_ref.shape[0], g * L : g * L + D] = raw_ref[:, g * D : (g + 1) * D].astype(ref.dtype)

    size = near_ref.shape[1]
    for number in range(regions):
        part = slice(number * size, (number + 1) * size)
        grad_s[part] = near_ref[number] + came_ref[number]

    def arrange(number, carry):
        source = pl.ds(pl.multiple_of(start_ref[number], shard), shard)
        order_s[pl.ds(pl.multiple_of(number * shard, shard), shard)] = (
            grad_s[source]
        )
        return carry

    lax.fori_loop(0, shards, arrange, 0)

    def some(rows_ref, first, step, sums):
        at = pl.ds(pl.multiple_of(step * NODE_STEP, NODE_STEP), NODE_STEP)
        into = pl.ds(pl.multiple_of(first + step * NODE_STEP, NODE_STEP), NODE_STEP)
        stored = rows_ref[at, MSG_PAD : MSG_PAD + L]
        held = stored.astype(jnp.float32) + rows_ref[at, MSG_PAD + L :].astype(jnp.float32)
        inputs = dot(rows_ref[at, :MSG_PAD], gi_s[...]) + bias_s[0:1]
        hidden = dot(stored, gh_s[...]) + bias_s[1:2]
        reset = jax.nn.sigmoid(inputs[:, :L] + hidden[:, :L])
        update = jax.nn.sigmoid(inputs[:, L : 2 * L] + hidden[:, L : 2 * L])
        fresh = hidden[:, 2 * L :]
        candidate = jnp.tanh(inputs[:, 2 * L :] + reset * fresh)
        d_state = order_s[into]
        d_third = d_state * (1.0 - update) * (1.0 - candidate * candidate)
        d_fresh = d_third * reset
        d_first = d_third * fresh * reset * (1.0 - reset)
        d_second = d_state * (held - candidate) * update * (1.0 - update)
        news = []
        for number, part in enumerate((d_first, d_second, d_third, d_fresh)):
            lanes_at = slice(number * L, (number + 1) * L)
            news.append(jnp.sum(part, axis=0, keepdims=True))
            upper_s[into, lanes_at], lower_s[into, lanes_at] = split_terms(part)
        state_s[into, :L], state_s[into, L:] = split_terms(grad_s[into])
        return sums + jnp.concatenate(news, axis=1)

    total = jnp.zeros((1, 4 * L), jnp.float32)
    wide_gi, wide_gh = 0.0, 0.0
    for part, rows_ref in enumerate(part_refs):
        first = part * part_nodes
        total = lax.fori_loop(
            0, part_nodes // NODE_STEP, functools.partial(some, rows_ref, first), total
        )
        messages = rows_ref[:, :MSG_PAD]
        stored = rows_ref[:, MSG_PAD : MSG_PAD + L]
        for ref in (upper_s, lower_s):
            terms = ref[first : first + part_nodes]
            wide_gi = wide_gi + dot_tn(messages, terms[:, : 3 * L])
            wide_gh = wide_gh + dot_tn(stored, terms)

    def gates(matrix, order):
        return jnp.concatenate([matrix[:, g * L : g * L + D] for g in order], axis=1)

    pieces = [
        gates(wide_gi[:MSG], (0, 1, 2)),
        gates(wide_gh[:D], (0, 1, 3)),
        gates(total, (0, 1, 2)),
        gates(total, (0, 1, 3)),
    ]
    mine = len(part_refs) * part_nodes // regions
    for number in range(regions):
        at = pl.ds(pl.multiple_of((2 * number + bit_ref[0]) * mine, mine), mine)
        pairs = table_ref[F : F + 16, at].astype(jnp.float32)
        static_s[:, number * mine : (number + 1) * mine] = pairs[0:1] * 128.0 + pairs[1:2]
    hot_rows(hot_s, static_s[...].astype(jnp.int32))
    by_feature = dot(hot_s[...], state_s[...])
    terms = split_terms(by_feature[:, :L] + by_feature[:, L:])
    wide = dot_tn(features_ref[...], terms[0]) + dot_tn(features_ref[...], terms[1])
    pieces.append(wide[:, :D])
    offset = 0
    for piece in pieces:
        flatten_into(flat_ref, tile_s, piece, offset)
        offset += piece.size
    firsts, count = windows(2 * keep_ref.shape[0], flat_ref.shape[0])
    for place, ref in enumerate((keep_ref, give_ref)):
        for number in range(ref.shape[0]):
            for bit in range(2):
                first = firsts[2 * number + bit]

                @pl.when(bit_ref[0] ^ place == bit)
                def copy(ref=ref, number=number, first=first):
                    ref[number, :count] = flat_ref[first : first + count]

            ref[number, count:] = jnp.broadcast_to(loss_ref[...], (ref.shape[1] - count, L))


def windows(regions, flat_rows):
    size = int(flat_rows * L) // regions
    firsts = [number * size // L for number in range(regions)]
    return firsts, max(-(-(number + 1) * size // L) - first for number, first in enumerate(firsts))


def node_grads(weights, start, rows, table_t, node_features, events, grads, loss, regions):
    flat_rows = EVENT_ROW + events.shape[0]
    nodes = grads[0].shape[0] * grads[0].shape[1]
    return kernel_call(
        node_kernel,
        [array_of((regions // 2, -(-(windows(regions, flat_rows)[1] + 1) // 8) * 8, L))] * 2,
        [start, my_bit("ev", 0)[None], *rows, table_t, events, *grads, loss, *weights, node_features],
        [
            ((flat_rows, L), jnp.float32),
            ((nodes, L), jnp.float32),
            ((3, MSG, L), jnp.float32),
            ((nodes, 4 * L), jnp.bfloat16),
            ((nodes, 4 * L), jnp.bfloat16),
            ((nodes, 2 * L), jnp.bfloat16),
            ((nodes, L), jnp.float32),
            ((node_features.shape[0], nodes), jnp.bfloat16),
            ((MSG_PAD, 3 * L), jnp.bfloat16),
            ((L, 3 * L), jnp.bfloat16),
            ((8, 3 * L), jnp.float32),
            ((1, nodes), jnp.float32),
        ],
        flops=8 * 10**9,
    )


def partner(array, name, bit):
    size = lax.axis_size(name)
    return lax.ppermute(array, name, [(i, i ^ (1 << bit)) for i in range(size)])


def my_bit(name, bit):
    return (lax.axis_index(name) >> bit) & 1


def bits_of(name):
    return (lax.axis_size(name) - 1).bit_length()


def exchange(held, done, name, bit):
    other = partner(held, name, bit)
    mine_first = my_bit(name, bit) == 0
    done = sorted(done + [(name == "neg", -bit)])
    place = done.index((name == "neg", -bit))
    parts = [jnp.where(mine_first, held, other), jnp.where(mine_first, other, held)]
    return jnp.stack(parts, axis=place), done


def crossed(array, first, second):
    size = lax.axis_size("ev")
    return lax.ppermute(
        array, "ev", [(i, i ^ (1 << (second if i & 1 else first))) for i in range(size)]
    )


def gather_neg(shard):
    held, done = shard, []
    for bit in range(bits_of("neg")):
        held, done = exchange(held, done, "neg", bit)
    return held, done


def gather_ev(held, done, beside=()):
    high = bits_of("ev") - 1
    for bit in range(1, high - 1):
        held, done = exchange(held, done, "ev", bit)
    odd = my_bit("ev", 0) == 1
    low_set, high_set = my_bit("ev", high - 1) == 1, my_bit("ev", high) == 1
    first_set, second_set = jnp.where(odd, high_set, low_set), jnp.where(odd, low_set, high_set)
    other = crossed(held, high - 1, high)
    held = jnp.stack([jnp.where(first_set, other, held), jnp.where(first_set, held, other)])
    other = crossed(held, high, high - 1)
    zero, one = jnp.where(second_set, other, held), jnp.where(second_set, held, other)
    held = jnp.stack(
        [
            jnp.stack([zero[0], jnp.where(odd, one[0], zero[1])]),
            jnp.stack([jnp.where(odd, zero[1], one[0]), one[1]]),
        ]
    )
    done = sorted(done + [(False, -high), (False, 1 - high)])
    if beside:
        held, *beside = lax.optimization_barrier((held, *beside))
    held, done = exchange(held, done, "ev", 0)
    return held, beside


def reduce_bit(held, bits, bit):
    place = bits.index(bit)
    mine = my_bit("ev", bit)
    keep = lax.dynamic_index_in_dim(held, mine, place, keepdims=False)
    give = lax.dynamic_index_in_dim(held, 1 - mine, place, keepdims=False)
    return keep + partner(give, "ev", bit), [other for other in bits if other != bit]


def scatter_ev(keep, give):
    count = bits_of("ev")
    bits = list(reversed(range(1, count)))
    held = (keep + partner(give, "ev", 0)).reshape((2,) * (count - 1) + keep.shape[1:])
    for bit in range(1, count - 2):
        held, bits = reduce_bit(held, bits, bit)
    middle = held.shape[-2] // 16 * 8
    parts = [(held[..., :middle, :], bits), (held[..., middle:, :], bits)]
    for turn in range(2):
        parts = [
            reduce_bit(part, left, bits[(turn + number) % 2])
            for number, (part, left) in enumerate(parts)
        ]
    return jnp.concatenate([part for part, left in parts], axis=-2)


def scatter_neg(blocks):
    count = bits_of("neg")
    held = blocks.reshape((2,) * count + blocks.shape[1:])
    for bit in range(count):
        mine, place = my_bit("neg", bit), count - 1 - bit
        keep = lax.dynamic_index_in_dim(held, mine, place, keepdims=False)
        give = lax.dynamic_index_in_dim(held, 1 - mine, place, keepdims=False)
        held = keep + partner(give, "neg", bit)
    return held


def lanes(flat):
    amount = flat.shape[-1]
    rows = -(-amount // 128)
    wide = jnp.pad(flat, [(0, 0)] * (flat.ndim - 1) + [(0, rows * 128 - amount)])
    return wide.reshape(flat.shape[:-1] + (rows, 128))


def from_digits(pairs, axis):
    pairs = pairs.astype(jnp.float32)
    high, low = (lax.index_in_dim(pairs, place, axis, keepdims=False) for place in (0, 1))
    return high * 128.0 + low


def on_device(
    master,
    first_moment,
    second_moment,
    memory,
    messages,
    static_ids,
    node_features,
    neighbours,
    neighbour_times,
    last_partner,
    last_deltas,
    last_edges,
    sources,
    targets,
    times,
    negatives,
    neg_counts,
):
    shard = master.shape[0]
    groups = lax.axis_size("neg")
    regions = lax.axis_size("ev")
    devices = regions * groups
    rank = lax.axis_index("neg")
    own_events = sources.shape[0]
    own_nodes = memory.shape[0]
    local_neg = negatives.shape[1]
    total_neg = local_neg * groups
    events_all = own_events * devices

    own_columns = by_lanes(negatives.T).reshape(-1, L)
    own_copy = lanes(master.astype(jnp.bfloat16))
    copy_rows = own_copy.shape[0]
    sent = jnp.concatenate(
        [own_copy, (own_columns >> 7).astype(jnp.bfloat16), (own_columns & 127).astype(jnp.bfloat16)]
    )
    copies, copies_done = exchange(sent, [], "neg", 0)
    copies, late_ids = lax.optimization_barrier((copies, static_ids))
    for bit in range(1, bits_of("neg")):
        copies, copies_done = exchange(copies, copies_done, "neg", bit)
    all_negatives = copies[..., copy_rows:, :].reshape(groups, -1, L)
    copies = copies[..., :copy_rows, :]

    rows, tail = pack(rank, neg_counts, static_ids, messages, memory, own_events // W)
    copies, rows = lax.optimization_barrier((copies, rows))
    high = bits_of("ev") - 1
    odd = my_bit("ev", 0) == 1
    far_neg = list(reversed(range(1, bits_of("neg"))))
    flips = [1 << bit for bit in far_neg] + [jnp.where(odd, 1 << (high - 2), 1 << (high - 1)) * groups]
    flips += [(1 << (bit - 1)) * groups for bit in range(1, high - 1)]
    start = ((lax.axis_index("ev") >> 1) * groups + rank)[None]
    for flip in flips:
        start = jnp.concatenate([start, start ^ flip])
    across = jnp.where(odd, 1 << (high - 1), 1 << (high - 2)) * groups
    start = jnp.concatenate([start, start ^ across, start ^ 1, start ^ across ^ 1]) * own_nodes
    for bit in far_neg:
        rows = jnp.concatenate([rows, partner(rows, "neg", bit)])

    ids, gaps, slots, valid, live = prepare(
        rank, sources, targets, times, neg_counts, all_negatives, neighbours, neighbour_times
    )
    copies, (valid, rows) = gather_ev(copies, copies_done, (valid, rows))
    rows = jnp.concatenate([rows, crossed(rows, high, high - 1)])
    for bit in range(1, high - 1):
        rows = jnp.concatenate([rows, partner(rows, "ev", bit)])

    flat = copies.reshape(devices, -1)[:, :shard].reshape(-1)
    early = unpack(flat)
    state, renewed = owner_pass(early, memory, messages, node_features[late_ids])
    sending = jnp.concatenate(
        [jnp.pad(state.astype(jnp.bfloat16), ((0, 0), (0, F - D))), tail[:, : L - F]], 1
    )
    flat, sending = lax.optimization_barrier((flat, sending))
    weights = event_weights(flat, NODE_PARAMS)
    table, table_done = gather_neg(sending)
    table, weights = lax.optimization_barrier((table, weights))
    table = gather_ev(table, table_done)[0]
    table = table.reshape(-1, L)
    biases = early["b_g"]
    table, rows, start, biases = lax.optimization_barrier((table, rows, start, biases))

    def far_device(device):
        place, near = divmod(device, groups)
        return (place ^ (1 << (high if place & 1 else high - 1))) * groups + (near ^ 1)

    far_rows = [
        crossed(rows, high - 1, high),
        partner(rows, "neg", 0),
        lax.ppermute(rows, ("ev", "neg"), [(i, far_device(i)) for i in range(devices)]),
    ]
    table_t = table.T
    local_loss, neg_total, keep, give, grad_event = event_step(
        weights,
        table_t,
        (ids, gaps, slots, valid, live),
        regions,
        own_nodes,
        events_all,
        own_events // W,
    )
    give, far_rows, local_loss, grad_event = lax.optimization_barrier(
        (give, far_rows, local_loss, grad_event)
    )
    came = partner(give, "ev", 0)
    flat_rows = shard * devices // L
    event_flat = flat_events(grad_event, NODE_PARAMS, flat_rows)
    kept_blocks, given_blocks = node_grads(
        (early["w_gi"], early["w_gh"], biases),
        start,
        [rows, *far_rows],
        table_t,
        node_features,
        event_flat,
        (keep, came),
        local_loss,
        regions,
    )
    block_rows = windows(regions, flat_rows)[1]
    summed = scatter_ev(kept_blocks, given_blocks)
    if shard * groups % L:
        first = lax.axis_index("ev") * (shard * groups) % L
        values = lax.dynamic_slice_in_dim(summed[:block_rows].reshape(-1), first, shard * groups)
        values = lanes(values)
    else:
        values = summed[:block_rows]
    firsts, part_rows = windows(groups, shard * groups / L)
    values = jnp.pad(values, ((0, max(0, firsts[-1] + part_rows - values.shape[0])), (0, 0)))
    shares = jnp.stack(
        [
            jnp.concatenate([values[first : first + part_rows], summed[block_rows:][:1]])
            for first in firsts
        ]
    )
    totals = scatter_neg(shares)
    loss = jnp.sum(totals[part_rows])
    first = rank * shard % L
    grad_shard = lax.dynamic_slice_in_dim(totals[:part_rows].reshape(-1), first, shard)
    new_master, new_first, new_second = adamw(master, first_moment, second_moment, grad_shard)
    codes = jnp.cos(
        last_deltas[:, None] * early["w_time"].astype(jnp.float32)
        + early["b_time"].astype(jnp.float32)
    )
    carried = jnp.concatenate(
        [
            sending[:, :D].astype(jnp.float32),
            table[last_partner][:, :D].astype(jnp.float32),
            codes,
            last_edges.astype(jnp.float32),
        ],
        1,
    )
    return (loss, neg_total, new_master, new_first, new_second, renewed, carried)


def solution(mesh):
    return jax.shard_map(
        on_device,
        mesh=mesh,
        in_specs=(
            P(("ev", "neg")),
            P(("ev", "neg")),
            P(("ev", "neg")),
            P(("ev", "neg"), None),
            P(("ev", "neg"), None),
            P(("ev", "neg")),
            P(),
            P(),
            P(),
            P(("ev", "neg")),
            P(("ev", "neg")),
            P(("ev", "neg"), None),
            P(("ev", "neg")),
            P(("ev", "neg")),
            P("ev"),
            P("ev", "neg"),
            P("ev"),
        ),
        out_specs=(
            P(),
            P(),
            P(("ev", "neg")),
            P(("ev", "neg")),
            P(("ev", "neg")),
            P(("ev", "neg"), None),
            P(("ev", "neg"), None),
        ),
        check_vma=False,
    )
```

```python
import functools
import math

import jax
import jax.numpy as jnp
from jax import lax
from jax.experimental import pallas as pl
from jax.experimental.pallas import tpu as pltpu
from jax.sharding import PartitionSpec as P

D = 100
TE = 100
NF = 413
PH = 100
HEADS = 2
NBR = 10
STEP = 10
HS = 50
MSG = 486
NODE_PARAMS = 3 * D * (MSG + D + 2) + NF * D


beta_one = 0.9
beta_two = 0.999
rate_lr = 0.02
decay_wd = 0.01
eps_adam = 1e-08

HP = 56
F = HEADS * HP
W = 128
LO = 256
L = 128
MSG_PAD = 512
CHUNK = 10
HOT = 2048
EVENT_ROW = 1696
NODE_STEP = 256
VMEM_BYTES = 60 * 1024 * 1024


def unpack(flat):
    layout = [
        ("w_gi", (MSG, 3 * D)),
        ("w_gh", (D, 3 * D)),
        ("b_g", (2, 3 * D)),
        ("w_feat", (NF, D)),
        ("w_time", (TE,)),
        ("b_time", (TE,)),
        ("w_query", (D + TE, D)),
        ("w_kv", (D + TE, 2 * D)),
        ("w_out", (D, D)),
        ("w_ps", (D, PH)),
        ("w_pd", (D, PH)),
        ("b_p1", (PH,)),
        ("w_p2", (PH,)),
        ("b_p2", (1,)),
    ]
    params = {}
    offset = 0
    for label, shape in layout:
        amount = math.prod(shape)
        params[label] = flat[offset : offset + amount].reshape(shape)
        offset += amount
    return params


def dot(left, right):
    return jnp.dot(left, right, preferred_element_type=jnp.float32)


def dot_nt(left, right):
    return lax.dot_general(
        left, right, (((1,), (1,)), ((), ())), preferred_element_type=jnp.float32
    )


def dot_tn(left, right):
    return lax.dot_general(
        left, right, (((0,), (0,)), ((), ())), preferred_element_type=jnp.float32
    )


def split_terms(value):
    first = value.astype(jnp.bfloat16)
    return first, (value - first.astype(jnp.float32)).astype(jnp.bfloat16)


def settled_terms(value):
    first = lax.optimization_barrier(value.astype(jnp.bfloat16))
    return first, (value - first.astype(jnp.float32)).astype(jnp.bfloat16)


def three_terms(value):
    first = value.astype(jnp.bfloat16)
    rest = value - first.astype(jnp.float32)
    second = rest.astype(jnp.bfloat16)
    return first, second, (rest - second.astype(jnp.float32)).astype(jnp.bfloat16)


def owner_pass(params, memory, messages, features):
    inputs = dot(messages, params["w_gi"]) + params["b_g"][0].astype(jnp.float32)
    hidden = dot(memory.astype(jnp.bfloat16), params["w_gh"]) + params["b_g"][1].astype(jnp.float32)
    reset = jax.nn.sigmoid(inputs[:, :D] + hidden[:, :D])
    update = jax.nn.sigmoid(inputs[:, D : 2 * D] + hidden[:, D : 2 * D])
    candidate = jnp.tanh(inputs[:, 2 * D :] + reset * hidden[:, 2 * D :])
    renewed = (1.0 - update) * candidate + update * memory
    return (renewed + dot(features, params["w_feat"]), renewed)


def adamw(master, first_state, second_state, grads):
    first_new = beta_one * first_state + (1.0 - beta_one) * grads
    second_new = beta_two * second_state + (1.0 - beta_two) * grads * grads
    corrected = (
        first_new
        / (1.0 - beta_one**STEP)
        / (jnp.sqrt(second_new / (1.0 - beta_two**STEP)) + eps_adam)
    )
    return (master - rate_lr * (corrected + decay_wd * master), first_new, second_new)


def sine_cosine(angle):
    turns = jnp.round(angle * (2.0 / math.pi))
    rest = angle - turns * 1.5703125
    rest = rest - turns * 4.837512969970703e-4
    rest = rest - turns * 7.549789948768648e-8
    square = rest * rest
    sine = rest + rest * square * (
        -1.6666654611e-1 + square * (8.3321608736e-3 - square * 1.9515295891e-4)
    )
    cosine = (
        1.0
        - 0.5 * square
        + square
        * square
        * (4.166664568298827e-2 + square * (-1.388731625493765e-3 + square * 2.443315711809948e-5))
    )
    quadrant = turns.astype(jnp.int32)
    odd = (quadrant & 1) == 1
    cos_value = jnp.where(odd, sine, cosine)
    sin_value = jnp.where(odd, cosine, sine)
    cos_value = jnp.where(((quadrant + 1) & 2) == 2, -cos_value, cos_value)
    sin_value = jnp.where((quadrant & 2) == 2, -sin_value, sin_value)
    return cos_value, sin_value


def any_angle(angle):
    return jnp.cos(angle), jnp.sin(angle)


def pair(value):
    return jnp.concatenate([value, value], axis=1)


def fold(value):
    return value[:, :W] + value[:, W:]


def tile(k):
    return slice(k * W, (k + 1) * W)


def hot_rows(hot_ref, ids, base=0):
    count = ids.shape[1]
    rows = lax.broadcasted_iota(jnp.int32, (LO, count), 0).astype(jnp.float32).astype(jnp.bfloat16)
    place = (ids & (LO - 1)).astype(jnp.float32)
    group = ids // LO - base // LO
    one, nought = jnp.ones_like(rows), jnp.zeros_like(rows)
    for number in range(hot_ref.shape[0] // LO):
        here = jnp.where(group == number, place, -1.0)
        here = jnp.broadcast_to(here, (LO, count)).astype(jnp.bfloat16)
        hot_ref[number * LO : (number + 1) * LO] = jnp.where(rows == here, one, nought)


def gather_columns(table_ref, hot_ref, ids):
    step = hot_ref.shape[0]
    found = None
    for base in range(0, table_ref.shape[1], step):
        hot_rows(hot_ref, ids, base)
        part = dot(table_ref[:, base : base + step], hot_ref[...])
        found = part if found is None else found + part
    return found


SRC, TGT, TIME, COUNT, NEG = 0, 1, 2, 3, 4
ID, AT, EVENT = 0, 1, 2
NEAR_ROWS = 16


def column_of(row, lanes_of):
    wide = jnp.transpose(jnp.broadcast_to(row, (L, row.shape[1])))
    return jnp.concatenate([wide] * (lanes_of // L), axis=1)


def pack_kernel(halves, rank_ref, numbers_ref, static_ref, messages_ref, memory_ref, rows_ref, tail_ref):
    rows_ref[...] = jnp.zeros_like(rows_ref)
    rows_ref[:, :MSG] = messages_ref[...]
    terms = split_terms(memory_ref[...])
    rows_ref[:, MSG_PAD : MSG_PAD + D] = terms[0]
    rows_ref[:, MSG_PAD + L : MSG_PAD + L + D] = terms[1]
    counts = numbers_ref[pl.ds(rank_ref[0] * halves, halves)].astype(jnp.float32)
    total = jnp.sum(jnp.sum(counts, axis=1, keepdims=True), axis=0, keepdims=True)
    static = column_of(static_ref[...].astype(jnp.float32), L).astype(jnp.int32)
    lane = lax.broadcasted_iota(jnp.int32, static.shape, 1)
    value = jnp.where(lane < 2, static, total.astype(jnp.int32))
    value = jnp.where((lane & 1) == 0, value >> 7, value & 127)
    tail_ref[...] = value.astype(jnp.float32).astype(jnp.bfloat16)


def pack(rank, counts, static_ids, messages, memory, halves):
    nodes = static_ids.shape[0]
    return kernel_call(
        functools.partial(pack_kernel, halves),
        [array_of((nodes, MSG_PAD + 2 * L), jnp.bfloat16), array_of((nodes, L), jnp.bfloat16)],
        [rank[None], by_lanes(counts), static_ids[None], messages, memory],
        [],
        flops=10**8,
    )


def prepare_kernel(
    rank_ref,
    source_ref,
    target_ref,
    times_ref,
    numbers_ref,
    digits_ref,
    near_ref,
    then_ref,
    ids_ref,
    gaps_ref,
    slots_ref,
    valid_ref,
    live_ref,
    event_s,
    pair_s,
    negatives_s,
    around_s,
    hot_s,
):
    groups, digit_rows, _ = digits_ref.shape
    rows = times_ref.shape[0]
    local = digit_rows // (2 * rows)
    columns = groups * local
    found = digits_ref[...].astype(jnp.float32)
    negatives_s[...] = found[:, : digit_rows // 2] * 128.0 + found[:, digit_rows // 2 :]
    halves = source_ref.shape[0]
    events = halves * W
    mine = pl.ds(rank_ref[0] * halves, halves)
    event_s[...] = jnp.zeros_like(event_s)
    for row, held in enumerate(
        [source_ref[...], target_ref[...], times_ref[mine], numbers_ref[mine]]
        + [
            negatives_s[group, pl.ds(j * rows + rank_ref[0] * halves, halves)]
            for group in range(groups)
            for j in range(local)
        ]
    ):
        held = held.astype(jnp.float32)
        for half in range(halves):
            event_s[row : row + 1, half * W : (half + 1) * W] = held[half : half + 1]
    counts = event_s[COUNT : COUNT + 1]
    shape = (events, events)
    earlier = lax.broadcasted_iota(jnp.int32, shape, 0) < lax.broadcasted_iota(jnp.int32, shape, 1)
    earlier = jnp.where(earlier, 1.0, 0.0).astype(jnp.bfloat16)
    event = lax.broadcasted_iota(jnp.int32, (1, events), 1).astype(jnp.float32)
    wanted = lax.broadcasted_iota(jnp.int32, (columns * events, events), 0).astype(jnp.float32)
    taken = jnp.zeros((1, 1), jnp.float32)
    packed = jnp.zeros((16, columns * events), jnp.float32)
    for number in range(columns):
        active = counts >= float(columns - number)
        ones = jnp.broadcast_to(jnp.where(active, 1.0, 0.0), (16, events))
        place = taken + dot(ones.astype(jnp.bfloat16), earlier)[0:1]
        taken = taken + jnp.sum(ones[0:1], axis=1, keepdims=True)
        place = jnp.where(active, place, -1.0)
        order = jnp.where(wanted == place, 1.0, 0.0).astype(jnp.bfloat16)
        row = NEG + number
        pair_s[...] = jnp.zeros_like(pair_s)
        pair_s[ID : ID + 1] = event_s[row : row + 1]
        pair_s[AT : AT + 1] = event_s[TIME : TIME + 1]
        pair_s[EVENT : EVENT + 1] = event
        thirds = dot_nt(jnp.concatenate(three_terms(pair_s[...]), axis=0), order)
        packed = packed + (thirds[:16] + thirds[16:32]) + thirds[32:]
    slot = lax.broadcasted_iota(jnp.int32, (1, columns * events), 1).astype(jnp.float32)
    valid = jnp.where(slot < taken, 1.0, 0.0)
    live_ref[0] = halves + (jnp.sum(counts).astype(jnp.int32) + W - 1) // W
    around_s[...] = jnp.zeros_like(around_s)
    near = near_ref[...]
    parts = [(near >> 7).astype(jnp.float32), (near & 127).astype(jnp.float32)]
    parts = [part.astype(jnp.bfloat16) for part in parts] + list(three_terms(then_ref[...]))
    for number, part in enumerate(parts):
        around_s[number * NEAR_ROWS : number * NEAR_ROWS + NBR] = part
    sets = [
        (event_s[SRC : SRC + 1], event_s[TIME : TIME + 1], event, jnp.ones((1, events))),
        (event_s[TGT : TGT + 1], event_s[TIME : TIME + 1], event, jnp.ones((1, events))),
    ]
    for number in range(columns):
        part = slice(number * events, (number + 1) * events)
        sets.append((packed[ID : ID + 1, part], packed[AT : AT + 1, part], packed[EVENT : EVENT + 1, part], valid[:, part]))
    for number, (nodes, times, of_event, counted) in enumerate(sets):
        nodes = nodes.astype(jnp.int32)
        found = gather_columns(around_s, hot_s, nodes)
        near = found[:NBR] * 128.0 + found[NEAR_ROWS : NEAR_ROWS + NBR]
        near = near.astype(jnp.int32)
        then = (
            found[2 * NEAR_ROWS : 2 * NEAR_ROWS + NBR] + found[3 * NEAR_ROWS : 3 * NEAR_ROWS + NBR]
        ) + found[4 * NEAR_ROWS : 4 * NEAR_ROWS + NBR]
        gaps = times - then
        for half in range(halves):
            block, lanes_at = number * halves + half, slice(half * W, (half + 1) * W)
            for k in range(NBR):
                ids_ref[block, :, tile(k)] = near[k : k + 1, lanes_at]
                gaps_ref[block, :, tile(k)] = gaps[k : k + 1, lanes_at]
            ids_ref[block, :, NBR * W :] = nodes[:, lanes_at]
            slots_ref[block] = of_event[:, lanes_at].astype(jnp.int32)
            valid_ref[block] = counted[:, lanes_at]


def step_kernel(
    halves,
    own_nodes,
    events_all,
    live_ref,
    bit_ref,
    table_ref,
    ids_ref,
    gaps_ref,
    slots_ref,
    valid_ref,
    wide_ref,
    kvt_ref,
    kv_ref,
    qt_ref,
    q_ref,
    square_ref,
    loss_ref,
    count_ref,
    keep_ref,
    give_ref,
    gkv_ref,
    gq_ref,
    gout_ref,
    gsource_ref,
    gother_ref,
    gtime_ref,
    gbase_ref,
    gp1_ref,
    gp2_ref,
    gend_ref,
    x_s,
    kv_s,
    sin_s,
    own_s,
    query_s,
    att_s,
    mix_s,
    z_s,
    dz_s,
    dsources_s,
    hot_s,
    right_s,
    upper_s,
    lower_s,
    rows_s,
    gkv_s,
    gq_s,
    gsquare_s,
    gwide_s,
):
    scale = 1.0 / math.sqrt(HS)
    near = NBR * W
    found = table_ref[F : F + 16].astype(jnp.float32)
    counted = jnp.sum(found, axis=1, keepdims=True)
    neg_total = (counted[2:3] * 128.0 + counted[3:4]) * (1.0 / own_nodes)
    count_ref[...] = jnp.broadcast_to(neg_total, (1, W))
    share = jnp.broadcast_to(1.0 / neg_total, (1, W))
    b_time = wide_ref[1]
    b_p1, w_p2 = wide_ref[2], wide_ref[3]
    b_p2 = wide_ref[4][0:1]
    zero_cos, zero_sin = any_angle(b_time)
    furthest = jnp.max(jnp.abs(gaps_ref[...])) * jnp.max(jnp.abs(wide_ref[0])) + jnp.max(
        jnp.abs(b_time)
    )
    moderate = furthest <= 8192.0
    zero_code = zero_cos.astype(jnp.bfloat16)
    for ref in (rows_s, right_s, gkv_s, gq_s, gsquare_s, gwide_s, dsources_s, loss_ref):
        ref[...] = jnp.zeros_like(ref)
    head_rows = (slice(0, HP), slice(HP, F))
    live = live_ref[0]

    def forward(trig, slot, block):
        for s in range(0, F, 16):
            rows = slice(s, s + 16)
            w_rows, b_rows = wide_ref[0, rows], wide_ref[1, rows]
            for k in range(NBR):
                angle = gaps_ref[block, :, tile(k)] * w_rows + b_rows
                cos_value, sin_value = trig(angle)
                sin_s[slot, rows, tile(k)] = sin_value
                x_s[slot, F + s : F + s + 16, tile(k)] = cos_value.astype(jnp.bfloat16)
        found = gather_columns(table_ref, hot_s, ids_ref[block])[:F].astype(jnp.bfloat16)
        x_s[slot, :F] = found[:, :near]
        own = found[:, near:]
        own_s[slot] = own
        query = dot(qt_ref[...], jnp.concatenate([own, zero_code], axis=0))
        query_s[slot] = query
        kv_s[slot] = dot(kvt_ref[...], x_s[slot])
        mixed = []
        for h, rows in enumerate(head_rows):
            scores = jnp.concatenate(
                [
                    jnp.sum(kv_s[slot, rows, tile(k)] * query[rows], axis=0, keepdims=True)
                    for k in range(NBR)
                ],
                axis=0,
            )
            scores = scores * scale
            powers = jnp.exp(scores - jnp.max(scores, axis=0, keepdims=True))
            att_s[slot, h] = powers / jnp.sum(powers, axis=0, keepdims=True)
            mixed_h = jnp.zeros((HP, W), jnp.float32)
            for k in range(NBR):
                values = kv_s[slot, F + h * HP : F + (h + 1) * HP, tile(k)]
                mixed_h = mixed_h + att_s[slot, h, k : k + 1] * values
            mixed.append(mixed_h)
        mixed = jnp.concatenate(mixed, axis=0).astype(jnp.bfloat16)
        mix_s[slot] = mixed
        emb = own.astype(jnp.float32) + dot(square_ref[0], mixed)
        z_s[:, pl.ds(pl.multiple_of(slot * W, W), W)] = emb.astype(jnp.bfloat16)

    def predict(base, amount):
        blocks = range(halves + base, halves + base + amount)
        valid = jnp.concatenate([valid_ref[block] for block in blocks], axis=1)
        of_slot = jnp.concatenate([slots_ref[block] for block in blocks], axis=1)
        z = z_s[:, halves * W : (halves + amount) * W].astype(jnp.float32)
        z = jnp.where(valid > 0.0, z, 0.0).astype(jnp.bfloat16)
        events = lax.broadcasted_iota(jnp.int32, (halves * W, amount * W), 0)
        of_event = jnp.where(events == of_slot, 1.0, 0.0).astype(jnp.bfloat16)
        source = dot(z_s[:, : halves * W], of_event).astype(jnp.bfloat16)
        before_all = dot(square_ref[2], source) + dot(square_ref[4], z)
        losses = jnp.zeros((1, W), jnp.float32)
        ends = jnp.zeros((1, W), jnp.float32)
        by_hidden = jnp.zeros((F, W), jnp.float32)
        by_before = jnp.zeros((F, W), jnp.float32)
        for number, block in enumerate(blocks):
            before = before_all[:, tile(number)] + b_p1
            inner = 0.7978845608028654 * (before + 0.044715 * before * before * before)
            bend = jnp.tanh(inner)
            hidden = (0.5 * before * (1.0 + bend)).astype(jnp.bfloat16).astype(jnp.float32)
            slope = 0.5 * (1.0 + bend) + 0.5 * before * (1.0 - bend * bend) * (
                0.7978845608028654 * (1.0 + 3.0 * 0.044715 * before * before)
            )
            score = jnp.sum(hidden * w_p2, axis=0, keepdims=True) + b_p2
            positive = block < 2 * halves
            sign = -1.0 if positive else 1.0
            weight = valid[:, tile(number)] * (1.0 / events_all if positive else share)
            signed = sign * score
            small = jnp.exp(-jnp.abs(signed))
            losses = losses + weight * (jnp.maximum(signed, 0.0) + jnp.log1p(small))
            sigmoid = jnp.where(signed >= 0.0, 1.0, small) / (1.0 + small)
            d_score = (sign * weight) * sigmoid
            by_hidden = by_hidden + hidden * d_score
            ends = ends + d_score
            d_before = w_p2 * d_score * slope
            by_before = by_before + d_before
            upper_s[:F, tile(number)], lower_s[:F, tile(number)] = split_terms(d_before)
        loss_ref[...] += losses
        gwide_s[2] += by_before
        gwide_s[3] += by_hidden
        gwide_s[4, 0:1] += ends
        d_z = 0.0
        for ref in (upper_s, lower_s):
            term = ref[:F, : amount * W]
            gsquare_s[2] += dot_nt(z, term)
            dsources_s[...] += dot_nt(term, of_event)
            d_z = d_z + dot(square_ref[5], term)
        dz_s[:, halves * W : (halves + amount) * W] = d_z

    def backward(slot, block):
        d_emb = dz_s[:, pl.ds(pl.multiple_of(slot * W, W), W)]
        terms = jnp.concatenate(split_terms(d_emb), axis=1)
        gsquare_s[0] += dot_nt(pair(mix_s[slot]), terms)
        d_mixed = fold(dot(square_ref[1], terms))
        d_query = []
        for h, rows in enumerate(head_rows):
            d_mixed_h, query_h = d_mixed[rows], query_s[slot, rows]
            value_rows = slice(F + h * HP, F + (h + 1) * HP)
            d_shares = jnp.concatenate(
                [
                    jnp.sum(kv_s[slot, value_rows, tile(k)] * d_mixed_h, axis=0, keepdims=True)
                    for k in range(NBR)
                ],
                axis=0,
            )
            part = att_s[slot, h]
            total = jnp.sum(part * d_shares, axis=0, keepdims=True)
            d_scores = part * (d_shares - total) * scale
            d_query_h = jnp.zeros((HP, W), jnp.float32)
            for k in range(NBR):
                d_score = d_scores[k : k + 1]
                d_query_h = d_query_h + d_score * kv_s[slot, rows, tile(k)]
                for at, d_part in (
                    (rows, d_score * query_h),
                    (value_rows, att_s[slot, h, k : k + 1] * d_mixed_h),
                ):
                    upper_s[at, tile(k)], lower_s[at, tile(k)] = split_terms(d_part)
            d_query.append(d_query_h)
        x = x_s[slot]
        upper, lower = upper_s[...], lower_s[...]
        gkv_s[...] += dot_nt(x, upper) + dot_nt(x, lower)
        d_x = dot(kv_ref[...], upper) + dot(kv_ref[...], lower)
        for s in range(0, F, 16):
            rows = slice(s, s + 16)
            to_b = jnp.zeros((16, W), jnp.float32)
            to_w = jnp.zeros((16, W), jnp.float32)
            for k in range(NBR):
                first, second = split_terms(d_x[rows, tile(k)])
                right_s[rows, tile(k)] = first
                right_s[L + s : L + s + 16, tile(k)] = second
                turned = sin_s[slot, rows, tile(k)] * d_x[F + s : F + s + 16, tile(k)]
                to_b = to_b + turned
                to_w = to_w + turned * gaps_ref[block, :, tile(k)]
            gwide_s[1, rows] -= to_b
            gwide_s[0, rows] -= to_w
        d_query = jnp.concatenate(d_query, axis=0)
        terms = jnp.concatenate(split_terms(d_query), axis=1)
        code = jnp.concatenate([own_s[slot], zero_code], axis=0)
        gq_s[...] += dot_nt(pair(code), terms)
        d_code = fold(dot(q_ref[...], terms))
        gwide_s[1] -= zero_sin * d_code[F:]
        right_s[:F, near:], right_s[L : L + F, near:] = split_terms(d_emb + d_code[:F])
        for base in range(0, rows_s.shape[0], hot_s.shape[0]):
            hot_rows(hot_s, ids_ref[block], base)
            rows_s[base : base + hot_s.shape[0]] += dot_nt(hot_s[...], right_s[...])

    most = ids_ref.shape[0] - halves
    chunks = -(-most // CHUNK)
    for chunk in range(chunks):
        base = chunk * CHUNK
        count = jnp.clip(live - base, 0, CHUNK)
        first = halves + base if chunk else 0

        def run_forward(trig, base=base, count=count, first=first):
            def one(block, carry):
                forward(trig, block - base, block)
                return carry

            lax.fori_loop(first, halves + base + count, one, 0)

        for usable, trig in ((moderate, sine_cosine), (jnp.logical_not(moderate), any_angle)):
            pl.when(usable)(functools.partial(run_forward, trig))
        predict(base, min(CHUNK, most - base))
        if chunk == chunks - 1:
            for half in range(halves):
                d_source = dsources_s[:, half * W : (half + 1) * W]
                terms = jnp.concatenate(split_terms(d_source), axis=1)
                gsquare_s[1] += dot_nt(pair(z_s[:, tile(half)]), terms)
                dz_s[:, tile(half)] = fold(dot(square_ref[3], terms))

        def back(slot, carry, base=base):
            backward(slot, jnp.where(slot < halves, slot, slot + base))
            return carry

        lax.fori_loop(0 if chunk == chunks - 1 else halves, halves + count, back, 0)
    region = keep_ref.shape[1]
    for number in range(keep_ref.shape[0]):
        for ref, bit in ((keep_ref, bit_ref[0]), (give_ref, 1 - bit_ref[0])):
            at = pl.ds(pl.multiple_of((2 * number + bit) * region, region), region)
            ref[number] = rows_s[at, :L] + rows_s[at, L:]

    def cut_rows(matrix):
        return jnp.concatenate([matrix[:D], matrix[F : F + D]], axis=0)

    def cut_heads(matrix, axis):
        return jnp.concatenate(
            [
                lax.slice_in_dim(matrix, h * HP, h * HP + HS, axis=axis)
                for h in range(matrix.shape[axis] // HP)
            ],
            axis=axis,
        )

    gkv_ref[...] = cut_heads(cut_rows(gkv_s[...]), 1)
    gq_ref[...] = cut_heads(cut_rows(gq_s[...]), 1)
    gout_ref[...] = cut_heads(gsquare_s[0], 0)[:, :D]
    gsource_ref[...] = gsquare_s[1][:D, :PH]
    gother_ref[...] = gsquare_s[2][:D, :PH]
    ones = jnp.ones((8, W), jnp.bfloat16)
    for number, ref in enumerate((gtime_ref, gbase_ref, gp1_ref, gp2_ref, gend_ref)):
        total = sum(dot_nt(ones, term) for term in three_terms(gwide_s[number]))
        ref[...] = total[0:1, : ref.shape[1]]


def kernel_call(kernel, outs, ins, scratch, flops):
    def place(array):
        scalars = len(array.shape) == 1 and array.dtype == jnp.int32
        return pl.BlockSpec(memory_space=pltpu.SMEM if scalars else pltpu.VMEM)

    return pl.pallas_call(
        kernel,
        out_shape=tuple(outs),
        in_specs=[place(array) for array in ins],
        out_specs=tuple(place(array) for array in outs),
        scratch_shapes=[pltpu.VMEM(shape, dtype) for shape, dtype in scratch],
        compiler_params=pltpu.CompilerParams(vmem_limit_bytes=VMEM_BYTES),
        cost_estimate=pl.CostEstimate(flops=flops, bytes_accessed=10**6, transcendentals=0),
    )(*ins)


def array_of(shape, dtype=jnp.float32):
    return jax.ShapeDtypeStruct(shape, dtype)


def by_lanes(flat):
    return flat.reshape(flat.shape[:-1] + (-1, W))


def prepare(rank, sources, targets, times, counts, negatives, neighbours, then):
    groups, digit_rows, _ = negatives.shape
    columns = groups * (digit_rows * W // (2 * times.shape[0]))
    events = sources.shape[0]
    halves = events // W
    blocks = halves * (2 + columns)
    nodes = neighbours.shape[0]
    return kernel_call(
        prepare_kernel,
        [
            array_of((blocks, 1, (NBR + 1) * W), jnp.int32),
            array_of((blocks, 1, NBR * W)),
            array_of((blocks, 1, W), jnp.int32),
            array_of((blocks, 1, W)),
            array_of((1,), jnp.int32),
        ],
        [
            rank[None],
            by_lanes(sources),
            by_lanes(targets),
            by_lanes(times),
            by_lanes(counts),
            negatives,
            neighbours.T,
            then.T,
        ],
        [
            ((-(-(NEG + columns) // 16) * 16, events), jnp.float32),
            ((16, events), jnp.float32),
            ((groups, digit_rows // 2, L), jnp.float32),
            ((5 * NEAR_ROWS, nodes), jnp.bfloat16),
            ((min(nodes, HOT), events), jnp.bfloat16),
        ],
        flops=4 * 10**9,
    )


def unflatten_from(flat_ref, tile_ref, shape, offset):
    count, width = shape
    tiles = -(-width // L)
    cycle = L // math.gcd(width, L)
    stride = width * cycle // L
    for first in range(min(cycle, count)):
        amount = -(-(count - first) // cycle)
        row, shift = divmod(offset + width * first, L)
        pieces = -(-(shift + width) // L)
        held = [
            flat_ref[pl.ds(row + piece, amount, stride=stride) if amount > 1 else slice(row + piece, row + piece + 1)]
            for piece in range(pieces)
        ]
        held = jnp.concatenate(held, axis=1) if pieces > 1 else held[0]
        held = held[:, shift : shift + width]
        rows = pl.ds(first, amount, stride=cycle) if amount > 1 else slice(first, first + 1)
        for number in range(tiles):
            part = held[:, number * L : (number + 1) * L]
            if part.shape[1] < L:
                part = jnp.concatenate([part, jnp.zeros((amount, L - part.shape[1]), jnp.float32)], axis=1)
            tile_ref[number, rows] = part
    tiled = [tile_ref[number, :count] for number in range(tiles)]
    return jnp.concatenate(tiled, axis=1)[:, :width] if tiles > 1 else tiled[0][:, :width]


def weights_kernel(
    offset, flat_in, kvt_ref, kv_ref, qt_ref, q_ref, square_ref, wide_ref, flat_s, tile_s, pad_s
):
    flat_s[...] = flat_in[...].astype(jnp.float32)

    def padded(value, row_parts, column_parts):
        pad_s[...] = jnp.zeros_like(pad_s)
        for r_from, r_to, r_size in row_parts:
            for c_from, c_to, c_size in column_parts:
                pad_s[r_to : r_to + r_size, c_to : c_to + c_size] = value[
                    r_from : r_from + r_size, c_from : c_from + c_size
                ]
        return pad_s[...]

    plain = [(0, 0, D)]
    twice = [(0, 0, D), (D, F, TE)]
    heads = [(h * HS, h * HP, HS) for h in range(HEADS)]
    all_heads = [(h * HS, h * HP, HS) for h in range(2 * HEADS)]

    def vector(width):
        nonlocal offset
        value = unflatten_from(flat_s, tile_s, (1, width), offset)
        offset += width
        return jnp.concatenate([value, jnp.zeros((1, L - width), jnp.float32)], axis=1)

    wide_ref[0] = column_of(vector(TE), W)[:F]
    wide_ref[1] = column_of(vector(TE), W)[:F]
    for shape, straight, turned, row_parts, column_parts in (
        ((D + TE, D), q_ref, qt_ref, twice, heads),
        ((D + TE, 2 * D), kv_ref, kvt_ref, twice, all_heads),
        ((D, D), square_ref.at[1], square_ref.at[0], heads, plain),
        ((D, PH), square_ref.at[3], square_ref.at[2], plain, plain),
        ((D, PH), square_ref.at[5], square_ref.at[4], plain, plain),
    ):
        full = padded(unflatten_from(flat_s, tile_s, shape, offset), row_parts, column_parts)
        offset += shape[0] * shape[1]
        n, m = straight.shape
        straight[...] = full[:n, :m].astype(jnp.bfloat16)
        turned[...] = jnp.transpose(full)[:m, :n].astype(jnp.bfloat16)
    wide_ref[2] = column_of(vector(PH), W)[:F]
    wide_ref[3] = column_of(vector(PH), W)[:F]
    wide_ref[4] = jnp.broadcast_to(vector(1)[:, :1], (F, W))


def event_weights(flat, offset):
    rows = flat.reshape(-1, L)[EVENT_ROW:]
    low_type = jnp.bfloat16
    return kernel_call(
        functools.partial(weights_kernel, offset - EVENT_ROW * L),
        [
            array_of((2 * F, 2 * F), low_type),
            array_of((2 * F, 2 * F), low_type),
            array_of((F, 2 * F), low_type),
            array_of((2 * F, F), low_type),
            array_of((6, F, F), low_type),
            array_of((5, F, W)),
        ],
        [rows],
        [
            (rows.shape, jnp.float32),
            ((2, -(-(D + TE) // 8) * 8, L), jnp.float32),
            ((2 * L, 2 * L), jnp.float32),
        ],
        flops=4 * 10**9,
    )


def event_step(weights, table_t, prepared, regions, own_nodes, events_all, halves):
    ids, gaps, slots, valid, live = prepared
    kvt, kv, qt, q, square, wide = weights
    nodes = table_t.shape[1]
    near = NBR * W
    full = near + W
    low_type, high_type = jnp.bfloat16, jnp.float32
    half_table = array_of((regions // 2, nodes // regions, L))
    places = halves + min(CHUNK, ids.shape[0] - halves)
    loss, count, keep, give, g_kv, g_q, g_out, g_source, g_other, *g_rows = kernel_call(
        functools.partial(step_kernel, halves, own_nodes, events_all),
        [
            array_of((1, W)),
            array_of((1, W)),
            half_table,
            half_table,
            array_of((D + TE, 2 * D)),
            array_of((D + TE, D)),
            array_of((D, D)),
            array_of((D, PH)),
            array_of((D, PH)),
            *[array_of((1, width)) for width in (TE, TE, PH, PH, 1)],
        ],
        [
            live,
            my_bit("ev", 0)[None],
            table_t,
            ids,
            gaps,
            slots,
            valid,
            wide,
            kvt,
            kv,
            qt,
            q,
            square,
        ],
        [
            ((places, 2 * F, near), low_type),
            ((places, 2 * F, near), high_type),
            ((places, F, near), high_type),
            ((places, F, W), low_type),
            ((places, F, W), high_type),
            ((places, HEADS, NBR, W), high_type),
            ((places, F, W), low_type),
            ((F, places * W), low_type),
            ((F, places * W), high_type),
            ((F, halves * W), high_type),
            ((min(nodes, HOT), full), low_type),
            ((2 * L, full), low_type),
            ((2 * F, near), low_type),
            ((2 * F, near), low_type),
            ((nodes, 2 * L), high_type),
            ((2 * F, 2 * F), high_type),
            ((2 * F, F), high_type),
            ((3, F, F), high_type),
            ((5, F, W), high_type),
        ],
        flops=4 * 10**10,
    )
    grads = [*g_rows[:2], g_q, g_kv, g_out, g_source, g_other, *g_rows[2:]]
    return loss, count[0, 0], keep, give, grads


def flatten_into(flat_ref, tile_ref, matrices, offset):
    count, width = 0, matrices[0].shape[1]
    tiles = -(-width // L)
    for matrix in matrices:
        rows = slice(count, count + matrix.shape[0])
        for number in range(tiles):
            part = matrix[:, number * L : (number + 1) * L]
            if part.shape[1] < L:
                blank = jnp.zeros((part.shape[0], L - part.shape[1]), jnp.float32)
                part = jnp.concatenate([part, blank], axis=1)
            tile_ref[number, rows] = part
        count = rows.stop
    cycle = L // math.gcd(width, L)
    stride = width * cycle // L

    def strided(first, amount, step):
        return pl.ds(first, amount, stride=step) if amount > 1 else slice(first, first + 1)

    carried = None
    for first in range(min(cycle, count)):
        amount = -(-(count - first) // cycle)
        row, shift = divmod(offset + width * first, L)
        pieces = -(-(shift + width) // L)
        parts = [tile_ref[number, strided(first, amount, cycle)] for number in range(tiles)]
        if shift:
            parts.insert(0, jnp.zeros((amount, shift), jnp.float32))
        held = jnp.concatenate(parts, axis=1) if len(parts) > 1 else parts[0]
        for piece in range(pieces):
            news = held[:, piece * L : min((piece + 1) * L, held.shape[1])]
            if news.shape[1] < L:
                blank = jnp.zeros((amount, L - news.shape[1]), jnp.float32)
                news = jnp.concatenate([news, blank], axis=1)
            whole = piece > 0 or shift == 0
            if carried is not None:
                left, at = carried
                news, whole, carried = news + left[:amount], True, None
                if left.shape[0] > amount:
                    at += stride * amount
                    flat_ref[at : at + 1] += left[amount:]
            if piece == pieces - 1 and (shift + width) % L:
                if whole:
                    carried = (news, row + piece)
                else:
                    flat_ref[strided(row + piece, amount, stride)] += news
            elif whole:
                flat_ref[strided(row + piece, amount, stride)] = news
            else:
                flat_ref[strided(row + piece, amount, stride)] += news
    if carried is not None:
        left, at = carried
        flat_ref[strided(at, left.shape[0], stride)] += left


def by_width(pieces):
    groups = []
    for piece in pieces:
        if groups and groups[-1][-1].shape[1] == piece.shape[1]:
            groups[-1].append(piece)
        else:
            groups.append([piece])
    return groups


def flatten_all(flat_ref, tile_ref, pieces, offset):
    for group in by_width(pieces):
        flatten_into(flat_ref, tile_ref, [piece[...] for piece in group], offset)
        offset += sum(math.prod(piece.shape) for piece in group)


def flatten_kernel(offset, *refs):
    *ins, flat_ref, tile_ref = refs
    flat_ref[...] = jnp.zeros_like(flat_ref)
    flatten_all(flat_ref, tile_ref, ins, offset)


def flat_events(pieces, offset, rows):
    deepest = max(sum(piece.shape[0] for piece in group) for group in by_width(pieces))
    return kernel_call(
        functools.partial(flatten_kernel, offset - EVENT_ROW * L),
        [array_of((rows - EVENT_ROW, L))],
        pieces,
        [((2, -(-deepest // 8) * 8, L), jnp.float32)],
        flops=2 * 10**9,
    )[0]


def node_kernel(
    start_ref,
    bit_ref,
    rows_a_ref,
    rows_b_ref,
    rows_c_ref,
    rows_d_ref,
    table_ref,
    events_ref,
    near_ref,
    came_ref,
    loss_ref,
    gi_ref,
    gh_ref,
    bias_ref,
    features_ref,
    keep_ref,
    give_ref,
    flat_ref,
    grad_s,
    tile_s,
    upper_s,
    lower_s,
    state_s,
    order_s,
    hot_s,
    gi_s,
    gh_s,
    bias_s,
    static_s,
):
    part_refs = (rows_a_ref, rows_b_ref, rows_c_ref, rows_d_ref)
    regions = near_ref.shape[0]
    part_nodes = rows_a_ref.shape[0]
    shards = start_ref.shape[0]
    shard = len(part_refs) * part_nodes // shards
    flat_ref[:EVENT_ROW] = jnp.zeros((EVENT_ROW, L), jnp.float32)
    flat_ref[EVENT_ROW:] = events_ref[...]
    for ref, raw_ref in ((gi_s, gi_ref), (gh_s, gh_ref), (bias_s, bias_ref)):
        ref[...] = jnp.zeros_like(ref)
        for g in range(3):
            ref[: raw_ref.shape[0], g * L : g * L + D] = raw_ref[:, g * D : (g + 1) * D].astype(ref.dtype)

    size = near_ref.shape[1]
    for number in range(regions):
        part = slice(number * size, (number + 1) * size)
        grad_s[part] = near_ref[number] + came_ref[number]

    def arrange(number, carry):
        source = pl.ds(pl.multiple_of(start_ref[number], shard), shard)
        order_s[pl.ds(pl.multiple_of(number * shard, shard), shard)] = (
            grad_s[source]
        )
        return carry

    lax.fori_loop(0, shards, arrange, 0)

    def some(rows_ref, first, step, sums):
        at = pl.ds(pl.multiple_of(step * NODE_STEP, NODE_STEP), NODE_STEP)
        into = pl.ds(pl.multiple_of(first + step * NODE_STEP, NODE_STEP), NODE_STEP)
        stored = rows_ref[at, MSG_PAD : MSG_PAD + L]
        held = stored.astype(jnp.float32) + rows_ref[at, MSG_PAD + L :].astype(jnp.float32)
        inputs = dot(rows_ref[at, :MSG_PAD], gi_s[...]) + bias_s[0:1]
        hidden = dot(stored, gh_s[...]) + bias_s[1:2]
        reset = jax.nn.sigmoid(inputs[:, :L] + hidden[:, :L])
        update = jax.nn.sigmoid(inputs[:, L : 2 * L] + hidden[:, L : 2 * L])
        fresh = hidden[:, 2 * L :]
        candidate = jnp.tanh(inputs[:, 2 * L :] + reset * fresh)
        d_state = order_s[into]
        d_third = d_state * (1.0 - update) * (1.0 - candidate * candidate)
        d_fresh = d_third * reset
        d_first = d_third * fresh * reset * (1.0 - reset)
        d_second = d_state * (held - candidate) * update * (1.0 - update)
        news = []
        for number, part in enumerate((d_first, d_second, d_third, d_fresh)):
            lanes_at = slice(number * L, (number + 1) * L)
            news.append(jnp.sum(part, axis=0, keepdims=True))
            upper_s[into, lanes_at], lower_s[into, lanes_at] = split_terms(part)
        state_s[into, :L], state_s[into, L:] = split_terms(grad_s[into])
        return sums + jnp.concatenate(news, axis=1)

    total = jnp.zeros((1, 4 * L), jnp.float32)
    wide_gi, wide_gh = 0.0, 0.0
    for part, rows_ref in enumerate(part_refs):
        first = part * part_nodes
        total = lax.fori_loop(
            0, part_nodes // NODE_STEP, functools.partial(some, rows_ref, first), total
        )
        messages = rows_ref[:, :MSG_PAD]
        stored = rows_ref[:, MSG_PAD : MSG_PAD + L]
        for ref in (upper_s, lower_s):
            terms = ref[first : first + part_nodes]
            wide_gi = wide_gi + dot_tn(messages, terms[:, : 3 * L])
            wide_gh = wide_gh + dot_tn(stored, terms)

    def gates(matrix, order):
        return jnp.concatenate([matrix[:, g * L : g * L + D] for g in order], axis=1)

    pieces = [
        gates(wide_gi[:MSG], (0, 1, 2)),
        gates(wide_gh[:D], (0, 1, 3)),
        gates(total, (0, 1, 2)),
        gates(total, (0, 1, 3)),
    ]
    mine = len(part_refs) * part_nodes // regions
    for number in range(regions):
        at = pl.ds(pl.multiple_of((2 * number + bit_ref[0]) * mine, mine), mine)
        pairs = table_ref[F : F + 16, at].astype(jnp.float32)
        static_s[:, number * mine : (number + 1) * mine] = pairs[0:1] * 128.0 + pairs[1:2]
    hot_rows(hot_s, static_s[...].astype(jnp.int32))
    by_feature = dot(hot_s[...], state_s[...])
    terms = split_terms(by_feature[:, :L] + by_feature[:, L:])
    wide = dot_tn(features_ref[...], terms[0]) + dot_tn(features_ref[...], terms[1])
    pieces.append(wide[:, :D])
    flatten_all(flat_ref, tile_s, pieces, 0)
    firsts, count = windows(2 * keep_ref.shape[0], flat_ref.shape[0])
    for place, ref in enumerate((keep_ref, give_ref)):
        for number in range(ref.shape[0]):
            for bit in range(2):
                first = firsts[2 * number + bit]

                @pl.when(bit_ref[0] ^ place == bit)
                def copy(ref=ref, number=number, first=first):
                    ref[number, :count] = flat_ref[first : first + count]

            ref[number, count:] = jnp.broadcast_to(loss_ref[...], (ref.shape[1] - count, L))


def windows(regions, flat_rows):
    size = int(flat_rows * L) // regions
    firsts = [number * size // L for number in range(regions)]
    return firsts, max(-(-(number + 1) * size // L) - first for number, first in enumerate(firsts))


def node_grads(weights, start, rows, table_t, node_features, events, grads, loss, regions):
    flat_rows = EVENT_ROW + events.shape[0]
    nodes = grads[0].shape[0] * grads[0].shape[1]
    return kernel_call(
        node_kernel,
        [array_of((regions // 2, -(-(windows(regions, flat_rows)[1] + 1) // 8) * 8, L))] * 2,
        [start, my_bit("ev", 0)[None], *rows, table_t, events, *grads, loss, *weights, node_features],
        [
            ((flat_rows, L), jnp.float32),
            ((nodes, L), jnp.float32),
            ((3, -(-(MSG + D + 2) // 8) * 8, L), jnp.float32),
            ((nodes, 4 * L), jnp.bfloat16),
            ((nodes, 4 * L), jnp.bfloat16),
            ((nodes, 2 * L), jnp.bfloat16),
            ((nodes, L), jnp.float32),
            ((node_features.shape[0], nodes), jnp.bfloat16),
            ((MSG_PAD, 3 * L), jnp.bfloat16),
            ((L, 3 * L), jnp.bfloat16),
            ((8, 3 * L), jnp.float32),
            ((1, nodes), jnp.float32),
        ],
        flops=8 * 10**9,
    )


def partner(array, name, bit):
    size = lax.axis_size(name)
    return lax.ppermute(array, name, [(i, i ^ (1 << bit)) for i in range(size)])


def my_bit(name, bit):
    return (lax.axis_index(name) >> bit) & 1


def bits_of(name):
    return (lax.axis_size(name) - 1).bit_length()


def exchange(held, done, name, bit):
    other = partner(held, name, bit)
    mine_first = my_bit(name, bit) == 0
    done = sorted(done + [(name == "neg", -bit)])
    place = done.index((name == "neg", -bit))
    parts = [jnp.where(mine_first, held, other), jnp.where(mine_first, other, held)]
    return jnp.stack(parts, axis=place), done


def crossed(array, first, second):
    size = lax.axis_size("ev")
    return lax.ppermute(
        array, "ev", [(i, i ^ (1 << (second if i & 1 else first))) for i in range(size)]
    )


def gather_neg(shard):
    held, done = shard, []
    for bit in range(bits_of("neg")):
        held, done = exchange(held, done, "neg", bit)
    return held, done


def gather_ev(held, done, beside=()):
    high = bits_of("ev") - 1
    for bit in range(1, high - 1):
        held, done = exchange(held, done, "ev", bit)
    odd = my_bit("ev", 0) == 1
    low_set, high_set = my_bit("ev", high - 1) == 1, my_bit("ev", high) == 1
    first_set, second_set = jnp.where(odd, high_set, low_set), jnp.where(odd, low_set, high_set)
    other = crossed(held, high - 1, high)
    held = jnp.stack([jnp.where(first_set, other, held), jnp.where(first_set, held, other)])
    other = crossed(held, high, high - 1)
    zero, one = jnp.where(second_set, other, held), jnp.where(second_set, held, other)
    held = jnp.stack(
        [
            jnp.stack([zero[0], jnp.where(odd, one[0], zero[1])]),
            jnp.stack([jnp.where(odd, zero[1], one[0]), one[1]]),
        ]
    )
    done = sorted(done + [(False, -high), (False, 1 - high)])
    if beside:
        held, *beside = lax.optimization_barrier((held, *beside))
    held, done = exchange(held, done, "ev", 0)
    return held, beside


def reduce_bit(held, bits, bit):
    place = bits.index(bit)
    mine = my_bit("ev", bit)
    keep = lax.dynamic_index_in_dim(held, mine, place, keepdims=False)
    give = lax.dynamic_index_in_dim(held, 1 - mine, place, keepdims=False)
    return keep + partner(give, "ev", bit), [other for other in bits if other != bit]


def scatter_ev(keep, give):
    count = bits_of("ev")
    bits = list(reversed(range(1, count)))
    held = (keep + partner(give, "ev", 0)).reshape((2,) * (count - 1) + keep.shape[1:])
    for bit in range(1, count - 2):
        held, bits = reduce_bit(held, bits, bit)
    middle = held.shape[-2] // 16 * 8
    parts = [(held[..., :middle, :], bits), (held[..., middle:, :], bits)]
    for turn in range(2):
        parts = [
            reduce_bit(part, left, bits[(turn + number) % 2])
            for number, (part, left) in enumerate(parts)
        ]
    return jnp.concatenate([part for part, left in parts], axis=-2)


def scatter_neg(blocks):
    count = bits_of("neg")
    held = blocks.reshape((2,) * count + blocks.shape[1:])
    for bit in range(count):
        mine, place = my_bit("neg", bit), count - 1 - bit
        keep = lax.dynamic_index_in_dim(held, mine, place, keepdims=False)
        give = lax.dynamic_index_in_dim(held, 1 - mine, place, keepdims=False)
        held = keep + partner(give, "neg", bit)
    return held


def lanes(flat):
    amount = flat.shape[-1]
    rows = -(-amount // 128)
    wide = jnp.pad(flat, [(0, 0)] * (flat.ndim - 1) + [(0, rows * 128 - amount)])
    return wide.reshape(flat.shape[:-1] + (rows, 128))


def from_digits(pairs, axis):
    pairs = pairs.astype(jnp.float32)
    high, low = (lax.index_in_dim(pairs, place, axis, keepdims=False) for place in (0, 1))
    return high * 128.0 + low


def on_device(
    master,
    first_moment,
    second_moment,
    memory,
    messages,
    static_ids,
    node_features,
    neighbours,
    neighbour_times,
    last_partner,
    last_deltas,
    last_edges,
    sources,
    targets,
    times,
    negatives,
    neg_counts,
):
    shard = master.shape[0]
    groups = lax.axis_size("neg")
    regions = lax.axis_size("ev")
    devices = regions * groups
    rank = lax.axis_index("neg")
    own_events = sources.shape[0]
    own_nodes = memory.shape[0]
    local_neg = negatives.shape[1]
    total_neg = local_neg * groups
    events_all = own_events * devices

    own_columns = by_lanes(negatives.T).reshape(-1, L)
    own_copy = lanes(master.astype(jnp.bfloat16))
    copy_rows = own_copy.shape[0]
    sent = jnp.concatenate(
        [own_copy, (own_columns >> 7).astype(jnp.bfloat16), (own_columns & 127).astype(jnp.bfloat16)]
    )
    copies, copies_done = exchange(sent, [], "neg", 0)
    copies, late_ids = lax.optimization_barrier((copies, static_ids))
    for bit in range(1, bits_of("neg")):
        copies, copies_done = exchange(copies, copies_done, "neg", bit)
    all_negatives = copies[..., copy_rows:, :].reshape(groups, -1, L)
    copies = copies[..., :copy_rows, :]

    rows, tail = pack(rank, neg_counts, static_ids, messages, memory, own_events // W)
    copies, rows = lax.optimization_barrier((copies, rows))
    high = bits_of("ev") - 1
    odd = my_bit("ev", 0) == 1
    far_neg = list(reversed(range(1, bits_of("neg"))))
    flips = [1 << bit for bit in far_neg] + [jnp.where(odd, 1 << (high - 2), 1 << (high - 1)) * groups]
    flips += [(1 << (bit - 1)) * groups for bit in range(1, high - 1)]
    start = ((lax.axis_index("ev") >> 1) * groups + rank)[None]
    for flip in flips:
        start = jnp.concatenate([start, start ^ flip])
    across = jnp.where(odd, 1 << (high - 1), 1 << (high - 2)) * groups
    start = jnp.concatenate([start, start ^ across, start ^ 1, start ^ across ^ 1]) * own_nodes
    for bit in far_neg:
        rows = jnp.concatenate([rows, partner(rows, "neg", bit)])

    ids, gaps, slots, valid, live = prepare(
        rank, sources, targets, times, neg_counts, all_negatives, neighbours, neighbour_times
    )
    copies, (valid, rows) = gather_ev(copies, copies_done, (valid, rows))
    rows = jnp.concatenate([rows, crossed(rows, high, high - 1)])
    for bit in range(1, high - 1):
        rows = jnp.concatenate([rows, partner(rows, "ev", bit)])

    flat = copies.reshape(devices, -1)[:, :shard].reshape(-1)
    early = unpack(flat)
    state, renewed = owner_pass(early, memory, messages, node_features[late_ids])
    sending = jnp.concatenate(
        [jnp.pad(state.astype(jnp.bfloat16), ((0, 0), (0, F - D))), tail[:, : L - F]], 1
    )
    flat, sending = lax.optimization_barrier((flat, sending))
    weights = event_weights(flat, NODE_PARAMS)
    table, table_done = gather_neg(sending)
    table, weights = lax.optimization_barrier((table, weights))
    table = gather_ev(table, table_done)[0]
    table = table.reshape(-1, L)
    biases = early["b_g"]
    table, rows, start, biases = lax.optimization_barrier((table, rows, start, biases))

    def far_device(device):
        place, near = divmod(device, groups)
        return (place ^ (1 << (high if place & 1 else high - 1))) * groups + (near ^ 1)

    far_rows = [
        crossed(rows, high - 1, high),
        partner(rows, "neg", 0),
        lax.ppermute(rows, ("ev", "neg"), [(i, far_device(i)) for i in range(devices)]),
    ]
    table_t = table.T
    local_loss, neg_total, keep, give, grad_event = event_step(
        weights,
        table_t,
        (ids, gaps, slots, valid, live),
        regions,
        own_nodes,
        events_all,
        own_events // W,
    )
    give, far_rows, local_loss, grad_event = lax.optimization_barrier(
        (give, far_rows, local_loss, grad_event)
    )
    came = partner(give, "ev", 0)
    flat_rows = shard * devices // L
    event_flat = flat_events(grad_event, NODE_PARAMS, flat_rows)
    kept_blocks, given_blocks = node_grads(
        (early["w_gi"], early["w_gh"], biases),
        start,
        [rows, *far_rows],
        table_t,
        node_features,
        event_flat,
        (keep, came),
        local_loss,
        regions,
    )
    block_rows = windows(regions, flat_rows)[1]
    summed = scatter_ev(kept_blocks, given_blocks)
    summed, last_partner, last_deltas = lax.optimization_barrier((summed, last_partner, last_deltas))
    if shard * groups % L:
        first = lax.axis_index("ev") * (shard * groups) % L
        values = lax.dynamic_slice_in_dim(summed[:block_rows].reshape(-1), first, shard * groups)
        values = lanes(values)
    else:
        values = summed[:block_rows]
    firsts, part_rows = windows(groups, shard * groups / L)
    values = jnp.pad(values, ((0, max(0, firsts[-1] + part_rows - values.shape[0])), (0, 0)))
    shares = jnp.stack(
        [
            jnp.concatenate([values[first : first + part_rows], summed[block_rows:][:1]])
            for first in firsts
        ]
    )
    totals = scatter_neg(shares)
    loss = jnp.sum(totals[part_rows])
    first = rank * shard % L
    grad_shard = lax.dynamic_slice_in_dim(totals[:part_rows].reshape(-1), first, shard)
    new_master, new_first, new_second = adamw(master, first_moment, second_moment, grad_shard)
    codes = jnp.cos(
        last_deltas[:, None] * early["w_time"].astype(jnp.float32)
        + early["b_time"].astype(jnp.float32)
    )
    carried = jnp.concatenate(
        [
            sending[:, :D].astype(jnp.float32),
            table[last_partner][:, :D].astype(jnp.float32),
            codes,
            last_edges.astype(jnp.float32),
        ],
        1,
    )
    return (loss, neg_total, new_master, new_first, new_second, renewed, carried)


def solution(mesh):
    return jax.shard_map(
        on_device,
        mesh=mesh,
        in_specs=(
            P(("ev", "neg")),
            P(("ev", "neg")),
            P(("ev", "neg")),
            P(("ev", "neg"), None),
            P(("ev", "neg"), None),
            P(("ev", "neg")),
            P(),
            P(),
            P(),
            P(("ev", "neg")),
            P(("ev", "neg")),
            P(("ev", "neg"), None),
            P(("ev", "neg")),
            P(("ev", "neg")),
            P("ev"),
            P("ev", "neg"),
            P("ev"),
        ),
        out_specs=(
            P(),
            P(),
            P(("ev", "neg")),
            P(("ev", "neg")),
            P(("ev", "neg")),
            P(("ev", "neg"), None),
            P(("ev", "neg"), None),
        ),
        check_vma=False,
    )
```

```python
import functools
import math

import jax
import jax.numpy as jnp
from jax import lax
from jax.experimental import pallas as pl
from jax.experimental.pallas import tpu as pltpu
from jax.sharding import PartitionSpec as P

D = 100
TE = 100
NF = 413
PH = 100
HEADS = 2
NBR = 10
STEP = 10
HS = 50
MSG = 486
NODE_PARAMS = 3 * D * (MSG + D + 2) + NF * D


beta_one = 0.9
beta_two = 0.999
rate_lr = 0.02
decay_wd = 0.01
eps_adam = 1e-08

HP = 56
F = HEADS * HP
W = 128
LO = 256
L = 128
MSG_PAD = 512
CHUNK = 10
HOT = 2048
EVENT_ROW = 1696
NODE_STEP = 256
VMEM_BYTES = 60 * 1024 * 1024


def unpack(flat):
    layout = [
        ("w_gi", (MSG, 3 * D)),
        ("w_gh", (D, 3 * D)),
        ("b_g", (2, 3 * D)),
        ("w_feat", (NF, D)),
        ("w_time", (TE,)),
        ("b_time", (TE,)),
        ("w_query", (D + TE, D)),
        ("w_kv", (D + TE, 2 * D)),
        ("w_out", (D, D)),
        ("w_ps", (D, PH)),
        ("w_pd", (D, PH)),
        ("b_p1", (PH,)),
        ("w_p2", (PH,)),
        ("b_p2", (1,)),
    ]
    params = {}
    offset = 0
    for label, shape in layout:
        amount = math.prod(shape)
        params[label] = flat[offset : offset + amount].reshape(shape)
        offset += amount
    return params


def dot(left, right):
    return jnp.dot(left, right, preferred_element_type=jnp.float32)


def dot_nt(left, right):
    return lax.dot_general(
        left, right, (((1,), (1,)), ((), ())), preferred_element_type=jnp.float32
    )


def dot_tn(left, right):
    return lax.dot_general(
        left, right, (((0,), (0,)), ((), ())), preferred_element_type=jnp.float32
    )


def split_terms(value):
    first = value.astype(jnp.bfloat16)
    return first, (value - first.astype(jnp.float32)).astype(jnp.bfloat16)


def settled_terms(value):
    first = lax.optimization_barrier(value.astype(jnp.bfloat16))
    return first, (value - first.astype(jnp.float32)).astype(jnp.bfloat16)


def three_terms(value):
    first = value.astype(jnp.bfloat16)
    rest = value - first.astype(jnp.float32)
    second = rest.astype(jnp.bfloat16)
    return first, second, (rest - second.astype(jnp.float32)).astype(jnp.bfloat16)


def owner_pass(params, memory, messages, features):
    inputs = dot(messages, params["w_gi"]) + params["b_g"][0].astype(jnp.float32)
    hidden = dot(memory.astype(jnp.bfloat16), params["w_gh"]) + params["b_g"][1].astype(jnp.float32)
    reset = jax.nn.sigmoid(inputs[:, :D] + hidden[:, :D])
    update = jax.nn.sigmoid(inputs[:, D : 2 * D] + hidden[:, D : 2 * D])
    candidate = jnp.tanh(inputs[:, 2 * D :] + reset * hidden[:, 2 * D :])
    renewed = (1.0 - update) * candidate + update * memory
    return (renewed + dot(features, params["w_feat"]), renewed)


def adamw(master, first_state, second_state, grads):
    first_new = beta_one * first_state + (1.0 - beta_one) * grads
    second_new = beta_two * second_state + (1.0 - beta_two) * grads * grads
    corrected = (
        first_new
        / (1.0 - beta_one**STEP)
        / (jnp.sqrt(second_new / (1.0 - beta_two**STEP)) + eps_adam)
    )
    return (master - rate_lr * (corrected + decay_wd * master), first_new, second_new)


def sine_cosine(angle):
    turns = jnp.round(angle * (2.0 / math.pi))
    rest = angle - turns * 1.5703125
    rest = rest - turns * 4.837512969970703e-4
    rest = rest - turns * 7.549789948768648e-8
    square = rest * rest
    sine = rest + rest * square * (
        -1.6666654611e-1 + square * (8.3321608736e-3 - square * 1.9515295891e-4)
    )
    cosine = (
        1.0
        - 0.5 * square
        + square
        * square
        * (4.166664568298827e-2 + square * (-1.388731625493765e-3 + square * 2.443315711809948e-5))
    )
    quadrant = turns.astype(jnp.int32)
    odd = (quadrant & 1) == 1
    cos_value = jnp.where(odd, sine, cosine)
    sin_value = jnp.where(odd, cosine, sine)
    cos_value = jnp.where(((quadrant + 1) & 2) == 2, -cos_value, cos_value)
    sin_value = jnp.where((quadrant & 2) == 2, -sin_value, sin_value)
    return cos_value, sin_value


def any_angle(angle):
    return jnp.cos(angle), jnp.sin(angle)


def pair(value):
    return jnp.concatenate([value, value], axis=1)


def fold(value):
    return value[:, :W] + value[:, W:]


def tile(k):
    return slice(k * W, (k + 1) * W)


def hot_rows(hot_ref, ids, base=0):
    count = ids.shape[1]
    rows = lax.broadcasted_iota(jnp.int32, (LO, count), 0).astype(jnp.float32).astype(jnp.bfloat16)
    place = (ids & (LO - 1)).astype(jnp.float32)
    group = ids // LO - base // LO
    one, nought = jnp.ones_like(rows), jnp.zeros_like(rows)
    for number in range(hot_ref.shape[0] // LO):
        here = jnp.where(group == number, place, -1.0)
        here = jnp.broadcast_to(here, (LO, count)).astype(jnp.bfloat16)
        hot_ref[number * LO : (number + 1) * LO] = jnp.where(rows == here, one, nought)


def gather_columns(table_ref, hot_ref, ids):
    step = hot_ref.shape[0]
    found = None
    for base in range(0, table_ref.shape[1], step):
        hot_rows(hot_ref, ids, base)
        part = dot(table_ref[:, base : base + step], hot_ref[...])
        found = part if found is None else found + part
    return found


SRC, TGT, TIME, COUNT, NEG = 0, 1, 2, 3, 4
ID, AT, EVENT = 0, 1, 2
NEAR_ROWS = 16


def column_of(row, lanes_of):
    wide = jnp.transpose(jnp.broadcast_to(row, (L, row.shape[1])))
    return jnp.concatenate([wide] * (lanes_of // L), axis=1)


def pack_kernel(halves, rank_ref, numbers_ref, static_ref, messages_ref, memory_ref, rows_ref, tail_ref):
    rows_ref[...] = jnp.zeros_like(rows_ref)
    rows_ref[:, :MSG] = messages_ref[...]
    terms = split_terms(memory_ref[...])
    rows_ref[:, MSG_PAD : MSG_PAD + D] = terms[0]
    rows_ref[:, MSG_PAD + L : MSG_PAD + L + D] = terms[1]
    counts = numbers_ref[pl.ds(rank_ref[0] * halves, halves)].astype(jnp.float32)
    total = jnp.sum(jnp.sum(counts, axis=1, keepdims=True), axis=0, keepdims=True)
    static = column_of(static_ref[...].astype(jnp.float32), L).astype(jnp.int32)
    lane = lax.broadcasted_iota(jnp.int32, static.shape, 1)
    value = jnp.where(lane < 2, static, total.astype(jnp.int32))
    value = jnp.where((lane & 1) == 0, value >> 7, value & 127)
    tail_ref[...] = value.astype(jnp.float32).astype(jnp.bfloat16)


def pack(rank, counts, static_ids, messages, memory, halves):
    nodes = static_ids.shape[0]
    return kernel_call(
        functools.partial(pack_kernel, halves),
        [array_of((nodes, MSG_PAD + 2 * L), jnp.bfloat16), array_of((nodes, L), jnp.bfloat16)],
        [rank[None], by_lanes(counts), static_ids[None], messages, memory],
        [],
        flops=10**8,
    )


def prepare_kernel(
    rank_ref,
    source_ref,
    target_ref,
    times_ref,
    numbers_ref,
    digits_ref,
    near_ref,
    then_ref,
    ids_ref,
    gaps_ref,
    slots_ref,
    valid_ref,
    live_ref,
    event_s,
    pair_s,
    negatives_s,
    around_s,
    hot_s,
):
    groups, digit_rows, _ = digits_ref.shape
    rows = times_ref.shape[0]
    local = digit_rows // (2 * rows)
    columns = groups * local
    found = digits_ref[...].astype(jnp.float32)
    negatives_s[...] = found[:, : digit_rows // 2] * 128.0 + found[:, digit_rows // 2 :]
    halves = source_ref.shape[0]
    events = halves * W
    mine = pl.ds(rank_ref[0] * halves, halves)
    event_s[...] = jnp.zeros_like(event_s)
    for row, held in enumerate(
        [source_ref[...], target_ref[...], times_ref[mine], numbers_ref[mine]]
        + [
            negatives_s[group, pl.ds(j * rows + rank_ref[0] * halves, halves)]
            for group in range(groups)
            for j in range(local)
        ]
    ):
        held = held.astype(jnp.float32)
        for half in range(halves):
            event_s[row : row + 1, half * W : (half + 1) * W] = held[half : half + 1]
    counts = event_s[COUNT : COUNT + 1]
    shape = (events, events)
    earlier = lax.broadcasted_iota(jnp.int32, shape, 0) < lax.broadcasted_iota(jnp.int32, shape, 1)
    earlier = jnp.where(earlier, 1.0, 0.0).astype(jnp.bfloat16)
    event = lax.broadcasted_iota(jnp.int32, (1, events), 1).astype(jnp.float32)
    wanted = lax.broadcasted_iota(jnp.int32, (columns * events, events), 0).astype(jnp.float32)
    taken = jnp.zeros((1, 1), jnp.float32)
    packed = jnp.zeros((16, columns * events), jnp.float32)
    for number in range(columns):
        active = counts >= float(columns - number)
        ones = jnp.broadcast_to(jnp.where(active, 1.0, 0.0), (16, events))
        place = taken + dot(ones.astype(jnp.bfloat16), earlier)[0:1]
        taken = taken + jnp.sum(ones[0:1], axis=1, keepdims=True)
        place = jnp.where(active, place, -1.0)
        order = jnp.where(wanted == place, 1.0, 0.0).astype(jnp.bfloat16)
        row = NEG + number
        pair_s[...] = jnp.zeros_like(pair_s)
        pair_s[ID : ID + 1] = event_s[row : row + 1]
        pair_s[AT : AT + 1] = event_s[TIME : TIME + 1]
        pair_s[EVENT : EVENT + 1] = event
        thirds = dot_nt(jnp.concatenate(three_terms(pair_s[...]), axis=0), order)
        packed = packed + (thirds[:16] + thirds[16:32]) + thirds[32:]
    slot = lax.broadcasted_iota(jnp.int32, (1, columns * events), 1).astype(jnp.float32)
    valid = jnp.where(slot < taken, 1.0, 0.0)
    live_ref[0] = halves + (jnp.sum(counts).astype(jnp.int32) + W - 1) // W
    around_s[...] = jnp.zeros_like(around_s)
    near = near_ref[...]
    parts = [(near >> 7).astype(jnp.float32), (near & 127).astype(jnp.float32)]
    parts = [part.astype(jnp.bfloat16) for part in parts] + list(three_terms(then_ref[...]))
    for number, part in enumerate(parts):
        around_s[number * NEAR_ROWS : number * NEAR_ROWS + NBR] = part
    sets = [
        (event_s[SRC : SRC + 1], event_s[TIME : TIME + 1], event, jnp.ones((1, events))),
        (event_s[TGT : TGT + 1], event_s[TIME : TIME + 1], event, jnp.ones((1, events))),
    ]
    for number in range(columns):
        part = slice(number * events, (number + 1) * events)
        sets.append((packed[ID : ID + 1, part], packed[AT : AT + 1, part], packed[EVENT : EVENT + 1, part], valid[:, part]))
    for number, (nodes, times, of_event, counted) in enumerate(sets):
        nodes = nodes.astype(jnp.int32)
        found = gather_columns(around_s, hot_s, nodes)
        near = found[:NBR] * 128.0 + found[NEAR_ROWS : NEAR_ROWS + NBR]
        near = near.astype(jnp.int32)
        then = (
            found[2 * NEAR_ROWS : 2 * NEAR_ROWS + NBR] + found[3 * NEAR_ROWS : 3 * NEAR_ROWS + NBR]
        ) + found[4 * NEAR_ROWS : 4 * NEAR_ROWS + NBR]
        gaps = times - then
        for half in range(halves):
            block, lanes_at = number * halves + half, slice(half * W, (half + 1) * W)
            for k in range(NBR):
                ids_ref[block, :, tile(k)] = near[k : k + 1, lanes_at]
                gaps_ref[block, :, tile(k)] = gaps[k : k + 1, lanes_at]
            ids_ref[block, :, NBR * W :] = nodes[:, lanes_at]
            slots_ref[block] = of_event[:, lanes_at].astype(jnp.int32)
            valid_ref[block] = counted[:, lanes_at]


def step_kernel(
    halves,
    own_nodes,
    events_all,
    live_ref,
    bit_ref,
    table_ref,
    ids_ref,
    gaps_ref,
    slots_ref,
    valid_ref,
    wide_ref,
    kvt_ref,
    kv_ref,
    qt_ref,
    q_ref,
    square_ref,
    loss_ref,
    count_ref,
    keep_ref,
    give_ref,
    gkv_ref,
    gq_ref,
    gout_ref,
    gsource_ref,
    gother_ref,
    gtime_ref,
    gbase_ref,
    gp1_ref,
    gp2_ref,
    gend_ref,
    x_s,
    kv_s,
    sin_s,
    own_s,
    query_s,
    att_s,
    mix_s,
    z_s,
    dz_s,
    dsources_s,
    hot_s,
    right_s,
    upper_s,
    lower_s,
    rows_s,
    gkv_s,
    gq_s,
    gsquare_s,
    gwide_s,
):
    scale = 1.0 / math.sqrt(HS)
    near = NBR * W
    found = table_ref[F : F + 16].astype(jnp.float32)
    counted = jnp.sum(found, axis=1, keepdims=True)
    neg_total = (counted[2:3] * 128.0 + counted[3:4]) * (1.0 / own_nodes)
    count_ref[...] = jnp.broadcast_to(neg_total, (1, W))
    share = jnp.broadcast_to(1.0 / neg_total, (1, W))
    b_time = wide_ref[1]
    b_p1, w_p2 = wide_ref[2], wide_ref[3]
    b_p2 = wide_ref[4][0:1]
    zero_cos, zero_sin = wide_ref[5], wide_ref[6]
    furthest = jnp.max(jnp.abs(gaps_ref[...])) * jnp.max(jnp.abs(wide_ref[0])) + jnp.max(
        jnp.abs(b_time)
    )
    moderate = furthest <= 8192.0
    zero_code = zero_cos.astype(jnp.bfloat16)
    for ref in (rows_s, right_s, gkv_s, gq_s, gsquare_s, gwide_s, dsources_s, loss_ref):
        ref[...] = jnp.zeros_like(ref)
    head_rows = (slice(0, HP), slice(HP, F))
    live = live_ref[0]

    def forward(trig, slot, block):
        for s in range(0, F, 16):
            rows = slice(s, s + 16)
            w_rows, b_rows = wide_ref[0, rows], wide_ref[1, rows]
            for k in range(NBR):
                angle = gaps_ref[block, :, tile(k)] * w_rows + b_rows
                cos_value, sin_value = trig(angle)
                sin_s[slot, rows, tile(k)] = sin_value
                x_s[slot, F + s : F + s + 16, tile(k)] = cos_value.astype(jnp.bfloat16)
        found = gather_columns(table_ref, hot_s, ids_ref[block])[:F].astype(jnp.bfloat16)
        x_s[slot, :F] = found[:, :near]
        own = found[:, near:]
        own_s[slot] = own
        query = dot(qt_ref[...], jnp.concatenate([own, zero_code], axis=0))
        query_s[slot] = query
        kv_s[slot] = dot(kvt_ref[...], x_s[slot])
        mixed = []
        for h, rows in enumerate(head_rows):
            scores = jnp.concatenate(
                [
                    jnp.sum(kv_s[slot, rows, tile(k)] * query[rows], axis=0, keepdims=True)
                    for k in range(NBR)
                ],
                axis=0,
            )
            scores = scores * scale
            powers = jnp.exp(scores - jnp.max(scores, axis=0, keepdims=True))
            att_s[slot, h] = powers / jnp.sum(powers, axis=0, keepdims=True)
            mixed_h = jnp.zeros((HP, W), jnp.float32)
            for k in range(NBR):
                values = kv_s[slot, F + h * HP : F + (h + 1) * HP, tile(k)]
                mixed_h = mixed_h + att_s[slot, h, k : k + 1] * values
            mixed.append(mixed_h)
        mixed = jnp.concatenate(mixed, axis=0).astype(jnp.bfloat16)
        mix_s[slot] = mixed
        emb = own.astype(jnp.float32) + dot(square_ref[0], mixed)
        z_s[:, pl.ds(pl.multiple_of(slot * W, W), W)] = emb.astype(jnp.bfloat16)

    def predict(base, amount):
        blocks = range(halves + base, halves + base + amount)
        valid = jnp.concatenate([valid_ref[block] for block in blocks], axis=1)
        of_slot = jnp.concatenate([slots_ref[block] for block in blocks], axis=1)
        z = z_s[:, halves * W : (halves + amount) * W].astype(jnp.float32)
        z = jnp.where(valid > 0.0, z, 0.0).astype(jnp.bfloat16)
        events = lax.broadcasted_iota(jnp.int32, (halves * W, amount * W), 0)
        of_event = jnp.where(events == of_slot, 1.0, 0.0).astype(jnp.bfloat16)
        source = dot(z_s[:, : halves * W], of_event).astype(jnp.bfloat16)
        before_all = dot(square_ref[2], source) + dot(square_ref[4], z)
        losses = jnp.zeros((1, W), jnp.float32)
        ends = jnp.zeros((1, W), jnp.float32)
        by_hidden = jnp.zeros((F, W), jnp.float32)
        by_before = jnp.zeros((F, W), jnp.float32)
        for number, block in enumerate(blocks):
            before = before_all[:, tile(number)] + b_p1
            inner = 0.7978845608028654 * (before + 0.044715 * before * before * before)
            bend = jnp.tanh(inner)
            hidden = (0.5 * before * (1.0 + bend)).astype(jnp.bfloat16).astype(jnp.float32)
            slope = 0.5 * (1.0 + bend) + 0.5 * before * (1.0 - bend * bend) * (
                0.7978845608028654 * (1.0 + 3.0 * 0.044715 * before * before)
            )
            score = jnp.sum(hidden * w_p2, axis=0, keepdims=True) + b_p2
            positive = block < 2 * halves
            sign = -1.0 if positive else 1.0
            weight = valid[:, tile(number)] * (1.0 / events_all if positive else share)
            signed = sign * score
            small = jnp.exp(-jnp.abs(signed))
            losses = losses + weight * (jnp.maximum(signed, 0.0) + jnp.log1p(small))
            sigmoid = jnp.where(signed >= 0.0, 1.0, small) / (1.0 + small)
            d_score = (sign * weight) * sigmoid
            by_hidden = by_hidden + hidden * d_score
            ends = ends + d_score
            d_before = w_p2 * d_score * slope
            by_before = by_before + d_before
            upper_s[:F, tile(number)], lower_s[:F, tile(number)] = split_terms(d_before)
        loss_ref[...] += losses
        gwide_s[2] += by_before
        gwide_s[3] += by_hidden
        gwide_s[4, 0:1] += ends
        d_z = 0.0
        for ref in (upper_s, lower_s):
            term = ref[:F, : amount * W]
            gsquare_s[2] += dot_nt(z, term)
            dsources_s[...] += dot_nt(term, of_event)
            d_z = d_z + dot(square_ref[5], term)
        dz_s[:, halves * W : (halves + amount) * W] = d_z

    def backward(slot, block):
        d_emb = dz_s[:, pl.ds(pl.multiple_of(slot * W, W), W)]
        terms = jnp.concatenate(split_terms(d_emb), axis=1)
        gsquare_s[0] += dot_nt(pair(mix_s[slot]), terms)
        d_mixed = fold(dot(square_ref[1], terms))
        d_query = []
        for h, rows in enumerate(head_rows):
            d_mixed_h, query_h = d_mixed[rows], query_s[slot, rows]
            value_rows = slice(F + h * HP, F + (h + 1) * HP)
            d_shares = jnp.concatenate(
                [
                    jnp.sum(kv_s[slot, value_rows, tile(k)] * d_mixed_h, axis=0, keepdims=True)
                    for k in range(NBR)
                ],
                axis=0,
            )
            part = att_s[slot, h]
            total = jnp.sum(part * d_shares, axis=0, keepdims=True)
            d_scores = part * (d_shares - total) * scale
            d_query_h = jnp.zeros((HP, W), jnp.float32)
            for k in range(NBR):
                d_score = d_scores[k : k + 1]
                d_query_h = d_query_h + d_score * kv_s[slot, rows, tile(k)]
                for at, d_part in (
                    (rows, d_score * query_h),
                    (value_rows, att_s[slot, h, k : k + 1] * d_mixed_h),
                ):
                    upper_s[at, tile(k)], lower_s[at, tile(k)] = split_terms(d_part)
            d_query.append(d_query_h)
        x = x_s[slot]
        upper, lower = upper_s[...], lower_s[...]
        gkv_s[...] += dot_nt(x, upper) + dot_nt(x, lower)
        d_x = dot(kv_ref[...], upper) + dot(kv_ref[...], lower)
        for s in range(0, F, 16):
            rows = slice(s, s + 16)
            to_b = jnp.zeros((16, W), jnp.float32)
            to_w = jnp.zeros((16, W), jnp.float32)
            for k in range(NBR):
                first, second = split_terms(d_x[rows, tile(k)])
                right_s[rows, tile(k)] = first
                right_s[L + s : L + s + 16, tile(k)] = second
                turned = sin_s[slot, rows, tile(k)] * d_x[F + s : F + s + 16, tile(k)]
                to_b = to_b + turned
                to_w = to_w + turned * gaps_ref[block, :, tile(k)]
            gwide_s[1, rows] -= to_b
            gwide_s[0, rows] -= to_w
        d_query = jnp.concatenate(d_query, axis=0)
        terms = jnp.concatenate(split_terms(d_query), axis=1)
        code = jnp.concatenate([own_s[slot], zero_code], axis=0)
        gq_s[...] += dot_nt(pair(code), terms)
        d_code = fold(dot(q_ref[...], terms))
        gwide_s[1] -= zero_sin * d_code[F:]
        right_s[:F, near:], right_s[L : L + F, near:] = split_terms(d_emb + d_code[:F])
        for base in range(0, rows_s.shape[0], hot_s.shape[0]):
            hot_rows(hot_s, ids_ref[block], base)
            rows_s[base : base + hot_s.shape[0]] += dot_nt(hot_s[...], right_s[...])

    most = ids_ref.shape[0] - halves
    chunks = -(-most // CHUNK)
    for chunk in range(chunks):
        base = chunk * CHUNK
        count = jnp.clip(live - base, 0, CHUNK)
        first = halves + base if chunk else 0

        def run_forward(trig, base=base, count=count, first=first):
            def one(block, carry):
                forward(trig, block - base, block)
                return carry

            lax.fori_loop(first, halves + base + count, one, 0)

        for usable, trig in ((moderate, sine_cosine), (jnp.logical_not(moderate), any_angle)):
            pl.when(usable)(functools.partial(run_forward, trig))
        predict(base, min(CHUNK, most - base))
        if chunk == chunks - 1:
            for half in range(halves):
                d_source = dsources_s[:, half * W : (half + 1) * W]
                terms = jnp.concatenate(split_terms(d_source), axis=1)
                gsquare_s[1] += dot_nt(pair(z_s[:, tile(half)]), terms)
                dz_s[:, tile(half)] = fold(dot(square_ref[3], terms))

        def back(slot, carry, base=base):
            backward(slot, jnp.where(slot < halves, slot, slot + base))
            return carry

        lax.fori_loop(0 if chunk == chunks - 1 else halves, halves + count, back, 0)
    region = keep_ref.shape[1]
    for number in range(keep_ref.shape[0]):
        for ref, bit in ((keep_ref, bit_ref[0]), (give_ref, 1 - bit_ref[0])):
            at = pl.ds(pl.multiple_of((2 * number + bit) * region, region), region)
            ref[number] = rows_s[at, :L] + rows_s[at, L:]

    def cut_rows(matrix):
        return jnp.concatenate([matrix[:D], matrix[F : F + D]], axis=0)

    def cut_heads(matrix, axis):
        return jnp.concatenate(
            [
                lax.slice_in_dim(matrix, h * HP, h * HP + HS, axis=axis)
                for h in range(matrix.shape[axis] // HP)
            ],
            axis=axis,
        )

    gkv_ref[...] = cut_heads(cut_rows(gkv_s[...]), 1)
    gq_ref[...] = cut_heads(cut_rows(gq_s[...]), 1)
    gout_ref[...] = cut_heads(gsquare_s[0], 0)[:, :D]
    gsource_ref[...] = gsquare_s[1][:D, :PH]
    gother_ref[...] = gsquare_s[2][:D, :PH]
    ones = jnp.ones((8, W), jnp.bfloat16)
    for number, ref in enumerate((gtime_ref, gbase_ref, gp1_ref, gp2_ref, gend_ref)):
        total = sum(dot_nt(ones, term) for term in three_terms(gwide_s[number]))
        ref[...] = total[0:1, : ref.shape[1]]


def kernel_call(kernel, outs, ins, scratch, flops):
    def place(array):
        scalars = len(array.shape) == 1 and array.dtype == jnp.int32
        return pl.BlockSpec(memory_space=pltpu.SMEM if scalars else pltpu.VMEM)

    return pl.pallas_call(
        kernel,
        out_shape=tuple(outs),
        in_specs=[place(array) for array in ins],
        out_specs=tuple(place(array) for array in outs),
        scratch_shapes=[pltpu.VMEM(shape, dtype) for shape, dtype in scratch],
        compiler_params=pltpu.CompilerParams(vmem_limit_bytes=VMEM_BYTES),
        cost_estimate=pl.CostEstimate(flops=flops, bytes_accessed=10**6, transcendentals=0),
    )(*ins)


def array_of(shape, dtype=jnp.float32):
    return jax.ShapeDtypeStruct(shape, dtype)


def by_lanes(flat):
    return flat.reshape(flat.shape[:-1] + (-1, W))


def prepare(rank, sources, targets, times, counts, negatives, neighbours, then):
    groups, digit_rows, _ = negatives.shape
    columns = groups * (digit_rows * W // (2 * times.shape[0]))
    events = sources.shape[0]
    halves = events // W
    blocks = halves * (2 + columns)
    nodes = neighbours.shape[0]
    return kernel_call(
        prepare_kernel,
        [
            array_of((blocks, 1, (NBR + 1) * W), jnp.int32),
            array_of((blocks, 1, NBR * W)),
            array_of((blocks, 1, W), jnp.int32),
            array_of((blocks, 1, W)),
            array_of((1,), jnp.int32),
        ],
        [
            rank[None],
            by_lanes(sources),
            by_lanes(targets),
            by_lanes(times),
            by_lanes(counts),
            negatives,
            neighbours.T,
            then.T,
        ],
        [
            ((-(-(NEG + columns) // 16) * 16, events), jnp.float32),
            ((16, events), jnp.float32),
            ((groups, digit_rows // 2, L), jnp.float32),
            ((5 * NEAR_ROWS, nodes), jnp.bfloat16),
            ((min(nodes, HOT), events), jnp.bfloat16),
        ],
        flops=4 * 10**9,
    )


def unflatten_from(flat_ref, tile_ref, shape, offset):
    count, width = shape
    tiles = -(-width // L)
    cycle = L // math.gcd(width, L)
    stride = width * cycle // L
    for first in range(min(cycle, count)):
        amount = -(-(count - first) // cycle)
        row, shift = divmod(offset + width * first, L)
        pieces = -(-(shift + width) // L)
        held = [
            flat_ref[pl.ds(row + piece, amount, stride=stride) if amount > 1 else slice(row + piece, row + piece + 1)]
            for piece in range(pieces)
        ]
        held = jnp.concatenate(held, axis=1) if pieces > 1 else held[0]
        held = held[:, shift : shift + width]
        rows = pl.ds(first, amount, stride=cycle) if amount > 1 else slice(first, first + 1)
        for number in range(tiles):
            part = held[:, number * L : (number + 1) * L]
            if part.shape[1] < L:
                part = jnp.concatenate([part, jnp.zeros((amount, L - part.shape[1]), jnp.float32)], axis=1)
            tile_ref[number, rows] = part
    tiled = [tile_ref[number, :count] for number in range(tiles)]
    return jnp.concatenate(tiled, axis=1)[:, :width] if tiles > 1 else tiled[0][:, :width]


def weights_kernel(
    offset, flat_in, kvt_ref, kv_ref, qt_ref, q_ref, square_ref, wide_ref, flat_s, tile_s, pad_s
):
    flat_s[...] = flat_in[...].astype(jnp.float32)

    def padded(value, row_parts, column_parts):
        pad_s[...] = jnp.zeros_like(pad_s)
        for r_from, r_to, r_size in row_parts:
            for c_from, c_to, c_size in column_parts:
                pad_s[r_to : r_to + r_size, c_to : c_to + c_size] = value[
                    r_from : r_from + r_size, c_from : c_from + c_size
                ]
        return pad_s[...]

    plain = [(0, 0, D)]
    twice = [(0, 0, D), (D, F, TE)]
    heads = [(h * HS, h * HP, HS) for h in range(HEADS)]
    all_heads = [(h * HS, h * HP, HS) for h in range(2 * HEADS)]

    def vector(width):
        nonlocal offset
        value = unflatten_from(flat_s, tile_s, (1, width), offset)
        offset += width
        return jnp.concatenate([value, jnp.zeros((1, L - width), jnp.float32)], axis=1)

    wide_ref[0] = column_of(vector(TE), W)[:F]
    base = vector(TE)
    wide_ref[1] = column_of(base, W)[:F]
    for number, value in enumerate(any_angle(base)):
        wide_ref[5 + number] = column_of(value, W)[:F]
    for shape, straight, turned, row_parts, column_parts in (
        ((D + TE, D), q_ref, qt_ref, twice, heads),
        ((D + TE, 2 * D), kv_ref, kvt_ref, twice, all_heads),
        ((D, D), square_ref.at[1], square_ref.at[0], heads, plain),
        ((D, PH), square_ref.at[3], square_ref.at[2], plain, plain),
        ((D, PH), square_ref.at[5], square_ref.at[4], plain, plain),
    ):
        full = padded(unflatten_from(flat_s, tile_s, shape, offset), row_parts, column_parts)
        offset += shape[0] * shape[1]
        n, m = straight.shape
        straight[...] = full[:n, :m].astype(jnp.bfloat16)
        turned[...] = jnp.transpose(full)[:m, :n].astype(jnp.bfloat16)
    wide_ref[2] = column_of(vector(PH), W)[:F]
    wide_ref[3] = column_of(vector(PH), W)[:F]
    wide_ref[4] = jnp.broadcast_to(vector(1)[:, :1], (F, W))


def event_weights(flat, offset):
    rows = flat.reshape(-1, L)[EVENT_ROW:]
    low_type = jnp.bfloat16
    return kernel_call(
        functools.partial(weights_kernel, offset - EVENT_ROW * L),
        [
            array_of((2 * F, 2 * F), low_type),
            array_of((2 * F, 2 * F), low_type),
            array_of((F, 2 * F), low_type),
            array_of((2 * F, F), low_type),
            array_of((6, F, F), low_type),
            array_of((7, F, W)),
        ],
        [rows],
        [
            (rows.shape, jnp.float32),
            ((2, -(-(D + TE) // 8) * 8, L), jnp.float32),
            ((2 * L, 2 * L), jnp.float32),
        ],
        flops=4 * 10**9,
    )


def event_step(weights, table_t, prepared, regions, own_nodes, events_all, halves):
    ids, gaps, slots, valid, live = prepared
    kvt, kv, qt, q, square, wide = weights
    nodes = table_t.shape[1]
    near = NBR * W
    full = near + W
    low_type, high_type = jnp.bfloat16, jnp.float32
    half_table = array_of((regions // 2, nodes // regions, L))
    places = halves + min(CHUNK, ids.shape[0] - halves)
    loss, count, keep, give, g_kv, g_q, g_out, g_source, g_other, *g_rows = kernel_call(
        functools.partial(step_kernel, halves, own_nodes, events_all),
        [
            array_of((1, W)),
            array_of((1, W)),
            half_table,
            half_table,
            array_of((D + TE, 2 * D)),
            array_of((D + TE, D)),
            array_of((D, D)),
            array_of((D, PH)),
            array_of((D, PH)),
            *[array_of((1, width)) for width in (TE, TE, PH, PH, 1)],
        ],
        [
            live,
            my_bit("ev", 0)[None],
            table_t,
            ids,
            gaps,
            slots,
            valid,
            wide,
            kvt,
            kv,
            qt,
            q,
            square,
        ],
        [
            ((places, 2 * F, near), low_type),
            ((places, 2 * F, near), high_type),
            ((places, F, near), high_type),
            ((places, F, W), low_type),
            ((places, F, W), high_type),
            ((places, HEADS, NBR, W), high_type),
            ((places, F, W), low_type),
            ((F, places * W), low_type),
            ((F, places * W), high_type),
            ((F, halves * W), high_type),
            ((min(nodes, HOT), full), low_type),
            ((2 * L, full), low_type),
            ((2 * F, near), low_type),
            ((2 * F, near), low_type),
            ((nodes, 2 * L), high_type),
            ((2 * F, 2 * F), high_type),
            ((2 * F, F), high_type),
            ((3, F, F), high_type),
            ((5, F, W), high_type),
        ],
        flops=4 * 10**10,
    )
    grads = [*g_rows[:2], g_q, g_kv, g_out, g_source, g_other, *g_rows[2:]]
    return loss, count[0, 0], keep, give, grads


def flatten_into(flat_ref, tile_ref, matrices, offset):
    count, width = 0, matrices[0].shape[1]
    tiles = -(-width // L)
    for matrix in matrices:
        rows = slice(count, count + matrix.shape[0])
        for number in range(tiles):
            part = matrix[:, number * L : (number + 1) * L]
            if part.shape[1] < L:
                blank = jnp.zeros((part.shape[0], L - part.shape[1]), jnp.float32)
                part = jnp.concatenate([part, blank], axis=1)
            tile_ref[number, rows] = part
        count = rows.stop
    cycle = L // math.gcd(width, L)
    stride = width * cycle // L

    def strided(first, amount, step):
        return pl.ds(first, amount, stride=step) if amount > 1 else slice(first, first + 1)

    carried = None
    for first in range(min(cycle, count)):
        amount = -(-(count - first) // cycle)
        row, shift = divmod(offset + width * first, L)
        pieces = -(-(shift + width) // L)
        parts = [tile_ref[number, strided(first, amount, cycle)] for number in range(tiles)]
        if shift:
            parts.insert(0, jnp.zeros((amount, shift), jnp.float32))
        held = jnp.concatenate(parts, axis=1) if len(parts) > 1 else parts[0]
        for piece in range(pieces):
            news = held[:, piece * L : min((piece + 1) * L, held.shape[1])]
            if news.shape[1] < L:
                blank = jnp.zeros((amount, L - news.shape[1]), jnp.float32)
                news = jnp.concatenate([news, blank], axis=1)
            whole = piece > 0 or shift == 0
            if carried is not None:
                left, at = carried
                news, whole, carried = news + left[:amount], True, None
                if left.shape[0] > amount:
                    at += stride * amount
                    flat_ref[at : at + 1] += left[amount:]
            if piece == pieces - 1 and (shift + width) % L:
                if whole:
                    carried = (news, row + piece)
                else:
                    flat_ref[strided(row + piece, amount, stride)] += news
            elif whole:
                flat_ref[strided(row + piece, amount, stride)] = news
            else:
                flat_ref[strided(row + piece, amount, stride)] += news
    if carried is not None:
        left, at = carried
        flat_ref[strided(at, left.shape[0], stride)] += left


def by_width(pieces):
    groups = []
    for piece in pieces:
        if groups and groups[-1][-1].shape[1] == piece.shape[1]:
            groups[-1].append(piece)
        else:
            groups.append([piece])
    return groups


def flatten_all(flat_ref, tile_ref, pieces, offset):
    for group in by_width(pieces):
        flatten_into(flat_ref, tile_ref, [piece[...] for piece in group], offset)
        offset += sum(math.prod(piece.shape) for piece in group)


def flatten_kernel(offset, *refs):
    *ins, flat_ref, tile_ref = refs
    flat_ref[...] = jnp.zeros_like(flat_ref)
    flatten_all(flat_ref, tile_ref, ins, offset)


def flat_events(pieces, offset, rows):
    deepest = max(sum(piece.shape[0] for piece in group) for group in by_width(pieces))
    return kernel_call(
        functools.partial(flatten_kernel, offset - EVENT_ROW * L),
        [array_of((rows - EVENT_ROW, L))],
        pieces,
        [((2, -(-deepest // 8) * 8, L), jnp.float32)],
        flops=2 * 10**9,
    )[0]


def node_kernel(
    start_ref,
    bit_ref,
    rows_a_ref,
    rows_b_ref,
    rows_c_ref,
    rows_d_ref,
    table_ref,
    events_ref,
    near_ref,
    came_ref,
    loss_ref,
    gi_ref,
    gh_ref,
    bias_ref,
    features_ref,
    keep_ref,
    give_ref,
    flat_ref,
    grad_s,
    tile_s,
    upper_s,
    lower_s,
    state_s,
    order_s,
    hot_s,
    gi_s,
    gh_s,
    bias_s,
    static_s,
):
    part_refs = (rows_a_ref, rows_b_ref, rows_c_ref, rows_d_ref)
    regions = near_ref.shape[0]
    part_nodes = rows_a_ref.shape[0]
    shards = start_ref.shape[0]
    shard = len(part_refs) * part_nodes // shards
    flat_ref[:EVENT_ROW] = jnp.zeros((EVENT_ROW, L), jnp.float32)
    flat_ref[EVENT_ROW:] = events_ref[...]
    for ref, raw_ref in ((gi_s, gi_ref), (gh_s, gh_ref), (bias_s, bias_ref)):
        ref[...] = jnp.zeros_like(ref)
        for g in range(3):
            ref[: raw_ref.shape[0], g * L : g * L + D] = raw_ref[:, g * D : (g + 1) * D].astype(ref.dtype)

    size = near_ref.shape[1]
    for number in range(regions):
        part = slice(number * size, (number + 1) * size)
        grad_s[part] = near_ref[number] + came_ref[number]

    def arrange(number, carry):
        source = pl.ds(pl.multiple_of(start_ref[number], shard), shard)
        order_s[pl.ds(pl.multiple_of(number * shard, shard), shard)] = (
            grad_s[source]
        )
        return carry

    lax.fori_loop(0, shards, arrange, 0)

    def some(rows_ref, first, step, sums):
        at = pl.ds(pl.multiple_of(step * NODE_STEP, NODE_STEP), NODE_STEP)
        into = pl.ds(pl.multiple_of(first + step * NODE_STEP, NODE_STEP), NODE_STEP)
        stored = rows_ref[at, MSG_PAD : MSG_PAD + L]
        held = stored.astype(jnp.float32) + rows_ref[at, MSG_PAD + L :].astype(jnp.float32)
        inputs = dot(rows_ref[at, :MSG_PAD], gi_s[...]) + bias_s[0:1]
        hidden = dot(stored, gh_s[...]) + bias_s[1:2]
        reset = jax.nn.sigmoid(inputs[:, :L] + hidden[:, :L])
        update = jax.nn.sigmoid(inputs[:, L : 2 * L] + hidden[:, L : 2 * L])
        fresh = hidden[:, 2 * L :]
        candidate = jnp.tanh(inputs[:, 2 * L :] + reset * fresh)
        d_state = order_s[into]
        d_third = d_state * (1.0 - update) * (1.0 - candidate * candidate)
        d_fresh = d_third * reset
        d_first = d_third * fresh * reset * (1.0 - reset)
        d_second = d_state * (held - candidate) * update * (1.0 - update)
        news = []
        for number, part in enumerate((d_first, d_second, d_third, d_fresh)):
            lanes_at = slice(number * L, (number + 1) * L)
            news.append(jnp.sum(part, axis=0, keepdims=True))
            upper_s[into, lanes_at], lower_s[into, lanes_at] = split_terms(part)
        state_s[into, :L], state_s[into, L:] = split_terms(grad_s[into])
        return sums + jnp.concatenate(news, axis=1)

    total = jnp.zeros((1, 4 * L), jnp.float32)
    wide_gi, wide_gh = 0.0, 0.0
    for part, rows_ref in enumerate(part_refs):
        first = part * part_nodes
        total = lax.fori_loop(
            0, part_nodes // NODE_STEP, functools.partial(some, rows_ref, first), total
        )
        messages = rows_ref[:, :MSG_PAD]
        stored = rows_ref[:, MSG_PAD : MSG_PAD + L]
        for ref in (upper_s, lower_s):
            terms = ref[first : first + part_nodes]
            wide_gi = wide_gi + dot_tn(messages, terms[:, : 3 * L])
            wide_gh = wide_gh + dot_tn(stored, terms)

    def gates(matrix, order):
        return jnp.concatenate([matrix[:, g * L : g * L + D] for g in order], axis=1)

    pieces = [
        gates(wide_gi[:MSG], (0, 1, 2)),
        gates(wide_gh[:D], (0, 1, 3)),
        gates(total, (0, 1, 2)),
        gates(total, (0, 1, 3)),
    ]
    mine = len(part_refs) * part_nodes // regions
    for number in range(regions):
        at = pl.ds(pl.multiple_of((2 * number + bit_ref[0]) * mine, mine), mine)
        pairs = table_ref[F : F + 16, at].astype(jnp.float32)
        static_s[:, number * mine : (number + 1) * mine] = pairs[0:1] * 128.0 + pairs[1:2]
    hot_rows(hot_s, static_s[...].astype(jnp.int32))
    by_feature = dot(hot_s[...], state_s[...])
    terms = split_terms(by_feature[:, :L] + by_feature[:, L:])
    wide = dot_tn(features_ref[...], terms[0]) + dot_tn(features_ref[...], terms[1])
    pieces.append(wide[:, :D])
    flatten_all(flat_ref, tile_s, pieces, 0)
    firsts, count = windows(2 * keep_ref.shape[0], flat_ref.shape[0])
    for place, ref in enumerate((keep_ref, give_ref)):
        for number in range(ref.shape[0]):
            for bit in range(2):
                first = firsts[2 * number + bit]

                @pl.when(bit_ref[0] ^ place == bit)
                def copy(ref=ref, number=number, first=first):
                    ref[number, :count] = flat_ref[first : first + count]

            ref[number, count:] = jnp.broadcast_to(loss_ref[...], (ref.shape[1] - count, L))


def windows(regions, flat_rows):
    size = int(flat_rows * L) // regions
    firsts = [number * size // L for number in range(regions)]
    return firsts, max(-(-(number + 1) * size // L) - first for number, first in enumerate(firsts))


def node_grads(weights, start, rows, table_t, node_features, events, grads, loss, regions):
    flat_rows = EVENT_ROW + events.shape[0]
    nodes = grads[0].shape[0] * grads[0].shape[1]
    return kernel_call(
        node_kernel,
        [array_of((regions // 2, -(-(windows(regions, flat_rows)[1] + 1) // 8) * 8, L))] * 2,
        [start, my_bit("ev", 0)[None], *rows, table_t, events, *grads, loss, *weights, node_features],
        [
            ((flat_rows, L), jnp.float32),
            ((nodes, L), jnp.float32),
            ((3, -(-(MSG + D + 2) // 8) * 8, L), jnp.float32),
            ((nodes, 4 * L), jnp.bfloat16),
            ((nodes, 4 * L), jnp.bfloat16),
            ((nodes, 2 * L), jnp.bfloat16),
            ((nodes, L), jnp.float32),
            ((node_features.shape[0], nodes), jnp.bfloat16),
            ((MSG_PAD, 3 * L), jnp.bfloat16),
            ((L, 3 * L), jnp.bfloat16),
            ((8, 3 * L), jnp.float32),
            ((1, nodes), jnp.float32),
        ],
        flops=8 * 10**9,
    )


def partner(array, name, bit):
    size = lax.axis_size(name)
    return lax.ppermute(array, name, [(i, i ^ (1 << bit)) for i in range(size)])


def my_bit(name, bit):
    return (lax.axis_index(name) >> bit) & 1


def bits_of(name):
    return (lax.axis_size(name) - 1).bit_length()


def exchange(held, done, name, bit):
    other = partner(held, name, bit)
    mine_first = my_bit(name, bit) == 0
    done = sorted(done + [(name == "neg", -bit)])
    place = done.index((name == "neg", -bit))
    parts = [jnp.where(mine_first, held, other), jnp.where(mine_first, other, held)]
    return jnp.stack(parts, axis=place), done


def crossed(array, first, second):
    size = lax.axis_size("ev")
    return lax.ppermute(
        array, "ev", [(i, i ^ (1 << (second if i & 1 else first))) for i in range(size)]
    )


def gather_neg(shard):
    held, done = shard, []
    for bit in range(bits_of("neg")):
        held, done = exchange(held, done, "neg", bit)
    return held, done


def gather_ev(held, done, beside=()):
    high = bits_of("ev") - 1
    for bit in range(1, high - 1):
        held, done = exchange(held, done, "ev", bit)
    odd = my_bit("ev", 0) == 1
    low_set, high_set = my_bit("ev", high - 1) == 1, my_bit("ev", high) == 1
    first_set, second_set = jnp.where(odd, high_set, low_set), jnp.where(odd, low_set, high_set)
    other = crossed(held, high - 1, high)
    held = jnp.stack([jnp.where(first_set, other, held), jnp.where(first_set, held, other)])
    other = crossed(held, high, high - 1)
    zero, one = jnp.where(second_set, other, held), jnp.where(second_set, held, other)
    held = jnp.stack(
        [
            jnp.stack([zero[0], jnp.where(odd, one[0], zero[1])]),
            jnp.stack([jnp.where(odd, zero[1], one[0]), one[1]]),
        ]
    )
    done = sorted(done + [(False, -high), (False, 1 - high)])
    if beside:
        held, *beside = lax.optimization_barrier((held, *beside))
    held, done = exchange(held, done, "ev", 0)
    return held, beside


def reduce_bit(held, bits, bit):
    place = bits.index(bit)
    mine = my_bit("ev", bit)
    keep = lax.dynamic_index_in_dim(held, mine, place, keepdims=False)
    give = lax.dynamic_index_in_dim(held, 1 - mine, place, keepdims=False)
    return keep + partner(give, "ev", bit), [other for other in bits if other != bit]


def scatter_ev(keep, give):
    count = bits_of("ev")
    bits = list(reversed(range(1, count)))
    held = (keep + partner(give, "ev", 0)).reshape((2,) * (count - 1) + keep.shape[1:])
    for bit in range(1, count - 2):
        held, bits = reduce_bit(held, bits, bit)
    middle = held.shape[-2] // 16 * 8
    parts = [(held[..., :middle, :], bits), (held[..., middle:, :], bits)]
    for turn in range(2):
        parts = [
            reduce_bit(part, left, bits[(turn + number) % 2])
            for number, (part, left) in enumerate(parts)
        ]
    return jnp.concatenate([part for part, left in parts], axis=-2)


def scatter_neg(blocks):
    count = bits_of("neg")
    held = blocks.reshape((2,) * count + blocks.shape[1:])
    for bit in range(count):
        mine, place = my_bit("neg", bit), count - 1 - bit
        keep = lax.dynamic_index_in_dim(held, mine, place, keepdims=False)
        give = lax.dynamic_index_in_dim(held, 1 - mine, place, keepdims=False)
        held = keep + partner(give, "neg", bit)
    return held


def lanes(flat):
    amount = flat.shape[-1]
    rows = -(-amount // 128)
    wide = jnp.pad(flat, [(0, 0)] * (flat.ndim - 1) + [(0, rows * 128 - amount)])
    return wide.reshape(flat.shape[:-1] + (rows, 128))


def from_digits(pairs, axis):
    pairs = pairs.astype(jnp.float32)
    high, low = (lax.index_in_dim(pairs, place, axis, keepdims=False) for place in (0, 1))
    return high * 128.0 + low


def on_device(
    master,
    first_moment,
    second_moment,
    memory,
    messages,
    static_ids,
    node_features,
    neighbours,
    neighbour_times,
    last_partner,
    last_deltas,
    last_edges,
    sources,
    targets,
    times,
    negatives,
    neg_counts,
):
    shard = master.shape[0]
    groups = lax.axis_size("neg")
    regions = lax.axis_size("ev")
    devices = regions * groups
    rank = lax.axis_index("neg")
    own_events = sources.shape[0]
    own_nodes = memory.shape[0]
    local_neg = negatives.shape[1]
    total_neg = local_neg * groups
    events_all = own_events * devices

    own_columns = by_lanes(negatives.T).reshape(-1, L)
    own_copy = lanes(master.astype(jnp.bfloat16))
    copy_rows = own_copy.shape[0]
    sent = jnp.concatenate(
        [own_copy, (own_columns >> 7).astype(jnp.bfloat16), (own_columns & 127).astype(jnp.bfloat16)]
    )
    copies, copies_done = exchange(sent, [], "neg", 0)
    copies, late_ids = lax.optimization_barrier((copies, static_ids))
    for bit in range(1, bits_of("neg")):
        copies, copies_done = exchange(copies, copies_done, "neg", bit)
    all_negatives = copies[..., copy_rows:, :].reshape(groups, -1, L)
    copies = copies[..., :copy_rows, :]

    rows, tail = pack(rank, neg_counts, static_ids, messages, memory, own_events // W)
    copies, rows, features = lax.optimization_barrier((copies, rows, node_features))
    high = bits_of("ev") - 1
    odd = my_bit("ev", 0) == 1
    far_neg = list(reversed(range(1, bits_of("neg"))))
    flips = [1 << bit for bit in far_neg] + [jnp.where(odd, 1 << (high - 2), 1 << (high - 1)) * groups]
    flips += [(1 << (bit - 1)) * groups for bit in range(1, high - 1)]
    start = ((lax.axis_index("ev") >> 1) * groups + rank)[None]
    for flip in flips:
        start = jnp.concatenate([start, start ^ flip])
    across = jnp.where(odd, 1 << (high - 1), 1 << (high - 2)) * groups
    start = jnp.concatenate([start, start ^ across, start ^ 1, start ^ across ^ 1]) * own_nodes
    for bit in far_neg:
        rows = jnp.concatenate([rows, partner(rows, "neg", bit)])

    ids, gaps, slots, valid, live = prepare(
        rank, sources, targets, times, neg_counts, all_negatives, neighbours, neighbour_times
    )
    copies, (valid, rows) = gather_ev(copies, copies_done, (valid, rows))
    rows = jnp.concatenate([rows, crossed(rows, high, high - 1)])
    for bit in range(1, high - 1):
        rows = jnp.concatenate([rows, partner(rows, "ev", bit)])

    flat = copies.reshape(devices, -1)[:, :shard].reshape(-1)
    early = unpack(flat)
    state, renewed = owner_pass(early, memory, messages, features[late_ids])
    sending = jnp.concatenate(
        [jnp.pad(state.astype(jnp.bfloat16), ((0, 0), (0, F - D))), tail[:, : L - F]], 1
    )
    flat, sending = lax.optimization_barrier((flat, sending))
    weights = event_weights(flat, NODE_PARAMS)
    table, table_done = gather_neg(sending)
    table, start, biases = lax.optimization_barrier((table, start, early["b_g"]))
    table, weights = gather_ev(table, table_done, weights)
    table = table.reshape(-1, L)
    table, rows = lax.optimization_barrier((table, rows))

    def far_device(device):
        place, near = divmod(device, groups)
        return (place ^ (1 << (high if place & 1 else high - 1))) * groups + (near ^ 1)

    far_rows = [
        crossed(rows, high - 1, high),
        partner(rows, "neg", 0),
        lax.ppermute(rows, ("ev", "neg"), [(i, far_device(i)) for i in range(devices)]),
    ]
    table_t = table.T
    local_loss, neg_total, keep, give, grad_event = event_step(
        weights,
        table_t,
        (ids, gaps, slots, valid, live),
        regions,
        own_nodes,
        events_all,
        own_events // W,
    )
    give, far_rows, local_loss, grad_event = lax.optimization_barrier(
        (give, far_rows, local_loss, grad_event)
    )
    came = partner(give, "ev", 0)
    flat_rows = shard * devices // L
    event_flat = flat_events(grad_event, NODE_PARAMS, flat_rows)
    kept_blocks, given_blocks = node_grads(
        (early["w_gi"], early["w_gh"], biases),
        start,
        [rows, *far_rows],
        table_t,
        features,
        event_flat,
        (keep, came),
        local_loss,
        regions,
    )
    block_rows = windows(regions, flat_rows)[1]
    summed = scatter_ev(kept_blocks, given_blocks)
    summed, last_partner, last_deltas = lax.optimization_barrier((summed, last_partner, last_deltas))
    if shard * groups % L:
        first = lax.axis_index("ev") * (shard * groups) % L
        values = lax.dynamic_slice_in_dim(summed[:block_rows].reshape(-1), first, shard * groups)
        values = lanes(values)
    else:
        values = summed[:block_rows]
    firsts, part_rows = windows(groups, shard * groups / L)
    values = jnp.pad(values, ((0, max(0, firsts[-1] + part_rows - values.shape[0])), (0, 0)))
    shares = jnp.stack(
        [
            jnp.concatenate([values[first : first + part_rows], summed[block_rows:][:1]])
            for first in firsts
        ]
    )
    totals = scatter_neg(shares)
    loss = jnp.sum(totals[part_rows])
    first = rank * shard % L
    grad_shard = lax.dynamic_slice_in_dim(totals[:part_rows].reshape(-1), first, shard)
    new_master, new_first, new_second = adamw(master, first_moment, second_moment, grad_shard)
    codes = jnp.cos(
        last_deltas[:, None] * early["w_time"].astype(jnp.float32)
        + early["b_time"].astype(jnp.float32)
    )
    carried = jnp.concatenate(
        [
            sending[:, :D].astype(jnp.float32),
            table[last_partner][:, :D].astype(jnp.float32),
            codes,
            last_edges.astype(jnp.float32),
        ],
        1,
    )
    return (loss, neg_total, new_master, new_first, new_second, renewed, carried)


def solution(mesh):
    return jax.shard_map(
        on_device,
        mesh=mesh,
        in_specs=(
            P(("ev", "neg")),
            P(("ev", "neg")),
            P(("ev", "neg")),
            P(("ev", "neg"), None),
            P(("ev", "neg"), None),
            P(("ev", "neg")),
            P(),
            P(),
            P(),
            P(("ev", "neg")),
            P(("ev", "neg")),
            P(("ev", "neg"), None),
            P(("ev", "neg")),
            P(("ev", "neg")),
            P("ev"),
            P("ev", "neg"),
            P("ev"),
        ),
        out_specs=(
            P(),
            P(),
            P(("ev", "neg")),
            P(("ev", "neg")),
            P(("ev", "neg")),
            P(("ev", "neg"), None),
            P(("ev", "neg"), None),
        ),
        check_vma=False,
    )
```

```python
import functools
import math

import jax
import jax.numpy as jnp
from jax import lax
from jax.experimental import pallas as pl
from jax.experimental.pallas import tpu as pltpu
from jax.sharding import PartitionSpec as P

D = 100
TE = 100
NF = 413
PH = 100
HEADS = 2
NBR = 10
STEP = 10
HS = 50
MSG = 486
NODE_PARAMS = 3 * D * (MSG + D + 2) + NF * D


beta_one = 0.9
beta_two = 0.999
rate_lr = 0.02
decay_wd = 0.01
eps_adam = 1e-08

HP = 56
F = HEADS * HP
W = 128
LO = 256
L = 128
MSG_PAD = 512
CHUNK = 10
HOT = 2048
EVENT_ROW = 1696
NODE_STEP = 256
VMEM_BYTES = 60 * 1024 * 1024


def unpack(flat):
    layout = [
        ("w_gi", (MSG, 3 * D)),
        ("w_gh", (D, 3 * D)),
        ("b_g", (2, 3 * D)),
        ("w_feat", (NF, D)),
        ("w_time", (TE,)),
        ("b_time", (TE,)),
        ("w_query", (D + TE, D)),
        ("w_kv", (D + TE, 2 * D)),
        ("w_out", (D, D)),
        ("w_ps", (D, PH)),
        ("w_pd", (D, PH)),
        ("b_p1", (PH,)),
        ("w_p2", (PH,)),
        ("b_p2", (1,)),
    ]
    params = {}
    offset = 0
    for label, shape in layout:
        amount = math.prod(shape)
        params[label] = flat[offset : offset + amount].reshape(shape)
        offset += amount
    return params


def dot(left, right):
    return jnp.dot(left, right, preferred_element_type=jnp.float32)


def dot_nt(left, right):
    return lax.dot_general(
        left, right, (((1,), (1,)), ((), ())), preferred_element_type=jnp.float32
    )


def dot_tn(left, right):
    return lax.dot_general(
        left, right, (((0,), (0,)), ((), ())), preferred_element_type=jnp.float32
    )


def split_terms(value):
    first = value.astype(jnp.bfloat16)
    return first, (value - first.astype(jnp.float32)).astype(jnp.bfloat16)


def settled_terms(value):
    first = lax.optimization_barrier(value.astype(jnp.bfloat16))
    return first, (value - first.astype(jnp.float32)).astype(jnp.bfloat16)


def three_terms(value):
    first = value.astype(jnp.bfloat16)
    rest = value - first.astype(jnp.float32)
    second = rest.astype(jnp.bfloat16)
    return first, second, (rest - second.astype(jnp.float32)).astype(jnp.bfloat16)


def owner_pass(params, memory, messages, features):
    inputs = dot(messages, params["w_gi"]) + params["b_g"][0].astype(jnp.float32)
    hidden = dot(memory.astype(jnp.bfloat16), params["w_gh"]) + params["b_g"][1].astype(jnp.float32)
    reset = jax.nn.sigmoid(inputs[:, :D] + hidden[:, :D])
    update = jax.nn.sigmoid(inputs[:, D : 2 * D] + hidden[:, D : 2 * D])
    candidate = jnp.tanh(inputs[:, 2 * D :] + reset * hidden[:, 2 * D :])
    renewed = (1.0 - update) * candidate + update * memory
    return (renewed + dot(features, params["w_feat"]), renewed)


def adamw(master, first_state, second_state, grads):
    first_new = beta_one * first_state + (1.0 - beta_one) * grads
    second_new = beta_two * second_state + (1.0 - beta_two) * grads * grads
    corrected = (
        first_new
        / (1.0 - beta_one**STEP)
        / (jnp.sqrt(second_new / (1.0 - beta_two**STEP)) + eps_adam)
    )
    return (master - rate_lr * (corrected + decay_wd * master), first_new, second_new)


def sine_cosine(angle):
    turns = jnp.round(angle * (2.0 / math.pi))
    rest = angle - turns * 1.5703125
    rest = rest - turns * 4.837512969970703e-4
    rest = rest - turns * 7.549789948768648e-8
    square = rest * rest
    sine = rest + rest * square * (
        -1.6666654611e-1 + square * (8.3321608736e-3 - square * 1.9515295891e-4)
    )
    cosine = (
        1.0
        - 0.5 * square
        + square
        * square
        * (4.166664568298827e-2 + square * (-1.388731625493765e-3 + square * 2.443315711809948e-5))
    )
    quadrant = turns.astype(jnp.int32)
    odd = (quadrant & 1) == 1
    cos_value = jnp.where(odd, sine, cosine)
    sin_value = jnp.where(odd, cosine, sine)
    cos_value = jnp.where(((quadrant + 1) & 2) == 2, -cos_value, cos_value)
    sin_value = jnp.where((quadrant & 2) == 2, -sin_value, sin_value)
    return cos_value, sin_value


def any_angle(angle):
    return jnp.cos(angle), jnp.sin(angle)


def pair(value):
    return jnp.concatenate([value, value], axis=1)


def fold(value):
    return value[:, :W] + value[:, W:]


def tile(k):
    return slice(k * W, (k + 1) * W)


def hot_rows(hot_ref, ids, base=0):
    count = ids.shape[1]
    rows = lax.broadcasted_iota(jnp.int32, (LO, count), 0).astype(jnp.float32).astype(jnp.bfloat16)
    place = (ids & (LO - 1)).astype(jnp.float32)
    group = ids // LO - base // LO
    one, nought = jnp.ones_like(rows), jnp.zeros_like(rows)
    for number in range(hot_ref.shape[0] // LO):
        here = jnp.where(group == number, place, -1.0)
        here = jnp.broadcast_to(here, (LO, count)).astype(jnp.bfloat16)
        hot_ref[number * LO : (number + 1) * LO] = jnp.where(rows == here, one, nought)


def gather_columns(table_ref, hot_ref, ids):
    step = hot_ref.shape[0]
    found = None
    for base in range(0, table_ref.shape[1], step):
        hot_rows(hot_ref, ids, base)
        part = dot(table_ref[:, base : base + step], hot_ref[...])
        found = part if found is None else found + part
    return found


SRC, TGT, TIME, COUNT, NEG = 0, 1, 2, 3, 4
ID, AT, EVENT = 0, 1, 2
NEAR_ROWS = 16


def column_of(row, lanes_of):
    wide = jnp.transpose(jnp.broadcast_to(row, (L, row.shape[1])))
    return jnp.concatenate([wide] * (lanes_of // L), axis=1)


def pack_kernel(halves, rank_ref, numbers_ref, static_ref, messages_ref, memory_ref, rows_ref, tail_ref):
    rows_ref[...] = jnp.zeros_like(rows_ref)
    rows_ref[:, :MSG] = messages_ref[...]
    terms = split_terms(memory_ref[...])
    rows_ref[:, MSG_PAD : MSG_PAD + D] = terms[0]
    rows_ref[:, MSG_PAD + L : MSG_PAD + L + D] = terms[1]
    counts = numbers_ref[pl.ds(rank_ref[0] * halves, halves)].astype(jnp.float32)
    total = jnp.sum(jnp.sum(counts, axis=1, keepdims=True), axis=0, keepdims=True)
    static = column_of(static_ref[...].astype(jnp.float32), L).astype(jnp.int32)
    lane = lax.broadcasted_iota(jnp.int32, static.shape, 1)
    value = jnp.where(lane < 2, static, total.astype(jnp.int32))
    value = jnp.where((lane & 1) == 0, value >> 7, value & 127)
    tail_ref[...] = value.astype(jnp.float32).astype(jnp.bfloat16)


def pack(rank, counts, static_ids, messages, memory, halves):
    nodes = static_ids.shape[0]
    return kernel_call(
        functools.partial(pack_kernel, halves),
        [array_of((nodes, MSG_PAD + 2 * L), jnp.bfloat16), array_of((nodes, L), jnp.bfloat16)],
        [rank[None], by_lanes(counts), static_ids[None], messages, memory],
        [],
        flops=10**8,
    )


def prepare_kernel(
    rank_ref,
    source_ref,
    target_ref,
    times_ref,
    numbers_ref,
    digits_ref,
    near_ref,
    then_ref,
    ids_ref,
    gaps_ref,
    slots_ref,
    valid_ref,
    live_ref,
    event_s,
    pair_s,
    negatives_s,
    around_s,
    hot_s,
):
    groups, digit_rows, _ = digits_ref.shape
    rows = times_ref.shape[0]
    local = digit_rows // (2 * rows)
    columns = groups * local
    found = digits_ref[...].astype(jnp.float32)
    negatives_s[...] = found[:, : digit_rows // 2] * 128.0 + found[:, digit_rows // 2 :]
    halves = source_ref.shape[0]
    events = halves * W
    mine = pl.ds(rank_ref[0] * halves, halves)
    event_s[...] = jnp.zeros_like(event_s)
    for row, held in enumerate(
        [source_ref[...], target_ref[...], times_ref[mine], numbers_ref[mine]]
        + [
            negatives_s[group, pl.ds(j * rows + rank_ref[0] * halves, halves)]
            for group in range(groups)
            for j in range(local)
        ]
    ):
        held = held.astype(jnp.float32)
        for half in range(halves):
            event_s[row : row + 1, half * W : (half + 1) * W] = held[half : half + 1]
    counts = event_s[COUNT : COUNT + 1]
    shape = (events, events)
    earlier = lax.broadcasted_iota(jnp.int32, shape, 0) < lax.broadcasted_iota(jnp.int32, shape, 1)
    earlier = jnp.where(earlier, 1.0, 0.0).astype(jnp.bfloat16)
    event = lax.broadcasted_iota(jnp.int32, (1, events), 1).astype(jnp.float32)
    wanted = lax.broadcasted_iota(jnp.int32, (columns * events, events), 0).astype(jnp.float32)
    taken = jnp.zeros((1, 1), jnp.float32)
    packed = jnp.zeros((16, columns * events), jnp.float32)
    for number in range(columns):
        active = counts >= float(columns - number)
        ones = jnp.broadcast_to(jnp.where(active, 1.0, 0.0), (16, events))
        place = taken + dot(ones.astype(jnp.bfloat16), earlier)[0:1]
        taken = taken + jnp.sum(ones[0:1], axis=1, keepdims=True)
        place = jnp.where(active, place, -1.0)
        order = jnp.where(wanted == place, 1.0, 0.0).astype(jnp.bfloat16)
        row = NEG + number
        pair_s[...] = jnp.zeros_like(pair_s)
        pair_s[ID : ID + 1] = event_s[row : row + 1]
        pair_s[AT : AT + 1] = event_s[TIME : TIME + 1]
        pair_s[EVENT : EVENT + 1] = event
        thirds = dot_nt(jnp.concatenate(three_terms(pair_s[...]), axis=0), order)
        packed = packed + (thirds[:16] + thirds[16:32]) + thirds[32:]
    slot = lax.broadcasted_iota(jnp.int32, (1, columns * events), 1).astype(jnp.float32)
    valid = jnp.where(slot < taken, 1.0, 0.0)
    live_ref[0] = halves + (jnp.sum(counts).astype(jnp.int32) + W - 1) // W
    around_s[...] = jnp.zeros_like(around_s)
    near = near_ref[...]
    parts = [(near >> 7).astype(jnp.float32), (near & 127).astype(jnp.float32)]
    parts = [part.astype(jnp.bfloat16) for part in parts] + list(three_terms(then_ref[...]))
    for number, part in enumerate(parts):
        around_s[number * NEAR_ROWS : number * NEAR_ROWS + NBR] = part
    sets = [
        (event_s[SRC : SRC + 1], event_s[TIME : TIME + 1], event, jnp.ones((1, events))),
        (event_s[TGT : TGT + 1], event_s[TIME : TIME + 1], event, jnp.ones((1, events))),
    ]
    for number in range(columns):
        part = slice(number * events, (number + 1) * events)
        sets.append((packed[ID : ID + 1, part], packed[AT : AT + 1, part], packed[EVENT : EVENT + 1, part], valid[:, part]))
    for number, (nodes, times, of_event, counted) in enumerate(sets):
        nodes = nodes.astype(jnp.int32)
        found = gather_columns(around_s, hot_s, nodes)
        near = found[:NBR] * 128.0 + found[NEAR_ROWS : NEAR_ROWS + NBR]
        near = near.astype(jnp.int32)
        then = (
            found[2 * NEAR_ROWS : 2 * NEAR_ROWS + NBR] + found[3 * NEAR_ROWS : 3 * NEAR_ROWS + NBR]
        ) + found[4 * NEAR_ROWS : 4 * NEAR_ROWS + NBR]
        gaps = times - then
        for half in range(halves):
            block, lanes_at = number * halves + half, slice(half * W, (half + 1) * W)
            for k in range(NBR):
                ids_ref[block, :, tile(k)] = near[k : k + 1, lanes_at]
                gaps_ref[block, :, tile(k)] = gaps[k : k + 1, lanes_at]
            ids_ref[block, :, NBR * W :] = nodes[:, lanes_at]
            slots_ref[block] = of_event[:, lanes_at].astype(jnp.int32)
            valid_ref[block] = counted[:, lanes_at]


def step_kernel(
    halves,
    own_nodes,
    events_all,
    live_ref,
    bit_ref,
    table_ref,
    ids_ref,
    gaps_ref,
    slots_ref,
    valid_ref,
    wide_ref,
    kvt_ref,
    kv_ref,
    qt_ref,
    q_ref,
    square_ref,
    loss_ref,
    count_ref,
    keep_ref,
    give_ref,
    gkv_ref,
    gq_ref,
    gout_ref,
    gsource_ref,
    gother_ref,
    gtime_ref,
    gbase_ref,
    gp1_ref,
    gp2_ref,
    gend_ref,
    x_s,
    kv_s,
    sin_s,
    own_s,
    query_s,
    att_s,
    mix_s,
    z_s,
    dz_s,
    dsources_s,
    hot_s,
    right_s,
    upper_s,
    lower_s,
    rows_s,
    gkv_s,
    gq_s,
    gsquare_s,
    gwide_s,
):
    scale = 1.0 / math.sqrt(HS)
    near = NBR * W
    found = table_ref[F : F + 16].astype(jnp.float32)
    counted = jnp.sum(found, axis=1, keepdims=True)
    neg_total = (counted[2:3] * 128.0 + counted[3:4]) * (1.0 / own_nodes)
    count_ref[...] = jnp.broadcast_to(neg_total, (1, W))
    share = jnp.broadcast_to(1.0 / neg_total, (1, W))
    b_time = wide_ref[1]
    b_p1, w_p2 = wide_ref[2], wide_ref[3]
    b_p2 = wide_ref[4][0:1]
    zero_cos, zero_sin = wide_ref[5], wide_ref[6]
    furthest = jnp.max(jnp.abs(gaps_ref[...])) * jnp.max(jnp.abs(wide_ref[0])) + jnp.max(
        jnp.abs(b_time)
    )
    moderate = furthest <= 8192.0
    zero_code = zero_cos.astype(jnp.bfloat16)
    for ref in (rows_s, right_s, gkv_s, gq_s, gsquare_s, gwide_s, dsources_s, loss_ref):
        ref[...] = jnp.zeros_like(ref)
    head_rows = (slice(0, HP), slice(HP, F))
    live = live_ref[0]

    def forward(trig, slot, block):
        for s in range(0, F, 16):
            rows = slice(s, s + 16)
            w_rows, b_rows = wide_ref[0, rows], wide_ref[1, rows]
            for k in range(NBR):
                angle = gaps_ref[block, :, tile(k)] * w_rows + b_rows
                cos_value, sin_value = trig(angle)
                sin_s[slot, rows, tile(k)] = sin_value
                x_s[slot, F + s : F + s + 16, tile(k)] = cos_value.astype(jnp.bfloat16)
        found = gather_columns(table_ref, hot_s, ids_ref[block])[:F].astype(jnp.bfloat16)
        x_s[slot, :F] = found[:, :near]
        own = found[:, near:]
        own_s[slot] = own
        query = dot(qt_ref[...], jnp.concatenate([own, zero_code], axis=0))
        query_s[slot] = query
        kv_s[slot] = dot(kvt_ref[...], x_s[slot])
        mixed = []
        for h, rows in enumerate(head_rows):
            scores = jnp.concatenate(
                [
                    jnp.sum(kv_s[slot, rows, tile(k)] * query[rows], axis=0, keepdims=True)
                    for k in range(NBR)
                ],
                axis=0,
            )
            scores = scores * scale
            powers = jnp.exp(scores - jnp.max(scores, axis=0, keepdims=True))
            att_s[slot, h] = powers / jnp.sum(powers, axis=0, keepdims=True)
            mixed_h = jnp.zeros((HP, W), jnp.float32)
            for k in range(NBR):
                values = kv_s[slot, F + h * HP : F + (h + 1) * HP, tile(k)]
                mixed_h = mixed_h + att_s[slot, h, k : k + 1] * values
            mixed.append(mixed_h)
        mixed = jnp.concatenate(mixed, axis=0).astype(jnp.bfloat16)
        mix_s[slot] = mixed
        emb = own.astype(jnp.float32) + dot(square_ref[0], mixed)
        z_s[:, pl.ds(pl.multiple_of(slot * W, W), W)] = emb.astype(jnp.bfloat16)

    def predict(base, amount):
        blocks = range(halves + base, halves + base + amount)
        valid = jnp.concatenate([valid_ref[block] for block in blocks], axis=1)
        of_slot = jnp.concatenate([slots_ref[block] for block in blocks], axis=1)
        z = z_s[:, halves * W : (halves + amount) * W].astype(jnp.float32)
        z = jnp.where(valid > 0.0, z, 0.0).astype(jnp.bfloat16)
        events = lax.broadcasted_iota(jnp.int32, (halves * W, amount * W), 0)
        of_event = jnp.where(events == of_slot, 1.0, 0.0).astype(jnp.bfloat16)
        source = dot(z_s[:, : halves * W], of_event).astype(jnp.bfloat16)
        before_all = dot(square_ref[2], source) + dot(square_ref[4], z)
        losses = jnp.zeros((1, W), jnp.float32)
        ends = jnp.zeros((1, W), jnp.float32)
        by_hidden = jnp.zeros((F, W), jnp.float32)
        by_before = jnp.zeros((F, W), jnp.float32)
        for number, block in enumerate(blocks):
            before = before_all[:, tile(number)] + b_p1
            inner = 0.7978845608028654 * (before + 0.044715 * before * before * before)
            bend = jnp.tanh(inner)
            hidden = (0.5 * before * (1.0 + bend)).astype(jnp.bfloat16).astype(jnp.float32)
            slope = 0.5 * (1.0 + bend) + 0.5 * before * (1.0 - bend * bend) * (
                0.7978845608028654 * (1.0 + 3.0 * 0.044715 * before * before)
            )
            score = jnp.sum(hidden * w_p2, axis=0, keepdims=True) + b_p2
            positive = block < 2 * halves
            sign = -1.0 if positive else 1.0
            weight = valid[:, tile(number)] * (1.0 / events_all if positive else share)
            signed = sign * score
            small = jnp.exp(-jnp.abs(signed))
            losses = losses + weight * (jnp.maximum(signed, 0.0) + jnp.log1p(small))
            sigmoid = jnp.where(signed >= 0.0, 1.0, small) / (1.0 + small)
            d_score = (sign * weight) * sigmoid
            by_hidden = by_hidden + hidden * d_score
            ends = ends + d_score
            d_before = w_p2 * d_score * slope
            by_before = by_before + d_before
            upper_s[:F, tile(number)], lower_s[:F, tile(number)] = split_terms(d_before)
        loss_ref[...] += losses
        gwide_s[2] += by_before
        gwide_s[3] += by_hidden
        gwide_s[4, 0:1] += ends
        d_z = 0.0
        for ref in (upper_s, lower_s):
            term = ref[:F, : amount * W]
            gsquare_s[2] += dot_nt(z, term)
            dsources_s[...] += dot_nt(term, of_event)
            d_z = d_z + dot(square_ref[5], term)
        dz_s[:, halves * W : (halves + amount) * W] = d_z

    def backward(slot, block):
        d_emb = dz_s[:, pl.ds(pl.multiple_of(slot * W, W), W)]
        terms = jnp.concatenate(split_terms(d_emb), axis=1)
        gsquare_s[0] += dot_nt(pair(mix_s[slot]), terms)
        d_mixed = fold(dot(square_ref[1], terms))
        d_query = []
        for h, rows in enumerate(head_rows):
            d_mixed_h, query_h = d_mixed[rows], query_s[slot, rows]
            value_rows = slice(F + h * HP, F + (h + 1) * HP)
            d_shares = jnp.concatenate(
                [
                    jnp.sum(kv_s[slot, value_rows, tile(k)] * d_mixed_h, axis=0, keepdims=True)
                    for k in range(NBR)
                ],
                axis=0,
            )
            part = att_s[slot, h]
            total = jnp.sum(part * d_shares, axis=0, keepdims=True)
            d_scores = part * (d_shares - total) * scale
            d_query_h = jnp.zeros((HP, W), jnp.float32)
            for k in range(NBR):
                d_score = d_scores[k : k + 1]
                d_query_h = d_query_h + d_score * kv_s[slot, rows, tile(k)]
                for at, d_part in (
                    (rows, d_score * query_h),
                    (value_rows, att_s[slot, h, k : k + 1] * d_mixed_h),
                ):
                    upper_s[at, tile(k)], lower_s[at, tile(k)] = split_terms(d_part)
            d_query.append(d_query_h)
        x = x_s[slot]
        upper, lower = upper_s[...], lower_s[...]
        gkv_s[...] += dot_nt(x, upper) + dot_nt(x, lower)
        d_x = dot(kv_ref[...], upper) + dot(kv_ref[...], lower)
        for s in range(0, F, 16):
            rows = slice(s, s + 16)
            to_b = jnp.zeros((16, W), jnp.float32)
            to_w = jnp.zeros((16, W), jnp.float32)
            for k in range(NBR):
                first, second = split_terms(d_x[rows, tile(k)])
                right_s[rows, tile(k)] = first
                right_s[L + s : L + s + 16, tile(k)] = second
                turned = sin_s[slot, rows, tile(k)] * d_x[F + s : F + s + 16, tile(k)]
                to_b = to_b + turned
                to_w = to_w + turned * gaps_ref[block, :, tile(k)]
            gwide_s[1, rows] -= to_b
            gwide_s[0, rows] -= to_w
        d_query = jnp.concatenate(d_query, axis=0)
        terms = jnp.concatenate(split_terms(d_query), axis=1)
        code = jnp.concatenate([own_s[slot], zero_code], axis=0)
        gq_s[...] += dot_nt(pair(code), terms)
        d_code = fold(dot(q_ref[...], terms))
        gwide_s[1] -= zero_sin * d_code[F:]
        right_s[:F, near:], right_s[L : L + F, near:] = split_terms(d_emb + d_code[:F])
        for base in range(0, rows_s.shape[0], hot_s.shape[0]):
            hot_rows(hot_s, ids_ref[block], base)
            rows_s[base : base + hot_s.shape[0]] += dot_nt(hot_s[...], right_s[...])

    most = ids_ref.shape[0] - halves
    chunks = -(-most // CHUNK)
    for chunk in range(chunks):
        base = chunk * CHUNK
        count = jnp.clip(live - base, 0, CHUNK)
        first = halves + base if chunk else 0

        def run_forward(trig, base=base, count=count, first=first):
            def one(block, carry):
                forward(trig, block - base, block)
                return carry

            lax.fori_loop(first, halves + base + count, one, 0)

        for usable, trig in ((moderate, sine_cosine), (jnp.logical_not(moderate), any_angle)):
            pl.when(usable)(functools.partial(run_forward, trig))
        predict(base, min(CHUNK, most - base))
        if chunk == chunks - 1:
            for half in range(halves):
                d_source = dsources_s[:, half * W : (half + 1) * W]
                terms = jnp.concatenate(split_terms(d_source), axis=1)
                gsquare_s[1] += dot_nt(pair(z_s[:, tile(half)]), terms)
                dz_s[:, tile(half)] = fold(dot(square_ref[3], terms))

        def back(slot, carry, base=base):
            backward(slot, jnp.where(slot < halves, slot, slot + base))
            return carry

        lax.fori_loop(0 if chunk == chunks - 1 else halves, halves + count, back, 0)
    region = keep_ref.shape[1]
    for number in range(keep_ref.shape[0]):
        for ref, bit in ((keep_ref, bit_ref[0]), (give_ref, 1 - bit_ref[0])):
            at = pl.ds(pl.multiple_of((2 * number + bit) * region, region), region)
            ref[number] = rows_s[at, :L] + rows_s[at, L:]

    def cut_rows(matrix):
        return jnp.concatenate([matrix[:D], matrix[F : F + D]], axis=0)

    def cut_heads(matrix, axis):
        return jnp.concatenate(
            [
                lax.slice_in_dim(matrix, h * HP, h * HP + HS, axis=axis)
                for h in range(matrix.shape[axis] // HP)
            ],
            axis=axis,
        )

    gkv_ref[...] = cut_heads(cut_rows(gkv_s[...]), 1)
    gq_ref[...] = cut_heads(cut_rows(gq_s[...]), 1)
    gout_ref[...] = cut_heads(gsquare_s[0], 0)[:, :D]
    gsource_ref[...] = gsquare_s[1][:D, :PH]
    gother_ref[...] = gsquare_s[2][:D, :PH]
    ones = jnp.ones((8, W), jnp.bfloat16)
    for number, ref in enumerate((gtime_ref, gbase_ref, gp1_ref, gp2_ref, gend_ref)):
        total = sum(dot_nt(ones, term) for term in three_terms(gwide_s[number]))
        ref[...] = total[0:1, : ref.shape[1]]


def kernel_call(kernel, outs, ins, scratch, flops):
    def place(array):
        scalars = len(array.shape) == 1 and array.dtype == jnp.int32
        return pl.BlockSpec(memory_space=pltpu.SMEM if scalars else pltpu.VMEM)

    return pl.pallas_call(
        kernel,
        out_shape=tuple(outs),
        in_specs=[place(array) for array in ins],
        out_specs=tuple(place(array) for array in outs),
        scratch_shapes=[pltpu.VMEM(shape, dtype) for shape, dtype in scratch],
        compiler_params=pltpu.CompilerParams(vmem_limit_bytes=VMEM_BYTES),
        cost_estimate=pl.CostEstimate(flops=flops, bytes_accessed=10**6, transcendentals=0),
    )(*ins)


def array_of(shape, dtype=jnp.float32):
    return jax.ShapeDtypeStruct(shape, dtype)


def by_lanes(flat):
    return flat.reshape(flat.shape[:-1] + (-1, W))


def prepare(rank, sources, targets, times, counts, negatives, neighbours, then):
    groups, digit_rows, _ = negatives.shape
    columns = groups * (digit_rows * W // (2 * times.shape[0]))
    events = sources.shape[0]
    halves = events // W
    blocks = halves * (2 + columns)
    nodes = neighbours.shape[0]
    return kernel_call(
        prepare_kernel,
        [
            array_of((blocks, 1, (NBR + 1) * W), jnp.int32),
            array_of((blocks, 1, NBR * W)),
            array_of((blocks, 1, W), jnp.int32),
            array_of((blocks, 1, W)),
            array_of((1,), jnp.int32),
        ],
        [
            rank[None],
            by_lanes(sources),
            by_lanes(targets),
            by_lanes(times),
            by_lanes(counts),
            negatives,
            neighbours.T,
            then.T,
        ],
        [
            ((-(-(NEG + columns) // 16) * 16, events), jnp.float32),
            ((16, events), jnp.float32),
            ((groups, digit_rows // 2, L), jnp.float32),
            ((5 * NEAR_ROWS, nodes), jnp.bfloat16),
            ((min(nodes, HOT), events), jnp.bfloat16),
        ],
        flops=4 * 10**9,
    )


def unflatten_from(flat_ref, tile_ref, shape, offset):
    count, width = shape
    tiles = -(-width // L)
    cycle = L // math.gcd(width, L)
    stride = width * cycle // L
    for first in range(min(cycle, count)):
        amount = -(-(count - first) // cycle)
        row, shift = divmod(offset + width * first, L)
        pieces = -(-(shift + width) // L)
        held = [
            flat_ref[pl.ds(row + piece, amount, stride=stride) if amount > 1 else slice(row + piece, row + piece + 1)]
            for piece in range(pieces)
        ]
        held = jnp.concatenate(held, axis=1) if pieces > 1 else held[0]
        held = held[:, shift : shift + width]
        rows = pl.ds(first, amount, stride=cycle) if amount > 1 else slice(first, first + 1)
        for number in range(tiles):
            part = held[:, number * L : (number + 1) * L]
            if part.shape[1] < L:
                part = jnp.concatenate([part, jnp.zeros((amount, L - part.shape[1]), jnp.float32)], axis=1)
            tile_ref[number, rows] = part
    tiled = [tile_ref[number, :count] for number in range(tiles)]
    return jnp.concatenate(tiled, axis=1)[:, :width] if tiles > 1 else tiled[0][:, :width]


def weights_kernel(
    offset, flat_in, kvt_ref, kv_ref, qt_ref, q_ref, square_ref, wide_ref, flat_s, tile_s, pad_s
):
    flat_s[...] = flat_in[...].astype(jnp.float32)

    def padded(value, row_parts, column_parts):
        pad_s[...] = jnp.zeros_like(pad_s)
        for r_from, r_to, r_size in row_parts:
            for c_from, c_to, c_size in column_parts:
                pad_s[r_to : r_to + r_size, c_to : c_to + c_size] = value[
                    r_from : r_from + r_size, c_from : c_from + c_size
                ]
        return pad_s[...]

    plain = [(0, 0, D)]
    twice = [(0, 0, D), (D, F, TE)]
    heads = [(h * HS, h * HP, HS) for h in range(HEADS)]
    all_heads = [(h * HS, h * HP, HS) for h in range(2 * HEADS)]

    def vector(width):
        nonlocal offset
        value = unflatten_from(flat_s, tile_s, (1, width), offset)
        offset += width
        return jnp.concatenate([value, jnp.zeros((1, L - width), jnp.float32)], axis=1)

    wide_ref[0] = column_of(vector(TE), W)[:F]
    base = vector(TE)
    wide_ref[1] = column_of(base, W)[:F]
    for number, value in enumerate(any_angle(base)):
        wide_ref[5 + number] = column_of(value, W)[:F]
    for shape, straight, turned, row_parts, column_parts in (
        ((D + TE, D), q_ref, qt_ref, twice, heads),
        ((D + TE, 2 * D), kv_ref, kvt_ref, twice, all_heads),
        ((D, D), square_ref.at[1], square_ref.at[0], heads, plain),
        ((D, PH), square_ref.at[3], square_ref.at[2], plain, plain),
        ((D, PH), square_ref.at[5], square_ref.at[4], plain, plain),
    ):
        full = padded(unflatten_from(flat_s, tile_s, shape, offset), row_parts, column_parts)
        offset += shape[0] * shape[1]
        n, m = straight.shape
        straight[...] = full[:n, :m].astype(jnp.bfloat16)
        turned[...] = jnp.transpose(full)[:m, :n].astype(jnp.bfloat16)
    wide_ref[2] = column_of(vector(PH), W)[:F]
    wide_ref[3] = column_of(vector(PH), W)[:F]
    wide_ref[4] = jnp.broadcast_to(vector(1)[:, :1], (F, W))


def event_weights(flat, offset):
    rows = flat.reshape(-1, L)[EVENT_ROW:]
    low_type = jnp.bfloat16
    return kernel_call(
        functools.partial(weights_kernel, offset - EVENT_ROW * L),
        [
            array_of((2 * F, 2 * F), low_type),
            array_of((2 * F, 2 * F), low_type),
            array_of((F, 2 * F), low_type),
            array_of((2 * F, F), low_type),
            array_of((6, F, F), low_type),
            array_of((7, F, W)),
        ],
        [rows],
        [
            (rows.shape, jnp.float32),
            ((2, -(-(D + TE) // 8) * 8, L), jnp.float32),
            ((2 * L, 2 * L), jnp.float32),
        ],
        flops=4 * 10**9,
    )


def event_step(weights, table_t, prepared, regions, own_nodes, events_all, halves):
    ids, gaps, slots, valid, live = prepared
    kvt, kv, qt, q, square, wide = weights
    nodes = table_t.shape[1]
    near = NBR * W
    full = near + W
    low_type, high_type = jnp.bfloat16, jnp.float32
    half_table = array_of((regions // 2, nodes // regions, L))
    places = halves + min(CHUNK, ids.shape[0] - halves)
    loss, count, keep, give, g_kv, g_q, g_out, g_source, g_other, *g_rows = kernel_call(
        functools.partial(step_kernel, halves, own_nodes, events_all),
        [
            array_of((1, W)),
            array_of((1, W)),
            half_table,
            half_table,
            array_of((D + TE, 2 * D)),
            array_of((D + TE, D)),
            array_of((D, D)),
            array_of((D, PH)),
            array_of((D, PH)),
            *[array_of((1, width)) for width in (TE, TE, PH, PH, 1)],
        ],
        [
            live,
            my_bit("ev", 0)[None],
            table_t,
            ids,
            gaps,
            slots,
            valid,
            wide,
            kvt,
            kv,
            qt,
            q,
            square,
        ],
        [
            ((places, 2 * F, near), low_type),
            ((places, 2 * F, near), high_type),
            ((places, F, near), high_type),
            ((places, F, W), low_type),
            ((places, F, W), high_type),
            ((places, HEADS, NBR, W), high_type),
            ((places, F, W), low_type),
            ((F, places * W), low_type),
            ((F, places * W), high_type),
            ((F, halves * W), high_type),
            ((min(nodes, HOT), full), low_type),
            ((2 * L, full), low_type),
            ((2 * F, near), low_type),
            ((2 * F, near), low_type),
            ((nodes, 2 * L), high_type),
            ((2 * F, 2 * F), high_type),
            ((2 * F, F), high_type),
            ((3, F, F), high_type),
            ((5, F, W), high_type),
        ],
        flops=4 * 10**10,
    )
    grads = [*g_rows[:2], g_q, g_kv, g_out, g_source, g_other, *g_rows[2:]]
    return loss, count[0, 0], keep, give, grads


def flatten_into(flat_ref, tile_ref, matrices, offset):
    count, width = 0, matrices[0].shape[1]
    tiles = -(-width // L)
    for matrix in matrices:
        rows = slice(count, count + matrix.shape[0])
        for number in range(tiles):
            part = matrix[:, number * L : (number + 1) * L]
            if part.shape[1] < L:
                blank = jnp.zeros((part.shape[0], L - part.shape[1]), jnp.float32)
                part = jnp.concatenate([part, blank], axis=1)
            tile_ref[number, rows] = part
        count = rows.stop
    cycle = L // math.gcd(width, L)
    stride = width * cycle // L

    def strided(first, amount, step):
        return pl.ds(first, amount, stride=step) if amount > 1 else slice(first, first + 1)

    carried = None
    for first in range(min(cycle, count)):
        amount = -(-(count - first) // cycle)
        row, shift = divmod(offset + width * first, L)
        pieces = -(-(shift + width) // L)
        parts = [tile_ref[number, strided(first, amount, cycle)] for number in range(tiles)]
        if shift:
            parts.insert(0, jnp.zeros((amount, shift), jnp.float32))
        held = jnp.concatenate(parts, axis=1) if len(parts) > 1 else parts[0]
        for piece in range(pieces):
            news = held[:, piece * L : min((piece + 1) * L, held.shape[1])]
            if news.shape[1] < L:
                blank = jnp.zeros((amount, L - news.shape[1]), jnp.float32)
                news = jnp.concatenate([news, blank], axis=1)
            whole = piece > 0 or shift == 0
            if carried is not None:
                left, at = carried
                news, whole, carried = news + left[:amount], True, None
                if left.shape[0] > amount:
                    at += stride * amount
                    flat_ref[at : at + 1] += left[amount:]
            if piece == pieces - 1 and (shift + width) % L:
                if whole:
                    carried = (news, row + piece)
                else:
                    flat_ref[strided(row + piece, amount, stride)] += news
            elif whole:
                flat_ref[strided(row + piece, amount, stride)] = news
            else:
                flat_ref[strided(row + piece, amount, stride)] += news
    if carried is not None:
        left, at = carried
        flat_ref[strided(at, left.shape[0], stride)] += left


def by_width(pieces):
    groups = []
    for piece in pieces:
        if groups and groups[-1][-1].shape[1] == piece.shape[1]:
            groups[-1].append(piece)
        else:
            groups.append([piece])
    return groups


def flatten_all(flat_ref, tile_ref, pieces, offset):
    for group in by_width(pieces):
        flatten_into(flat_ref, tile_ref, [piece[...] for piece in group], offset)
        offset += sum(math.prod(piece.shape) for piece in group)


def flatten_kernel(offset, *refs):
    *ins, flat_ref, tile_ref = refs
    flat_ref[...] = jnp.zeros_like(flat_ref)
    flatten_all(flat_ref, tile_ref, ins, offset)


def flat_events(pieces, offset, rows):
    deepest = max(sum(piece.shape[0] for piece in group) for group in by_width(pieces))
    return kernel_call(
        functools.partial(flatten_kernel, offset - EVENT_ROW * L),
        [array_of((rows - EVENT_ROW, L))],
        pieces,
        [((2, -(-deepest // 8) * 8, L), jnp.float32)],
        flops=2 * 10**9,
    )[0]


def node_kernel(
    start_ref,
    bit_ref,
    rows_a_ref,
    rows_b_ref,
    rows_c_ref,
    rows_d_ref,
    table_ref,
    events_ref,
    near_ref,
    came_ref,
    loss_ref,
    gi_ref,
    gh_ref,
    bias_ref,
    features_ref,
    keep_a_ref,
    keep_b_ref,
    give_a_ref,
    give_b_ref,
    flat_ref,
    grad_s,
    tile_s,
    upper_s,
    lower_s,
    state_s,
    order_s,
    hot_s,
    gi_s,
    gh_s,
    bias_s,
    static_s,
):
    part_refs = (rows_a_ref, rows_b_ref, rows_c_ref, rows_d_ref)
    regions = near_ref.shape[0]
    part_nodes = rows_a_ref.shape[0]
    shards = start_ref.shape[0]
    shard = len(part_refs) * part_nodes // shards
    flat_ref[:EVENT_ROW] = jnp.zeros((EVENT_ROW, L), jnp.float32)
    flat_ref[EVENT_ROW:] = events_ref[...]
    for ref, raw_ref in ((gi_s, gi_ref), (gh_s, gh_ref), (bias_s, bias_ref)):
        ref[...] = jnp.zeros_like(ref)
        for g in range(3):
            ref[: raw_ref.shape[0], g * L : g * L + D] = raw_ref[:, g * D : (g + 1) * D].astype(ref.dtype)

    size = near_ref.shape[1]
    for number in range(regions):
        part = slice(number * size, (number + 1) * size)
        grad_s[part] = near_ref[number] + came_ref[number]

    def arrange(number, carry):
        source = pl.ds(pl.multiple_of(start_ref[number], shard), shard)
        order_s[pl.ds(pl.multiple_of(number * shard, shard), shard)] = (
            grad_s[source]
        )
        return carry

    lax.fori_loop(0, shards, arrange, 0)

    def some(rows_ref, first, step, sums):
        at = pl.ds(pl.multiple_of(step * NODE_STEP, NODE_STEP), NODE_STEP)
        into = pl.ds(pl.multiple_of(first + step * NODE_STEP, NODE_STEP), NODE_STEP)
        stored = rows_ref[at, MSG_PAD : MSG_PAD + L]
        held = stored.astype(jnp.float32) + rows_ref[at, MSG_PAD + L :].astype(jnp.float32)
        inputs = dot(rows_ref[at, :MSG_PAD], gi_s[...]) + bias_s[0:1]
        hidden = dot(stored, gh_s[...]) + bias_s[1:2]
        reset = jax.nn.sigmoid(inputs[:, :L] + hidden[:, :L])
        update = jax.nn.sigmoid(inputs[:, L : 2 * L] + hidden[:, L : 2 * L])
        fresh = hidden[:, 2 * L :]
        candidate = jnp.tanh(inputs[:, 2 * L :] + reset * fresh)
        d_state = order_s[into]
        d_third = d_state * (1.0 - update) * (1.0 - candidate * candidate)
        d_fresh = d_third * reset
        d_first = d_third * fresh * reset * (1.0 - reset)
        d_second = d_state * (held - candidate) * update * (1.0 - update)
        news = []
        for number, part in enumerate((d_first, d_second, d_third, d_fresh)):
            lanes_at = slice(number * L, (number + 1) * L)
            news.append(jnp.sum(part, axis=0, keepdims=True))
            upper_s[into, lanes_at], lower_s[into, lanes_at] = split_terms(part)
        state_s[into, :L], state_s[into, L:] = split_terms(grad_s[into])
        return sums + jnp.concatenate(news, axis=1)

    total = jnp.zeros((1, 4 * L), jnp.float32)
    wide_gi, wide_gh = 0.0, 0.0
    for part, rows_ref in enumerate(part_refs):
        first = part * part_nodes
        total = lax.fori_loop(
            0, part_nodes // NODE_STEP, functools.partial(some, rows_ref, first), total
        )
        messages = rows_ref[:, :MSG_PAD]
        stored = rows_ref[:, MSG_PAD : MSG_PAD + L]
        for ref in (upper_s, lower_s):
            terms = ref[first : first + part_nodes]
            wide_gi = wide_gi + dot_tn(messages, terms[:, : 3 * L])
            wide_gh = wide_gh + dot_tn(stored, terms)

    def gates(matrix, order):
        return jnp.concatenate([matrix[:, g * L : g * L + D] for g in order], axis=1)

    pieces = [
        gates(wide_gi[:MSG], (0, 1, 2)),
        gates(wide_gh[:D], (0, 1, 3)),
        gates(total, (0, 1, 2)),
        gates(total, (0, 1, 3)),
    ]
    mine = len(part_refs) * part_nodes // regions
    for number in range(regions):
        at = pl.ds(pl.multiple_of((2 * number + bit_ref[0]) * mine, mine), mine)
        pairs = table_ref[F : F + 16, at].astype(jnp.float32)
        static_s[:, number * mine : (number + 1) * mine] = pairs[0:1] * 128.0 + pairs[1:2]
    hot_rows(hot_s, static_s[...].astype(jnp.int32))
    by_feature = dot(hot_s[...], state_s[...])
    terms = split_terms(by_feature[:, :L] + by_feature[:, L:])
    wide = dot_tn(features_ref[...], terms[0]) + dot_tn(features_ref[...], terms[1])
    pieces.append(wide[:, :D])
    flatten_all(flat_ref, tile_s, pieces, 0)
    half = keep_a_ref.shape[1]
    firsts, count = windows(2 * keep_a_ref.shape[0], flat_ref.shape[0])
    for place, refs in enumerate(((keep_a_ref, keep_b_ref), (give_a_ref, give_b_ref))):
        for number in range(keep_a_ref.shape[0]):
            for bit in range(2):
                first = firsts[2 * number + bit]

                @pl.when(bit_ref[0] ^ place == bit)
                def copy(refs=refs, number=number, first=first):
                    refs[0][number] = flat_ref[first : first + half]
                    refs[1][number, : count - half] = flat_ref[first + half : first + count]

            blank = refs[1].shape[1] - (count - half)
            refs[1][number, count - half :] = jnp.broadcast_to(loss_ref[...], (blank, L))


def windows(regions, flat_rows):
    size = int(flat_rows * L) // regions
    firsts = [number * size // L for number in range(regions)]
    return firsts, max(-(-(number + 1) * size // L) - first for number, first in enumerate(firsts))


def node_grads(weights, start, node_rows, table_t, node_features, events, grads, loss, regions):
    flat_rows = EVENT_ROW + events.shape[0]
    nodes = grads[0].shape[0] * grads[0].shape[1]
    rows_out = -(-(windows(regions, flat_rows)[1] + 1) // 8) * 8
    half = rows_out // 16 * 8
    return kernel_call(
        node_kernel,
        [array_of((regions // 2, rows, L)) for rows in (half, rows_out - half)] * 2,
        [start, my_bit("ev", 0)[None], *node_rows, table_t, events, *grads, loss, *weights, node_features],
        [
            ((flat_rows, L), jnp.float32),
            ((nodes, L), jnp.float32),
            ((3, -(-(MSG + D + 2) // 8) * 8, L), jnp.float32),
            ((nodes, 4 * L), jnp.bfloat16),
            ((nodes, 4 * L), jnp.bfloat16),
            ((nodes, 2 * L), jnp.bfloat16),
            ((nodes, L), jnp.float32),
            ((node_features.shape[0], nodes), jnp.bfloat16),
            ((MSG_PAD, 3 * L), jnp.bfloat16),
            ((L, 3 * L), jnp.bfloat16),
            ((8, 3 * L), jnp.float32),
            ((1, nodes), jnp.float32),
        ],
        flops=8 * 10**9,
    )


def partner(array, name, bit):
    size = lax.axis_size(name)
    return lax.ppermute(array, name, [(i, i ^ (1 << bit)) for i in range(size)])


def my_bit(name, bit):
    return (lax.axis_index(name) >> bit) & 1


def bits_of(name):
    return (lax.axis_size(name) - 1).bit_length()


def exchange(held, done, name, bit):
    other = partner(held, name, bit)
    mine_first = my_bit(name, bit) == 0
    done = sorted(done + [(name == "neg", -bit)])
    place = done.index((name == "neg", -bit))
    parts = [jnp.where(mine_first, held, other), jnp.where(mine_first, other, held)]
    return jnp.stack(parts, axis=place), done


def crossed(array, first, second):
    size = lax.axis_size("ev")
    return lax.ppermute(
        array, "ev", [(i, i ^ (1 << (second if i & 1 else first))) for i in range(size)]
    )


def gather_neg(shard):
    held, done = shard, []
    for bit in range(bits_of("neg")):
        held, done = exchange(held, done, "neg", bit)
    return held, done


def gather_ev(held, done, beside=()):
    high = bits_of("ev") - 1
    for bit in range(1, high - 1):
        held, done = exchange(held, done, "ev", bit)
    odd = my_bit("ev", 0) == 1
    low_set, high_set = my_bit("ev", high - 1) == 1, my_bit("ev", high) == 1
    first_set, second_set = jnp.where(odd, high_set, low_set), jnp.where(odd, low_set, high_set)
    other = crossed(held, high - 1, high)
    held = jnp.stack([jnp.where(first_set, other, held), jnp.where(first_set, held, other)])
    other = crossed(held, high, high - 1)
    zero, one = jnp.where(second_set, other, held), jnp.where(second_set, held, other)
    held = jnp.stack(
        [
            jnp.stack([zero[0], jnp.where(odd, one[0], zero[1])]),
            jnp.stack([jnp.where(odd, zero[1], one[0]), one[1]]),
        ]
    )
    done = sorted(done + [(False, -high), (False, 1 - high)])
    if beside:
        held, *beside = lax.optimization_barrier((held, *beside))
    held, done = exchange(held, done, "ev", 0)
    return held, beside


def reduce_bit(held, bits, bit):
    place = bits.index(bit)
    mine = my_bit("ev", bit)
    keep = lax.dynamic_index_in_dim(held, mine, place, keepdims=False)
    give = lax.dynamic_index_in_dim(held, 1 - mine, place, keepdims=False)
    return keep + partner(give, "ev", bit), [other for other in bits if other != bit]


def scatter_ev(keeps, gives):
    count = bits_of("ev")
    bits = list(reversed(range(1, count)))
    parts = []
    for keep, give in zip(keeps, gives):
        held, left = (keep + partner(give, "ev", 0)).reshape((2,) * (count - 1) + keep.shape[1:]), bits
        for bit in range(1, count - 2):
            held, left = reduce_bit(held, left, bit)
        parts.append((held, left))
    turns = parts[0][1]
    for turn in range(2):
        parts = [
            reduce_bit(part, left, turns[(turn + number) % 2])
            for number, (part, left) in enumerate(parts)
        ]
    return jnp.concatenate([part for part, left in parts], axis=-2)


def scatter_neg(blocks):
    count = bits_of("neg")
    held = blocks.reshape((2,) * count + blocks.shape[1:])
    for bit in range(count):
        mine, place = my_bit("neg", bit), count - 1 - bit
        keep = lax.dynamic_index_in_dim(held, mine, place, keepdims=False)
        give = lax.dynamic_index_in_dim(held, 1 - mine, place, keepdims=False)
        held = keep + partner(give, "neg", bit)
    return held


def lanes(flat):
    amount = flat.shape[-1]
    rows = -(-amount // 128)
    wide = jnp.pad(flat, [(0, 0)] * (flat.ndim - 1) + [(0, rows * 128 - amount)])
    return wide.reshape(flat.shape[:-1] + (rows, 128))


def from_digits(pairs, axis):
    pairs = pairs.astype(jnp.float32)
    high, low = (lax.index_in_dim(pairs, place, axis, keepdims=False) for place in (0, 1))
    return high * 128.0 + low


def on_device(
    master,
    first_moment,
    second_moment,
    memory,
    messages,
    static_ids,
    node_features,
    neighbours,
    neighbour_times,
    last_partner,
    last_deltas,
    last_edges,
    sources,
    targets,
    times,
    negatives,
    neg_counts,
):
    shard = master.shape[0]
    groups = lax.axis_size("neg")
    regions = lax.axis_size("ev")
    devices = regions * groups
    rank = lax.axis_index("neg")
    own_events = sources.shape[0]
    own_nodes = memory.shape[0]
    local_neg = negatives.shape[1]
    total_neg = local_neg * groups
    events_all = own_events * devices

    own_columns = by_lanes(negatives.T).reshape(-1, L)
    own_copy = lanes(master.astype(jnp.bfloat16))
    copy_rows = own_copy.shape[0]
    sent = jnp.concatenate(
        [own_copy, (own_columns >> 7).astype(jnp.bfloat16), (own_columns & 127).astype(jnp.bfloat16)]
    )
    copies, copies_done = exchange(sent, [], "neg", 0)
    copies, late_ids = lax.optimization_barrier((copies, static_ids))
    for bit in range(1, bits_of("neg")):
        copies, copies_done = exchange(copies, copies_done, "neg", bit)
    all_negatives = copies[..., copy_rows:, :].reshape(groups, -1, L)
    copies = copies[..., :copy_rows, :]

    rows, tail = pack(rank, neg_counts, static_ids, messages, memory, own_events // W)
    copies, rows, features = lax.optimization_barrier((copies, rows, node_features))
    high = bits_of("ev") - 1
    odd = my_bit("ev", 0) == 1
    far_neg = list(reversed(range(1, bits_of("neg"))))
    flips = [1 << bit for bit in far_neg] + [jnp.where(odd, 1 << (high - 2), 1 << (high - 1)) * groups]
    flips += [(1 << (bit - 1)) * groups for bit in range(1, high - 1)]
    start = ((lax.axis_index("ev") >> 1) * groups + rank)[None]
    for flip in flips:
        start = jnp.concatenate([start, start ^ flip])
    across = jnp.where(odd, 1 << (high - 1), 1 << (high - 2)) * groups
    start = jnp.concatenate([start, start ^ across, start ^ 1, start ^ across ^ 1]) * own_nodes
    for bit in far_neg:
        rows = jnp.concatenate([rows, partner(rows, "neg", bit)])

    ids, gaps, slots, valid, live = prepare(
        rank, sources, targets, times, neg_counts, all_negatives, neighbours, neighbour_times
    )
    copies, (valid, rows) = gather_ev(copies, copies_done, (valid, rows))
    rows = jnp.concatenate([rows, crossed(rows, high, high - 1)])
    for bit in range(1, high - 1):
        rows = jnp.concatenate([rows, partner(rows, "ev", bit)])

    flat = copies.reshape(devices, -1)[:, :shard].reshape(-1)
    early = unpack(flat)
    state, renewed = owner_pass(early, memory, messages, features[late_ids])
    sending = jnp.concatenate(
        [jnp.pad(state.astype(jnp.bfloat16), ((0, 0), (0, F - D))), tail[:, : L - F]], 1
    )
    flat, sending = lax.optimization_barrier((flat, sending))
    weights = event_weights(flat, NODE_PARAMS)
    table, table_done = gather_neg(sending)
    table, start, biases = lax.optimization_barrier((table, start, early["b_g"]))
    table, weights = gather_ev(table, table_done, weights)
    table = table.reshape(-1, L)
    table, rows = lax.optimization_barrier((table, rows))

    def far_device(device):
        place, near = divmod(device, groups)
        return (place ^ (1 << (high if place & 1 else high - 1))) * groups + (near ^ 1)

    far_rows = [
        crossed(rows, high - 1, high),
        partner(rows, "neg", 0),
        lax.ppermute(rows, ("ev", "neg"), [(i, far_device(i)) for i in range(devices)]),
    ]
    table_t = table.T
    local_loss, neg_total, keep, give, grad_event = event_step(
        weights,
        table_t,
        (ids, gaps, slots, valid, live),
        regions,
        own_nodes,
        events_all,
        own_events // W,
    )
    give, far_rows, local_loss, grad_event = lax.optimization_barrier(
        (give, far_rows, local_loss, grad_event)
    )
    came = partner(give, "ev", 0)
    flat_rows = shard * devices // L
    event_flat = flat_events(grad_event, NODE_PARAMS, flat_rows)
    upper_kept, lower_kept, upper_given, lower_given = node_grads(
        (early["w_gi"], early["w_gh"], biases),
        start,
        [rows, *far_rows],
        table_t,
        features,
        event_flat,
        (keep, came),
        local_loss,
        regions,
    )
    block_rows = windows(regions, flat_rows)[1]
    summed = scatter_ev((upper_kept, lower_kept), (upper_given, lower_given))
    summed, last_partner, last_deltas = lax.optimization_barrier((summed, last_partner, last_deltas))
    if shard * groups % L:
        first = lax.axis_index("ev") * (shard * groups) % L
        values = lax.dynamic_slice_in_dim(summed[:block_rows].reshape(-1), first, shard * groups)
        values = lanes(values)
    else:
        values = summed[:block_rows]
    firsts, part_rows = windows(groups, shard * groups / L)
    values = jnp.pad(values, ((0, max(0, firsts[-1] + part_rows - values.shape[0])), (0, 0)))
    shares = jnp.stack(
        [
            jnp.concatenate([values[first : first + part_rows], summed[block_rows:][:1]])
            for first in firsts
        ]
    )
    totals = scatter_neg(shares)
    loss = jnp.sum(totals[part_rows])
    first = rank * shard % L
    grad_shard = lax.dynamic_slice_in_dim(totals[:part_rows].reshape(-1), first, shard)
    new_master, new_first, new_second = adamw(master, first_moment, second_moment, grad_shard)
    codes = jnp.cos(
        last_deltas[:, None] * early["w_time"].astype(jnp.float32)
        + early["b_time"].astype(jnp.float32)
    )
    carried = jnp.concatenate(
        [
            sending[:, :D].astype(jnp.float32),
            table[last_partner][:, :D].astype(jnp.float32),
            codes,
            last_edges.astype(jnp.float32),
        ],
        1,
    )
    return (loss, neg_total, new_master, new_first, new_second, renewed, carried)


def solution(mesh):
    return jax.shard_map(
        on_device,
        mesh=mesh,
        in_specs=(
            P(("ev", "neg")),
            P(("ev", "neg")),
            P(("ev", "neg")),
            P(("ev", "neg"), None),
            P(("ev", "neg"), None),
            P(("ev", "neg")),
            P(),
            P(),
            P(),
            P(("ev", "neg")),
            P(("ev", "neg")),
            P(("ev", "neg"), None),
            P(("ev", "neg")),
            P(("ev", "neg")),
            P("ev"),
            P("ev", "neg"),
            P("ev"),
        ),
        out_specs=(
            P(),
            P(),
            P(("ev", "neg")),
            P(("ev", "neg")),
            P(("ev", "neg")),
            P(("ev", "neg"), None),
            P(("ev", "neg"), None),
        ),
        check_vma=False,
    )
```

```python
import functools
import math

import jax
import jax.numpy as jnp
from jax import lax
from jax.experimental import pallas as pl
from jax.experimental.pallas import tpu as pltpu
from jax.sharding import PartitionSpec as P

D = 100
TE = 100
NF = 413
PH = 100
HEADS = 2
NBR = 10
STEP = 10
HS = 50
MSG = 486
NODE_PARAMS = 3 * D * (MSG + D + 2) + NF * D


beta_one = 0.9
beta_two = 0.999
rate_lr = 0.02
decay_wd = 0.01
eps_adam = 1e-08

HP = 56
F = HEADS * HP
W = 128
LO = 256
L = 128
MSG_PAD = 512
CHUNK = 10
HOT = 2048
EVENT_ROW = 1696
NODE_STEP = 256
VMEM_BYTES = 60 * 1024 * 1024


def unpack(flat):
    layout = [
        ("w_gi", (MSG, 3 * D)),
        ("w_gh", (D, 3 * D)),
        ("b_g", (2, 3 * D)),
        ("w_feat", (NF, D)),
        ("w_time", (TE,)),
        ("b_time", (TE,)),
        ("w_query", (D + TE, D)),
        ("w_kv", (D + TE, 2 * D)),
        ("w_out", (D, D)),
        ("w_ps", (D, PH)),
        ("w_pd", (D, PH)),
        ("b_p1", (PH,)),
        ("w_p2", (PH,)),
        ("b_p2", (1,)),
    ]
    params = {}
    offset = 0
    for label, shape in layout:
        amount = math.prod(shape)
        params[label] = flat[offset : offset + amount].reshape(shape)
        offset += amount
    return params


def dot(left, right):
    return jnp.dot(left, right, preferred_element_type=jnp.float32)


def dot_nt(left, right):
    return lax.dot_general(
        left, right, (((1,), (1,)), ((), ())), preferred_element_type=jnp.float32
    )


def dot_tn(left, right):
    return lax.dot_general(
        left, right, (((0,), (0,)), ((), ())), preferred_element_type=jnp.float32
    )


def split_terms(value):
    first = value.astype(jnp.bfloat16)
    return first, (value - first.astype(jnp.float32)).astype(jnp.bfloat16)


def settled_terms(value):
    first = lax.optimization_barrier(value.astype(jnp.bfloat16))
    return first, (value - first.astype(jnp.float32)).astype(jnp.bfloat16)


def three_terms(value):
    first = value.astype(jnp.bfloat16)
    rest = value - first.astype(jnp.float32)
    second = rest.astype(jnp.bfloat16)
    return first, second, (rest - second.astype(jnp.float32)).astype(jnp.bfloat16)


def owner_pass(params, memory, messages, features):
    inputs = dot(messages, params["w_gi"]) + params["b_g"][0].astype(jnp.float32)
    hidden = dot(memory.astype(jnp.bfloat16), params["w_gh"]) + params["b_g"][1].astype(jnp.float32)
    reset = jax.nn.sigmoid(inputs[:, :D] + hidden[:, :D])
    update = jax.nn.sigmoid(inputs[:, D : 2 * D] + hidden[:, D : 2 * D])
    candidate = jnp.tanh(inputs[:, 2 * D :] + reset * hidden[:, 2 * D :])
    renewed = (1.0 - update) * candidate + update * memory
    return (renewed + dot(features, params["w_feat"]), renewed)


def adamw(master, first_state, second_state, grads):
    first_new = beta_one * first_state + (1.0 - beta_one) * grads
    second_new = beta_two * second_state + (1.0 - beta_two) * grads * grads
    corrected = (
        first_new
        / (1.0 - beta_one**STEP)
        / (jnp.sqrt(second_new / (1.0 - beta_two**STEP)) + eps_adam)
    )
    return (master - rate_lr * (corrected + decay_wd * master), first_new, second_new)


def sine_cosine(angle):
    turns = jnp.round(angle * (2.0 / math.pi))
    rest = angle - turns * 1.5703125
    rest = rest - turns * 4.837512969970703e-4
    rest = rest - turns * 7.549789948768648e-8
    square = rest * rest
    sine = rest + rest * square * (
        -1.6666654611e-1 + square * (8.3321608736e-3 - square * 1.9515295891e-4)
    )
    cosine = (
        1.0
        - 0.5 * square
        + square
        * square
        * (4.166664568298827e-2 + square * (-1.388731625493765e-3 + square * 2.443315711809948e-5))
    )
    quadrant = turns.astype(jnp.int32)
    odd = (quadrant & 1) == 1
    cos_value = jnp.where(odd, sine, cosine)
    sin_value = jnp.where(odd, cosine, sine)
    cos_value = jnp.where(((quadrant + 1) & 2) == 2, -cos_value, cos_value)
    sin_value = jnp.where((quadrant & 2) == 2, -sin_value, sin_value)
    return cos_value, sin_value


def any_angle(angle):
    return jnp.cos(angle), jnp.sin(angle)


def pair(value):
    return jnp.concatenate([value, value], axis=1)


def fold(value):
    return value[:, :W] + value[:, W:]


def tile(k):
    return slice(k * W, (k + 1) * W)


def hot_rows(hot_ref, ids, base=0):
    count = ids.shape[1]
    rows = lax.broadcasted_iota(jnp.int32, (LO, count), 0).astype(jnp.float32).astype(jnp.bfloat16)
    place = (ids & (LO - 1)).astype(jnp.float32)
    group = ids // LO - base // LO
    one, nought = jnp.ones_like(rows), jnp.zeros_like(rows)
    for number in range(hot_ref.shape[0] // LO):
        here = jnp.where(group == number, place, -1.0)
        here = jnp.broadcast_to(here, (LO, count)).astype(jnp.bfloat16)
        hot_ref[number * LO : (number + 1) * LO] = jnp.where(rows == here, one, nought)


def gather_columns(table_ref, hot_ref, ids):
    step = hot_ref.shape[0]
    found = None
    for base in range(0, table_ref.shape[1], step):
        hot_rows(hot_ref, ids, base)
        part = dot(table_ref[:, base : base + step], hot_ref[...])
        found = part if found is None else found + part
    return found


SRC, TGT, TIME, COUNT, NEG = 0, 1, 2, 3, 4
ID, AT, EVENT = 0, 1, 2
NEAR_ROWS = 16


def column_of(row, lanes_of):
    wide = jnp.transpose(jnp.broadcast_to(row, (L, row.shape[1])))
    return jnp.concatenate([wide] * (lanes_of // L), axis=1)


def pack_kernel(halves, rank_ref, numbers_ref, static_ref, messages_ref, memory_ref, rows_ref, tail_ref):
    rows_ref[...] = jnp.zeros_like(rows_ref)
    rows_ref[:, :MSG] = messages_ref[...]
    terms = split_terms(memory_ref[...])
    rows_ref[:, MSG_PAD : MSG_PAD + D] = terms[0]
    rows_ref[:, MSG_PAD + L : MSG_PAD + L + D] = terms[1]
    counts = numbers_ref[pl.ds(rank_ref[0] * halves, halves)].astype(jnp.float32)
    total = jnp.sum(jnp.sum(counts, axis=1, keepdims=True), axis=0, keepdims=True)
    static = column_of(static_ref[...].astype(jnp.float32), L).astype(jnp.int32)
    lane = lax.broadcasted_iota(jnp.int32, static.shape, 1)
    value = jnp.where(lane < 2, static, total.astype(jnp.int32))
    value = jnp.where((lane & 1) == 0, value >> 7, value & 127)
    tail_ref[...] = value.astype(jnp.float32).astype(jnp.bfloat16)


def pack(rank, counts, static_ids, messages, memory, halves):
    nodes = static_ids.shape[0]
    return kernel_call(
        functools.partial(pack_kernel, halves),
        [array_of((nodes, MSG_PAD + 2 * L), jnp.bfloat16), array_of((nodes, L), jnp.bfloat16)],
        [rank[None], by_lanes(counts), static_ids[None], messages, memory],
        [],
        flops=10**8,
    )


def prepare_kernel(
    rank_ref,
    source_ref,
    target_ref,
    times_ref,
    numbers_ref,
    digits_ref,
    near_ref,
    then_ref,
    ids_ref,
    gaps_ref,
    slots_ref,
    valid_ref,
    live_ref,
    event_s,
    pair_s,
    negatives_s,
    around_s,
    hot_s,
):
    groups, digit_rows, _ = digits_ref.shape
    rows = times_ref.shape[0]
    local = digit_rows // (2 * rows)
    columns = groups * local
    found = digits_ref[...].astype(jnp.float32)
    negatives_s[...] = found[:, : digit_rows // 2] * 128.0 + found[:, digit_rows // 2 :]
    halves = source_ref.shape[0]
    events = halves * W
    mine = pl.ds(rank_ref[0] * halves, halves)
    event_s[...] = jnp.zeros_like(event_s)
    for row, held in enumerate(
        [source_ref[...], target_ref[...], times_ref[mine], numbers_ref[mine]]
        + [
            negatives_s[group, pl.ds(j * rows + rank_ref[0] * halves, halves)]
            for group in range(groups)
            for j in range(local)
        ]
    ):
        held = held.astype(jnp.float32)
        for half in range(halves):
            event_s[row : row + 1, half * W : (half + 1) * W] = held[half : half + 1]
    counts = event_s[COUNT : COUNT + 1]
    shape = (events, events)
    earlier = lax.broadcasted_iota(jnp.int32, shape, 0) < lax.broadcasted_iota(jnp.int32, shape, 1)
    earlier = jnp.where(earlier, 1.0, 0.0).astype(jnp.bfloat16)
    event = lax.broadcasted_iota(jnp.int32, (1, events), 1).astype(jnp.float32)
    wanted = lax.broadcasted_iota(jnp.int32, (columns * events, events), 0).astype(jnp.float32)
    taken = jnp.zeros((1, 1), jnp.float32)
    packed = jnp.zeros((16, columns * events), jnp.float32)
    for number in range(columns):
        active = counts >= float(columns - number)
        ones = jnp.broadcast_to(jnp.where(active, 1.0, 0.0), (16, events))
        place = taken + dot(ones.astype(jnp.bfloat16), earlier)[0:1]
        taken = taken + jnp.sum(ones[0:1], axis=1, keepdims=True)
        place = jnp.where(active, place, -1.0)
        order = jnp.where(wanted == place, 1.0, 0.0).astype(jnp.bfloat16)
        row = NEG + number
        pair_s[...] = jnp.zeros_like(pair_s)
        pair_s[ID : ID + 1] = event_s[row : row + 1]
        pair_s[AT : AT + 1] = event_s[TIME : TIME + 1]
        pair_s[EVENT : EVENT + 1] = event
        thirds = dot_nt(jnp.concatenate(three_terms(pair_s[...]), axis=0), order)
        packed = packed + (thirds[:16] + thirds[16:32]) + thirds[32:]
    slot = lax.broadcasted_iota(jnp.int32, (1, columns * events), 1).astype(jnp.float32)
    valid = jnp.where(slot < taken, 1.0, 0.0)
    live_ref[0] = halves + (jnp.sum(counts).astype(jnp.int32) + W - 1) // W
    around_s[...] = jnp.zeros_like(around_s)
    near = near_ref[...]
    parts = [(near >> 7).astype(jnp.float32), (near & 127).astype(jnp.float32)]
    parts = [part.astype(jnp.bfloat16) for part in parts] + list(three_terms(then_ref[...]))
    for number, part in enumerate(parts):
        around_s[number * NEAR_ROWS : number * NEAR_ROWS + NBR] = part
    sets = [
        (event_s[SRC : SRC + 1], event_s[TIME : TIME + 1], event, jnp.ones((1, events))),
        (event_s[TGT : TGT + 1], event_s[TIME : TIME + 1], event, jnp.ones((1, events))),
    ]
    for number in range(columns):
        part = slice(number * events, (number + 1) * events)
        sets.append((packed[ID : ID + 1, part], packed[AT : AT + 1, part], packed[EVENT : EVENT + 1, part], valid[:, part]))
    for number, (nodes, times, of_event, counted) in enumerate(sets):
        nodes = nodes.astype(jnp.int32)
        found = gather_columns(around_s, hot_s, nodes)
        near = found[:NBR] * 128.0 + found[NEAR_ROWS : NEAR_ROWS + NBR]
        near = near.astype(jnp.int32)
        then = (
            found[2 * NEAR_ROWS : 2 * NEAR_ROWS + NBR] + found[3 * NEAR_ROWS : 3 * NEAR_ROWS + NBR]
        ) + found[4 * NEAR_ROWS : 4 * NEAR_ROWS + NBR]
        gaps = times - then
        for half in range(halves):
            block, lanes_at = number * halves + half, slice(half * W, (half + 1) * W)
            for k in range(NBR):
                ids_ref[block, :, tile(k)] = near[k : k + 1, lanes_at]
                gaps_ref[block, :, tile(k)] = gaps[k : k + 1, lanes_at]
            ids_ref[block, :, NBR * W :] = nodes[:, lanes_at]
            slots_ref[block] = of_event[:, lanes_at].astype(jnp.int32)
            valid_ref[block] = counted[:, lanes_at]


def step_kernel(
    halves,
    own_nodes,
    events_all,
    live_ref,
    bit_ref,
    table_ref,
    ids_ref,
    gaps_ref,
    slots_ref,
    valid_ref,
    wide_ref,
    kvt_ref,
    kv_ref,
    qt_ref,
    q_ref,
    square_ref,
    loss_ref,
    count_ref,
    keep_ref,
    give_ref,
    gkv_ref,
    gq_ref,
    gout_ref,
    gsource_ref,
    gother_ref,
    gtime_ref,
    gbase_ref,
    gp1_ref,
    gp2_ref,
    gend_ref,
    x_s,
    kv_s,
    sin_s,
    own_s,
    query_s,
    att_s,
    mix_s,
    z_s,
    dz_s,
    dsources_s,
    hot_s,
    right_s,
    upper_s,
    lower_s,
    rows_s,
    gkv_s,
    gq_s,
    gsquare_s,
    gwide_s,
):
    scale = 1.0 / math.sqrt(HS)
    near = NBR * W
    found = table_ref[F : F + 16].astype(jnp.float32)
    counted = jnp.sum(found, axis=1, keepdims=True)
    neg_total = (counted[2:3] * 128.0 + counted[3:4]) * (1.0 / own_nodes)
    count_ref[...] = jnp.broadcast_to(neg_total, (1, W))
    share = jnp.broadcast_to(1.0 / neg_total, (1, W))
    b_time = wide_ref[1]
    b_p1, w_p2 = wide_ref[2], wide_ref[3]
    b_p2 = wide_ref[4][0:1]
    zero_cos, zero_sin = wide_ref[5], wide_ref[6]
    furthest = jnp.max(jnp.abs(gaps_ref[...])) * jnp.max(jnp.abs(wide_ref[0])) + jnp.max(
        jnp.abs(b_time)
    )
    moderate = furthest <= 8192.0
    zero_code = zero_cos.astype(jnp.bfloat16)
    for ref in (rows_s, right_s, gkv_s, gq_s, gsquare_s, gwide_s, dsources_s, loss_ref):
        ref[...] = jnp.zeros_like(ref)
    head_rows = (slice(0, HP), slice(HP, F))
    live = live_ref[0]

    def forward(trig, slot, block):
        for s in range(0, F, 16):
            rows = slice(s, s + 16)
            w_rows, b_rows = wide_ref[0, rows], wide_ref[1, rows]
            for k in range(NBR):
                angle = gaps_ref[block, :, tile(k)] * w_rows + b_rows
                cos_value, sin_value = trig(angle)
                sin_s[slot, rows, tile(k)] = sin_value
                x_s[slot, F + s : F + s + 16, tile(k)] = cos_value.astype(jnp.bfloat16)
        found = gather_columns(table_ref, hot_s, ids_ref[block])[:F].astype(jnp.bfloat16)
        x_s[slot, :F] = found[:, :near]
        own = found[:, near:]
        own_s[slot] = own
        query = dot(qt_ref[...], jnp.concatenate([own, zero_code], axis=0))
        query_s[slot] = query
        kv_s[slot] = dot(kvt_ref[...], x_s[slot])
        mixed = []
        for h, rows in enumerate(head_rows):
            scores = jnp.concatenate(
                [
                    jnp.sum(kv_s[slot, rows, tile(k)] * query[rows], axis=0, keepdims=True)
                    for k in range(NBR)
                ],
                axis=0,
            )
            scores = scores * scale
            powers = jnp.exp(scores - jnp.max(scores, axis=0, keepdims=True))
            att_s[slot, h] = powers / jnp.sum(powers, axis=0, keepdims=True)
            mixed_h = jnp.zeros((HP, W), jnp.float32)
            for k in range(NBR):
                values = kv_s[slot, F + h * HP : F + (h + 1) * HP, tile(k)]
                mixed_h = mixed_h + att_s[slot, h, k : k + 1] * values
            mixed.append(mixed_h)
        mixed = jnp.concatenate(mixed, axis=0).astype(jnp.bfloat16)
        mix_s[slot] = mixed
        emb = own.astype(jnp.float32) + dot(square_ref[0], mixed)
        z_s[:, pl.ds(pl.multiple_of(slot * W, W), W)] = emb.astype(jnp.bfloat16)

    def predict(base, amount):
        blocks = range(halves + base, halves + base + amount)
        valid = jnp.concatenate([valid_ref[block] for block in blocks], axis=1)
        of_slot = jnp.concatenate([slots_ref[block] for block in blocks], axis=1)
        z = z_s[:, halves * W : (halves + amount) * W].astype(jnp.float32)
        z = jnp.where(valid > 0.0, z, 0.0).astype(jnp.bfloat16)
        events = lax.broadcasted_iota(jnp.int32, (halves * W, amount * W), 0)
        of_event = jnp.where(events == of_slot, 1.0, 0.0).astype(jnp.bfloat16)
        source = dot(z_s[:, : halves * W], of_event).astype(jnp.bfloat16)
        before_all = dot(square_ref[2], source) + dot(square_ref[4], z)
        losses = jnp.zeros((1, W), jnp.float32)
        ends = jnp.zeros((1, W), jnp.float32)
        by_hidden = jnp.zeros((F, W), jnp.float32)
        by_before = jnp.zeros((F, W), jnp.float32)
        for number, block in enumerate(blocks):
            before = before_all[:, tile(number)] + b_p1
            inner = 0.7978845608028654 * (before + 0.044715 * before * before * before)
            bend = jnp.tanh(inner)
            hidden = (0.5 * before * (1.0 + bend)).astype(jnp.bfloat16).astype(jnp.float32)
            slope = 0.5 * (1.0 + bend) + 0.5 * before * (1.0 - bend * bend) * (
                0.7978845608028654 * (1.0 + 3.0 * 0.044715 * before * before)
            )
            score = jnp.sum(hidden * w_p2, axis=0, keepdims=True) + b_p2
            positive = block < 2 * halves
            sign = -1.0 if positive else 1.0
            weight = valid[:, tile(number)] * (1.0 / events_all if positive else share)
            signed = sign * score
            small = jnp.exp(-jnp.abs(signed))
            losses = losses + weight * (jnp.maximum(signed, 0.0) + jnp.log1p(small))
            sigmoid = jnp.where(signed >= 0.0, 1.0, small) / (1.0 + small)
            d_score = (sign * weight) * sigmoid
            by_hidden = by_hidden + hidden * d_score
            ends = ends + d_score
            d_before = w_p2 * d_score * slope
            by_before = by_before + d_before
            upper_s[:F, tile(number)], lower_s[:F, tile(number)] = split_terms(d_before)
        loss_ref[...] += losses
        gwide_s[2] += by_before
        gwide_s[3] += by_hidden
        gwide_s[4, 0:1] += ends
        d_z = 0.0
        for ref in (upper_s, lower_s):
            term = ref[:F, : amount * W]
            gsquare_s[2] += dot_nt(z, term)
            dsources_s[...] += dot_nt(term, of_event)
            d_z = d_z + dot(square_ref[5], term)
        dz_s[:, halves * W : (halves + amount) * W] = d_z

    def backward(slot, block):
        d_emb = dz_s[:, pl.ds(pl.multiple_of(slot * W, W), W)]
        terms = jnp.concatenate(split_terms(d_emb), axis=1)
        gsquare_s[0] += dot_nt(pair(mix_s[slot]), terms)
        d_mixed = fold(dot(square_ref[1], terms))
        d_query = []
        for h, rows in enumerate(head_rows):
            d_mixed_h, query_h = d_mixed[rows], query_s[slot, rows]
            value_rows = slice(F + h * HP, F + (h + 1) * HP)
            d_shares = jnp.concatenate(
                [
                    jnp.sum(kv_s[slot, value_rows, tile(k)] * d_mixed_h, axis=0, keepdims=True)
                    for k in range(NBR)
                ],
                axis=0,
            )
            part = att_s[slot, h]
            total = jnp.sum(part * d_shares, axis=0, keepdims=True)
            d_scores = part * (d_shares - total) * scale
            d_query_h = jnp.zeros((HP, W), jnp.float32)
            for k in range(NBR):
                d_score = d_scores[k : k + 1]
                d_query_h = d_query_h + d_score * kv_s[slot, rows, tile(k)]
                for at, d_part in (
                    (rows, d_score * query_h),
                    (value_rows, att_s[slot, h, k : k + 1] * d_mixed_h),
                ):
                    upper_s[at, tile(k)], lower_s[at, tile(k)] = split_terms(d_part)
            d_query.append(d_query_h)
        x = x_s[slot]
        upper, lower = upper_s[...], lower_s[...]
        gkv_s[...] += dot_nt(x, upper) + dot_nt(x, lower)
        d_x = dot(kv_ref[...], upper) + dot(kv_ref[...], lower)
        for s in range(0, F, 16):
            rows = slice(s, s + 16)
            to_b = jnp.zeros((16, W), jnp.float32)
            to_w = jnp.zeros((16, W), jnp.float32)
            for k in range(NBR):
                first, second = split_terms(d_x[rows, tile(k)])
                right_s[rows, tile(k)] = first
                right_s[L + s : L + s + 16, tile(k)] = second
                turned = sin_s[slot, rows, tile(k)] * d_x[F + s : F + s + 16, tile(k)]
                to_b = to_b + turned
                to_w = to_w + turned * gaps_ref[block, :, tile(k)]
            gwide_s[1, rows] -= to_b
            gwide_s[0, rows] -= to_w
        d_query = jnp.concatenate(d_query, axis=0)
        terms = jnp.concatenate(split_terms(d_query), axis=1)
        code = jnp.concatenate([own_s[slot], zero_code], axis=0)
        gq_s[...] += dot_nt(pair(code), terms)
        d_code = fold(dot(q_ref[...], terms))
        gwide_s[1] -= zero_sin * d_code[F:]
        right_s[:F, near:], right_s[L : L + F, near:] = split_terms(d_emb + d_code[:F])
        for base in range(0, rows_s.shape[0], hot_s.shape[0]):
            hot_rows(hot_s, ids_ref[block], base)
            rows_s[base : base + hot_s.shape[0]] += dot_nt(hot_s[...], right_s[...])

    most = ids_ref.shape[0] - halves
    chunks = -(-most // CHUNK)
    for chunk in range(chunks):
        base = chunk * CHUNK
        count = jnp.clip(live - base, 0, CHUNK)
        first = halves + base if chunk else 0

        def run_forward(trig, base=base, count=count, first=first):
            def one(block, carry):
                forward(trig, block - base, block)
                return carry

            lax.fori_loop(first, halves + base + count, one, 0)

        for usable, trig in ((moderate, sine_cosine), (jnp.logical_not(moderate), any_angle)):
            pl.when(usable)(functools.partial(run_forward, trig))
        predict(base, min(CHUNK, most - base))
        if chunk == chunks - 1:
            for half in range(halves):
                d_source = dsources_s[:, half * W : (half + 1) * W]
                terms = jnp.concatenate(split_terms(d_source), axis=1)
                gsquare_s[1] += dot_nt(pair(z_s[:, tile(half)]), terms)
                dz_s[:, tile(half)] = fold(dot(square_ref[3], terms))

        def back(slot, carry, base=base):
            backward(slot, jnp.where(slot < halves, slot, slot + base))
            return carry

        lax.fori_loop(0 if chunk == chunks - 1 else halves, halves + count, back, 0)
    region = keep_ref.shape[1]
    for number in range(keep_ref.shape[0]):
        for ref, bit in ((keep_ref, bit_ref[0]), (give_ref, 1 - bit_ref[0])):
            at = pl.ds(pl.multiple_of((2 * number + bit) * region, region), region)
            ref[number] = rows_s[at, :L] + rows_s[at, L:]

    def cut_rows(matrix):
        return jnp.concatenate([matrix[:D], matrix[F : F + D]], axis=0)

    def cut_heads(matrix, axis):
        return jnp.concatenate(
            [
                lax.slice_in_dim(matrix, h * HP, h * HP + HS, axis=axis)
                for h in range(matrix.shape[axis] // HP)
            ],
            axis=axis,
        )

    gkv_ref[...] = cut_heads(cut_rows(gkv_s[...]), 1)
    gq_ref[...] = cut_heads(cut_rows(gq_s[...]), 1)
    gout_ref[...] = cut_heads(gsquare_s[0], 0)[:, :D]
    gsource_ref[...] = gsquare_s[1][:D, :PH]
    gother_ref[...] = gsquare_s[2][:D, :PH]
    ones = jnp.ones((8, W), jnp.bfloat16)
    for number, ref in enumerate((gtime_ref, gbase_ref, gp1_ref, gp2_ref, gend_ref)):
        total = sum(dot_nt(ones, term) for term in three_terms(gwide_s[number]))
        ref[...] = total[0:1, : ref.shape[1]]


def kernel_call(kernel, outs, ins, scratch, flops):
    def place(array):
        scalars = len(array.shape) == 1 and array.dtype == jnp.int32
        return pl.BlockSpec(memory_space=pltpu.SMEM if scalars else pltpu.VMEM)

    return pl.pallas_call(
        kernel,
        out_shape=tuple(outs),
        in_specs=[place(array) for array in ins],
        out_specs=tuple(place(array) for array in outs),
        scratch_shapes=[pltpu.VMEM(shape, dtype) for shape, dtype in scratch],
        compiler_params=pltpu.CompilerParams(vmem_limit_bytes=VMEM_BYTES),
        cost_estimate=pl.CostEstimate(flops=flops, bytes_accessed=10**6, transcendentals=0),
    )(*ins)


def array_of(shape, dtype=jnp.float32):
    return jax.ShapeDtypeStruct(shape, dtype)


def by_lanes(flat):
    return flat.reshape(flat.shape[:-1] + (-1, W))


def prepare(rank, sources, targets, times, counts, negatives, neighbours, then):
    groups, digit_rows, _ = negatives.shape
    columns = groups * (digit_rows * W // (2 * times.shape[0]))
    events = sources.shape[0]
    halves = events // W
    blocks = halves * (2 + columns)
    nodes = neighbours.shape[0]
    return kernel_call(
        prepare_kernel,
        [
            array_of((blocks, 1, (NBR + 1) * W), jnp.int32),
            array_of((blocks, 1, NBR * W)),
            array_of((blocks, 1, W), jnp.int32),
            array_of((blocks, 1, W)),
            array_of((1,), jnp.int32),
        ],
        [
            rank[None],
            by_lanes(sources),
            by_lanes(targets),
            by_lanes(times),
            by_lanes(counts),
            negatives,
            neighbours.T,
            then.T,
        ],
        [
            ((-(-(NEG + columns) // 16) * 16, events), jnp.float32),
            ((16, events), jnp.float32),
            ((groups, digit_rows // 2, L), jnp.float32),
            ((5 * NEAR_ROWS, nodes), jnp.bfloat16),
            ((min(nodes, HOT), events), jnp.bfloat16),
        ],
        flops=4 * 10**9,
    )


def unflatten_from(flat_ref, tile_ref, shape, offset):
    count, width = shape
    tiles = -(-width // L)
    cycle = L // math.gcd(width, L)
    stride = width * cycle // L
    for first in range(min(cycle, count)):
        amount = -(-(count - first) // cycle)
        row, shift = divmod(offset + width * first, L)
        pieces = -(-(shift + width) // L)
        held = [
            flat_ref[pl.ds(row + piece, amount, stride=stride) if amount > 1 else slice(row + piece, row + piece + 1)]
            for piece in range(pieces)
        ]
        held = jnp.concatenate(held, axis=1) if pieces > 1 else held[0]
        held = held[:, shift : shift + width]
        rows = pl.ds(first, amount, stride=cycle) if amount > 1 else slice(first, first + 1)
        for number in range(tiles):
            part = held[:, number * L : (number + 1) * L]
            if part.shape[1] < L:
                part = jnp.concatenate([part, jnp.zeros((amount, L - part.shape[1]), jnp.float32)], axis=1)
            tile_ref[number, rows] = part
    tiled = [tile_ref[number, :count] for number in range(tiles)]
    return jnp.concatenate(tiled, axis=1)[:, :width] if tiles > 1 else tiled[0][:, :width]


def weights_kernel(
    offset, flat_in, kvt_ref, kv_ref, qt_ref, q_ref, square_ref, wide_ref, flat_s, tile_s, pad_s
):
    flat_s[...] = flat_in[...].astype(jnp.float32)

    def padded(value, row_parts, column_parts):
        pad_s[...] = jnp.zeros_like(pad_s)
        for r_from, r_to, r_size in row_parts:
            for c_from, c_to, c_size in column_parts:
                pad_s[r_to : r_to + r_size, c_to : c_to + c_size] = value[
                    r_from : r_from + r_size, c_from : c_from + c_size
                ]
        return pad_s[...]

    plain = [(0, 0, D)]
    twice = [(0, 0, D), (D, F, TE)]
    heads = [(h * HS, h * HP, HS) for h in range(HEADS)]
    all_heads = [(h * HS, h * HP, HS) for h in range(2 * HEADS)]

    def vector(width):
        nonlocal offset
        value = unflatten_from(flat_s, tile_s, (1, width), offset)
        offset += width
        return jnp.concatenate([value, jnp.zeros((1, L - width), jnp.float32)], axis=1)

    wide_ref[0] = column_of(vector(TE), W)[:F]
    base = vector(TE)
    wide_ref[1] = column_of(base, W)[:F]
    for number, value in enumerate(any_angle(base)):
        wide_ref[5 + number] = column_of(value, W)[:F]
    for shape, straight, turned, row_parts, column_parts in (
        ((D + TE, D), q_ref, qt_ref, twice, heads),
        ((D + TE, 2 * D), kv_ref, kvt_ref, twice, all_heads),
        ((D, D), square_ref.at[1], square_ref.at[0], heads, plain),
        ((D, PH), square_ref.at[3], square_ref.at[2], plain, plain),
        ((D, PH), square_ref.at[5], square_ref.at[4], plain, plain),
    ):
        full = padded(unflatten_from(flat_s, tile_s, shape, offset), row_parts, column_parts)
        offset += shape[0] * shape[1]
        n, m = straight.shape
        straight[...] = full[:n, :m].astype(jnp.bfloat16)
        turned[...] = jnp.transpose(full)[:m, :n].astype(jnp.bfloat16)
    wide_ref[2] = column_of(vector(PH), W)[:F]
    wide_ref[3] = column_of(vector(PH), W)[:F]
    wide_ref[4] = jnp.broadcast_to(vector(1)[:, :1], (F, W))


def event_weights(flat, offset):
    rows = flat.reshape(-1, L)[EVENT_ROW:]
    low_type = jnp.bfloat16
    return kernel_call(
        functools.partial(weights_kernel, offset - EVENT_ROW * L),
        [
            array_of((2 * F, 2 * F), low_type),
            array_of((2 * F, 2 * F), low_type),
            array_of((F, 2 * F), low_type),
            array_of((2 * F, F), low_type),
            array_of((6, F, F), low_type),
            array_of((7, F, W)),
        ],
        [rows],
        [
            (rows.shape, jnp.float32),
            ((2, -(-(D + TE) // 8) * 8, L), jnp.float32),
            ((2 * L, 2 * L), jnp.float32),
        ],
        flops=4 * 10**9,
    )


def event_step(weights, table_t, prepared, regions, own_nodes, events_all, halves):
    ids, gaps, slots, valid, live = prepared
    kvt, kv, qt, q, square, wide = weights
    nodes = table_t.shape[1]
    near = NBR * W
    full = near + W
    low_type, high_type = jnp.bfloat16, jnp.float32
    half_table = array_of((regions // 2, nodes // regions, L))
    places = halves + min(CHUNK, ids.shape[0] - halves)
    loss, count, keep, give, g_kv, g_q, g_out, g_source, g_other, *g_rows = kernel_call(
        functools.partial(step_kernel, halves, own_nodes, events_all),
        [
            array_of((1, W)),
            array_of((1, W)),
            half_table,
            half_table,
            array_of((D + TE, 2 * D)),
            array_of((D + TE, D)),
            array_of((D, D)),
            array_of((D, PH)),
            array_of((D, PH)),
            *[array_of((1, width)) for width in (TE, TE, PH, PH, 1)],
        ],
        [
            live,
            my_bit("ev", 0)[None],
            table_t,
            ids,
            gaps,
            slots,
            valid,
            wide,
            kvt,
            kv,
            qt,
            q,
            square,
        ],
        [
            ((places, 2 * F, near), low_type),
            ((places, 2 * F, near), high_type),
            ((places, F, near), high_type),
            ((places, F, W), low_type),
            ((places, F, W), high_type),
            ((places, HEADS, NBR, W), high_type),
            ((places, F, W), low_type),
            ((F, places * W), low_type),
            ((F, places * W), high_type),
            ((F, halves * W), high_type),
            ((min(nodes, HOT), full), low_type),
            ((2 * L, full), low_type),
            ((2 * F, near), low_type),
            ((2 * F, near), low_type),
            ((nodes, 2 * L), high_type),
            ((2 * F, 2 * F), high_type),
            ((2 * F, F), high_type),
            ((3, F, F), high_type),
            ((5, F, W), high_type),
        ],
        flops=4 * 10**10,
    )
    grads = [*g_rows[:2], g_q, g_kv, g_out, g_source, g_other, *g_rows[2:]]
    return loss, count[0, 0], keep, give, grads


def flatten_into(flat_ref, tile_ref, matrices, offset):
    count, width = 0, matrices[0].shape[1]
    tiles = -(-width // L)
    for matrix in matrices:
        rows = slice(count, count + matrix.shape[0])
        for number in range(tiles):
            part = matrix[:, number * L : (number + 1) * L]
            if part.shape[1] < L:
                blank = jnp.zeros((part.shape[0], L - part.shape[1]), jnp.float32)
                part = jnp.concatenate([part, blank], axis=1)
            tile_ref[number, rows] = part
        count = rows.stop
    cycle = L // math.gcd(width, L)
    stride = width * cycle // L

    def strided(first, amount, step):
        return pl.ds(first, amount, stride=step) if amount > 1 else slice(first, first + 1)

    carried = None
    for first in range(min(cycle, count)):
        amount = -(-(count - first) // cycle)
        row, shift = divmod(offset + width * first, L)
        pieces = -(-(shift + width) // L)
        parts = [tile_ref[number, strided(first, amount, cycle)] for number in range(tiles)]
        if shift:
            parts.insert(0, jnp.zeros((amount, shift), jnp.float32))
        held = jnp.concatenate(parts, axis=1) if len(parts) > 1 else parts[0]
        for piece in range(pieces):
            news = held[:, piece * L : min((piece + 1) * L, held.shape[1])]
            if news.shape[1] < L:
                blank = jnp.zeros((amount, L - news.shape[1]), jnp.float32)
                news = jnp.concatenate([news, blank], axis=1)
            whole = piece > 0 or shift == 0
            if carried is not None:
                left, at = carried
                news, whole, carried = news + left[:amount], True, None
                if left.shape[0] > amount:
                    at += stride * amount
                    flat_ref[at : at + 1] += left[amount:]
            if piece == pieces - 1 and (shift + width) % L:
                if whole:
                    carried = (news, row + piece)
                else:
                    flat_ref[strided(row + piece, amount, stride)] += news
            elif whole:
                flat_ref[strided(row + piece, amount, stride)] = news
            else:
                flat_ref[strided(row + piece, amount, stride)] += news
    if carried is not None:
        left, at = carried
        flat_ref[strided(at, left.shape[0], stride)] += left


def by_width(pieces):
    groups = []
    for piece in pieces:
        if groups and groups[-1][-1].shape[1] == piece.shape[1]:
            groups[-1].append(piece)
        else:
            groups.append([piece])
    return groups


def flatten_all(flat_ref, tile_ref, pieces, offset):
    for group in by_width(pieces):
        flatten_into(flat_ref, tile_ref, [piece[...] for piece in group], offset)
        offset += sum(math.prod(piece.shape) for piece in group)


def flatten_kernel(offset, *refs):
    *ins, flat_ref, tile_ref = refs
    flat_ref[...] = jnp.zeros_like(flat_ref)
    flatten_all(flat_ref, tile_ref, ins, offset)


def flat_events(pieces, offset, rows):
    deepest = max(sum(piece.shape[0] for piece in group) for group in by_width(pieces))
    return kernel_call(
        functools.partial(flatten_kernel, offset - EVENT_ROW * L),
        [array_of((rows - EVENT_ROW, L))],
        pieces,
        [((2, -(-deepest // 8) * 8, L), jnp.float32)],
        flops=2 * 10**9,
    )[0]


def node_kernel(
    start_ref,
    bit_ref,
    rows_a_ref,
    rows_b_ref,
    rows_c_ref,
    rows_d_ref,
    table_ref,
    events_ref,
    near_ref,
    came_ref,
    loss_ref,
    gi_ref,
    gh_ref,
    bias_ref,
    features_ref,
    keep_a_ref,
    keep_b_ref,
    give_a_ref,
    give_b_ref,
    flat_ref,
    grad_s,
    tile_s,
    upper_s,
    lower_s,
    state_s,
    order_s,
    hot_s,
    gi_s,
    gh_s,
    bias_s,
    static_s,
):
    part_refs = (rows_a_ref, rows_b_ref, rows_c_ref, rows_d_ref)
    regions = near_ref.shape[0]
    part_nodes = rows_a_ref.shape[0]
    shards = start_ref.shape[0]
    shard = len(part_refs) * part_nodes // shards
    flat_ref[:EVENT_ROW] = jnp.zeros((EVENT_ROW, L), jnp.float32)
    flat_ref[EVENT_ROW:] = events_ref[...]
    for ref, raw_ref in ((gi_s, gi_ref), (gh_s, gh_ref), (bias_s, bias_ref)):
        ref[...] = jnp.zeros_like(ref)
        for g in range(3):
            ref[: raw_ref.shape[0], g * L : g * L + D] = raw_ref[:, g * D : (g + 1) * D].astype(ref.dtype)

    size = near_ref.shape[1]
    for number in range(regions):
        part = slice(number * size, (number + 1) * size)
        grad_s[part] = near_ref[number] + came_ref[number]

    def arrange(number, carry):
        source = pl.ds(pl.multiple_of(start_ref[number], shard), shard)
        order_s[pl.ds(pl.multiple_of(number * shard, shard), shard)] = (
            grad_s[source]
        )
        return carry

    lax.fori_loop(0, shards, arrange, 0)

    def some(rows_ref, first, step, sums):
        at = pl.ds(pl.multiple_of(step * NODE_STEP, NODE_STEP), NODE_STEP)
        into = pl.ds(pl.multiple_of(first + step * NODE_STEP, NODE_STEP), NODE_STEP)
        stored = rows_ref[at, MSG_PAD : MSG_PAD + L]
        held = stored.astype(jnp.float32) + rows_ref[at, MSG_PAD + L :].astype(jnp.float32)
        inputs = dot(rows_ref[at, :MSG_PAD], gi_s[...]) + bias_s[0:1]
        hidden = dot(stored, gh_s[...]) + bias_s[1:2]
        reset = jax.nn.sigmoid(inputs[:, :L] + hidden[:, :L])
        update = jax.nn.sigmoid(inputs[:, L : 2 * L] + hidden[:, L : 2 * L])
        fresh = hidden[:, 2 * L :]
        candidate = jnp.tanh(inputs[:, 2 * L :] + reset * fresh)
        d_state = order_s[into]
        d_third = d_state * (1.0 - update) * (1.0 - candidate * candidate)
        d_fresh = d_third * reset
        d_first = d_third * fresh * reset * (1.0 - reset)
        d_second = d_state * (held - candidate) * update * (1.0 - update)
        news = []
        for number, part in enumerate((d_first, d_second, d_third, d_fresh)):
            lanes_at = slice(number * L, (number + 1) * L)
            news.append(jnp.sum(part, axis=0, keepdims=True))
            upper_s[into, lanes_at], lower_s[into, lanes_at] = split_terms(part)
        state_s[into, :L], state_s[into, L:] = split_terms(grad_s[into])
        return sums + jnp.concatenate(news, axis=1)

    total = jnp.zeros((1, 4 * L), jnp.float32)
    wide_gi, wide_gh = 0.0, 0.0
    for part, rows_ref in enumerate(part_refs):
        first = part * part_nodes
        total = lax.fori_loop(
            0, part_nodes // NODE_STEP, functools.partial(some, rows_ref, first), total
        )
        messages = rows_ref[:, :MSG_PAD]
        stored = rows_ref[:, MSG_PAD : MSG_PAD + L]
        for ref in (upper_s, lower_s):
            terms = ref[first : first + part_nodes]
            wide_gi = wide_gi + dot_tn(messages, terms[:, : 3 * L])
            wide_gh = wide_gh + dot_tn(stored, terms)

    def gates(matrix, order):
        return jnp.concatenate([matrix[:, g * L : g * L + D] for g in order], axis=1)

    pieces = [
        gates(wide_gi[:MSG], (0, 1, 2)),
        gates(wide_gh[:D], (0, 1, 3)),
        gates(total, (0, 1, 2)),
        gates(total, (0, 1, 3)),
    ]
    mine = len(part_refs) * part_nodes // regions
    for number in range(regions):
        at = pl.ds(pl.multiple_of((2 * number + bit_ref[0]) * mine, mine), mine)
        pairs = table_ref[F : F + 16, at].astype(jnp.float32)
        static_s[:, number * mine : (number + 1) * mine] = pairs[0:1] * 128.0 + pairs[1:2]
    hot_rows(hot_s, static_s[...].astype(jnp.int32))
    by_feature = dot(hot_s[...], state_s[...])
    terms = split_terms(by_feature[:, :L] + by_feature[:, L:])
    wide = dot_tn(features_ref[...], terms[0]) + dot_tn(features_ref[...], terms[1])
    pieces.append(wide[:, :D])
    flatten_all(flat_ref, tile_s, pieces, 0)
    half = keep_a_ref.shape[1]
    firsts, count = windows(2 * keep_a_ref.shape[0], flat_ref.shape[0])
    for place, refs in enumerate(((keep_a_ref, keep_b_ref), (give_a_ref, give_b_ref))):
        for number in range(keep_a_ref.shape[0]):
            for bit in range(2):
                first = firsts[2 * number + bit]

                @pl.when(bit_ref[0] ^ place == bit)
                def copy(refs=refs, number=number, first=first):
                    refs[0][number] = flat_ref[first : first + half]
                    refs[1][number, : count - half] = flat_ref[first + half : first + count]

            blank = refs[1].shape[1] - (count - half)
            refs[1][number, count - half :] = jnp.broadcast_to(loss_ref[...], (blank, L))


def windows(regions, flat_rows):
    size = int(flat_rows * L) // regions
    firsts = [number * size // L for number in range(regions)]
    return firsts, max(-(-(number + 1) * size // L) - first for number, first in enumerate(firsts))


def node_grads(weights, start, node_rows, table_t, node_features, events, grads, loss, regions):
    flat_rows = EVENT_ROW + events.shape[0]
    nodes = grads[0].shape[0] * grads[0].shape[1]
    rows_out = -(-(windows(regions, flat_rows)[1] + 1) // 8) * 8
    half = rows_out // 16 * 8
    return kernel_call(
        node_kernel,
        [array_of((regions // 2, rows, L)) for rows in (half, rows_out - half)] * 2,
        [start, my_bit("ev", 0)[None], *node_rows, table_t, events, *grads, loss, *weights, node_features],
        [
            ((flat_rows, L), jnp.float32),
            ((nodes, L), jnp.float32),
            ((3, -(-(MSG + D + 2) // 8) * 8, L), jnp.float32),
            ((nodes, 4 * L), jnp.bfloat16),
            ((nodes, 4 * L), jnp.bfloat16),
            ((nodes, 2 * L), jnp.bfloat16),
            ((nodes, L), jnp.float32),
            ((node_features.shape[0], nodes), jnp.bfloat16),
            ((MSG_PAD, 3 * L), jnp.bfloat16),
            ((L, 3 * L), jnp.bfloat16),
            ((8, 3 * L), jnp.float32),
            ((1, nodes), jnp.float32),
        ],
        flops=8 * 10**9,
    )


def partner(array, name, bit):
    size = lax.axis_size(name)
    return lax.ppermute(array, name, [(i, i ^ (1 << bit)) for i in range(size)])


def my_bit(name, bit):
    return (lax.axis_index(name) >> bit) & 1


def bits_of(name):
    return (lax.axis_size(name) - 1).bit_length()


def exchange(held, done, name, bit):
    other = partner(held, name, bit)
    mine_first = my_bit(name, bit) == 0
    done = sorted(done + [(name == "neg", -bit)])
    place = done.index((name == "neg", -bit))
    parts = [jnp.where(mine_first, held, other), jnp.where(mine_first, other, held)]
    return jnp.stack(parts, axis=place), done


def crossed(array, first, second):
    size = lax.axis_size("ev")
    return lax.ppermute(
        array, "ev", [(i, i ^ (1 << (second if i & 1 else first))) for i in range(size)]
    )


def gather_neg(shard):
    held, done = shard, []
    for bit in range(bits_of("neg")):
        held, done = exchange(held, done, "neg", bit)
    return held, done


def gather_ev(held, done, beside=()):
    high = bits_of("ev") - 1
    for bit in range(1, high - 1):
        held, done = exchange(held, done, "ev", bit)
    odd = my_bit("ev", 0) == 1
    low_set, high_set = my_bit("ev", high - 1) == 1, my_bit("ev", high) == 1
    first_set, second_set = jnp.where(odd, high_set, low_set), jnp.where(odd, low_set, high_set)
    other = crossed(held, high - 1, high)
    held = jnp.stack([jnp.where(first_set, other, held), jnp.where(first_set, held, other)])
    other = crossed(held, high, high - 1)
    zero, one = jnp.where(second_set, other, held), jnp.where(second_set, held, other)
    held = jnp.stack(
        [
            jnp.stack([zero[0], jnp.where(odd, one[0], zero[1])]),
            jnp.stack([jnp.where(odd, zero[1], one[0]), one[1]]),
        ]
    )
    done = sorted(done + [(False, -high), (False, 1 - high)])
    if beside:
        held, *beside = lax.optimization_barrier((held, *beside))
    held, done = exchange(held, done, "ev", 0)
    return held, beside


def reduce_bit(held, bits, bit):
    place = bits.index(bit)
    mine = my_bit("ev", bit)
    keep = lax.dynamic_index_in_dim(held, mine, place, keepdims=False)
    give = lax.dynamic_index_in_dim(held, 1 - mine, place, keepdims=False)
    return keep + partner(give, "ev", bit), [other for other in bits if other != bit]


def scatter_ev(keeps, gives):
    count = bits_of("ev")
    bits = list(reversed(range(1, count)))
    parts = []
    for keep, give in zip(keeps, gives):
        held, left = (keep + partner(give, "ev", 0)).reshape((2,) * (count - 1) + keep.shape[1:]), bits
        for bit in range(1, count - 2):
            held, left = reduce_bit(held, left, bit)
        parts.append((held, left))
    turns = parts[0][1]
    for turn in range(2):
        parts = [
            reduce_bit(part, left, turns[(turn + number) % 2])
            for number, (part, left) in enumerate(parts)
        ]
    return jnp.concatenate([part for part, left in parts], axis=-2)


def scatter_neg(blocks):
    count = bits_of("neg")
    held = blocks.reshape((2,) * count + blocks.shape[1:])
    for bit in range(count):
        mine, place = my_bit("neg", bit), count - 1 - bit
        keep = lax.dynamic_index_in_dim(held, mine, place, keepdims=False)
        give = lax.dynamic_index_in_dim(held, 1 - mine, place, keepdims=False)
        held = keep + partner(give, "neg", bit)
    return held


def lanes(flat):
    amount = flat.shape[-1]
    rows = -(-amount // 128)
    wide = jnp.pad(flat, [(0, 0)] * (flat.ndim - 1) + [(0, rows * 128 - amount)])
    return wide.reshape(flat.shape[:-1] + (rows, 128))


def from_digits(pairs, axis):
    pairs = pairs.astype(jnp.float32)
    high, low = (lax.index_in_dim(pairs, place, axis, keepdims=False) for place in (0, 1))
    return high * 128.0 + low


def on_device(
    master,
    first_moment,
    second_moment,
    memory,
    messages,
    static_ids,
    node_features,
    neighbours,
    neighbour_times,
    last_partner,
    last_deltas,
    last_edges,
    sources,
    targets,
    times,
    negatives,
    neg_counts,
):
    shard = master.shape[0]
    groups = lax.axis_size("neg")
    regions = lax.axis_size("ev")
    devices = regions * groups
    rank = lax.axis_index("neg")
    own_events = sources.shape[0]
    own_nodes = memory.shape[0]
    local_neg = negatives.shape[1]
    total_neg = local_neg * groups
    events_all = own_events * devices

    own_columns = by_lanes(negatives.T).reshape(-1, L)
    own_copy = lanes(master.astype(jnp.bfloat16))
    copy_rows = own_copy.shape[0]
    sent = jnp.concatenate(
        [own_copy, (own_columns >> 7).astype(jnp.bfloat16), (own_columns & 127).astype(jnp.bfloat16)]
    )
    copies, copies_done = exchange(sent, [], "neg", 0)
    copies, late_ids = lax.optimization_barrier((copies, static_ids))
    for bit in range(1, bits_of("neg")):
        copies, copies_done = exchange(copies, copies_done, "neg", bit)
    all_negatives = copies[..., copy_rows:, :].reshape(groups, -1, L)
    copies = copies[..., :copy_rows, :]

    rows, tail = pack(rank, neg_counts, static_ids, messages, memory, own_events // W)
    copies, rows, features = lax.optimization_barrier((copies, rows, node_features))
    high = bits_of("ev") - 1
    odd = my_bit("ev", 0) == 1
    far_neg = list(reversed(range(1, bits_of("neg"))))
    flips = [1 << bit for bit in far_neg] + [jnp.where(odd, 1 << (high - 2), 1 << (high - 1)) * groups]
    flips += [(1 << (bit - 1)) * groups for bit in range(1, high - 1)]
    start = ((lax.axis_index("ev") >> 1) * groups + rank)[None]
    for flip in flips:
        start = jnp.concatenate([start, start ^ flip])
    across = jnp.where(odd, 1 << (high - 1), 1 << (high - 2)) * groups
    start = jnp.concatenate([start, start ^ across, start ^ 1, start ^ across ^ 1]) * own_nodes
    for bit in far_neg:
        rows = jnp.concatenate([rows, partner(rows, "neg", bit)])

    ids, gaps, slots, valid, live = prepare(
        rank, sources, targets, times, neg_counts, all_negatives, neighbours, neighbour_times
    )
    copies, (valid, rows) = gather_ev(copies, copies_done, (valid, rows))
    rows = jnp.concatenate([rows, crossed(rows, high, high - 1)])
    for bit in range(1, high - 1):
        rows = jnp.concatenate([rows, partner(rows, "ev", bit)])

    flat = copies.reshape(devices, -1)[:, :shard].reshape(-1)
    early = unpack(flat)
    state, renewed = owner_pass(early, memory, messages, features[late_ids])
    sending = jnp.concatenate(
        [jnp.pad(state.astype(jnp.bfloat16), ((0, 0), (0, F - D))), tail[:, : L - F]], 1
    )
    flat, sending = lax.optimization_barrier((flat, sending))
    weights = event_weights(flat, NODE_PARAMS)
    table, table_done = gather_neg(sending)
    table, start, biases = lax.optimization_barrier((table, start, early["b_g"]))
    table, weights = gather_ev(table, table_done, weights)
    table = table.reshape(-1, L)

    def far_device(device):
        place, near = divmod(device, groups)
        return (place ^ (1 << (high if place & 1 else high - 1))) * groups + (near ^ 1)

    far_rows = [
        crossed(rows, high - 1, high),
        partner(rows, "neg", 0),
        lax.ppermute(rows, ("ev", "neg"), [(i, far_device(i)) for i in range(devices)]),
    ]
    table_t = table.T
    local_loss, neg_total, keep, give, grad_event = event_step(
        weights,
        table_t,
        (ids, gaps, slots, valid, live),
        regions,
        own_nodes,
        events_all,
        own_events // W,
    )
    give, far_rows, local_loss, grad_event = lax.optimization_barrier(
        (give, far_rows, local_loss, grad_event)
    )
    came = partner(give, "ev", 0)
    flat_rows = shard * devices // L
    event_flat = flat_events(grad_event, NODE_PARAMS, flat_rows)
    upper_kept, lower_kept, upper_given, lower_given = node_grads(
        (early["w_gi"], early["w_gh"], biases),
        start,
        [rows, *far_rows],
        table_t,
        features,
        event_flat,
        (keep, came),
        local_loss,
        regions,
    )
    block_rows = windows(regions, flat_rows)[1]
    summed = scatter_ev((upper_kept, lower_kept), (upper_given, lower_given))
    summed, last_partner, last_deltas = lax.optimization_barrier((summed, last_partner, last_deltas))
    if shard * groups % L:
        first = lax.axis_index("ev") * (shard * groups) % L
        values = lax.dynamic_slice_in_dim(summed[:block_rows].reshape(-1), first, shard * groups)
        values = lanes(values)
    else:
        values = summed[:block_rows]
    firsts, part_rows = windows(groups, shard * groups / L)
    values = jnp.pad(values, ((0, max(0, firsts[-1] + part_rows - values.shape[0])), (0, 0)))
    shares = jnp.stack(
        [
            jnp.concatenate([values[first : first + part_rows], summed[block_rows:][:1]])
            for first in firsts
        ]
    )
    totals = scatter_neg(shares)
    loss = jnp.sum(totals[part_rows])
    first = rank * shard % L
    grad_shard = lax.dynamic_slice_in_dim(totals[:part_rows].reshape(-1), first, shard)
    new_master, new_first, new_second = adamw(master, first_moment, second_moment, grad_shard)
    codes = jnp.cos(
        last_deltas[:, None] * early["w_time"].astype(jnp.float32)
        + early["b_time"].astype(jnp.float32)
    )
    carried = jnp.concatenate(
        [
            sending[:, :D].astype(jnp.float32),
            table[last_partner][:, :D].astype(jnp.float32),
            codes,
            last_edges.astype(jnp.float32),
        ],
        1,
    )
    return (loss, neg_total, new_master, new_first, new_second, renewed, carried)


def solution(mesh):
    return jax.shard_map(
        on_device,
        mesh=mesh,
        in_specs=(
            P(("ev", "neg")),
            P(("ev", "neg")),
            P(("ev", "neg")),
            P(("ev", "neg"), None),
            P(("ev", "neg"), None),
            P(("ev", "neg")),
            P(),
            P(),
            P(),
            P(("ev", "neg")),
            P(("ev", "neg")),
            P(("ev", "neg"), None),
            P(("ev", "neg")),
            P(("ev", "neg")),
            P("ev"),
            P("ev", "neg"),
            P("ev"),
        ),
        out_specs=(
            P(),
            P(),
            P(("ev", "neg")),
            P(("ev", "neg")),
            P(("ev", "neg")),
            P(("ev", "neg"), None),
            P(("ev", "neg"), None),
        ),
        check_vma=False,
    )
```
